32 devices in a mesh: req: 4 (over y, core), exp: 8 (over z, x).
Axes of the slice: x: 2, y: 2, z: 4, core: 2. Of those that a mesh axis runs over, the one named last changes fastest.
Arguments:
- resid: bfloat16 [2048, 2048], P(('req', 'exp')), may hold values from -27 to 27
- queries: bfloat16 [2048, 2048], P(('req', 'exp')), may hold values from -6 to 6
- cache_key: bfloat16 [64, 128, 2048], P(('req', 'exp')), may hold values from -6 to 6
- cache_value: bfloat16 [64, 128, 2048], P(('req', 'exp')), may hold values from -6 to 6
- page_table: int32 [16, 4], P('req'), may hold values from 0 to 15, as said below
- row_request: int32 [2048], P('req'), may hold values from 0 to 3, as said below
- row_position: int32 [2048], P('req'), may hold values from 0 to 511, as said below
- out_proj: bfloat16 [2048, 2048], P('exp'), may hold values from -0.375 to 0.375
- norm_gain: float32 [2048], replicated, may hold values from 0.5 to 1.5
- expert_gate: bfloat16 [32, 2048, 1408], P(('req', 'exp')), as said below
- expert_up: bfloat16 [32, 2048, 1408], P(('req', 'exp')), as said below
- expert_down: bfloat16 [32, 1408, 2048], P(('req', 'exp')), as said below
- shared_gate: bfloat16 [2048, 5632], P(None, 'exp'), may hold values from -0.125 to 0.125
- shared_up: bfloat16 [2048, 5632], P(None, 'exp'), may hold values from -0.125 to 0.125
- shared_down: bfloat16 [5632, 2048], P('exp'), may hold values from -0.078125 to 0.078125
- shared_scalar: bfloat16 [2048], replicated, may hold values from -0.375 to 0.375
- slot_expert: int32 [32], replicated, may hold values from 0 to 14, as said below
- route_expert: int32 [2048, 4], replicated, may hold values from 0 to 14, as said below
- route_gate: float32 [2048, 4], P(('req', 'exp')), may hold values from 0.05 to 0.5
Outputs:
- output: bfloat16 [2048, 2048], P(('req', 'exp'))
The draws below stay inside these ranges and needn't reach their ends.
Inputs may be any that keep to these rules, and one draw needn't show every extreme that they name: `page_table`: within each request group the table names each of the group's 16 pages once; page p of group g lies on the device of req index g and exp index p // 2. `row_request`: each group's rows are in order of request; every request has one row or more; half of the requests of a group have exactly one row. `row_position`: the rows of one request hold consecutive positions ending at the request's length minus one. `slot_expert`: every expert is held by one slot or more. `route_expert`: each row names 4 different experts. In each aligned block of 64 rows (the rows of one device) no expert is named more than 24 times, and one expert is named exactly 24 times in every block. `expert_gate`: slots that hold the same expert hold equal weights. `expert_up`: slots that hold the same expert hold equal weights. `expert_down`: slots that hold the same expert hold equal weights.
All inputs are finite; a program needn't handle non-finite values.
Results may differ from the reference program's by a relative error of at most 0.006.
Values may be sent and summed in bfloat16 or wider, within the bound.
No kernel may reach another device: no remote copies, remote signals or barrier semaphores. Data moves between devices by JAX's collectives and lax.ppermute only.
A program may use at most 128 MiB of HBM per device.

```python
import math
import jax
import jax.numpy as jnp
from jax import lax

D = 2048
HEADS = 16
HEAD_DIM = 128
FF = 1408
SH_FF = 5632
TOPK = 4
PAGE = 128
TOK_DEV = 64
REQS_G = 4
GROUPS = 4
GROUP_ROWS = 512
ROWS = 2048
SLOTS = 32
EXPERTS = 15
CAP = 24
PAGES_G = 16
MAXP = 4


def group_layout(key):
    half = REQS_G // 2
    key_order, key_spread, key_length, key_table = jax.random.split(key, 4)
    requests = jax.random.permutation(key_order, REQS_G).astype(jnp.int32)
    prefill_total = GROUP_ROWS - half
    base = prefill_total // half
    spread = jax.random.randint(key_spread, (half // 2,), -(base // 4), base // 4 + 1)
    deltas = jnp.stack([spread, -spread], axis=1).reshape(-1)
    prefill_counts = (base + deltas).at[half - 1].add(prefill_total - base * half).astype(jnp.int32)
    counts = jnp.zeros((REQS_G,), jnp.int32).at[requests[:half]].set(1).at[requests[half:]].set(prefill_counts)
    full = MAXP * PAGE
    lengths = jax.random.randint(key_length, (REQS_G,), counts, full + 1).astype(jnp.int32)
    lengths = lengths.at[requests[0]].set(full).at[requests[half]].set(counts[requests[half]])
    starts = jnp.cumsum(counts) - counts
    row_ids = jnp.arange(GROUP_ROWS, dtype=jnp.int32)
    request = jnp.sum((row_ids[:, None] >= starts[None, :]).astype(jnp.int32), axis=1) - 1
    position = lengths[request] - counts[request] + row_ids - starts[request]
    table = jax.random.permutation(key_table, PAGES_G).astype(jnp.int32).reshape(REQS_G, MAXP)
    return (table, request.astype(jnp.int32), position.astype(jnp.int32))


def all_layouts(key):
    base_key = jax.random.fold_in(key, 11)
    return jax.vmap(lambda group: group_layout(jax.random.fold_in(base_key, group)))(jnp.arange(GROUPS))


def draw_page_table(key, part):
    return all_layouts(key)[0].reshape(GROUPS * REQS_G, MAXP)


def draw_row_request(key, part):
    return all_layouts(key)[1].reshape(ROWS)


def draw_row_position(key, part):
    return all_layouts(key)[2].reshape(ROWS)


def hot_expert(key):
    return jax.random.randint(jax.random.fold_in(key, 3), (), 0, EXPERTS)


def draw_slot_expert(key, part):
    key_pick, key_order = jax.random.split(jax.random.fold_in(key, 5))
    extra = SLOTS - EXPERTS
    picks = jax.random.randint(key_pick, (extra,), 0, EXPERTS)
    picks = jnp.where(jnp.arange(extra) % 4 == 0, hot_expert(key), picks)
    holders = jnp.concatenate([jnp.arange(EXPERTS), picks]).astype(jnp.int32)
    return jax.random.permutation(key_order, holders)


def draw_route_expert(key, part):
    hot = hot_expert(key)
    others = (hot + 1 + jnp.arange(EXPERTS - 1)) % EXPERTS
    block_key = jax.random.fold_in(key, 17)

    def block(index):
        key_map, key_rows = jax.random.split(jax.random.fold_in(block_key, index))
        mapping = jax.random.permutation(key_map, others)
        cycle = (jnp.arange(TOK_DEV)[:, None] * TOPK + jnp.arange(TOPK)[None, :]) % (EXPERTS - 1)
        chosen = mapping[cycle]
        marked = jnp.zeros((TOK_DEV,), jnp.int32).at[jax.random.permutation(key_rows, TOK_DEV)[:CAP]].set(1)
        first = jnp.where(marked == 1, hot, chosen[:, 0])
        return jnp.concatenate([first[:, None], chosen[:, 1:]], axis=1).astype(jnp.int32)
    return jax.vmap(block)(jnp.arange(SLOTS)).reshape(ROWS, TOPK)


def expert_tensor(key, salt, shape, fan_in):
    holders = draw_slot_expert(key, 0)
    salt_key = jax.random.fold_in(key, salt)

    def one(expert):
        values = jax.random.normal(jax.random.fold_in(salt_key, expert), shape, jnp.float32)
        return jnp.clip(values, -6.0, 6.0) * fan_in ** (-0.5)
    return jax.vmap(one)(holders)


def draw_expert_gate(key, part):
    return expert_tensor(key, 41, (D, FF), D).astype(jnp.bfloat16)


def draw_expert_up(key, part):
    return expert_tensor(key, 43, (D, FF), D).astype(jnp.bfloat16)


def draw_expert_down(key, part):
    return expert_tensor(key, 47, (FF, D), FF).astype(jnp.bfloat16)


def draw_queries(key, part):
    noise_key = jax.random.fold_in(key, 21)
    return jnp.clip(1.5 * jax.random.normal(noise_key, (ROWS, D), jnp.float32), -6.0, 6.0).astype(jnp.bfloat16)


def draw_cache_key(key, part):
    noise_key = jax.random.fold_in(key, 23)
    shape = (GROUPS * PAGES_G, PAGE, D)
    return jnp.clip(jax.random.normal(noise_key, shape, jnp.float32), -6.0, 6.0).astype(jnp.bfloat16)


def draw_resid(key, part):
    key_rows, key_cols, key_noise = jax.random.split(jax.random.fold_in(key, 31), 3)
    low = math.log(0.3)
    high = math.log(3.0)
    row_scale = jnp.exp(jax.random.uniform(key_rows, (ROWS, 1), jnp.float32, low, high))
    col_scale = jnp.exp(jax.random.uniform(key_cols, (1, D), jnp.float32, low, high))
    noise = jnp.clip(jax.random.normal(key_noise, (ROWS, D), jnp.float32), -3.0, 3.0)
    return (noise * row_scale * col_scale).astype(jnp.bfloat16)


def shard_levels(stream_key, dims, cuts, least, high):
    def one(axis_at, blocks):
        steps = jax.random.uniform(jax.random.fold_in(jax.random.fold_in(stream_key, 6), axis_at), (blocks,), jnp.float32, least / len(cuts), high / len(cuts))
        return jnp.repeat(jnp.exp(steps), dims[axis_at] // blocks).reshape((-1,) + (1,) * (len(dims) - axis_at - 1))

    factor_of = one(*cuts[0])
    for cut in cuts[1:]:
        factor_of = factor_of * one(*cut)
    return factor_of


def scatter_about(own_key, extent, scale, most, pieces=(), kind=jnp.bfloat16):
    drawn = scale * jax.random.normal(own_key, extent, jnp.float32)
    if pieces:
        drawn = drawn * shard_levels(own_key, extent, pieces, -0.22, 0.18)
    return jnp.clip(drawn, -most, most).astype(kind)


def setup_inputs(seed: int = 0) -> dict:
    splits = jax.random.split(jax.random.key(seed), 20)
    resid = draw_resid(jax.random.fold_in(splits[19], 71), 0)
    queries = draw_queries(jax.random.fold_in(splits[19], 71), 0)
    cache_key = draw_cache_key(jax.random.fold_in(splits[19], 71), 0)
    cache_value = scatter_about(splits[3], (GROUPS * PAGES_G, PAGE, D), 1.0, 6.0, ((0, 32),))
    page_table = draw_page_table(jax.random.fold_in(splits[19], 71), 0)
    row_request = draw_row_request(jax.random.fold_in(splits[19], 71), 0)
    row_position = draw_row_position(jax.random.fold_in(splits[19], 71), 0)
    out_proj = scatter_about(splits[7], (D, D), (D // 8) ** -0.5, 0.375, ((0, 8),))
    norm_gain = jnp.clip(1.0 + 0.1 * jax.random.normal(splits[8], (D,), jnp.float32), 0.5, 1.5)
    expert_gate = draw_expert_gate(jax.random.fold_in(splits[19], 71), 0)
    expert_up = draw_expert_up(jax.random.fold_in(splits[19], 71), 0)
    expert_down = draw_expert_down(jax.random.fold_in(splits[19], 71), 0)
    shared_gate = scatter_about(splits[12], (D, SH_FF), D ** -0.5, 0.125, ((1, 8),))
    shared_up = scatter_about(splits[13], (D, SH_FF), D ** -0.5, 0.125, ((1, 8),))
    shared_down = scatter_about(splits[14], (SH_FF, D), SH_FF ** -0.5, 0.078125, ((0, 8),))
    shared_scalar = scatter_about(splits[15], (D,), (D // 8) ** -0.5, 0.375)
    slot_expert = draw_slot_expert(jax.random.fold_in(splits[19], 71), 0)
    route_expert = draw_route_expert(jax.random.fold_in(splits[19], 71), 0)
    route_gate = jnp.clip(jnp.exp(math.log(0.5) - 2.3025851 * jax.random.uniform(splits[18], (ROWS, TOPK), jnp.float32) ** shard_levels(splits[18], (ROWS, TOPK), ((0, 32),), -0.2, 0.2)), 0.05, 0.5)
    return dict(resid=resid, queries=queries, cache_key=cache_key, cache_value=cache_value, page_table=page_table, row_request=row_request, row_position=row_position, out_proj=out_proj, norm_gain=norm_gain, expert_gate=expert_gate, expert_up=expert_up, expert_down=expert_down, shared_gate=shared_gate, shared_up=shared_up, shared_down=shared_down, shared_scalar=shared_scalar, slot_expert=slot_expert, route_expert=route_expert, route_gate=route_gate)


def expert_block(rows, gate_w, up_w, down_w):
    gate = jnp.dot(rows, gate_w, preferred_element_type=jnp.float32)
    upper = jnp.dot(rows, up_w, preferred_element_type=jnp.float32)
    hidden = (jax.nn.silu(gate) * upper).astype(jnp.bfloat16)
    return jnp.dot(hidden, down_w, preferred_element_type=jnp.float32).astype(jnp.bfloat16)

def group_attention(inputs):
    query_rows, keys, values, table, request, position = inputs
    page_ids = jnp.arange(PAGES_G, dtype=jnp.int32)
    hits = (table[None, :, :] == page_ids[:, None, None]).astype(jnp.int32)
    page_request = lax.optimization_barrier(jnp.sum(hits * jnp.arange(REQS_G, dtype=jnp.int32)[None, :, None], axis=(1, 2)))
    page_slot = lax.optimization_barrier(jnp.sum(hits * jnp.arange(MAXP, dtype=jnp.int32)[None, None, :], axis=(1, 2)))
    key_position = (page_slot[:, None] * PAGE + jnp.arange(PAGE, dtype=jnp.int32)[None, :]).reshape(-1)
    key_request = jnp.repeat(page_request, PAGE)
    visible = (request[:, None] == key_request[None, :]) & (key_position[None, :] <= position[:, None])
    query_heads = query_rows.astype(jnp.float32).reshape(GROUP_ROWS, HEADS, HEAD_DIM)
    key_heads = keys.astype(jnp.float32).reshape(PAGES_G * PAGE, HEADS, HEAD_DIM)
    value_heads = values.astype(jnp.float32).reshape(PAGES_G * PAGE, HEADS, HEAD_DIM)
    scores = jnp.einsum('rhd,khd->hrk', query_heads, key_heads) * HEAD_DIM ** (-0.5)
    scores = jnp.where(visible[None], scores, -1e+30)
    top = lax.optimization_barrier(jnp.max(scores, axis=2))
    weights = jnp.where(visible[None], jnp.exp(scores - top[:, :, None]), 0.0)
    denominators = jnp.transpose(lax.optimization_barrier(jnp.sum(weights, axis=2)))
    rounded = weights.astype(jnp.bfloat16).astype(jnp.float32)
    numerators = jnp.einsum('hrk,khd->rhd', rounded, value_heads)
    attention = numerators / denominators[:, :, None]
    return attention.reshape(GROUP_ROWS, D).astype(jnp.bfloat16)

def reference(resid, queries, cache_key, cache_value, page_table, row_request, row_position, out_proj, norm_gain, expert_gate, expert_up, expert_down, shared_gate, shared_up, shared_down, shared_scalar, slot_expert, route_expert, route_gate):
    attention = lax.map(group_attention, (queries.reshape(GROUPS, GROUP_ROWS, D), cache_key.reshape(GROUPS, PAGES_G, PAGE, D), cache_value.reshape(GROUPS, PAGES_G, PAGE, D), page_table.reshape(GROUPS, REQS_G, MAXP), row_request.reshape(GROUPS, GROUP_ROWS), row_position.reshape(GROUPS, GROUP_ROWS))).reshape(ROWS, D)
    stream = resid.astype(jnp.float32) + jnp.dot(attention, out_proj, preferred_element_type=jnp.float32)
    scale_row = lax.rsqrt(lax.optimization_barrier(jnp.mean(stream * stream, axis=1, keepdims=True)) + 1e-06)
    normed = (stream * scale_row * norm_gain[None, :]).astype(jnp.bfloat16)
    shared_hidden = (jax.nn.silu(jnp.dot(normed, shared_gate, preferred_element_type=jnp.float32)) * jnp.dot(normed, shared_up, preferred_element_type=jnp.float32)).astype(jnp.bfloat16)
    shared_out = jnp.dot(shared_hidden, shared_down, preferred_element_type=jnp.float32)
    shared_scale = jax.nn.sigmoid(jnp.dot(normed, shared_scalar, preferred_element_type=jnp.float32))
    entries = ROWS * TOPK
    flat_expert = route_expert.reshape(-1)
    flat_row = jnp.arange(entries, dtype=jnp.int32) // TOPK
    flat_gate = route_gate.reshape(-1)
    order = jnp.argsort(flat_expert, stable=True).astype(jnp.int32)
    expert_ids = jnp.arange(EXPERTS, dtype=jnp.int32)
    counts = lax.optimization_barrier(jnp.sum((flat_expert[:, None] == expert_ids[None, :]).astype(jnp.int32), axis=0))
    starts = jnp.cumsum(counts) - counts
    limit = SLOTS * CAP

    def one_expert(total, expert):
        offsets = jnp.arange(limit, dtype=jnp.int32)
        picked = order[jnp.minimum(starts[expert] + offsets, entries - 1)]
        valid = offsets < counts[expert]
        holder = jnp.argmax(slot_expert == expert)
        rows = normed[flat_row[picked]]
        result = expert_block(rows, expert_gate[holder], expert_up[holder], expert_down[holder])
        term = jnp.where(valid[:, None], result.astype(jnp.float32) * flat_gate[picked][:, None], 0.0)
        return (total.at[flat_row[picked]].add(term), None)
    routed, _ = lax.scan(one_expert, jnp.zeros((ROWS, D), jnp.float32), expert_ids)
    return (stream + shared_scale[:, None] * shared_out + routed).astype(jnp.bfloat16)
```

```python
import functools
import math

import jax
import jax.numpy as jnp
from jax import lax
from jax.experimental import pallas as pl
from jax.experimental.pallas import tpu as pltpu
from jax.sharding import PartitionSpec as P

HEAD_DIM = 128
TOPK = 4
CORES = 2
Z_CHIPS = 4


def attend_kernel(
    tokens, tok_rows, scale, order, moved, row_req, row_pos, key_req, key_pos, proj, out
):
    step = pl.program_id(0)
    sources = [order[step * 2], order[step * 2 + 1]]
    holders = moved.shape[0]
    columns = moved.shape[2]
    request = jnp.concatenate([row_req[s] for s in sources], axis=0)
    position = jnp.concatenate([row_pos[s] for s in sources], axis=0)
    visible = (request == key_req[...]) & (key_pos[...] <= position)
    parts = []
    for head in range(columns // HEAD_DIM):
        cols = slice(head * HEAD_DIM, (head + 1) * HEAD_DIM)
        query = jnp.concatenate([moved[s, 2 * tokens :, cols] for s in sources], axis=0)
        keys = moved[:, :tokens, cols].reshape(holders * tokens, HEAD_DIM)
        values = moved[:, tokens : 2 * tokens, cols].reshape(holders * tokens, HEAD_DIM)
        scores = (
            lax.dot_general(
                query, keys, (((1,), (1,)), ((), ())), preferred_element_type=jnp.float32
            )
            * scale
        )
        scores = jnp.where(visible, scores, -1e30)
        top = jnp.max(scores, axis=1, keepdims=True)
        weights = jnp.where(visible, jnp.exp(scores - top), 0.0)
        total = jnp.sum(weights, axis=1, keepdims=True)
        summed = jnp.dot(
            weights.astype(jnp.bfloat16), values, preferred_element_type=jnp.float32
        )
        parts.append((summed / total).astype(jnp.bfloat16))
    attention = jnp.concatenate(parts, axis=1) if len(parts) > 1 else parts[0]
    out[...] = jnp.dot(attention, proj[...], preferred_element_type=jnp.float32).astype(
        jnp.bfloat16
    )


def attend(moved, order, row_request, row_position, key_request, key_position, proj, tokens):
    holders, _, columns = moved.shape
    tok_rows = moved.shape[1] - 2 * tokens
    width = proj.shape[1]
    keys = holders * tokens
    whole = lambda *shape: pl.BlockSpec(shape, lambda i, order: (0,) * len(shape))
    return pl.pallas_call(
        functools.partial(attend_kernel, tokens, tok_rows, HEAD_DIM ** (-0.5)),
        out_shape=jax.ShapeDtypeStruct((holders * tok_rows, width), jnp.bfloat16),
        grid_spec=pltpu.PrefetchScalarGridSpec(
            num_scalar_prefetch=1,
            grid=(holders // 2,),
            in_specs=[
                whole(*moved.shape),
                whole(holders, tok_rows, 1),
                whole(holders, tok_rows, 1),
                whole(1, keys),
                whole(1, keys),
                whole(*proj.shape),
            ],
            out_specs=pl.BlockSpec((2 * tok_rows, width), lambda i, order: (i, 0)),
        ),
        compiler_params=pltpu.CompilerParams(vmem_limit_bytes=48 * 1024 * 1024),
        cost_estimate=pl.CostEstimate(
            flops=4 * holders * tok_rows * (keys * columns + columns * width),
            bytes_accessed=2 * (moved.size + proj.size + holders * tok_rows * width),
            transcendentals=holders * tok_rows * keys * columns // HEAD_DIM,
        ),
    )(
        order,
        moved,
        row_request.reshape(holders, tok_rows, 1),
        row_position.reshape(holders, tok_rows, 1),
        key_request.reshape(1, keys),
        key_position.reshape(1, keys),
        proj,
    )


def rms_normed(stream, norm_gain):
    scale_row = lax.rsqrt(jnp.mean(stream * stream, axis=1, keepdims=True) + 1e-06)
    return (stream * scale_row * norm_gain[None, :]).astype(jnp.bfloat16)


def shards(
    resid,
    queries,
    cache_key,
    cache_value,
    page_table,
    row_request,
    row_position,
    out_proj,
    norm_gain,
    expert_gate,
    expert_up,
    expert_down,
    shared_gate,
    shared_up,
    shared_down,
    shared_scalar,
    slot_expert,
    route_expert,
    route_gate,
):
    f32, bf16, i32 = jnp.float32, jnp.bfloat16, jnp.int32
    exp_count = lax.axis_size("exp")
    req_count = lax.axis_size("req")
    slot_count = exp_count * req_count
    nz, nc = math.gcd(Z_CHIPS, exp_count), CORES
    nx, ny = exp_count // nz, req_count // nc
    exp_index = lax.axis_index("exp")
    req_index = lax.axis_index("req")
    own_slot = req_index * exp_count + exp_index
    iz, ix = exp_index // nx, exp_index % nx
    iy, ic = req_index // nc, req_index % nc
    tok_rows, width = resid.shape
    pages_here, page_len, _ = cache_key.shape
    req_slots, max_pages = page_table.shape
    tokens = pages_here * page_len
    capacity = 3 * tok_rows * TOPK // slot_count

    def shift(value, along, by):
        if along in "zx":
            pairs = [
                (
                    z * nx + x,
                    ((z + by) % nz) * nx + x if along == "z" else z * nx + (x + by) % nx,
                )
                for z in range(nz)
                for x in range(nx)
            ]
            return lax.ppermute(value, "exp", pairs)
        pairs = [
            (
                y * nc + c,
                ((y + by) % ny) * nc + c if along == "y" else y * nc + (c + by) % nc,
            )
            for y in range(ny)
            for c in range(nc)
        ]
        return lax.ppermute(value, "req", pairs)

    rel_exp = jnp.stack(
        [((iz - dz) % nz) * nx + (ix - dx) % nx for dz in range(nz) for dx in range(nx)]
    ).astype(i32)
    rel_req = jnp.stack(
        [((iy - dy) % ny) * nc + (ic - dc) % nc for dy in range(ny) for dc in range(nc)]
    ).astype(i32)

    columns = width // exp_count
    by_heads = lambda a: jnp.transpose(a.reshape(-1, exp_count, columns), (1, 0, 2))
    moved = lax.all_to_all(
        jnp.concatenate([by_heads(cache_key), by_heads(cache_value), by_heads(queries)], axis=1),
        "exp",
        split_axis=0,
        concat_axis=0,
        tiled=True,
    )
    page_ids = jnp.arange(pages_here * exp_count, dtype=i32)
    hits = (page_table[None, :, :] == page_ids[:, None, None]).astype(i32)
    page_request = jnp.sum(hits * jnp.arange(req_slots, dtype=i32)[None, :, None], axis=(1, 2))
    page_slot = jnp.sum(hits * jnp.arange(max_pages, dtype=i32)[None, None, :], axis=(1, 2))
    key_position = page_slot[:, None] * page_len + jnp.arange(page_len, dtype=i32)[None, :]
    key_request = jnp.broadcast_to(page_request[:, None], key_position.shape)
    mixed = attend(
        moved, rel_exp, row_request, row_position, key_request, key_position, out_proj, tokens
    ).reshape(nz, nx, tok_rows, width)

    total = resid.astype(f32)
    for dz in reversed(range(nz)):
        line = mixed[dz, 0].astype(f32)
        for dx in range(1, nx):
            line = line + shift(mixed[dz, dx], "x", -dx).astype(f32)
        total = total + (shift(line.astype(bf16), "z", -dz).astype(f32) if dz else line)
    stream = total
    normed = rms_normed(stream, norm_gain)

    slot_ids = jnp.arange(slot_count, dtype=i32)
    own_mark = slot_ids == own_slot
    own_expert = jnp.sum(jnp.where(own_mark, slot_expert, 0))
    twins = slot_expert == own_expert
    copies = jnp.sum(twins.astype(i32))
    own_rank = jnp.sum((twins & (slot_ids < own_slot)).astype(i32))
    named = route_expert == own_expert
    all_gates = lax.all_gather(route_gate, ("req", "exp"), axis=0, tiled=True)
    row_gate = jnp.sum(jnp.where(named, all_gates, 0.0), axis=1).reshape(slot_count, tok_rows)
    mine = (
        jnp.any(named, axis=1).reshape(slot_count, tok_rows)
        & (slot_ids % copies == own_rank)[:, None]
    )
    rel_slots = (rel_req[:, None] * exp_count + rel_exp[None, :]).reshape(-1)
    chunk_rows = exp_count * tok_rows
    entries = exp_count * capacity
    row_gate = row_gate[rel_slots].reshape(req_count, chunk_rows)
    mine = mine[rel_slots].reshape(req_count, chunk_rows)
    place = jnp.cumsum(mine.astype(i32), axis=1) - 1
    pick = (
        (place[:, None, :] == jnp.arange(entries, dtype=i32)[None, :, None]) & mine[:, None, :]
    ).astype(bf16)

    piece = {}
    for dz in range(nz):
        piece[dz, 0, 0] = shift(normed, "z", dz) if dz else normed
    x_first = {dz: dz < (nz + 1) // 2 for dz in range(nz)}
    for dz in range(nz):
        if x_first[dz]:
            for dx in range(1, nx):
                piece[dz, dx, 0] = shift(piece[dz, 0, 0], "x", dx)
            for dx in range(nx):
                for dy in range(1, ny):
                    piece[dz, dx, dy] = shift(piece[dz, dx, 0], "y", dy)
        else:
            for dx in range(1, nx):
                piece[dz, dx, 0] = shift(piece[dz, 0, 0], "x", dx)
            for dy in range(1, ny):
                piece[dz, 0, dy] = shift(piece[dz, 0, 0], "y", dy)
                for dx in range(1, nx):
                    piece[dz, dx, dy] = shift(piece[dz, 0, dy], "x", dx)
    chunks = {}
    for dy in range(ny):
        chunks[dy, 0] = jnp.concatenate(
            [piece[dz, dx, dy] for dz in range(nz) for dx in range(nx)], axis=0
        )
        for dc in range(1, nc):
            chunks[dy, dc] = shift(chunks[dy, 0], "core", dc)

    def routed(dy, dc):
        index = dy * nc + dc
        rows = jnp.dot(pick[index], chunks[dy, dc], preferred_element_type=f32).astype(bf16)
        gate = jnp.dot(rows, expert_gate[0], preferred_element_type=f32)
        upper = jnp.dot(rows, expert_up[0], preferred_element_type=f32)
        hidden = (jax.nn.silu(gate) * upper).astype(bf16)
        answer = jnp.dot(hidden, expert_down[0], preferred_element_type=f32).astype(bf16)
        placed = lax.dot_general(
            pick[index], answer, (((0,), (0,)), ((), ())), preferred_element_type=f32
        )
        return placed * row_gate[index][:, None]

    own = chunks[0, 0]
    gate = jnp.dot(own, shared_gate, preferred_element_type=f32)
    upper = jnp.dot(own, shared_up, preferred_element_type=f32)
    shared_hidden = (jax.nn.silu(gate) * upper).astype(bf16)
    shared_scale = jax.nn.sigmoid(jnp.dot(own, shared_scalar, preferred_element_type=f32))
    shared = shared_scale[:, None] * jnp.dot(
        shared_hidden, shared_down, preferred_element_type=f32
    )

    sums = {}
    for dy in range(ny):
        here = routed(dy, 0)
        if dy == 0:
            here = here + shared
        for dc in range(1, nc):
            here = here + shift(routed(dy, dc).astype(bf16), "core", -dc).astype(f32)
        here = here.astype(bf16).reshape(nz, nx, tok_rows, width)
        for dz in range(nz):
            for dx in range(nx):
                sums[dz, dx, dy] = here[dz, dx]
    total = stream
    for dz in reversed(range(nz)):
        line = {}
        if x_first[dz]:
            for dx in range(nx):
                line[dx] = sums[dz, dx, 0].astype(f32)
                for dy in range(1, ny):
                    line[dx] = line[dx] + shift(sums[dz, dx, dy], "y", -dy).astype(f32)
            out = line[0]
            for dx in range(1, nx):
                out = out + shift(line[dx].astype(bf16), "x", -dx).astype(f32)
        else:
            for dy in range(ny):
                line[dy] = sums[dz, 0, dy].astype(f32)
                for dx in range(1, nx):
                    line[dy] = line[dy] + shift(sums[dz, dx, dy], "x", -dx).astype(f32)
            out = line[0]
            for dy in range(1, ny):
                out = out + shift(line[dy].astype(bf16), "y", -dy).astype(f32)
        total = total + (shift(out.astype(bf16), "z", -dz).astype(f32) if dz else out)
    return total.astype(bf16)


def solution(mesh):
    placed = (
        P(("req", "exp"), None),
        P(("req", "exp"), None),
        P(("req", "exp"), None, None),
        P(("req", "exp"), None, None),
        P("req", None),
        P("req"),
        P("req"),
        P("exp", None),
        P(),
        P(("req", "exp"), None, None),
        P(("req", "exp"), None, None),
        P(("req", "exp"), None, None),
        P(None, "exp"),
        P(None, "exp"),
        P("exp", None),
        P(),
        P(),
        P(),
        P(("req", "exp"), None),
    )
    return jax.shard_map(
        shards, mesh=mesh, in_specs=placed, out_specs=P(("req", "exp"), None), check_vma=False
    )
```

```python
import functools
import math

import jax
import jax.numpy as jnp
from jax import lax
from jax.experimental import pallas as pl
from jax.experimental.pallas import tpu as pltpu
from jax.sharding import PartitionSpec as P

HEAD_DIM = 128
TOPK = 4
CORES = 2
Z_CHIPS = 4


def attend_kernel(
    tokens, tok_rows, scale, order, moved, row_req, row_pos, key_req, key_pos, proj, out
):
    step = pl.program_id(0)
    sources = [order[step * 2], order[step * 2 + 1]]
    holders = moved.shape[0]
    columns = moved.shape[2]
    request = jnp.concatenate([row_req[s] for s in sources], axis=0)
    position = jnp.concatenate([row_pos[s] for s in sources], axis=0)
    visible = (request == key_req[...]) & (key_pos[...] <= position)
    parts = []
    for head in range(columns // HEAD_DIM):
        cols = slice(head * HEAD_DIM, (head + 1) * HEAD_DIM)
        query = jnp.concatenate([moved[s, 2 * tokens :, cols] for s in sources], axis=0)
        keys = moved[:, :tokens, cols].reshape(holders * tokens, HEAD_DIM)
        values = moved[:, tokens : 2 * tokens, cols].reshape(holders * tokens, HEAD_DIM)
        scores = (
            lax.dot_general(
                query, keys, (((1,), (1,)), ((), ())), preferred_element_type=jnp.float32
            )
            * scale
        )
        scores = jnp.where(visible, scores, -1e30)
        top = jnp.max(scores, axis=1, keepdims=True)
        weights = jnp.where(visible, jnp.exp(scores - top), 0.0)
        total = jnp.sum(weights, axis=1, keepdims=True)
        summed = jnp.dot(
            weights.astype(jnp.bfloat16), values, preferred_element_type=jnp.float32
        )
        parts.append((summed / total).astype(jnp.bfloat16))
    attention = jnp.concatenate(parts, axis=1) if len(parts) > 1 else parts[0]
    out[...] = jnp.dot(attention, proj[...], preferred_element_type=jnp.float32).astype(
        jnp.bfloat16
    )


def attend(moved, order, row_request, row_position, key_request, key_position, proj, tokens):
    holders, _, columns = moved.shape
    blocks = order.shape[0]
    tok_rows = moved.shape[1] - 2 * tokens
    width = proj.shape[1]
    keys = holders * tokens
    whole = lambda *shape: pl.BlockSpec(shape, lambda i, order: (0,) * len(shape))
    return pl.pallas_call(
        functools.partial(attend_kernel, tokens, tok_rows, HEAD_DIM ** (-0.5)),
        out_shape=jax.ShapeDtypeStruct((blocks * tok_rows, width), jnp.bfloat16),
        grid_spec=pltpu.PrefetchScalarGridSpec(
            num_scalar_prefetch=1,
            grid=(blocks // 2,),
            in_specs=[
                whole(*moved.shape),
                whole(holders, tok_rows, 1),
                whole(holders, tok_rows, 1),
                whole(1, keys),
                whole(1, keys),
                whole(*proj.shape),
            ],
            out_specs=pl.BlockSpec((2 * tok_rows, width), lambda i, order: (i, 0)),
        ),
        compiler_params=pltpu.CompilerParams(vmem_limit_bytes=48 * 1024 * 1024),
        cost_estimate=pl.CostEstimate(
            flops=2 * blocks * tok_rows * columns * (2 * keys + width),
            bytes_accessed=2 * (moved.size + proj.size + blocks * tok_rows * width),
            transcendentals=blocks * tok_rows * keys * columns // HEAD_DIM,
        ),
    )(
        order,
        moved,
        row_request.reshape(holders, tok_rows, 1),
        row_position.reshape(holders, tok_rows, 1),
        key_request.reshape(1, keys),
        key_position.reshape(1, keys),
        proj,
    )


def join_kernel(count, *refs):
    parts, out, sems = refs[:count], refs[count], refs[count + 1]
    rows = parts[0].shape[0]
    copies = [
        pltpu.make_async_copy(part, out.at[pl.ds(i * rows, rows)], sems.at[i])
        for i, part in enumerate(parts)
    ]
    for copy in copies:
        copy.start()
    for copy in copies:
        copy.wait()


def join(parts):
    rows, width = parts[0].shape
    any_spec = pl.BlockSpec(memory_space=pl.ANY)
    return pl.pallas_call(
        functools.partial(join_kernel, len(parts)),
        out_shape=jax.ShapeDtypeStruct((len(parts) * rows, width), parts[0].dtype),
        in_specs=[any_spec] * len(parts),
        out_specs=any_spec,
        scratch_shapes=[pltpu.SemaphoreType.DMA((len(parts),))],
        cost_estimate=pl.CostEstimate(
            flops=0, bytes_accessed=4 * len(parts) * rows * width, transcendentals=0
        ),
    )(*parts)


def silu(value):
    return value / (1.0 + jnp.exp(-value))


def shared_kernel(rows, scalar, gate_w, up_w, down_w, out, gate_v, up_v, down_v, sems):
    copies = [
        pltpu.make_async_copy(src, dst, sems.at[i])
        for i, (src, dst) in enumerate(((gate_w, gate_v), (up_w, up_v), (down_w, down_v)))
    ]
    for copy in copies:
        copy.start()
    block = rows[...]
    logit = jnp.sum(
        block.astype(jnp.float32) * scalar[...].astype(jnp.float32), axis=1, keepdims=True
    )
    scale = 1.0 / (1.0 + jnp.exp(-logit))
    copies[0].wait()
    gate = jnp.dot(block, gate_v[...], preferred_element_type=jnp.float32)
    copies[1].wait()
    upper = jnp.dot(block, up_v[...], preferred_element_type=jnp.float32)
    hidden = (silu(gate) * upper).astype(jnp.bfloat16)
    copies[2].wait()
    result = jnp.dot(hidden, down_v[...], preferred_element_type=jnp.float32)
    out[...] = (scale * result).astype(jnp.bfloat16)


def shared_expert(rows, scalar, gate_w, up_w, down_w):
    any_spec = pl.BlockSpec(memory_space=pl.ANY)
    vmem = pl.BlockSpec(memory_space=pltpu.VMEM)
    return pl.pallas_call(
        shared_kernel,
        out_shape=jax.ShapeDtypeStruct(rows.shape, jnp.bfloat16),
        in_specs=[vmem, vmem, any_spec, any_spec, any_spec],
        out_specs=vmem,
        scratch_shapes=[
            pltpu.VMEM(gate_w.shape, jnp.bfloat16),
            pltpu.VMEM(up_w.shape, jnp.bfloat16),
            pltpu.VMEM(down_w.shape, jnp.bfloat16),
            pltpu.SemaphoreType.DMA((3,)),
        ],
        compiler_params=pltpu.CompilerParams(vmem_limit_bytes=48 * 1024 * 1024),
        cost_estimate=pl.CostEstimate(
            flops=6 * rows.shape[0] * gate_w.size,
            bytes_accessed=6 * gate_w.size + 4 * rows.size,
            transcendentals=rows.shape[0] * gate_w.shape[1],
        ),
    )(rows, scalar.reshape(1, -1), gate_w, up_w, down_w)


def routed_kernel(
    count, entries, *refs
):
    chunks, refs = refs[:count], refs[count:]
    place_row, place_col, row_gate, extra, gate_w, up_w, down_w = refs[:7]
    outs, refs = refs[7 : 7 + count], refs[7 + count :]
    packed, gate_v, up_v, down_v, sems = refs
    copies = [
        pltpu.make_async_copy(src.at[0], dst, sems.at[i])
        for i, (src, dst) in enumerate(((gate_w, gate_v), (up_w, up_v), (down_w, down_v)))
    ]
    for copy in copies:
        copy.start()
    size = chunks[0].shape[0]
    for c in range(count):
        wanted = lax.broadcasted_iota(jnp.int32, (entries, size), 0)
        pick = jnp.where(place_row[c] == wanted, 1.0, 0.0).astype(jnp.bfloat16)
        packed[c * entries : (c + 1) * entries, :] = jnp.dot(
            pick, chunks[c][...], preferred_element_type=jnp.float32
        ).astype(jnp.bfloat16)
    copies[0].wait()
    gate = jnp.dot(packed[...], gate_v[...], preferred_element_type=jnp.float32)
    copies[1].wait()
    upper = jnp.dot(packed[...], up_v[...], preferred_element_type=jnp.float32)
    hidden = (silu(gate) * upper).astype(jnp.bfloat16)
    copies[2].wait()
    answer = jnp.dot(hidden, down_v[...], preferred_element_type=jnp.float32).astype(
        jnp.bfloat16
    )
    for c in range(count):
        wanted = lax.broadcasted_iota(jnp.int32, (size, entries), 1)
        put = jnp.where(place_col[c] == wanted, 1.0, 0.0).astype(jnp.bfloat16)
        placed = row_gate[c] * jnp.dot(
            put,
            answer[c * entries : (c + 1) * entries, :],
            preferred_element_type=jnp.float32,
        )
        if c == 0 and extra.shape[0] == size:
            placed = placed + extra[...].astype(jnp.float32)
        outs[c][...] = placed.astype(jnp.bfloat16)


def routed_expert(chunks, place, row_gate, extra, gate_w, up_w, down_w, entries):
    count = len(chunks)
    size, width = chunks[0].shape
    hidden = gate_w.shape[2]
    any_spec = pl.BlockSpec(memory_space=pl.ANY)
    vmem = pl.BlockSpec(memory_space=pltpu.VMEM)
    if extra is None:
        extra = jnp.zeros((8, 128), jnp.bfloat16)
    return pl.pallas_call(
        functools.partial(routed_kernel, count, entries),
        out_shape=[jax.ShapeDtypeStruct((size, width), jnp.bfloat16)] * count,
        in_specs=[vmem] * (count + 4) + [any_spec] * 3,
        out_specs=[vmem] * count,
        scratch_shapes=[
            pltpu.VMEM((count * entries, width), jnp.bfloat16),
            pltpu.VMEM((width, hidden), jnp.bfloat16),
            pltpu.VMEM((width, hidden), jnp.bfloat16),
            pltpu.VMEM((hidden, width), jnp.bfloat16),
            pltpu.SemaphoreType.DMA((3,)),
        ],
        compiler_params=pltpu.CompilerParams(vmem_limit_bytes=56 * 1024 * 1024),
        cost_estimate=pl.CostEstimate(
            flops=2 * count * entries * (3 * gate_w.size + 2 * size * width),
            bytes_accessed=6 * gate_w.size + 4 * count * size * width,
            transcendentals=count * entries * hidden,
        ),
    )(
        *chunks,
        place.reshape(count, 1, size),
        place.reshape(count, size, 1),
        row_gate.reshape(count, size, 1),
        extra,
        gate_w,
        up_w,
        down_w,
    )


def rms_normed(stream, norm_gain):
    scale_row = lax.rsqrt(jnp.mean(stream * stream, axis=1, keepdims=True) + 1e-06)
    return (stream * scale_row * norm_gain[None, :]).astype(jnp.bfloat16)


def shards(
    resid,
    queries,
    cache_key,
    cache_value,
    page_table,
    row_request,
    row_position,
    out_proj,
    norm_gain,
    expert_gate,
    expert_up,
    expert_down,
    shared_gate,
    shared_up,
    shared_down,
    shared_scalar,
    slot_expert,
    route_expert,
    route_gate,
):
    f32, bf16, i32 = jnp.float32, jnp.bfloat16, jnp.int32
    exp_count = lax.axis_size("exp")
    req_count = lax.axis_size("req")
    slot_count = exp_count * req_count
    nz, nc = math.gcd(Z_CHIPS, exp_count), CORES
    nx, ny = exp_count // nz, req_count // nc
    exp_index = lax.axis_index("exp")
    req_index = lax.axis_index("req")
    own_slot = req_index * exp_count + exp_index
    iz, ix = exp_index // nx, exp_index % nx
    iy, ic = req_index // nc, req_index % nc
    tok_rows, width = resid.shape
    pages_here, page_len, _ = cache_key.shape
    req_slots, max_pages = page_table.shape
    tokens = pages_here * page_len
    capacity = 3 * tok_rows * TOPK // slot_count

    def shift(value, along, by):
        if along in "zx":
            pairs = [
                (
                    z * nx + x,
                    ((z + by) % nz) * nx + x if along == "z" else z * nx + (x + by) % nx,
                )
                for z in range(nz)
                for x in range(nx)
            ]
            return lax.ppermute(value, "exp", pairs)
        pairs = [
            (
                y * nc + c,
                ((y + by) % ny) * nc + c if along == "y" else y * nc + (c + by) % nc,
            )
            for y in range(ny)
            for c in range(nc)
        ]
        return lax.ppermute(value, "req", pairs)

    rel_exp = jnp.stack(
        [((iz - dz) % nz) * nx + (ix - dx) % nx for dz in range(nz) for dx in range(nx)]
    ).astype(i32)
    rel_req = jnp.stack(
        [((iy - dy) % ny) * nc + (ic - dc) % nc for dy in range(ny) for dc in range(nc)]
    ).astype(i32)

    columns = width // exp_count
    by_heads = lambda a: jnp.transpose(a.reshape(-1, exp_count, columns), (1, 0, 2))
    moved = lax.all_to_all(
        jnp.concatenate([by_heads(cache_key), by_heads(cache_value), by_heads(queries)], axis=1),
        "exp",
        split_axis=0,
        concat_axis=0,
        tiled=True,
    )
    page_ids = jnp.arange(pages_here * exp_count, dtype=i32)
    hits = (page_table[None, :, :] == page_ids[:, None, None]).astype(i32)
    page_request = jnp.sum(hits * jnp.arange(req_slots, dtype=i32)[None, :, None], axis=(1, 2))
    page_slot = jnp.sum(hits * jnp.arange(max_pages, dtype=i32)[None, None, :], axis=(1, 2))
    key_position = page_slot[:, None] * page_len + jnp.arange(page_len, dtype=i32)[None, :]
    key_request = jnp.broadcast_to(page_request[:, None], key_position.shape)
    slot_ids = jnp.arange(slot_count, dtype=i32)
    own_mark = slot_ids == own_slot
    own_expert = jnp.sum(jnp.where(own_mark, slot_expert, 0))
    twins = slot_expert == own_expert
    copies = jnp.sum(twins.astype(i32))
    own_rank = jnp.sum((twins & (slot_ids < own_slot)).astype(i32))
    gates = jnp.transpose(route_gate)
    gates = jnp.stack([shift(gates, "z", dz) if dz else gates for dz in range(nz)])
    gates = jnp.stack([shift(gates, "x", dx) if dx else gates for dx in range(nx)], axis=1)
    gates = jnp.stack([shift(gates, "y", dy) if dy else gates for dy in range(ny)])
    gates = jnp.stack([shift(gates, "core", dc) if dc else gates for dc in range(nc)], axis=1)
    gates = gates.reshape(slot_count, TOPK, tok_rows)
    rel_slots = (rel_req[:, None] * exp_count + rel_exp[None, :]).reshape(-1)
    named = (route_expert == own_expert).reshape(slot_count, tok_rows, TOPK)[rel_slots]
    named = jnp.transpose(named, (0, 2, 1))
    chunk_rows = exp_count * tok_rows
    entries = -(-exp_count * capacity // 16) * 16
    row_gate = jnp.sum(jnp.where(named, gates, 0.0), axis=1).reshape(ny, nc, chunk_rows)
    mine = jnp.any(named, axis=1) & (rel_slots % copies == own_rank)[:, None]
    mine = mine.reshape(ny, nc, chunk_rows)
    place = jnp.where(mine, jnp.cumsum(mine.astype(i32), axis=2) - 1, -1)
    moved, place, row_gate = lax.optimization_barrier((moved, place, row_gate))

    half = exp_count // 2
    mixed = [
        attend(moved, o, row_request, row_position, key_request, key_position, out_proj, tokens)
        .reshape(nz // 2, nx, tok_rows, width)
        for o in (rel_exp[:half], rel_exp[half:])
    ]

    total = resid.astype(f32)
    for dz in reversed(range(nz)):
        line = mixed[dz // (nz // 2)][dz % (nz // 2), 0].astype(f32)
        for dx in range(1, nx):
            line = line + shift(mixed[dz // (nz // 2)][dz % (nz // 2), dx], "x", -dx).astype(f32)
        total = total + (shift(line.astype(bf16), "z", -dz).astype(f32) if dz else line)
    stream = total
    normed = rms_normed(stream, norm_gain)

    piece = {}
    for dz in range(nz):
        piece[dz, 0, 0] = shift(normed, "z", dz) if dz else normed
    x_first = {dz: dz < (nz + 1) // 2 for dz in range(nz)}
    for dz in range(nz):
        if x_first[dz]:
            for dx in range(1, nx):
                piece[dz, dx, 0] = shift(piece[dz, 0, 0], "x", dx)
            for dx in range(nx):
                for dy in range(1, ny):
                    piece[dz, dx, dy] = shift(piece[dz, dx, 0], "y", dy)
        else:
            for dx in range(1, nx):
                piece[dz, dx, 0] = shift(piece[dz, 0, 0], "x", dx)
            for dy in range(1, ny):
                piece[dz, 0, dy] = shift(piece[dz, 0, 0], "y", dy)
                for dx in range(1, nx):
                    piece[dz, dx, dy] = shift(piece[dz, 0, dy], "x", dx)
    chunks = {}
    for dy in range(ny):
        chunks[dy, 0] = join([piece[dz, dx, dy] for dz in range(nz) for dx in range(nx)])
        for dc in range(1, nc):
            chunks[dy, dc] = shift(chunks[dy, 0], "core", dc)

    sums = {}
    for dy in range(ny):
        extra = None
        if dy == 0:
            extra = shared_expert(
                chunks[0, 0], shared_scalar, shared_gate, shared_up, shared_down
            )
        answers = routed_expert(
            [chunks[dy, dc] for dc in range(nc)],
            place[dy],
            row_gate[dy],
            extra,
            expert_gate,
            expert_up,
            expert_down,
            entries,
        )
        here = answers[0].astype(f32)
        for dc in range(1, nc):
            here = here + shift(answers[dc], "core", -dc).astype(f32)
        here = here.astype(bf16).reshape(nz, nx, tok_rows, width)
        for dz in range(nz):
            for dx in range(nx):
                sums[dz, dx, dy] = here[dz, dx]
    total = stream
    for dz in reversed(range(nz)):
        line = {}
        if x_first[dz]:
            for dx in range(nx):
                line[dx] = sums[dz, dx, 0].astype(f32)
                for dy in range(1, ny):
                    line[dx] = line[dx] + shift(sums[dz, dx, dy], "y", -dy).astype(f32)
            out = line[0]
            for dx in range(1, nx):
                out = out + shift(line[dx].astype(bf16), "x", -dx).astype(f32)
        else:
            for dy in range(ny):
                line[dy] = sums[dz, 0, dy].astype(f32)
                for dx in range(1, nx):
                    line[dy] = line[dy] + shift(sums[dz, dx, dy], "x", -dx).astype(f32)
            out = line[0]
            for dy in range(1, ny):
                out = out + shift(line[dy].astype(bf16), "y", -dy).astype(f32)
        total = total + (shift(out.astype(bf16), "z", -dz).astype(f32) if dz else out)
    return total.astype(bf16)


def solution(mesh):
    placed = (
        P(("req", "exp"), None),
        P(("req", "exp"), None),
        P(("req", "exp"), None, None),
        P(("req", "exp"), None, None),
        P("req", None),
        P("req"),
        P("req"),
        P("exp", None),
        P(),
        P(("req", "exp"), None, None),
        P(("req", "exp"), None, None),
        P(("req", "exp"), None, None),
        P(None, "exp"),
        P(None, "exp"),
        P("exp", None),
        P(),
        P(),
        P(),
        P(("req", "exp"), None),
    )
    return jax.shard_map(
        shards, mesh=mesh, in_specs=placed, out_specs=P(("req", "exp"), None), check_vma=False
    )
```

```python
import functools

import jax
import jax.numpy as jnp
from jax import lax
from jax.experimental import pallas as pl
from jax.experimental.pallas import tpu as pltpu
from jax.sharding import PartitionSpec as P

HEAD_DIM = 128
TOPK = 4
CORES = 2
Z_CHIPS = 4


def pack_kernel(order, *refs):
    parts, out = refs[:-1], refs[-1]
    at = 0
    for part in parts:
        rows = part.shape[0]
        out[at : at + rows, :] = part[...]
        at += rows


def pack(parts, order, columns):
    count = order.shape[0]
    rows = sum(p.shape[0] for p in parts)
    return pl.pallas_call(
        pack_kernel,
        out_shape=jax.ShapeDtypeStruct((rows, count * columns), parts[0].dtype),
        grid_spec=pltpu.PrefetchScalarGridSpec(
            num_scalar_prefetch=1,
            grid=(count,),
            in_specs=[
                pl.BlockSpec((p.shape[0], columns), lambda j, order: (0, order[j]))
                for p in parts
            ],
            out_specs=pl.BlockSpec((rows, columns), lambda j, order: (0, j)),
        ),
        cost_estimate=pl.CostEstimate(
            flops=0, bytes_accessed=4 * rows * count * columns, transcendentals=0
        ),
    )(order, *parts)


def attend_kernel(members, tokens, page_len, scale, page_req, page_slot, *refs):
    blocks, far, refs = refs[:members], refs[members : 2 * members], refs[2 * members :]
    row_req, row_pos, out, level = refs
    keys = jnp.concatenate([block[:tokens, :] for block in blocks], axis=0)
    values = jnp.concatenate([block[tokens : 2 * tokens, :] for block in blocks], axis=0)
    near = [block[2 * tokens :, :] for block in blocks]
    size = sum(q.shape[0] for q in near)
    for side, query in enumerate((near, [q[...] for q in far])):
        lanes = slice(side * size, (side + 1) * size)
        query = jnp.concatenate(query, axis=0)
        request, position = row_req[:, lanes], row_pos[:, lanes]
        scores = (
            lax.dot_general(
                keys, query, (((1,), (1,)), ((), ())), preferred_element_type=jnp.float32
            )
            * scale
        )
        token = lax.broadcasted_iota(jnp.int32, (page_len, size), 0)
        visible = jnp.concatenate(
            [
                (request == page_req[page]) & (token + page_slot[page] * page_len <= position)
                for page in range(members * tokens // page_len)
            ],
            axis=0,
        )
        scores = jnp.where(visible, scores, -1e30)
        top = jnp.max(scores, axis=0, keepdims=True)
        weights = jnp.where(visible, jnp.exp(scores - top), 0.0)
        total = jnp.sum(weights, axis=0, keepdims=True)
        summed = lax.dot_general(
            values,
            weights.astype(jnp.bfloat16),
            (((0,), (0,)), ((), ())),
            preferred_element_type=jnp.float32,
        )
        seen = total > 0.0
        total = jnp.where(seen, total, 1.0)
        out[:, lanes] = (summed / total).astype(jnp.bfloat16)
        level[0, :, lanes] = jnp.where(seen, top + jnp.log(total), -1e30)


def attend(blocks, far, row_req, row_pos, page_req, page_slot, page_len):
    members, rows = len(blocks), row_req.shape[1]
    block_rows, columns = blocks[0].shape
    tok_rows = far[0].shape[0]
    tokens = (block_rows - tok_rows) // 2
    heads = columns // HEAD_DIM
    by_head = lambda n: pl.BlockSpec((n, HEAD_DIM), lambda h, *_: (0, h))
    whole = pl.BlockSpec((1, rows), lambda h, *_: (0, 0))
    return pl.pallas_call(
        functools.partial(attend_kernel, members, tokens, page_len, HEAD_DIM ** (-0.5)),
        out_shape=[
            jax.ShapeDtypeStruct((columns, rows), jnp.bfloat16),
            jax.ShapeDtypeStruct((heads, 1, rows), jnp.float32),
        ],
        grid_spec=pltpu.PrefetchScalarGridSpec(
            num_scalar_prefetch=2,
            grid=(heads,),
            in_specs=[by_head(block_rows)] * members + [by_head(tok_rows)] * members + [whole] * 2,
            out_specs=[
                pl.BlockSpec((HEAD_DIM, rows), lambda h, *_: (h, 0)),
                pl.BlockSpec((1, 1, rows), lambda h, *_: (h, 0, 0)),
            ],
        ),
        compiler_params=pltpu.CompilerParams(vmem_limit_bytes=48 * 1024 * 1024),
        cost_estimate=pl.CostEstimate(
            flops=4 * rows * members * tokens * columns,
            bytes_accessed=2 * members * (block_rows + tok_rows) * columns,
            transcendentals=rows * members * tokens * heads,
        ),
    )(page_req, page_slot, *blocks, *far, row_req, row_pos)


def project_kernel(mine, mine_level, theirs, their_level, proj, out):
    parts = []
    for head in range(mine.shape[0] // HEAD_DIM):
        dims = slice(head * HEAD_DIM, (head + 1) * HEAD_DIM)
        share = 1.0 / (1.0 + jnp.exp(their_level[head] - mine_level[head]))
        other = 1.0 / (1.0 + jnp.exp(mine_level[head] - their_level[head]))
        both = share * mine[dims, :].astype(jnp.float32) + other * theirs[dims, :].astype(
            jnp.float32
        )
        parts.append(both.astype(jnp.bfloat16))
    attention = jnp.concatenate(parts, axis=0) if len(parts) > 1 else parts[0]
    out[...] = lax.dot_general(
        attention, proj[...], (((0,), (0,)), ((), ())), preferred_element_type=jnp.float32
    ).astype(jnp.bfloat16)


def project(mine, mine_level, theirs, their_level, proj):
    columns, width = proj.shape
    rows = mine.shape[1]
    heads = columns // HEAD_DIM
    size = rows // 4
    return pl.pallas_call(
        project_kernel,
        out_shape=jax.ShapeDtypeStruct((rows, width), jnp.bfloat16),
        grid=(4,),
        in_specs=[
            pl.BlockSpec((columns, size), lambda i: (0, i)),
            pl.BlockSpec((heads, 1, size), lambda i: (0, 0, i)),
            pl.BlockSpec((columns, size), lambda i: (0, (i + 2) % 4)),
            pl.BlockSpec((heads, 1, size), lambda i: (0, 0, (i + 2) % 4)),
            pl.BlockSpec((columns, width), lambda i: (0, 0)),
        ],
        out_specs=pl.BlockSpec((size, width), lambda i: (i, 0)),
        cost_estimate=pl.CostEstimate(
            flops=2 * rows * columns * width,
            bytes_accessed=2 * (2 * columns * rows + columns * width + rows * width),
            transcendentals=2 * rows * heads,
        ),
    )(mine, mine_level, theirs, their_level, proj)


def join_kernel(*refs):
    parts, out = refs[:-1], refs[-1]
    rows = parts[0].shape[0]
    for i, part in enumerate(parts):
        out[i * rows : (i + 1) * rows, :] = part[...]


def join(parts):
    rows, width = parts[0].shape
    vmem = pl.BlockSpec(memory_space=pltpu.VMEM)
    return pl.pallas_call(
        join_kernel,
        out_shape=jax.ShapeDtypeStruct((len(parts) * rows, width), parts[0].dtype),
        in_specs=[vmem] * len(parts),
        out_specs=vmem,
        cost_estimate=pl.CostEstimate(
            flops=0, bytes_accessed=4 * len(parts) * rows * width, transcendentals=0
        ),
    )(*parts)


def silu(value):
    return value / (1.0 + jnp.exp(-value))


def shared_kernel(rows, scalar, gate_w, up_w, down_w, out, gate_v, up_v, down_v, sems):
    copies = [
        pltpu.make_async_copy(src, dst, sems.at[i])
        for i, (src, dst) in enumerate(((gate_w, gate_v), (up_w, up_v), (down_w, down_v)))
    ]
    for copy in copies:
        copy.start()
    block = rows[...]
    logit = jnp.sum(
        block.astype(jnp.float32) * scalar[...].astype(jnp.float32), axis=1, keepdims=True
    )
    scale = 1.0 / (1.0 + jnp.exp(-logit))
    copies[0].wait()
    across = (((1,), (1,)), ((), ()))
    gate = lax.dot_general(block, gate_v[...], across, preferred_element_type=jnp.float32)
    copies[1].wait()
    upper = lax.dot_general(block, up_v[...], across, preferred_element_type=jnp.float32)
    hidden = (silu(gate) * upper).astype(jnp.bfloat16)
    copies[2].wait()
    result = jnp.dot(hidden, down_v[...], preferred_element_type=jnp.float32)
    out[...] = (scale * result).astype(jnp.bfloat16)


def shared_expert(rows, scalar, gate_w, up_w, down_w):
    any_spec = pl.BlockSpec(memory_space=pl.ANY)
    vmem = pl.BlockSpec(memory_space=pltpu.VMEM)
    return pl.pallas_call(
        shared_kernel,
        out_shape=jax.ShapeDtypeStruct(rows.shape, jnp.bfloat16),
        in_specs=[vmem, vmem, any_spec, any_spec, any_spec],
        out_specs=vmem,
        scratch_shapes=[
            pltpu.VMEM(gate_w.shape, jnp.bfloat16),
            pltpu.VMEM(up_w.shape, jnp.bfloat16),
            pltpu.VMEM(down_w.shape, jnp.bfloat16),
            pltpu.SemaphoreType.DMA((3,)),
        ],
        compiler_params=pltpu.CompilerParams(vmem_limit_bytes=48 * 1024 * 1024),
        cost_estimate=pl.CostEstimate(
            flops=6 * rows.shape[0] * gate_w.size,
            bytes_accessed=6 * gate_w.size + 4 * rows.size,
            transcendentals=rows.shape[0] * gate_w.shape[0],
        ),
    )(rows, scalar.reshape(1, -1), gate_w, up_w, down_w)


def routed_kernel(count, entries, *refs):
    chunks, refs = refs[:count], refs[count:]
    place_row, place_col, row_gate, extra, gate_w, up_w, down_w = refs[:7]
    outs, refs = refs[7 : 7 + count], refs[7 + count :]
    packed, gate_v, up_v, down_v, sems = refs
    copies = [
        pltpu.make_async_copy(src.at[0], dst, sems.at[i])
        for i, (src, dst) in enumerate(((gate_w, gate_v), (up_w, up_v), (down_w, down_v)))
    ]
    for copy in copies:
        copy.start()
    size = chunks[0].shape[0]
    for c in range(count):
        wanted = lax.broadcasted_iota(jnp.int32, (entries, size), 0)
        pick = jnp.where(place_row[c] == wanted, 1.0, 0.0).astype(jnp.bfloat16)
        packed[c * entries : (c + 1) * entries, :] = jnp.dot(
            pick, chunks[c][...], preferred_element_type=jnp.float32
        ).astype(jnp.bfloat16)
    copies[0].wait()
    gate = jnp.dot(packed[...], gate_v[...], preferred_element_type=jnp.float32)
    copies[1].wait()
    upper = jnp.dot(packed[...], up_v[...], preferred_element_type=jnp.float32)
    hidden = (silu(gate) * upper).astype(jnp.bfloat16)
    copies[2].wait()
    answer = jnp.dot(hidden, down_v[...], preferred_element_type=jnp.float32).astype(
        jnp.bfloat16
    )
    for c in range(count):
        wanted = lax.broadcasted_iota(jnp.int32, (size, entries), 1)
        put = jnp.where(place_col[c] == wanted, 1.0, 0.0).astype(jnp.bfloat16)
        placed = row_gate[c] * jnp.dot(
            put,
            answer[c * entries : (c + 1) * entries, :],
            preferred_element_type=jnp.float32,
        )
        if c == 0 and extra.shape[0] == size:
            placed = placed + extra[...].astype(jnp.float32)
        outs[c][...] = placed.astype(jnp.bfloat16)


def routed_expert(chunks, place, row_gate, extra, gate_w, up_w, down_w, entries):
    count = len(chunks)
    size, width = chunks[0].shape
    hidden = gate_w.shape[2]
    any_spec = pl.BlockSpec(memory_space=pl.ANY)
    vmem = pl.BlockSpec(memory_space=pltpu.VMEM)
    if extra is None:
        extra = jnp.zeros((8, 128), jnp.bfloat16)
    return pl.pallas_call(
        functools.partial(routed_kernel, count, entries),
        out_shape=[jax.ShapeDtypeStruct((size, width), jnp.bfloat16)] * count,
        in_specs=[vmem] * (count + 4) + [any_spec] * 3,
        out_specs=[vmem] * count,
        scratch_shapes=[
            pltpu.VMEM((count * entries, width), jnp.bfloat16),
            pltpu.VMEM((width, hidden), jnp.bfloat16),
            pltpu.VMEM((width, hidden), jnp.bfloat16),
            pltpu.VMEM((hidden, width), jnp.bfloat16),
            pltpu.SemaphoreType.DMA((3,)),
        ],
        compiler_params=pltpu.CompilerParams(vmem_limit_bytes=56 * 1024 * 1024),
        cost_estimate=pl.CostEstimate(
            flops=2 * count * entries * (3 * gate_w.size + 2 * size * width),
            bytes_accessed=6 * gate_w.size + 4 * count * size * width,
            transcendentals=count * entries * hidden,
        ),
    )(
        *chunks,
        place.reshape(count, 1, size),
        place.reshape(count, size, 1),
        row_gate.reshape(count, size, 1),
        extra,
        gate_w,
        up_w,
        down_w,
    )


def rms_normed(stream, norm_gain):
    scale_row = lax.rsqrt(jnp.mean(stream * stream, axis=1, keepdims=True) + 1e-06)
    return (stream * scale_row * norm_gain[None, :]).astype(jnp.bfloat16)


def shards(
    resid,
    queries,
    cache_key,
    cache_value,
    page_table,
    row_request,
    row_position,
    out_proj,
    norm_gain,
    expert_gate,
    expert_up,
    expert_down,
    shared_gate,
    shared_up,
    shared_down,
    shared_scalar,
    slot_expert,
    route_expert,
    route_gate,
):
    f32, bf16, i32 = jnp.float32, jnp.bfloat16, jnp.int32
    exp_count = lax.axis_size("exp")
    req_count = lax.axis_size("req")
    slot_count = exp_count * req_count
    nc, nx, ny = CORES, exp_count // Z_CHIPS, req_count // CORES
    exp_index = lax.axis_index("exp")
    req_index = lax.axis_index("req")
    own_slot = req_index * exp_count + exp_index
    iz, ix = exp_index // nx, exp_index % nx
    ih, il = iz // 2, iz % 2
    iy, ic = req_index // nc, req_index % nc
    tok_rows, width = resid.shape
    pages_here, page_len, _ = cache_key.shape
    req_slots, max_pages = page_table.shape
    tokens = pages_here * page_len
    capacity = 3 * tok_rows * TOPK // slot_count

    zs = [(dh, dl) for dh in range(2) for dl in range(2)]

    def send(value, dh, dl, dx):
        if not (dh or dl or dx % nx):
            return value
        pairs = [
            (
                (h * 2 + l) * nx + x,
                ((h + dh) % 2 * 2 + (l + dl) % 2) * nx + (x + dx) % nx,
            )
            for h in range(2)
            for l in range(2)
            for x in range(nx)
        ]
        return lax.ppermute(value, "exp", pairs)

    def send_req(value, dy, dc):
        if not (dy % ny or dc % nc):
            return value
        pairs = [
            (y * nc + c, (y + dy) % ny * nc + (c + dc) % nc)
            for y in range(ny)
            for c in range(nc)
        ]
        return lax.ppermute(value, "req", pairs)

    rel_exp = jnp.stack(
        [
            ((ih + dh) % 2 * 2 + (il + dl) % 2) * nx + (ix - dx) % nx
            for dh, dl in zs
            for dx in range(nx)
        ]
    ).astype(i32)
    rel_req = jnp.stack(
        [((iy - dy) % ny) * nc + (ic - dc) % nc for dy in range(ny) for dc in range(nc)]
    ).astype(i32)

    columns = width // exp_count
    keys = cache_key.reshape(tokens, width)
    values = cache_value.reshape(tokens, width)
    far_queries = send(queries, 1, 0, 0)
    members = [(dl, dx) for dl in range(2) for dx in range(nx)]
    orders = [
        jnp.stack(
            [((ih + j) % 2 * 2 + (il + dl) % 2) * nx + (ix + dx) % nx for j in range(2)]
        ).astype(i32)
        for dl, dx in members
    ]
    blocks = {}
    for m in reversed(range(len(members))):
        blocks[m] = send(pack([keys, values, queries], orders[m], columns), 0, *members[m])
    far = [
        send(pack([far_queries], orders[m], columns), 0, *members[m])
        for m in range(len(members))
    ]
    blocks = [blocks[m] for m in range(len(members))]
    page_ids = (
        rel_exp[: len(members), None] * pages_here + jnp.arange(pages_here, dtype=i32)[None, :]
    ).reshape(-1)
    hits = (page_table[None, :, :] == page_ids[:, None, None]).astype(i32)
    page_request = jnp.sum(hits * jnp.arange(req_slots, dtype=i32)[None, :, None], axis=(1, 2))
    page_slot = jnp.sum(hits * jnp.arange(max_pages, dtype=i32)[None, None, :], axis=(1, 2))
    rel_rows = lambda a: a.reshape(exp_count, tok_rows)[rel_exp].reshape(1, -1)
    partial, level = attend(
        blocks,
        far,
        rel_rows(row_request),
        rel_rows(row_position),
        page_request,
        page_slot,
        page_len,
    )
    other = send(partial[columns:], 1, 0, 0)
    other_level = send(level[columns // HEAD_DIM :], 1, 0, 0)

    slot_ids = jnp.arange(slot_count, dtype=i32)
    own_mark = slot_ids == own_slot
    own_expert = jnp.sum(jnp.where(own_mark, slot_expert, 0))
    twins = slot_expert == own_expert
    copies = jnp.sum(twins.astype(i32))
    own_rank = jnp.sum((twins & (slot_ids < own_slot)).astype(i32))
    gates = jnp.transpose(route_gate)
    gates = jnp.stack([send_req(gates, 0, dc) for dc in range(nc)])
    gates = jnp.stack([send_req(gates, dy, 0) for dy in range(ny)])
    gates = jnp.stack([send(gates, 0, 0, dx) for dx in range(nx)], axis=2)
    gates = jnp.stack([send(gates, 0, dl, 0) for dl in range(2)], axis=2)
    gates = jnp.stack([send(gates, dh, 0, 0) for dh in range(2)], axis=2)
    gates = gates.reshape(slot_count, TOPK, tok_rows)
    rel_slots = (rel_req[:, None] * exp_count + rel_exp[None, :]).reshape(-1)
    named = (route_expert == own_expert).reshape(slot_count, tok_rows, TOPK)[rel_slots]
    named = jnp.transpose(named, (0, 2, 1))
    chunk_rows = exp_count * tok_rows
    entries = -(-exp_count * capacity // 16) * 16
    row_gate = jnp.sum(jnp.where(named, gates, 0.0), axis=1).reshape(ny, nc, chunk_rows)
    mine = jnp.any(named, axis=1) & (rel_slots % copies == own_rank)[:, None]
    mine = mine.reshape(ny, nc, chunk_rows)
    place = jnp.where(mine, jnp.cumsum(mine.astype(i32), axis=2) - 1, -1)
    other, place, row_gate = lax.optimization_barrier((other, place, row_gate))

    mixed = project(partial, level, other, other_level, out_proj)
    mixed = mixed.reshape(len(zs), nx, tok_rows, width)
    total = resid.astype(f32)
    for i in reversed(range(len(zs))):
        line = mixed[i, 0].astype(f32)
        for dx in range(1, nx):
            line = line + send(mixed[i, dx], 0, 0, -dx).astype(f32)
        total = total + (send(line.astype(bf16), *zs[i], 0).astype(f32) if i else line)
    stream = total
    normed = rms_normed(stream, norm_gain)

    piece = {}
    for i in reversed(range(len(zs))):
        piece[i, 0, 0] = send(normed, *zs[i], 0)
    x_first = [dh == 0 for dh, dl in zs]
    for i in range(len(zs)):
        for dx in range(1, nx):
            piece[i, dx, 0] = send(piece[i, 0, 0], 0, 0, dx)
        if x_first[i]:
            for dx in range(nx):
                for dy in range(1, ny):
                    piece[i, dx, dy] = send_req(piece[i, dx, 0], dy, 0)
        else:
            for dy in range(1, ny):
                piece[i, 0, dy] = send_req(piece[i, 0, 0], dy, 0)
                for dx in range(1, nx):
                    piece[i, dx, dy] = send(piece[i, 0, dy], 0, 0, dx)
    chunks = {}
    for dy in range(ny):
        chunks[dy, 0] = join([piece[i, dx, dy] for i in range(len(zs)) for dx in range(nx)])
        for dc in range(1, nc):
            chunks[dy, dc] = send_req(chunks[dy, 0], 0, dc)

    sums = {}
    for dy in range(ny):
        extra = None
        if dy == 0:
            extra = shared_expert(
                chunks[0, 0], shared_scalar, shared_gate.T, shared_up.T, shared_down
            )
        answers = routed_expert(
            [chunks[dy, dc] for dc in range(nc)],
            place[dy],
            row_gate[dy],
            extra,
            expert_gate,
            expert_up,
            expert_down,
            entries,
        )
        here = answers[0].astype(f32)
        for dc in range(1, nc):
            here = here + send_req(answers[dc], 0, -dc).astype(f32)
        here = here.astype(bf16).reshape(len(zs), nx, tok_rows, width)
        for i in range(len(zs)):
            for dx in range(nx):
                sums[i, dx, dy] = here[i, dx]
    total = stream
    for i in reversed(range(len(zs))):
        line = {}
        if x_first[i]:
            for dx in range(nx):
                line[dx] = sums[i, dx, 0].astype(f32)
                for dy in range(1, ny):
                    line[dx] = line[dx] + send_req(sums[i, dx, dy], -dy, 0).astype(f32)
            out = line[0]
            for dx in range(1, nx):
                out = out + send(line[dx].astype(bf16), 0, 0, -dx).astype(f32)
        else:
            for dy in range(ny):
                line[dy] = sums[i, 0, dy].astype(f32)
                for dx in range(1, nx):
                    line[dy] = line[dy] + send(sums[i, dx, dy], 0, 0, -dx).astype(f32)
            out = line[0]
            for dy in range(1, ny):
                out = out + send_req(line[dy].astype(bf16), -dy, 0).astype(f32)
        total = total + (send(out.astype(bf16), *zs[i], 0).astype(f32) if i else out)
    return total.astype(bf16)


def solution(mesh):
    placed = (
        P(("req", "exp"), None),
        P(("req", "exp"), None),
        P(("req", "exp"), None, None),
        P(("req", "exp"), None, None),
        P("req", None),
        P("req"),
        P("req"),
        P("exp", None),
        P(),
        P(("req", "exp"), None, None),
        P(("req", "exp"), None, None),
        P(("req", "exp"), None, None),
        P(None, "exp"),
        P(None, "exp"),
        P("exp", None),
        P(),
        P(),
        P(),
        P(("req", "exp"), None),
    )
    return jax.shard_map(
        shards, mesh=mesh, in_specs=placed, out_specs=P(("req", "exp"), None), check_vma=False
    )
```

```python
import functools

import jax
import jax.numpy as jnp
from jax import lax
from jax.experimental import pallas as pl
from jax.experimental.pallas import tpu as pltpu
from jax.sharding import PartitionSpec as P

HEAD_DIM = 128
TOPK = 4
CORES = 2
Z_CHIPS = 4


def pack_kernel(members, order, keys, values, queries, gates, blocks, far):
    weights = gates[...]
    high = weights.astype(jnp.bfloat16).astype(jnp.float32)
    middle = (weights - high).astype(jnp.bfloat16).astype(jnp.float32)
    low = weights - high - middle
    weights = jnp.concatenate([high, middle, low, jnp.zeros_like(low)], axis=0)
    weights = weights.astype(jnp.bfloat16)
    for m in range(members):
        tokens, rows = keys[m].shape[0], queries[m].shape[0]
        blocks[m][:tokens, :] = keys[m][...]
        blocks[m][tokens : 2 * tokens, :] = values[m][...]
        blocks[m][2 * tokens : 2 * tokens + rows, :] = queries[m][...]
        blocks[m][2 * tokens + rows :, :] = weights
        far[m][...] = queries[m][...]


def pack(keys, values, queries, gates, order, columns):
    members = order.shape[0] // 2
    tokens, rows = keys.shape[0], queries.shape[0]
    block_rows = 2 * tokens + rows + 4 * gates.shape[0]

    def kernel(order, *refs):
        group = lambda i: refs[i * members : (i + 1) * members]
        pack_kernel(
            members,
            order,
            group(0),
            group(1),
            group(2),
            refs[3 * members],
            refs[3 * members + 1 : 4 * members + 1],
            refs[4 * members + 1 :],
        )

    def column(n, m):
        return pl.BlockSpec((n, columns), lambda j, order: (0, order[2 * m + j]))

    result = pl.pallas_call(
        kernel,
        out_shape=[jax.ShapeDtypeStruct((block_rows, 2 * columns), keys.dtype)] * members
        + [jax.ShapeDtypeStruct((rows, 2 * columns), keys.dtype)] * members,
        grid_spec=pltpu.PrefetchScalarGridSpec(
            num_scalar_prefetch=1,
            grid=(2,),
            in_specs=[column(n, m) for n in (tokens, tokens, rows) for m in range(members)]
            + [pl.BlockSpec((gates.shape[0], columns), lambda j, order: (0, j))],
            out_specs=[pl.BlockSpec((block_rows, columns), lambda j, order: (0, j))] * members
            + [pl.BlockSpec((rows, columns), lambda j, order: (0, 1 - j))] * members,
        ),
        compiler_params=pltpu.CompilerParams(vmem_limit_bytes=32 * 1024 * 1024),
        cost_estimate=pl.CostEstimate(
            flops=0, bytes_accessed=8 * members * block_rows * columns, transcendentals=0
        ),
    )(order, *[keys] * members, *[values] * members, *[queries] * members, gates)
    return result[:members], result[members:]


def attend_kernel(members, tokens, page_len, scale, page_req, page_slot, *refs):
    blocks, far, refs = refs[:members], refs[members : 2 * members], refs[2 * members :]
    row_req, row_pos, out, level = refs
    keys = jnp.concatenate([block[:tokens, :] for block in blocks], axis=0)
    values = jnp.concatenate([block[tokens : 2 * tokens, :] for block in blocks], axis=0)
    tok_rows = far[0].shape[0]
    near = [block[2 * tokens : 2 * tokens + tok_rows, :] for block in blocks]
    size = sum(q.shape[0] for q in near)
    for side, query in enumerate((near, [q[...] for q in far])):
        lanes = slice(side * size, (side + 1) * size)
        query = jnp.concatenate(query, axis=0)
        request, position = row_req[:, lanes], row_pos[:, lanes]
        scores = (
            lax.dot_general(
                keys, query, (((1,), (1,)), ((), ())), preferred_element_type=jnp.float32
            )
            * scale
        )
        token = lax.broadcasted_iota(jnp.int32, (page_len, size), 0)
        visible = jnp.concatenate(
            [
                (request == page_req[page]) & (token + page_slot[page] * page_len <= position)
                for page in range(members * tokens // page_len)
            ],
            axis=0,
        )
        scores = jnp.where(visible, scores, -1e30)
        top = jnp.max(scores, axis=0, keepdims=True)
        weights = jnp.where(visible, jnp.exp(scores - top), 0.0)
        total = jnp.sum(weights, axis=0, keepdims=True)
        summed = lax.dot_general(
            values,
            weights.astype(jnp.bfloat16),
            (((0,), (0,)), ((), ())),
            preferred_element_type=jnp.float32,
        )
        seen = total > 0.0
        total = jnp.where(seen, total, 1.0)
        out[:, lanes] = (summed / total).astype(jnp.bfloat16)
        level[0, :, lanes] = jnp.where(seen, top + jnp.log(total), -1e30)


def attend(blocks, far, row_req, row_pos, page_req, page_slot, page_len, tokens):
    members, rows = len(blocks), row_req.shape[1]
    block_rows, columns = blocks[0].shape
    tok_rows = far[0].shape[0]
    heads = columns // HEAD_DIM
    by_head = lambda n: pl.BlockSpec((n, HEAD_DIM), lambda h, *_: (0, h))
    whole = pl.BlockSpec((1, rows), lambda h, *_: (0, 0))
    return pl.pallas_call(
        functools.partial(attend_kernel, members, tokens, page_len, HEAD_DIM ** (-0.5)),
        out_shape=[
            jax.ShapeDtypeStruct((columns, rows), jnp.bfloat16),
            jax.ShapeDtypeStruct((heads, 1, rows), jnp.float32),
        ],
        grid_spec=pltpu.PrefetchScalarGridSpec(
            num_scalar_prefetch=2,
            grid=(heads,),
            in_specs=[by_head(block_rows)] * members + [by_head(tok_rows)] * members + [whole] * 2,
            out_specs=[
                pl.BlockSpec((HEAD_DIM, rows), lambda h, *_: (h, 0)),
                pl.BlockSpec((1, 1, rows), lambda h, *_: (h, 0, 0)),
            ],
        ),
        compiler_params=pltpu.CompilerParams(vmem_limit_bytes=48 * 1024 * 1024),
        cost_estimate=pl.CostEstimate(
            flops=4 * rows * members * tokens * columns,
            bytes_accessed=2 * members * (block_rows + tok_rows) * columns,
            transcendentals=rows * members * tokens * heads,
        ),
    )(page_req, page_slot, *blocks, *far, row_req, row_pos)


def project_kernel(mine, mine_level, theirs, their_level, proj, stay, go):
    parts = []
    for head in range(mine.shape[0] // HEAD_DIM):
        dims = slice(head * HEAD_DIM, (head + 1) * HEAD_DIM)
        share = 1.0 / (1.0 + jnp.exp(their_level[head] - mine_level[head]))
        other = 1.0 / (1.0 + jnp.exp(mine_level[head] - their_level[head]))
        both = share * mine[dims, :].astype(jnp.float32) + other * theirs[dims, :].astype(
            jnp.float32
        )
        parts.append(both.astype(jnp.bfloat16))
    attention = jnp.concatenate(parts, axis=0) if len(parts) > 1 else parts[0]
    mixed = lax.dot_general(
        attention, proj[...], (((0,), (0,)), ((), ())), preferred_element_type=jnp.float32
    )
    rows = stay.shape[0]
    stay[...] = mixed[:rows, :]
    go[...] = mixed[rows:, :].astype(jnp.bfloat16)


def project(place, mine, mine_level, theirs, their_level, proj, tok_rows):
    columns, width = proj.shape
    heads = columns // HEAD_DIM
    size = mine.shape[1] // 4
    return pl.pallas_call(
        project_kernel,
        out_shape=[
            jax.ShapeDtypeStruct((tok_rows, width), jnp.float32),
            jax.ShapeDtypeStruct((size - tok_rows, width), jnp.bfloat16),
        ],
        grid=(1,),
        in_specs=[
            pl.BlockSpec((columns, size), lambda i: (0, place)),
            pl.BlockSpec((heads, 1, size), lambda i: (0, 0, place)),
            pl.BlockSpec((columns, size), lambda i: (0, (place + 2) % 4)),
            pl.BlockSpec((heads, 1, size), lambda i: (0, 0, (place + 2) % 4)),
            pl.BlockSpec((columns, width), lambda i: (0, 0)),
        ],
        out_specs=[
            pl.BlockSpec((tok_rows, width), lambda i: (0, 0)),
            pl.BlockSpec((size - tok_rows, width), lambda i: (0, 0)),
        ],
        cost_estimate=pl.CostEstimate(
            flops=2 * size * columns * width,
            bytes_accessed=2 * (2 * columns * size + columns * width + size * width),
            transcendentals=2 * size * heads,
        ),
    )(mine, mine_level, theirs, their_level, proj)


def add_kernel(*refs):
    parts, out = refs[:-1], refs[-1]
    total = parts[0][...].astype(jnp.float32)
    for part in parts[1:]:
        total = total + part[...].astype(jnp.float32)
    out[...] = total.astype(out.dtype)


def add_up(parts, dtype):
    vmem = pl.BlockSpec(memory_space=pltpu.VMEM)
    return pl.pallas_call(
        add_kernel,
        out_shape=jax.ShapeDtypeStruct(parts[0].shape, dtype),
        in_specs=[vmem] * len(parts),
        out_specs=vmem,
        cost_estimate=pl.CostEstimate(
            flops=len(parts) * parts[0].size,
            bytes_accessed=4 * len(parts) * parts[0].size,
            transcendentals=0,
        ),
    )(*parts)


def join_kernel(*refs):
    parts, out = refs[:-1], refs[-1]
    rows = parts[0].shape[0]
    for i, part in enumerate(parts):
        out[i * rows : (i + 1) * rows, :] = part[...]


def join(parts):
    rows, width = parts[0].shape
    vmem = pl.BlockSpec(memory_space=pltpu.VMEM)
    return pl.pallas_call(
        join_kernel,
        out_shape=jax.ShapeDtypeStruct((len(parts) * rows, width), parts[0].dtype),
        in_specs=[vmem] * len(parts),
        out_specs=vmem,
        cost_estimate=pl.CostEstimate(
            flops=0, bytes_accessed=4 * len(parts) * rows * width, transcendentals=0
        ),
    )(*parts)


def silu(value):
    return value / (1.0 + jnp.exp(-value))


def shared_kernel(rows, scalar, gate_w, up_w, down_w, out, gate_v, up_v, down_v, sems):
    copies = [
        pltpu.make_async_copy(src, dst, sems.at[i])
        for i, (src, dst) in enumerate(((gate_w, gate_v), (up_w, up_v), (down_w, down_v)))
    ]
    for copy in copies:
        copy.start()
    block = rows[...]
    logit = jnp.sum(
        block.astype(jnp.float32) * scalar[...].astype(jnp.float32), axis=1, keepdims=True
    )
    scale = 1.0 / (1.0 + jnp.exp(-logit))
    copies[0].wait()
    across = (((1,), (1,)), ((), ()))
    gate = lax.dot_general(block, gate_v[...], across, preferred_element_type=jnp.float32)
    copies[1].wait()
    upper = lax.dot_general(block, up_v[...], across, preferred_element_type=jnp.float32)
    hidden = (silu(gate) * upper).astype(jnp.bfloat16)
    copies[2].wait()
    result = jnp.dot(hidden, down_v[...], preferred_element_type=jnp.float32)
    out[...] = (scale * result).astype(jnp.bfloat16)


def shared_expert(rows, scalar, gate_w, up_w, down_w):
    any_spec = pl.BlockSpec(memory_space=pl.ANY)
    vmem = pl.BlockSpec(memory_space=pltpu.VMEM)
    return pl.pallas_call(
        shared_kernel,
        out_shape=jax.ShapeDtypeStruct(rows.shape, jnp.bfloat16),
        in_specs=[vmem, vmem, any_spec, any_spec, any_spec],
        out_specs=vmem,
        scratch_shapes=[
            pltpu.VMEM(gate_w.shape, jnp.bfloat16),
            pltpu.VMEM(up_w.shape, jnp.bfloat16),
            pltpu.VMEM(down_w.shape, jnp.bfloat16),
            pltpu.SemaphoreType.DMA((3,)),
        ],
        compiler_params=pltpu.CompilerParams(vmem_limit_bytes=48 * 1024 * 1024),
        cost_estimate=pl.CostEstimate(
            flops=6 * rows.shape[0] * gate_w.size,
            bytes_accessed=6 * gate_w.size + 4 * rows.size,
            transcendentals=rows.shape[0] * gate_w.shape[0],
        ),
    )(rows, scalar.reshape(1, -1), gate_w, up_w, down_w)


def routed_kernel(count, entries, has_extra, *refs):
    chunks, refs = refs[:count], refs[count:]
    place, row_gate, extra, gate_w, up_w, down_w = refs[:6]
    outs, refs = refs[6 : 6 + count], refs[6 + count :]
    rows, packed, gate_v, up_v, down_v, extra_v, sems = refs
    moves = [(chunks[c], rows.at[c]) for c in range(count)]
    moves += [(gate_w.at[0], gate_v), (up_w.at[0], up_v), (down_w.at[0], down_v)]
    if has_extra:
        moves.append((extra, extra_v))
    copies = [
        pltpu.make_async_copy(src, dst, sems.at[i]) for i, (src, dst) in enumerate(moves)
    ]
    for copy in copies:
        copy.start()
    size = chunks[0].shape[0]
    wanted = lax.broadcasted_iota(jnp.int32, (entries, size), 0)
    picks, weights = [], []
    for c in range(count):
        pick = jnp.where(place[c] == wanted, 1.0, 0.0)
        picks.append(pick.astype(jnp.bfloat16))
        weights.append(jnp.sum(pick * row_gate[c], axis=1, keepdims=True))
        copies[c].wait()
        packed[c * entries : (c + 1) * entries, :] = jnp.dot(
            picks[c], rows[c], preferred_element_type=jnp.float32
        ).astype(jnp.bfloat16)
    copies[count].wait()
    gate = jnp.dot(packed[...], gate_v[...], preferred_element_type=jnp.float32)
    copies[count + 1].wait()
    upper = jnp.dot(packed[...], up_v[...], preferred_element_type=jnp.float32)
    hidden = (silu(gate) * upper).astype(jnp.bfloat16)
    copies[count + 2].wait()
    answer = jnp.dot(hidden, down_v[...], preferred_element_type=jnp.float32).astype(
        jnp.bfloat16
    )
    if has_extra:
        copies[count + 3].wait()
    for c in range(count):
        scaled = answer[c * entries : (c + 1) * entries, :].astype(jnp.float32) * weights[c]
        placed = lax.dot_general(
            picks[c],
            scaled.astype(jnp.bfloat16),
            (((0,), (0,)), ((), ())),
            preferred_element_type=jnp.float32,
        )
        if c == 0 and has_extra:
            placed = placed + extra_v[...].astype(jnp.float32)
        outs[c][...] = placed.astype(jnp.bfloat16)


def routed_expert(chunks, place, row_gate, extra, gate_w, up_w, down_w, entries):
    count = len(chunks)
    size, width = chunks[0].shape
    hidden = gate_w.shape[2]
    any_spec = pl.BlockSpec(memory_space=pl.ANY)
    vmem = pl.BlockSpec(memory_space=pltpu.VMEM)
    has_extra = extra is not None
    if not has_extra:
        extra = jnp.zeros((16, 128), jnp.bfloat16)
    return pl.pallas_call(
        functools.partial(routed_kernel, count, entries, has_extra),
        out_shape=[jax.ShapeDtypeStruct((size, width), jnp.bfloat16)] * count,
        in_specs=[any_spec] * count + [vmem] * 2 + [any_spec] * 4,
        out_specs=[vmem] * count,
        scratch_shapes=[
            pltpu.VMEM((count, size, width), jnp.bfloat16),
            pltpu.VMEM((count * entries, width), jnp.bfloat16),
            pltpu.VMEM((width, hidden), jnp.bfloat16),
            pltpu.VMEM((width, hidden), jnp.bfloat16),
            pltpu.VMEM((hidden, width), jnp.bfloat16),
            pltpu.VMEM(extra.shape, jnp.bfloat16),
            pltpu.SemaphoreType.DMA((count + 4,)),
        ],
        compiler_params=pltpu.CompilerParams(vmem_limit_bytes=56 * 1024 * 1024),
        cost_estimate=pl.CostEstimate(
            flops=2 * count * entries * (3 * gate_w.size + 2 * size * width),
            bytes_accessed=6 * gate_w.size + 4 * count * size * width,
            transcendentals=count * entries * hidden,
        ),
    )(*chunks, place, row_gate, extra, gate_w, up_w, down_w)


def rms_normed(stream, norm_gain):
    scale_row = lax.rsqrt(jnp.mean(stream * stream, axis=1, keepdims=True) + 1e-06)
    return (stream * scale_row * norm_gain[None, :]).astype(jnp.bfloat16)


def shards(
    resid,
    queries,
    cache_key,
    cache_value,
    page_table,
    row_request,
    row_position,
    out_proj,
    norm_gain,
    expert_gate,
    expert_up,
    expert_down,
    shared_gate,
    shared_up,
    shared_down,
    shared_scalar,
    slot_expert,
    route_expert,
    route_gate,
):
    f32, bf16, i32 = jnp.float32, jnp.bfloat16, jnp.int32
    exp_count = lax.axis_size("exp")
    req_count = lax.axis_size("req")
    slot_count = exp_count * req_count
    nc, nx, ny = CORES, exp_count // Z_CHIPS, req_count // CORES
    exp_index = lax.axis_index("exp")
    req_index = lax.axis_index("req")
    own_slot = req_index * exp_count + exp_index
    iz, ix = exp_index // nx, exp_index % nx
    ih, il = iz // 2, iz % 2
    iy, ic = req_index // nc, req_index % nc
    tok_rows, width = resid.shape
    pages_here, page_len, _ = cache_key.shape
    req_slots, max_pages = page_table.shape
    tokens = pages_here * page_len
    capacity = 3 * tok_rows * TOPK // slot_count

    zs = [(dh, dl) for dh in range(2) for dl in range(2)]

    def send(value, dh, dl, dx):
        if not (dh or dl or dx % nx):
            return value
        pairs = [
            (
                (h * 2 + l) * nx + x,
                ((h + dh) % 2 * 2 + (l + dl) % 2) * nx + (x + dx) % nx,
            )
            for h in range(2)
            for l in range(2)
            for x in range(nx)
        ]
        return lax.ppermute(value, "exp", pairs)

    def send_req(value, dy, dc):
        if not (dy % ny or dc % nc):
            return value
        pairs = [
            (y * nc + c, (y + dy) % ny * nc + (c + dc) % nc)
            for y in range(ny)
            for c in range(nc)
        ]
        return lax.ppermute(value, "req", pairs)

    rel_exp = jnp.stack(
        [
            ((ih + dh) % 2 * 2 + (il + dl) % 2) * nx + (ix - dx) % nx
            for dh, dl in zs
            for dx in range(nx)
        ]
    ).astype(i32)
    rel_req = jnp.stack(
        [((iy - dy) % ny) * nc + (ic - dc) % nc for dy in range(ny) for dc in range(nc)]
    ).astype(i32)

    columns = width // exp_count
    keys = cache_key.reshape(tokens, width)
    values = cache_value.reshape(tokens, width)
    members = [(dl, dx) for dl in range(2) for dx in range(nx)]
    order = jnp.stack(
        [
            ((ih + j) % 2 * 2 + (il + dl) % 2) * nx + (ix + dx) % nx
            for dl, dx in members
            for j in range(2)
        ]
    ).astype(i32)
    gates = jnp.pad(jnp.transpose(route_gate), ((0, 0), (0, 2 * columns - tok_rows)))
    blocks, far = pack(keys, values, queries, gates, order, columns)
    blocks = [send(blocks[m], 0, *members[m]) for m in range(len(members))]
    far = [send(far[m], 1, *members[m]) for m in range(len(members))]
    page_ids = (
        rel_exp[: len(members), None] * pages_here + jnp.arange(pages_here, dtype=i32)[None, :]
    ).reshape(-1)
    hits = (page_table[None, :, :] == page_ids[:, None, None]).astype(i32)
    page_request = jnp.sum(hits * jnp.arange(req_slots, dtype=i32)[None, :, None], axis=(1, 2))
    page_slot = jnp.sum(hits * jnp.arange(max_pages, dtype=i32)[None, None, :], axis=(1, 2))
    rel_rows = lambda a: a.reshape(exp_count, tok_rows)[rel_exp].reshape(1, -1)
    partial, level = attend(
        blocks,
        far,
        rel_rows(row_request),
        rel_rows(row_position),
        page_request,
        page_slot,
        page_len,
        tokens,
    )
    other = send(partial[columns:], 1, 0, 0)
    other_level = send(level[columns // HEAD_DIM :], 1, 0, 0)

    slot_ids = jnp.arange(slot_count, dtype=i32)
    own_mark = slot_ids == own_slot
    own_expert = jnp.sum(jnp.where(own_mark, slot_expert, 0))
    twins = slot_expert == own_expert
    copies = jnp.sum(twins.astype(i32))
    own_rank = jnp.sum((twins & (slot_ids < own_slot)).astype(i32))
    gates = [block[2 * tokens + tok_rows :, :tok_rows].astype(f32) for block in blocks]
    gates = jnp.stack([g[:TOPK] + g[TOPK : 2 * TOPK] + g[2 * TOPK : 3 * TOPK] for g in gates])
    gates = gates.reshape(2, nx, TOPK, tok_rows)
    gates = jnp.stack([send(gates, dh, 0, 0) for dh in range(2)])
    gates = jnp.stack([send_req(gates, dy, 0) for dy in range(ny)])
    gates = jnp.stack([send_req(gates, 0, dc) for dc in range(nc)], axis=1)
    gates = jnp.transpose(gates, (0, 1, 4, 2, 3, 5, 6)).reshape(slot_count, TOPK, tok_rows)
    rel_exp = jnp.transpose(rel_exp.reshape(len(zs), nx)).reshape(-1)
    rel_slots = (rel_req[:, None] * exp_count + rel_exp[None, :]).reshape(-1)
    named = (route_expert == own_expert).reshape(slot_count, tok_rows, TOPK)[rel_slots]
    named = jnp.transpose(named, (0, 2, 1))
    chunk_rows = exp_count * tok_rows
    entries = -(-exp_count * capacity // 16) * 16
    row_gate = jnp.sum(jnp.where(named, gates, 0.0), axis=1).reshape(ny, nc, chunk_rows)
    mine = jnp.any(named, axis=1) & (rel_slots % copies == own_rank)[:, None]
    mine = mine.reshape(ny, nc, chunk_rows)
    place = jnp.where(mine, jnp.cumsum(mine.astype(i32), axis=2) - 1, -1)
    place = place.reshape(ny, nc, 1, chunk_rows)
    row_gate = row_gate.reshape(ny, nc, 1, chunk_rows)

    total = resid.astype(f32)
    stays, goes = {}, {}
    for i in reversed(range(len(zs))):
        stays[i], go = project(i, partial, level, other, other_level, out_proj, tok_rows)
        goes[i] = [
            send(go[(dx - 1) * tok_rows : dx * tok_rows], 0, 0, -dx) for dx in range(1, nx)
        ]
    for i in reversed(range(len(zs))):
        if i:
            line = add_up([stays[i]] + goes[i], bf16)
            total = total + send(line, *zs[i], 0).astype(f32)
        else:
            total = total + stays[i]
            for come in goes[i]:
                total = total + come.astype(f32)
    stream = total
    normed = rms_normed(stream, norm_gain)
    normed, place, row_gate = lax.optimization_barrier((normed, place, row_gate))

    line = [send(normed, *zs[i], 0) for i in range(len(zs))]
    piece = {}
    for i in range(len(zs)):
        piece[i, 0, 0] = line[i]
        new = {}
        for dy in range(1, ny):
            new[i, 0, dy] = send_req(line[i], dy, 0)
        for dx in range(1, nx):
            new[i, dx, 0] = send(line[i], 0, 0, dx)
            if i:
                for dy in range(1, ny):
                    new[i - 1, dx, dy] = send(piece[i - 1, 0, dy], 0, 0, dx)
        names = list(new)
        tied = lax.optimization_barrier([new[name] for name in names] + line[i + 1 : i + 2])
        if i + 1 < len(zs):
            line[i + 1] = tied[-1]
        for name, value in zip(names, tied):
            piece[name] = value
    last = len(zs) - 1
    for dy in range(1, ny):
        for dx in range(1, nx):
            piece[last, dx, dy] = send(piece[last, 0, dy], 0, 0, dx)

    def chunk_of(dy):
        return join([piece[i, dx, dy] for dx in range(nx) for i in range(len(zs))])

    def answers_of(dy, chunk, partners, extra):
        answers = routed_expert(
            [chunk] + partners,
            place[dy],
            row_gate[dy],
            extra,
            expert_gate,
            expert_up,
            expert_down,
            entries,
        )
        here = answers[0].astype(f32)
        for dc in range(1, nc):
            here = here + send_req(answers[dc], 0, -dc).astype(f32)
        return here.astype(bf16).reshape(nx, len(zs), tok_rows, width)

    partners_of = lambda chunk: [send_req(chunk, 0, dc) for dc in range(1, nc)]
    chunk = chunk_of(0)
    partners = partners_of(chunk)
    extra = shared_expert(chunk, shared_scalar, shared_gate.T, shared_up.T, shared_down)
    sums, later = {}, {}
    for dy in range(ny):
        if dy + 1 < ny:
            names = [(i, dx, dy + 1) for dx in range(nx) for i in range(len(zs))]
            tied = lax.optimization_barrier(
                [extra] + partners + [piece[name] for name in names]
            ) if extra is not None else None
            if tied is not None:
                extra, partners = tied[0], list(tied[1 : 1 + len(partners)])
                for name, value in zip(names, tied[1 + len(partners) :]):
                    piece[name] = value
            following = chunk_of(dy + 1)
            following_partners = partners_of(following)
        here = answers_of(dy, chunk, partners, extra)
        half = len(zs) // 2
        for low in (half, 0):
            group = here[0, low : low + half].astype(f32)
            for dx in range(1, nx):
                group = group + send(here[dx, low : low + half], 0, 0, -dx).astype(f32)
            for i in range(half):
                sums[low + i, dy] = group[i]
        if dy + 1 < ny:
            chunk, partners, extra = following, following_partners, None

    total = stream
    for i in reversed(range(len(zs))):
        parts = [sums[i, 0]] + [send_req(sums[i, dy].astype(bf16), -dy, 0) for dy in range(1, ny)]
        if i:
            total = total + send(add_up(parts, bf16), *zs[i], 0).astype(f32)
        else:
            for part in parts:
                total = total + part.astype(f32)
    return total.astype(bf16)


def solution(mesh):
    placed = (
        P(("req", "exp"), None),
        P(("req", "exp"), None),
        P(("req", "exp"), None, None),
        P(("req", "exp"), None, None),
        P("req", None),
        P("req"),
        P("req"),
        P("exp", None),
        P(),
        P(("req", "exp"), None, None),
        P(("req", "exp"), None, None),
        P(("req", "exp"), None, None),
        P(None, "exp"),
        P(None, "exp"),
        P("exp", None),
        P(),
        P(),
        P(),
        P(("req", "exp"), None),
    )
    return jax.shard_map(
        shards, mesh=mesh, in_specs=placed, out_specs=P(("req", "exp"), None), check_vma=False
    )
```

```python
import functools

import jax
import jax.numpy as jnp
from jax import lax
from jax.experimental import pallas as pl
from jax.experimental.pallas import tpu as pltpu
from jax.sharding import PartitionSpec as P

HEAD_DIM = 128
TOPK = 4
CORES = 2
Z_CHIPS = 4


def pack_kernel(members, *refs):
    keys, values, queries = (refs[i * members : (i + 1) * members] for i in range(3))
    gates, blocks = refs[3 * members], refs[3 * members + 1 :]
    weights = gates[...]
    high = weights.astype(jnp.bfloat16).astype(jnp.float32)
    middle = (weights - high).astype(jnp.bfloat16).astype(jnp.float32)
    low = weights - high - middle
    weights = jnp.concatenate([high, middle, low, jnp.zeros_like(low)], axis=0)
    weights = weights.astype(jnp.bfloat16)
    for m in range(members):
        tokens, rows = keys[m].shape[0], queries[m].shape[0]
        blocks[m][:tokens, :] = keys[m][...]
        blocks[m][tokens : 2 * tokens, :] = values[m][...]
        blocks[m][2 * tokens : 2 * tokens + rows, :] = queries[m][...]
        blocks[m][2 * tokens + rows :, :] = weights


def pack_far_kernel(members, *refs):
    for m in range(members):
        refs[members + m][...] = refs[m][...]


def pack(parts, gates, order, columns):
    members = order.shape[0] // 2
    rows = sum(p.shape[0] for p in parts) + (0 if gates is None else 4 * gates.shape[0])
    kernel = functools.partial(pack_far_kernel if gates is None else pack_kernel, members)

    def column(n, m):
        return pl.BlockSpec((n, columns), lambda j, order: (0, order[2 * m + j]))

    in_specs = [column(p.shape[0], m) for p in parts for m in range(members)]
    operands = [p for p in parts for m in range(members)]
    if gates is not None:
        in_specs.append(pl.BlockSpec((gates.shape[0], columns), lambda j, order: (0, j)))
        operands.append(gates)
    return pl.pallas_call(
        lambda order, *refs: kernel(*refs),
        out_shape=[jax.ShapeDtypeStruct((rows, 2 * columns), parts[0].dtype)] * members,
        grid_spec=pltpu.PrefetchScalarGridSpec(
            num_scalar_prefetch=1,
            grid=(2,),
            in_specs=in_specs,
            out_specs=[pl.BlockSpec((rows, columns), lambda j, order: (0, j))] * members,
        ),
        compiler_params=pltpu.CompilerParams(vmem_limit_bytes=32 * 1024 * 1024),
        cost_estimate=pl.CostEstimate(
            flops=0, bytes_accessed=8 * members * rows * columns, transcendentals=0
        ),
    )(order, *operands)


def attend_kernel(members, tokens, page_len, scale, page_req, page_slot, *refs):
    blocks, far, refs = refs[:members], refs[members : 2 * members], refs[2 * members :]
    row_req, row_pos, out, level = refs
    keys = jnp.concatenate([block[:tokens, :] for block in blocks], axis=0)
    values = jnp.concatenate([block[tokens : 2 * tokens, :] for block in blocks], axis=0)
    tok_rows = far[0].shape[0]
    near = [block[2 * tokens : 2 * tokens + tok_rows, :] for block in blocks]
    size = sum(q.shape[0] for q in near)
    for side, query in enumerate((near, [q[...] for q in far])):
        lanes = slice(side * size, (side + 1) * size)
        query = jnp.concatenate(query, axis=0)
        request, position = row_req[:, lanes], row_pos[:, lanes]
        scores = (
            lax.dot_general(
                keys, query, (((1,), (1,)), ((), ())), preferred_element_type=jnp.float32
            )
            * scale
        )
        token = lax.broadcasted_iota(jnp.int32, (page_len, size), 0)
        visible = jnp.concatenate(
            [
                (request == page_req[page]) & (token + page_slot[page] * page_len <= position)
                for page in range(members * tokens // page_len)
            ],
            axis=0,
        )
        scores = jnp.where(visible, scores, -1e30)
        top = jnp.max(scores, axis=0, keepdims=True)
        weights = jnp.where(visible, jnp.exp(scores - top), 0.0)
        total = jnp.sum(weights, axis=0, keepdims=True)
        summed = lax.dot_general(
            values,
            weights.astype(jnp.bfloat16),
            (((0,), (0,)), ((), ())),
            preferred_element_type=jnp.float32,
        )
        seen = total > 0.0
        total = jnp.where(seen, total, 1.0)
        out[:, lanes] = (summed / total).astype(jnp.bfloat16)
        level[0, :, lanes] = jnp.where(seen, top + jnp.log(total), -1e30)


def attend(blocks, far, row_req, row_pos, page_req, page_slot, page_len, tokens):
    members, rows = len(blocks), row_req.shape[1]
    block_rows, columns = blocks[0].shape
    tok_rows = far[0].shape[0]
    heads = columns // HEAD_DIM
    by_head = lambda n: pl.BlockSpec((n, HEAD_DIM), lambda h, *_: (0, h))
    whole = pl.BlockSpec((1, rows), lambda h, *_: (0, 0))
    return pl.pallas_call(
        functools.partial(attend_kernel, members, tokens, page_len, HEAD_DIM ** (-0.5)),
        out_shape=[
            jax.ShapeDtypeStruct((columns, rows), jnp.bfloat16),
            jax.ShapeDtypeStruct((heads, 1, rows), jnp.float32),
        ],
        grid_spec=pltpu.PrefetchScalarGridSpec(
            num_scalar_prefetch=2,
            grid=(heads,),
            in_specs=[by_head(block_rows)] * members + [by_head(tok_rows)] * members + [whole] * 2,
            out_specs=[
                pl.BlockSpec((HEAD_DIM, rows), lambda h, *_: (h, 0)),
                pl.BlockSpec((1, 1, rows), lambda h, *_: (h, 0, 0)),
            ],
        ),
        compiler_params=pltpu.CompilerParams(vmem_limit_bytes=48 * 1024 * 1024),
        cost_estimate=pl.CostEstimate(
            flops=4 * rows * members * tokens * columns,
            bytes_accessed=2 * members * (block_rows + tok_rows) * columns,
            transcendentals=rows * members * tokens * heads,
        ),
    )(page_req, page_slot, *blocks, *far, row_req, row_pos)


def project_kernel(mine, mine_level, theirs, their_level, proj, stay, *gos):
    place = 3 - pl.program_id(0)
    parts = []
    for head in range(mine.shape[0] // HEAD_DIM):
        dims = slice(head * HEAD_DIM, (head + 1) * HEAD_DIM)
        share = 1.0 / (1.0 + jnp.exp(their_level[head] - mine_level[head]))
        other = 1.0 / (1.0 + jnp.exp(mine_level[head] - their_level[head]))
        both = share * mine[dims, :].astype(jnp.float32) + other * theirs[dims, :].astype(
            jnp.float32
        )
        parts.append(both.astype(jnp.bfloat16))
    attention = jnp.concatenate(parts, axis=0) if len(parts) > 1 else parts[0]
    mixed = lax.dot_general(
        attention, proj[...], (((0,), (0,)), ((), ())), preferred_element_type=jnp.float32
    )
    rows = stay.shape[0]
    stay[...] = mixed[:rows, :]
    for i, go in enumerate(gos):
        @pl.when(place == i)
        def _(go=go):
            go[...] = mixed[rows:, :].astype(jnp.bfloat16)


def project(mine, mine_level, theirs, their_level, proj, tok_rows):
    columns, width = proj.shape
    heads = columns // HEAD_DIM
    size = mine.shape[1] // 4
    return pl.pallas_call(
        project_kernel,
        out_shape=[jax.ShapeDtypeStruct((4 * tok_rows, width), jnp.float32)]
        + [jax.ShapeDtypeStruct((size - tok_rows, width), jnp.bfloat16)] * 4,
        grid=(4,),
        in_specs=[
            pl.BlockSpec((columns, size), lambda i: (0, 3 - i)),
            pl.BlockSpec((heads, 1, size), lambda i: (0, 0, 3 - i)),
            pl.BlockSpec((columns, size), lambda i: (0, (5 - i) % 4)),
            pl.BlockSpec((heads, 1, size), lambda i: (0, 0, (5 - i) % 4)),
            pl.BlockSpec((columns, width), lambda i: (0, 0)),
        ],
        out_specs=[pl.BlockSpec((tok_rows, width), lambda i: (3 - i, 0))]
        + [pl.BlockSpec((size - tok_rows, width), lambda i: (0, 0))] * 4,
        cost_estimate=pl.CostEstimate(
            flops=8 * size * columns * width,
            bytes_accessed=2 * (8 * columns * size + columns * width + 4 * size * width),
            transcendentals=8 * size * heads,
        ),
    )(mine, mine_level, theirs, their_level, proj)


def join_kernel(*refs):
    parts, out = refs[:-1], refs[-1]
    rows = parts[0].shape[0]
    for i, part in enumerate(parts):
        out[i * rows : (i + 1) * rows, :] = part[...]


def join(parts):
    rows, width = parts[0].shape
    vmem = pl.BlockSpec(memory_space=pltpu.VMEM)
    return pl.pallas_call(
        join_kernel,
        out_shape=jax.ShapeDtypeStruct((len(parts) * rows, width), parts[0].dtype),
        in_specs=[vmem] * len(parts),
        out_specs=vmem,
        cost_estimate=pl.CostEstimate(
            flops=0, bytes_accessed=4 * len(parts) * rows * width, transcendentals=0
        ),
    )(*parts)


def silu(value):
    return value / (1.0 + jnp.exp(-value))


def shared_kernel(rows, scalar, gate_w, up_w, down_w, out, gate_v, up_v, down_v, sems):
    copies = [
        pltpu.make_async_copy(src, dst, sems.at[i])
        for i, (src, dst) in enumerate(((gate_w, gate_v), (up_w, up_v), (down_w, down_v)))
    ]
    for copy in copies:
        copy.start()
    block = rows[...]
    logit = jnp.sum(
        block.astype(jnp.float32) * scalar[...].astype(jnp.float32), axis=1, keepdims=True
    )
    scale = 1.0 / (1.0 + jnp.exp(-logit))
    copies[0].wait()
    across = (((1,), (1,)), ((), ()))
    gate = lax.dot_general(block, gate_v[...], across, preferred_element_type=jnp.float32)
    copies[1].wait()
    upper = lax.dot_general(block, up_v[...], across, preferred_element_type=jnp.float32)
    hidden = (silu(gate) * upper).astype(jnp.bfloat16)
    copies[2].wait()
    result = jnp.dot(hidden, down_v[...], preferred_element_type=jnp.float32)
    out[...] = (scale * result).astype(jnp.bfloat16)


def shared_expert(rows, scalar, gate_w, up_w, down_w):
    any_spec = pl.BlockSpec(memory_space=pl.ANY)
    vmem = pl.BlockSpec(memory_space=pltpu.VMEM)
    return pl.pallas_call(
        shared_kernel,
        out_shape=jax.ShapeDtypeStruct(rows.shape, jnp.bfloat16),
        in_specs=[vmem, vmem, any_spec, any_spec, any_spec],
        out_specs=vmem,
        scratch_shapes=[
            pltpu.VMEM(gate_w.shape, jnp.bfloat16),
            pltpu.VMEM(up_w.shape, jnp.bfloat16),
            pltpu.VMEM(down_w.shape, jnp.bfloat16),
            pltpu.SemaphoreType.DMA((3,)),
        ],
        compiler_params=pltpu.CompilerParams(vmem_limit_bytes=48 * 1024 * 1024),
        cost_estimate=pl.CostEstimate(
            flops=6 * rows.shape[0] * gate_w.size,
            bytes_accessed=6 * gate_w.size + 4 * rows.size,
            transcendentals=rows.shape[0] * gate_w.shape[0],
        ),
    )(rows, scalar.reshape(1, -1), gate_w, up_w, down_w)


def routed_kernel(count, entries, has_extra, *refs):
    chunks, refs = refs[:count], refs[count:]
    place, row_gate, extra, gate_w, up_w, down_w = refs[:6]
    outs, refs = refs[6 : 6 + count], refs[6 + count :]
    rows, packed, gate_v, up_v, down_v, extra_v, sems = refs
    moves = [(chunks[c], rows.at[c]) for c in range(count)]
    moves += [(gate_w.at[0], gate_v), (up_w.at[0], up_v), (down_w.at[0], down_v)]
    if has_extra:
        moves.append((extra, extra_v))
    copies = [
        pltpu.make_async_copy(src, dst, sems.at[i]) for i, (src, dst) in enumerate(moves)
    ]
    for copy in copies:
        copy.start()
    size = chunks[0].shape[0]
    wanted = lax.broadcasted_iota(jnp.int32, (entries, size), 0)
    picks, weights = [], []
    for c in range(count):
        pick = jnp.where(place[c] == wanted, 1.0, 0.0)
        picks.append(pick.astype(jnp.bfloat16))
        weights.append(jnp.sum(pick * row_gate[c], axis=1, keepdims=True))
        copies[c].wait()
        packed[c * entries : (c + 1) * entries, :] = jnp.dot(
            picks[c], rows[c], preferred_element_type=jnp.float32
        ).astype(jnp.bfloat16)
    copies[count].wait()
    gate = jnp.dot(packed[...], gate_v[...], preferred_element_type=jnp.float32)
    copies[count + 1].wait()
    upper = jnp.dot(packed[...], up_v[...], preferred_element_type=jnp.float32)
    hidden = (silu(gate) * upper).astype(jnp.bfloat16)
    copies[count + 2].wait()
    answer = jnp.dot(hidden, down_v[...], preferred_element_type=jnp.float32).astype(
        jnp.bfloat16
    )
    if has_extra:
        copies[count + 3].wait()
    for c in range(count):
        scaled = answer[c * entries : (c + 1) * entries, :].astype(jnp.float32) * weights[c]
        placed = lax.dot_general(
            picks[c],
            scaled.astype(jnp.bfloat16),
            (((0,), (0,)), ((), ())),
            preferred_element_type=jnp.float32,
        )
        if c == 0 and has_extra:
            placed = placed + extra_v[...].astype(jnp.float32)
        outs[c][...] = placed.astype(jnp.bfloat16)


def routed_expert(chunks, place, row_gate, extra, gate_w, up_w, down_w, entries):
    count = len(chunks)
    size, width = chunks[0].shape
    hidden = gate_w.shape[2]
    any_spec = pl.BlockSpec(memory_space=pl.ANY)
    vmem = pl.BlockSpec(memory_space=pltpu.VMEM)
    has_extra = extra is not None
    if not has_extra:
        extra = jnp.zeros((16, 128), jnp.bfloat16)
    return pl.pallas_call(
        functools.partial(routed_kernel, count, entries, has_extra),
        out_shape=[jax.ShapeDtypeStruct((size, width), jnp.bfloat16)] * count,
        in_specs=[any_spec] * count + [vmem] * 2 + [any_spec] * 4,
        out_specs=[vmem] * count,
        scratch_shapes=[
            pltpu.VMEM((count, size, width), jnp.bfloat16),
            pltpu.VMEM((count * entries, width), jnp.bfloat16),
            pltpu.VMEM((width, hidden), jnp.bfloat16),
            pltpu.VMEM((width, hidden), jnp.bfloat16),
            pltpu.VMEM((hidden, width), jnp.bfloat16),
            pltpu.VMEM(extra.shape, jnp.bfloat16),
            pltpu.SemaphoreType.DMA((count + 4,)),
        ],
        compiler_params=pltpu.CompilerParams(vmem_limit_bytes=56 * 1024 * 1024),
        cost_estimate=pl.CostEstimate(
            flops=2 * count * entries * (3 * gate_w.size + 2 * size * width),
            bytes_accessed=6 * gate_w.size + 4 * count * size * width,
            transcendentals=count * entries * hidden,
        ),
    )(*chunks, place, row_gate, extra, gate_w, up_w, down_w)


def rms_normed(stream, norm_gain):
    scale_row = lax.rsqrt(jnp.mean(stream * stream, axis=1, keepdims=True) + 1e-06)
    return (stream * scale_row * norm_gain[None, :]).astype(jnp.bfloat16)


def shards(
    resid,
    queries,
    cache_key,
    cache_value,
    page_table,
    row_request,
    row_position,
    out_proj,
    norm_gain,
    expert_gate,
    expert_up,
    expert_down,
    shared_gate,
    shared_up,
    shared_down,
    shared_scalar,
    slot_expert,
    route_expert,
    route_gate,
):
    f32, bf16, i32 = jnp.float32, jnp.bfloat16, jnp.int32
    exp_count = lax.axis_size("exp")
    req_count = lax.axis_size("req")
    slot_count = exp_count * req_count
    nc, nx, ny = CORES, exp_count // Z_CHIPS, req_count // CORES
    exp_index = lax.axis_index("exp")
    req_index = lax.axis_index("req")
    own_slot = req_index * exp_count + exp_index
    iz, ix = exp_index // nx, exp_index % nx
    ih, il = iz // 2, iz % 2
    iy, ic = req_index // nc, req_index % nc
    tok_rows, width = resid.shape
    pages_here, page_len, _ = cache_key.shape
    req_slots, max_pages = page_table.shape
    tokens = pages_here * page_len
    capacity = 3 * tok_rows * TOPK // slot_count

    zs = [(dh, dl) for dh in range(2) for dl in range(2)]

    def send(value, dh, dl, dx):
        if not (dh or dl or dx % nx):
            return value
        pairs = [
            (
                (h * 2 + l) * nx + x,
                ((h + dh) % 2 * 2 + (l + dl) % 2) * nx + (x + dx) % nx,
            )
            for h in range(2)
            for l in range(2)
            for x in range(nx)
        ]
        return lax.ppermute(value, "exp", pairs)

    def send_req(value, dy, dc):
        if not (dy % ny or dc % nc):
            return value
        pairs = [
            (y * nc + c, (y + dy) % ny * nc + (c + dc) % nc)
            for y in range(ny)
            for c in range(nc)
        ]
        return lax.ppermute(value, "req", pairs)

    rel_exp = jnp.stack(
        [
            ((ih + dh) % 2 * 2 + (il + dl) % 2) * nx + (ix - dx) % nx
            for dh, dl in zs
            for dx in range(nx)
        ]
    ).astype(i32)
    rel_req = jnp.stack(
        [((iy - dy) % ny) * nc + (ic - dc) % nc for dy in range(ny) for dc in range(nc)]
    ).astype(i32)

    columns = width // exp_count
    keys = cache_key.reshape(tokens, width)
    values = cache_value.reshape(tokens, width)
    far_queries = send(queries, 1, 0, 0)
    members = [(dl, dx) for dl in range(2) for dx in range(nx)]
    order = jnp.stack(
        [
            ((ih + j) % 2 * 2 + (il + dl) % 2) * nx + (ix + dx) % nx
            for dl, dx in members
            for j in range(2)
        ]
    ).astype(i32)
    gates = jnp.pad(jnp.transpose(route_gate), ((0, 0), (0, 2 * columns - tok_rows)))
    blocks = pack([keys, values, queries], gates, order, columns)
    blocks = [send(blocks[m], 0, *members[m]) for m in range(len(members))]
    far = pack([far_queries], None, order, columns)
    far = [send(far[m], 0, *members[m]) for m in range(len(members))]
    page_ids = (
        rel_exp[: len(members), None] * pages_here + jnp.arange(pages_here, dtype=i32)[None, :]
    ).reshape(-1)
    hits = (page_table[None, :, :] == page_ids[:, None, None]).astype(i32)
    page_request = jnp.sum(hits * jnp.arange(req_slots, dtype=i32)[None, :, None], axis=(1, 2))
    page_slot = jnp.sum(hits * jnp.arange(max_pages, dtype=i32)[None, None, :], axis=(1, 2))
    rel_rows = lambda a: a.reshape(exp_count, tok_rows)[rel_exp].reshape(1, -1)
    partial, level = attend(
        blocks,
        far,
        rel_rows(row_request),
        rel_rows(row_position),
        page_request,
        page_slot,
        page_len,
        tokens,
    )
    other = send(partial[columns:], 1, 0, 0)
    other_level = send(level[columns // HEAD_DIM :], 1, 0, 0)

    slot_ids = jnp.arange(slot_count, dtype=i32)
    own_mark = slot_ids == own_slot
    own_expert = jnp.sum(jnp.where(own_mark, slot_expert, 0))
    twins = slot_expert == own_expert
    copies = jnp.sum(twins.astype(i32))
    own_rank = jnp.sum((twins & (slot_ids < own_slot)).astype(i32))
    gates = [block[2 * tokens + tok_rows :, :tok_rows].astype(f32) for block in blocks]
    gates = jnp.stack([g[:TOPK] + g[TOPK : 2 * TOPK] + g[2 * TOPK : 3 * TOPK] for g in gates])
    gates = gates.reshape(2, nx, TOPK, tok_rows)
    gates = jnp.stack([send(gates, dh, 0, 0) for dh in range(2)])
    gates = jnp.stack([send_req(gates, dy, 0) for dy in range(ny)])
    gates = jnp.stack([send_req(gates, 0, dc) for dc in range(nc)], axis=1)
    gates = jnp.transpose(gates, (0, 1, 4, 2, 3, 5, 6)).reshape(slot_count, TOPK, tok_rows)
    rel_exp = jnp.transpose(rel_exp.reshape(len(zs), nx)).reshape(-1)
    rel_slots = (rel_req[:, None] * exp_count + rel_exp[None, :]).reshape(-1)
    named = (route_expert == own_expert).reshape(slot_count, tok_rows, TOPK)[rel_slots]
    named = jnp.transpose(named, (0, 2, 1))
    chunk_rows = exp_count * tok_rows
    entries = -(-exp_count * capacity // 16) * 16
    row_gate = jnp.sum(jnp.where(named, gates, 0.0), axis=1).reshape(ny, nc, chunk_rows)
    mine = jnp.any(named, axis=1) & (rel_slots % copies == own_rank)[:, None]
    mine = mine.reshape(ny, nc, chunk_rows)
    place = jnp.where(mine, jnp.cumsum(mine.astype(i32), axis=2) - 1, -1)
    place = place.reshape(ny, nc, 1, chunk_rows)
    row_gate = row_gate.reshape(ny, nc, 1, chunk_rows)

    tie = lax.optimization_barrier
    last = len(zs) - 1

    stay, *goes = project(partial, level, other, other_level, out_proj, tok_rows)
    stay = stay.reshape(len(zs), tok_rows, width)
    comes = [
        [send(go[(dx - 1) * tok_rows : dx * tok_rows], 0, 0, -dx) for dx in range(1, nx)]
        for go in goes
    ]
    lines = {}
    for i in reversed(range(len(zs))):
        line = stay[i]
        for come in comes[i]:
            line = line + come.astype(f32)
        if i:
            line = line.astype(bf16)
            comes[i - 1], line = tie((comes[i - 1], line))
            line = send(line, *zs[i], 0)
        lines[i] = line
    stream = resid.astype(f32) + lines[0]
    for i in range(1, len(zs)):
        stream = stream + lines[i].astype(f32)
    normed = rms_normed(stream, norm_gain)
    normed, place, row_gate = tie((normed, place, row_gate))

    line = [send(normed, *zs[i], 0) for i in range(len(zs))]
    piece = {}
    for i in range(len(zs)):
        piece[i, 0, 0] = line[i]
        for dx in range(1, nx):
            piece[i, dx, 0] = send(line[i], 0, 0, dx)
        for dy in range(1, ny):
            piece[i, 0, dy] = send_req(line[i], dy, 0)
    piece = tie(piece)
    for dy in range(1, ny):
        for dx in range(1, nx):
            for i in range(len(zs)):
                piece[i, dx, dy] = send(piece[i, 0, dy], 0, 0, dx)

    chunk_of = lambda dy: join([piece[i, dx, dy] for dx in range(nx) for i in range(len(zs))])
    partners_of = lambda chunk: [send_req(chunk, 0, dc) for dc in range(1, nc)]
    chunk = chunk_of(0)
    partners = partners_of(chunk)
    extra = shared_expert(chunk, shared_scalar, shared_gate.T, shared_up.T, shared_down)
    if ny > 1:
        half = [(i, dx, 1) for dx in range(1, nx) for i in range(len(zs) // 2)]
        extra, partners, *arrived = tie((extra, partners, *[piece[n] for n in half]))
        for name, value in zip(half, arrived):
            piece[name] = value

    sums = {}
    for dy in range(ny):
        answers = routed_expert(
            [chunk] + partners,
            place[dy],
            row_gate[dy],
            extra,
            expert_gate,
            expert_up,
            expert_down,
            entries,
        )
        extra = None
        answers, *rest = tie((answers, *[piece[i, dx, d] for i, dx, d in piece if d == dy + 1]))
        for name, value in zip([n for n in piece if n[2] == dy + 1], rest):
            piece[name] = value
        others = [send_req(answers[dc], 0, -dc) for dc in range(1, nc)]
        if dy + 1 < ny:
            chunk = chunk_of(dy + 1)
            chunk, others = tie((chunk, others))
            partners = partners_of(chunk)
        here = answers[0].astype(f32)
        for come in others:
            here = here + come.astype(f32)
        here = here.reshape(nx, len(zs), tok_rows, width)
        gone = here[1:].astype(bf16)
        if dy + 1 < ny:
            partners, gone = tie((partners, gone))
            comes = [send(gone[dx - 1], 0, 0, -dx) for dx in range(1, nx)]
            comes = [[come[i] for come in comes] for i in range(len(zs))]
        else:
            comes = [
                [send(gone[dx - 1, i], 0, 0, -dx) for dx in range(1, nx)] for i in range(len(zs))
            ]
        sums[dy] = (here[0], comes)

    lines = {}
    for i in reversed(range(len(zs))):
        total = {}
        for dy in range(ny):
            here, comes = sums[dy]
            total[dy] = here[i]
            for come in comes[i]:
                total[dy] = total[dy] + come.astype(f32)
        goes = [total[dy].astype(bf16) for dy in range(1, ny)]
        if i:
            comes = sums[ny - 1][1]
            comes[i - 1], goes = tie((comes[i - 1], goes))
        lines[i] = (total[0], [send_req(go, -dy, 0) for dy, go in enumerate(goes, 1)])
    home = stream
    arrived = {}
    for i in reversed(range(len(zs))):
        total, comes = lines[i]
        for come in comes:
            total = total + come.astype(f32)
        if i:
            total = total.astype(bf16)
            here, comes = lines[i - 1]
            comes, total = tie((comes, total))
            lines[i - 1] = (here, comes)
            arrived[i] = send(total, *zs[i], 0)
        else:
            home = home + total
    for i in range(1, len(zs)):
        home = home + arrived[i].astype(f32)
    total = home
    return total.astype(bf16)


def solution(mesh):
    placed = (
        P(("req", "exp"), None),
        P(("req", "exp"), None),
        P(("req", "exp"), None, None),
        P(("req", "exp"), None, None),
        P("req", None),
        P("req"),
        P("req"),
        P("exp", None),
        P(),
        P(("req", "exp"), None, None),
        P(("req", "exp"), None, None),
        P(("req", "exp"), None, None),
        P(None, "exp"),
        P(None, "exp"),
        P("exp", None),
        P(),
        P(),
        P(),
        P(("req", "exp"), None),
    )
    return jax.shard_map(
        shards, mesh=mesh, in_specs=placed, out_specs=P(("req", "exp"), None), check_vma=False
    )
```

```python
import functools

import jax
import jax.numpy as jnp
from jax import lax
from jax.experimental import pallas as pl
from jax.experimental.pallas import tpu as pltpu
from jax.sharding import PartitionSpec as P

HEAD_DIM = 128
TOPK = 4
CORES = 2
Z_CHIPS = 4


def pack_kernel(members, *refs):
    keys, values, queries = (refs[i * members : (i + 1) * members] for i in range(3))
    gates, blocks = refs[3 * members], refs[3 * members + 1 :]
    weights = gates[...]
    high = weights.astype(jnp.bfloat16).astype(jnp.float32)
    middle = (weights - high).astype(jnp.bfloat16).astype(jnp.float32)
    low = weights - high - middle
    weights = jnp.concatenate([high, middle, low, jnp.zeros_like(low)], axis=0)
    weights = weights.astype(jnp.bfloat16)
    for m in range(members):
        tokens, rows = keys[m].shape[0], queries[m].shape[0]
        blocks[m][:tokens, :] = keys[m][...]
        blocks[m][tokens : 2 * tokens, :] = values[m][...]
        blocks[m][2 * tokens : 2 * tokens + rows, :] = queries[m][...]
        blocks[m][2 * tokens + rows :, :] = weights


def pack_far_kernel(members, *refs):
    for m in range(members):
        refs[members + m][...] = refs[m][...]


def pack(parts, gates, order, columns):
    members = order.shape[0] // 2
    rows = sum(p.shape[0] for p in parts) + (0 if gates is None else 4 * gates.shape[0])
    kernel = functools.partial(pack_far_kernel if gates is None else pack_kernel, members)

    def column(n, m):
        return pl.BlockSpec((n, columns), lambda j, order: (0, order[2 * m + j]))

    in_specs = [column(p.shape[0], m) for p in parts for m in range(members)]
    operands = [p for p in parts for m in range(members)]
    if gates is not None:
        in_specs.append(pl.BlockSpec((gates.shape[0], columns), lambda j, order: (0, j)))
        operands.append(gates)
    return pl.pallas_call(
        lambda order, *refs: kernel(*refs),
        out_shape=[jax.ShapeDtypeStruct((rows, 2 * columns), parts[0].dtype)] * members,
        grid_spec=pltpu.PrefetchScalarGridSpec(
            num_scalar_prefetch=1,
            grid=(2,),
            in_specs=in_specs,
            out_specs=[pl.BlockSpec((rows, columns), lambda j, order: (0, j))] * members,
        ),
        compiler_params=pltpu.CompilerParams(vmem_limit_bytes=32 * 1024 * 1024),
        cost_estimate=pl.CostEstimate(
            flops=0, bytes_accessed=8 * members * rows * columns, transcendentals=0
        ),
    )(order, *operands)


def attend_kernel(members, tokens, page_len, scale, page_req, page_slot, *refs):
    blocks, far, refs = refs[:members], refs[members : 2 * members], refs[2 * members :]
    row_req, row_pos, out, level = refs
    keys = jnp.concatenate([block[:tokens, :] for block in blocks], axis=0)
    values = jnp.concatenate([block[tokens : 2 * tokens, :] for block in blocks], axis=0)
    tok_rows = far[0].shape[0]
    near = [block[2 * tokens : 2 * tokens + tok_rows, :] for block in blocks]
    size = sum(q.shape[0] for q in near)
    for side, query in enumerate((near, [q[...] for q in far])):
        lanes = slice(side * size, (side + 1) * size)
        query = jnp.concatenate(query, axis=0)
        request, position = row_req[:, lanes], row_pos[:, lanes]
        scores = (
            lax.dot_general(
                keys, query, (((1,), (1,)), ((), ())), preferred_element_type=jnp.float32
            )
            * scale
        )
        token = lax.broadcasted_iota(jnp.int32, (page_len, size), 0)
        visible = jnp.concatenate(
            [
                (request == page_req[page]) & (token + page_slot[page] * page_len <= position)
                for page in range(members * tokens // page_len)
            ],
            axis=0,
        )
        scores = jnp.where(visible, scores, -1e30)
        top = jnp.max(scores, axis=0, keepdims=True)
        weights = jnp.where(visible, jnp.exp(scores - top), 0.0)
        total = jnp.sum(weights, axis=0, keepdims=True)
        summed = lax.dot_general(
            values,
            weights.astype(jnp.bfloat16),
            (((0,), (0,)), ((), ())),
            preferred_element_type=jnp.float32,
        )
        seen = total > 0.0
        total = jnp.where(seen, total, 1.0)
        out[:, lanes] = (summed / total).astype(jnp.bfloat16)
        level[0, :, lanes] = jnp.where(seen, top + jnp.log(total), -1e30)


def attend(blocks, far, row_req, row_pos, page_req, page_slot, page_len, tokens):
    members, rows = len(blocks), row_req.shape[1]
    block_rows, columns = blocks[0].shape
    tok_rows = far[0].shape[0]
    heads = columns // HEAD_DIM
    by_head = lambda n: pl.BlockSpec((n, HEAD_DIM), lambda h, *_: (0, h))
    whole = pl.BlockSpec((1, rows), lambda h, *_: (0, 0))
    return pl.pallas_call(
        functools.partial(attend_kernel, members, tokens, page_len, HEAD_DIM ** (-0.5)),
        out_shape=[
            jax.ShapeDtypeStruct((columns, rows), jnp.bfloat16),
            jax.ShapeDtypeStruct((heads, 1, rows), jnp.float32),
        ],
        grid_spec=pltpu.PrefetchScalarGridSpec(
            num_scalar_prefetch=2,
            grid=(heads,),
            in_specs=[by_head(block_rows)] * members + [by_head(tok_rows)] * members + [whole] * 2,
            out_specs=[
                pl.BlockSpec((HEAD_DIM, rows), lambda h, *_: (h, 0)),
                pl.BlockSpec((1, 1, rows), lambda h, *_: (h, 0, 0)),
            ],
        ),
        compiler_params=pltpu.CompilerParams(vmem_limit_bytes=48 * 1024 * 1024),
        cost_estimate=pl.CostEstimate(
            flops=4 * rows * members * tokens * columns,
            bytes_accessed=2 * members * (block_rows + tok_rows) * columns,
            transcendentals=rows * members * tokens * heads,
        ),
    )(page_req, page_slot, *blocks, *far, row_req, row_pos)


def project_kernel(mine, mine_level, theirs, their_level, proj, stay, go):
    parts = []
    for head in range(mine.shape[0] // HEAD_DIM):
        dims = slice(head * HEAD_DIM, (head + 1) * HEAD_DIM)
        share = 1.0 / (1.0 + jnp.exp(their_level[head] - mine_level[head]))
        other = 1.0 / (1.0 + jnp.exp(mine_level[head] - their_level[head]))
        both = share * mine[dims, :].astype(jnp.float32) + other * theirs[dims, :].astype(
            jnp.float32
        )
        parts.append(both.astype(jnp.bfloat16))
    attention = jnp.concatenate(parts, axis=0) if len(parts) > 1 else parts[0]
    mixed = lax.dot_general(
        attention, proj[...], (((0,), (0,)), ((), ())), preferred_element_type=jnp.float32
    )
    rows = stay.shape[1]
    stay[0] = mixed[:rows, :]
    go[0] = mixed[rows:, :].astype(jnp.bfloat16)


def project(pair, mine, mine_level, theirs, their_level, proj, tok_rows):
    columns, width = proj.shape
    heads = columns // HEAD_DIM
    size = mine.shape[1] // 4
    here, there = 2 * pair, 2 * (1 - pair)
    return pl.pallas_call(
        project_kernel,
        out_shape=[
            jax.ShapeDtypeStruct((2, tok_rows, width), jnp.float32),
            jax.ShapeDtypeStruct((2, size - tok_rows, width), jnp.bfloat16),
        ],
        grid=(2,),
        in_specs=[
            pl.BlockSpec((columns, size), lambda i: (0, here + i)),
            pl.BlockSpec((heads, 1, size), lambda i: (0, 0, here + i)),
            pl.BlockSpec((columns, size), lambda i: (0, there + i)),
            pl.BlockSpec((heads, 1, size), lambda i: (0, 0, there + i)),
            pl.BlockSpec((columns, width), lambda i: (0, 0)),
        ],
        out_specs=[
            pl.BlockSpec((1, tok_rows, width), lambda i: (i, 0, 0)),
            pl.BlockSpec((1, size - tok_rows, width), lambda i: (i, 0, 0)),
        ],
        cost_estimate=pl.CostEstimate(
            flops=4 * size * columns * width,
            bytes_accessed=2 * (4 * columns * size + columns * width + 2 * size * width),
            transcendentals=4 * size * heads,
        ),
    )(mine, mine_level, theirs, their_level, proj)


def join_kernel(*refs):
    parts, out = refs[:-1], refs[-1]
    rows = parts[0].shape[0]
    for i, part in enumerate(parts):
        out[i * rows : (i + 1) * rows, :] = part[...]


def join(parts):
    rows, width = parts[0].shape
    vmem = pl.BlockSpec(memory_space=pltpu.VMEM)
    return pl.pallas_call(
        join_kernel,
        out_shape=jax.ShapeDtypeStruct((len(parts) * rows, width), parts[0].dtype),
        in_specs=[vmem] * len(parts),
        out_specs=vmem,
        cost_estimate=pl.CostEstimate(
            flops=0, bytes_accessed=4 * len(parts) * rows * width, transcendentals=0
        ),
    )(*parts)


def silu(value):
    return value / (1.0 + jnp.exp(-value))


def shared_kernel(rows, scalar, gate_w, up_w, down_w, out, gate_v, up_v, down_v, sems):
    copies = [
        pltpu.make_async_copy(src, dst, sems.at[i])
        for i, (src, dst) in enumerate(((gate_w, gate_v), (up_w, up_v), (down_w, down_v)))
    ]
    for copy in copies:
        copy.start()
    block = rows[...]
    logit = jnp.sum(
        block.astype(jnp.float32) * scalar[...].astype(jnp.float32), axis=1, keepdims=True
    )
    scale = 1.0 / (1.0 + jnp.exp(-logit))
    copies[0].wait()
    across = (((1,), (1,)), ((), ()))
    gate = lax.dot_general(block, gate_v[...], across, preferred_element_type=jnp.float32)
    copies[1].wait()
    upper = lax.dot_general(block, up_v[...], across, preferred_element_type=jnp.float32)
    hidden = (silu(gate) * upper).astype(jnp.bfloat16)
    copies[2].wait()
    result = jnp.dot(hidden, down_v[...], preferred_element_type=jnp.float32)
    out[...] = (scale * result).astype(jnp.bfloat16)


def shared_expert(rows, scalar, gate_w, up_w, down_w):
    any_spec = pl.BlockSpec(memory_space=pl.ANY)
    vmem = pl.BlockSpec(memory_space=pltpu.VMEM)
    return pl.pallas_call(
        shared_kernel,
        out_shape=jax.ShapeDtypeStruct(rows.shape, jnp.bfloat16),
        in_specs=[vmem, vmem, any_spec, any_spec, any_spec],
        out_specs=vmem,
        scratch_shapes=[
            pltpu.VMEM(gate_w.shape, jnp.bfloat16),
            pltpu.VMEM(up_w.shape, jnp.bfloat16),
            pltpu.VMEM(down_w.shape, jnp.bfloat16),
            pltpu.SemaphoreType.DMA((3,)),
        ],
        compiler_params=pltpu.CompilerParams(vmem_limit_bytes=48 * 1024 * 1024),
        cost_estimate=pl.CostEstimate(
            flops=6 * rows.shape[0] * gate_w.size,
            bytes_accessed=6 * gate_w.size + 4 * rows.size,
            transcendentals=rows.shape[0] * gate_w.shape[0],
        ),
    )(rows, scalar.reshape(1, -1), gate_w, up_w, down_w)


def routed_kernel(parts, entries, has_extra, *refs):
    count, total = len(parts), sum(parts)
    pieces, refs = refs[:total], refs[total:]
    place, row_gate, extra, gate_w, up_w, down_w = refs[:6]
    outs, refs = refs[6 : 6 + count], refs[6 + count :]
    rows, packed, gate_v, up_v, down_v, extra_v, sems = refs
    moves, chunk_copies = [], []
    for c, n in enumerate(parts):
        at = 0
        chunk_copies.append(range(len(moves), len(moves) + n))
        for piece in pieces[sum(parts[:c]) : sum(parts[: c + 1])]:
            moves.append((piece, rows.at[c, pl.ds(at, piece.shape[0])]))
            at += piece.shape[0]
    moves += [(gate_w.at[0], gate_v), (up_w.at[0], up_v), (down_w.at[0], down_v)]
    if has_extra:
        moves.append((extra, extra_v))
    copies = [
        pltpu.make_async_copy(src, dst, sems.at[i]) for i, (src, dst) in enumerate(moves)
    ]
    for copy in copies:
        copy.start()
    size = rows.shape[1]
    wanted = lax.broadcasted_iota(jnp.int32, (entries, size), 0)
    picks, weights = [], []
    for c in range(count):
        pick = jnp.where(place[c] == wanted, 1.0, 0.0)
        picks.append(pick.astype(jnp.bfloat16))
        weights.append(jnp.sum(pick * row_gate[c], axis=1, keepdims=True))
        for i in chunk_copies[c]:
            copies[i].wait()
        packed[c * entries : (c + 1) * entries, :] = jnp.dot(
            picks[c], rows[c], preferred_element_type=jnp.float32
        ).astype(jnp.bfloat16)
    copies[total].wait()
    gate = jnp.dot(packed[...], gate_v[...], preferred_element_type=jnp.float32)
    copies[total + 1].wait()
    upper = jnp.dot(packed[...], up_v[...], preferred_element_type=jnp.float32)
    hidden = (silu(gate) * upper).astype(jnp.bfloat16)
    copies[total + 2].wait()
    answer = jnp.dot(hidden, down_v[...], preferred_element_type=jnp.float32).astype(
        jnp.bfloat16
    )
    if has_extra:
        copies[total + 3].wait()
    for c in range(count):
        scaled = answer[c * entries : (c + 1) * entries, :].astype(jnp.float32) * weights[c]
        placed = lax.dot_general(
            picks[c],
            scaled.astype(jnp.bfloat16),
            (((0,), (0,)), ((), ())),
            preferred_element_type=jnp.float32,
        )
        if c == 0 and has_extra:
            placed = placed + extra_v[...].astype(jnp.float32)
        outs[c][...] = placed.astype(jnp.bfloat16)


def routed_expert(chunks, place, row_gate, extra, gate_w, up_w, down_w, entries):
    count = len(chunks)
    parts = [len(chunk) for chunk in chunks]
    total = sum(parts)
    size = sum(piece.shape[0] for piece in chunks[0])
    width = chunks[0][0].shape[1]
    hidden = gate_w.shape[2]
    any_spec = pl.BlockSpec(memory_space=pl.ANY)
    vmem = pl.BlockSpec(memory_space=pltpu.VMEM)
    has_extra = extra is not None
    if not has_extra:
        extra = jnp.zeros((16, 128), jnp.bfloat16)
    return pl.pallas_call(
        functools.partial(routed_kernel, parts, entries, has_extra),
        out_shape=[jax.ShapeDtypeStruct((size, width), jnp.bfloat16)] * count,
        in_specs=[any_spec] * total + [vmem] * 2 + [any_spec] * 4,
        out_specs=[vmem] * count,
        scratch_shapes=[
            pltpu.VMEM((count, size, width), jnp.bfloat16),
            pltpu.VMEM((count * entries, width), jnp.bfloat16),
            pltpu.VMEM((width, hidden), jnp.bfloat16),
            pltpu.VMEM((width, hidden), jnp.bfloat16),
            pltpu.VMEM((hidden, width), jnp.bfloat16),
            pltpu.VMEM(extra.shape, jnp.bfloat16),
            pltpu.SemaphoreType.DMA((total + 4,)),
        ],
        compiler_params=pltpu.CompilerParams(vmem_limit_bytes=56 * 1024 * 1024),
        cost_estimate=pl.CostEstimate(
            flops=2 * count * entries * (3 * gate_w.size + 2 * size * width),
            bytes_accessed=6 * gate_w.size + 4 * count * size * width,
            transcendentals=count * entries * hidden,
        ),
    )(*[piece for chunk in chunks for piece in chunk], place, row_gate, extra, gate_w, up_w, down_w)


def rms_normed(stream, norm_gain):
    scale_row = lax.rsqrt(jnp.mean(stream * stream, axis=1, keepdims=True) + 1e-06)
    return (stream * scale_row * norm_gain[None, :]).astype(jnp.bfloat16)


def shards(
    resid,
    queries,
    cache_key,
    cache_value,
    page_table,
    row_request,
    row_position,
    out_proj,
    norm_gain,
    expert_gate,
    expert_up,
    expert_down,
    shared_gate,
    shared_up,
    shared_down,
    shared_scalar,
    slot_expert,
    route_expert,
    route_gate,
):
    f32, bf16, i32 = jnp.float32, jnp.bfloat16, jnp.int32
    exp_count = lax.axis_size("exp")
    req_count = lax.axis_size("req")
    slot_count = exp_count * req_count
    nc, nx, ny = CORES, exp_count // Z_CHIPS, req_count // CORES
    exp_index = lax.axis_index("exp")
    req_index = lax.axis_index("req")
    own_slot = req_index * exp_count + exp_index
    iz, ix = exp_index // nx, exp_index % nx
    ih, il = iz // 2, iz % 2
    iy, ic = req_index // nc, req_index % nc
    tok_rows, width = resid.shape
    pages_here, page_len, _ = cache_key.shape
    req_slots, max_pages = page_table.shape
    tokens = pages_here * page_len
    capacity = 3 * tok_rows * TOPK // slot_count

    zs = [(dh, dl) for dh in range(2) for dl in range(2)]

    def send(value, dh, dl, dx):
        if not (dh or dl or dx % nx):
            return value
        pairs = [
            (
                (h * 2 + l) * nx + x,
                ((h + dh) % 2 * 2 + (l + dl) % 2) * nx + (x + dx) % nx,
            )
            for h in range(2)
            for l in range(2)
            for x in range(nx)
        ]
        return lax.ppermute(value, "exp", pairs)

    def send_req(value, dy, dc):
        if not (dy % ny or dc % nc):
            return value
        pairs = [
            (y * nc + c, (y + dy) % ny * nc + (c + dc) % nc)
            for y in range(ny)
            for c in range(nc)
        ]
        return lax.ppermute(value, "req", pairs)

    rel_exp = jnp.stack(
        [
            ((ih + dh) % 2 * 2 + (il + dl) % 2) * nx + (ix - dx) % nx
            for dh, dl in zs
            for dx in range(nx)
        ]
    ).astype(i32)
    rel_req = jnp.stack(
        [((iy - dy) % ny) * nc + (ic - dc) % nc for dy in range(ny) for dc in range(nc)]
    ).astype(i32)

    columns = width // exp_count
    keys = cache_key.reshape(tokens, width)
    values = cache_value.reshape(tokens, width)
    far_queries = send(queries, 1, 0, 0)
    members = [(dl, dx) for dl in range(2) for dx in range(nx)]
    order = jnp.stack(
        [
            ((ih + j) % 2 * 2 + (il + dl) % 2) * nx + (ix + dx) % nx
            for dl, dx in members
            for j in range(2)
        ]
    ).astype(i32)
    gates = jnp.pad(jnp.transpose(route_gate), ((0, 0), (0, 2 * columns - tok_rows)))
    blocks = pack([keys, values, queries], gates, order, columns)
    blocks = [send(blocks[m], 0, *members[m]) for m in range(len(members))]
    far = pack([far_queries], None, order, columns)
    far = [send(far[m], 0, *members[m]) for m in range(len(members))]
    page_ids = (
        rel_exp[: len(members), None] * pages_here + jnp.arange(pages_here, dtype=i32)[None, :]
    ).reshape(-1)
    hits = (page_table[None, :, :] == page_ids[:, None, None]).astype(i32)
    page_request = jnp.sum(hits * jnp.arange(req_slots, dtype=i32)[None, :, None], axis=(1, 2))
    page_slot = jnp.sum(hits * jnp.arange(max_pages, dtype=i32)[None, None, :], axis=(1, 2))
    rel_rows = lambda a: a.reshape(exp_count, tok_rows)[rel_exp].reshape(1, -1)
    gates = [block[2 * tokens + tok_rows :, :tok_rows].astype(f32) for block in blocks]
    gates = jnp.stack([g[:TOPK] + g[TOPK : 2 * TOPK] + g[2 * TOPK : 3 * TOPK] for g in gates])
    gates = gates.reshape(2, nx, TOPK, tok_rows)
    gates = jnp.stack([send(gates, dh, 0, 0) for dh in range(2)])
    partial, level = attend(
        blocks,
        far,
        rel_rows(row_request),
        rel_rows(row_position),
        page_request,
        page_slot,
        page_len,
        tokens,
    )
    partial, level, gates = lax.optimization_barrier((partial, level, gates))
    gates = jnp.stack([send_req(gates, dy, 0) for dy in range(ny)])
    other = send(partial[columns:], 1, 0, 0)
    other_level = send(level[columns // HEAD_DIM :], 1, 0, 0)
    other, other_level, gates = lax.optimization_barrier((other, other_level, gates))

    slot_ids = jnp.arange(slot_count, dtype=i32)
    own_mark = slot_ids == own_slot
    own_expert = jnp.sum(jnp.where(own_mark, slot_expert, 0))
    twins = slot_expert == own_expert
    copies = jnp.sum(twins.astype(i32))
    own_rank = jnp.sum((twins & (slot_ids < own_slot)).astype(i32))
    gates = jnp.stack([send_req(gates, 0, dc) for dc in range(nc)], axis=1)
    gates = jnp.transpose(gates, (0, 1, 4, 2, 3, 5, 6)).reshape(slot_count, TOPK, tok_rows)
    rel_exp = jnp.transpose(rel_exp.reshape(len(zs), nx)).reshape(-1)
    rel_slots = (rel_req[:, None] * exp_count + rel_exp[None, :]).reshape(-1)
    named = (route_expert == own_expert).reshape(slot_count, tok_rows, TOPK)[rel_slots]
    named = jnp.transpose(named, (0, 2, 1))
    chunk_rows = exp_count * tok_rows
    entries = -(-exp_count * capacity // 16) * 16
    row_gate = jnp.sum(jnp.where(named, gates, 0.0), axis=1).reshape(ny, nc, chunk_rows)
    mine = jnp.any(named, axis=1) & (rel_slots % copies == own_rank)[:, None]
    mine = mine.reshape(ny, nc, chunk_rows)
    place = jnp.where(mine, jnp.cumsum(mine.astype(i32), axis=2) - 1, -1)
    place = place.reshape(ny, nc, 1, chunk_rows)
    row_gate = row_gate.reshape(ny, nc, 1, chunk_rows)

    tie = lax.optimization_barrier
    last = len(zs) - 1

    tie = lax.optimization_barrier

    stays, comes = {}, {}
    mine = partial
    for pair in (1, 0):
        stays[pair], go = project(pair, mine, level, other, other_level, out_proj, tok_rows)
        mine, _ = tie((partial, go))
        go = go.reshape(2, nx - 1, tok_rows, width)
        comes[pair] = [send(go[:, dx - 1], 0, 0, -dx) for dx in range(1, nx)]
    stream = resid.astype(f32)
    arrived = []
    for pair in (1, 0):
        line = stays[pair]
        for come in comes[pair]:
            line = line + come.astype(f32)
        for i in (1, 0):
            if pair or i:
                go = line[i].astype(bf16)
                comes[0], _ = tie((comes[0], go))
                arrived.append(send(go, *zs[2 * pair + i], 0))
            else:
                stream = stream + line[0]
    for come in arrived:
        stream = stream + come.astype(f32)
    normed = rms_normed(stream, norm_gain)
    normed, place, row_gate = tie((normed, place, row_gate))

    line = [send(normed, *zs[i], 0) for i in range(len(zs))]
    piece = {}
    for i in range(len(zs)):
        piece[i, 0, 0] = line[i]
        for dx in range(1, nx):
            piece[i, dx, 0] = send(line[i], 0, 0, dx)
        for dy in range(1, ny):
            piece[i, 0, dy] = send_req(line[i], dy, 0)
    piece = tie(piece)
    chunk = join([piece[i, dx, 0] for dx in range(nx) for i in range(len(zs))])
    chunks = {(0, 0): [chunk]}
    for dc in range(1, nc):
        chunks[0, dc] = [send_req(chunk, 0, dc)]
    for dy in range(1, ny):
        half = join([piece[i, 0, dy] for i in range(len(zs))])
        chunks[dy, 0] = [send(half, 0, 0, dx) for dx in range(nx)]
    extra = shared_expert(chunk, shared_scalar, shared_gate.T, shared_up.T, shared_down)
    partners = [chunks[0, dc] for dc in range(1, nc)]
    extra, partners = tie((extra, partners))
    for dc in range(1, nc):
        chunks[0, dc] = partners[dc - 1]

    kept, comes = {}, {}
    for dy in range(ny):
        answers = routed_expert(
            [chunks[dy, dc] for dc in range(nc)],
            place[dy],
            row_gate[dy],
            extra,
            expert_gate,
            expert_up,
            expert_down,
            entries,
        )
        extra = None
        if dy:
            answers, comes[dy - 1][1] = tie((answers, comes[dy - 1][1]))
        if dy + 1 < ny:
            answers, chunks[dy + 1, 0] = tie((answers, chunks[dy + 1, 0]))
            for dc in range(1, nc):
                chunks[dy + 1, dc] = [send_req(part, 0, dc) for part in chunks[dy + 1, 0]]
        others = [send_req(answers[dc], 0, -dc) for dc in range(1, nc)]
        parts = [answers[0]] + others
        comes[dy] = {}
        for pair in (1, 0):
            gone = [
                part.reshape(nx, 2, 2, tok_rows, width)[1:, pair].astype(f32) for part in parts
            ]
            gone = sum(gone[1:], gone[0]).astype(bf16)
            comes[dy][pair] = [send(gone[dx - 1], 0, 0, -dx) for dx in range(1, nx)]
            if pair:
                parts, _ = tie((parts, gone))
        if dy + 1 < ny:
            following = [chunks[dy + 1, dc] for dc in range(nc)]
            following, _ = tie((following, gone))
            for dc in range(nc):
                chunks[dy + 1, dc] = following[dc]
        elif dy:
            parts, comes[dy - 1][0] = tie((parts, comes[dy - 1][0]))
        kept[dy] = parts

    def line_of(dy, pair):
        line = [p.reshape(nx, 2, 2, tok_rows, width)[0, pair].astype(f32) for p in kept[dy]]
        return sum([come.astype(f32) for come in comes[dy][pair]], sum(line[1:], line[0]))

    home = stream
    over_y, arrived = {}, []
    for pair in (1, 0):
        goes = [line_of(dy, pair).astype(bf16) for dy in range(1, ny)]
        over_y[pair] = [send_req(go, -dy, 0) for dy, go in enumerate(goes, 1)]
        if pair:
            comes[ny - 1][0], _ = tie((comes[ny - 1][0], goes))
    for pair in (1, 0):
        total = sum([come.astype(f32) for come in over_y[pair]], line_of(0, pair))
        for i in (1, 0):
            if pair or i:
                go = total[i].astype(bf16)
                over_y[0], _ = tie((over_y[0], go))
                arrived.append(send(go, *zs[2 * pair + i], 0))
            else:
                home = home + total[0]
    for come in arrived:
        home = home + come.astype(f32)
    total = home
    return total.astype(bf16)


def solution(mesh):
    placed = (
        P(("req", "exp"), None),
        P(("req", "exp"), None),
        P(("req", "exp"), None, None),
        P(("req", "exp"), None, None),
        P("req", None),
        P("req"),
        P("req"),
        P("exp", None),
        P(),
        P(("req", "exp"), None, None),
        P(("req", "exp"), None, None),
        P(("req", "exp"), None, None),
        P(None, "exp"),
        P(None, "exp"),
        P("exp", None),
        P(),
        P(),
        P(),
        P(("req", "exp"), None),
    )
    return jax.shard_map(
        shards, mesh=mesh, in_specs=placed, out_specs=P(("req", "exp"), None), check_vma=False
    )
```

```python
import functools

import jax
import jax.numpy as jnp
from jax import lax
from jax.experimental import pallas as pl
from jax.experimental.pallas import tpu as pltpu
from jax.sharding import PartitionSpec as P

HEAD_DIM = 128
TOPK = 4
CORES = 2
Z_CHIPS = 4


def pack_kernel(members, *refs):
    keys, values, queries = (refs[i * members : (i + 1) * members] for i in range(3))
    gates, blocks = refs[3 * members], refs[3 * members + 1 :]
    weights = gates[...]
    high = weights.astype(jnp.bfloat16).astype(jnp.float32)
    middle = (weights - high).astype(jnp.bfloat16).astype(jnp.float32)
    low = weights - high - middle
    weights = jnp.concatenate([high, middle, low, jnp.zeros_like(low)], axis=0)
    weights = weights.astype(jnp.bfloat16)
    for m in range(members):
        tokens, rows = keys[m].shape[0], queries[m].shape[0]
        blocks[m][:tokens, :] = keys[m][...]
        blocks[m][tokens : 2 * tokens, :] = values[m][...]
        blocks[m][2 * tokens : 2 * tokens + rows, :] = queries[m][...]
        blocks[m][2 * tokens + rows :, :] = weights


def pack_far_kernel(members, *refs):
    for m in range(members):
        refs[members + m][...] = refs[m][...]


def pack(parts, gates, order, columns):
    members = order.shape[0] // 2
    rows = sum(p.shape[0] for p in parts) + (0 if gates is None else 4 * gates.shape[0])
    kernel = functools.partial(pack_far_kernel if gates is None else pack_kernel, members)

    def column(n, m):
        return pl.BlockSpec((n, columns), lambda j, order: (0, order[2 * m + j]))

    in_specs = [column(p.shape[0], m) for p in parts for m in range(members)]
    operands = [p for p in parts for m in range(members)]
    if gates is not None:
        in_specs.append(pl.BlockSpec((gates.shape[0], columns), lambda j, order: (0, j)))
        operands.append(gates)
    return pl.pallas_call(
        lambda order, *refs: kernel(*refs),
        out_shape=[jax.ShapeDtypeStruct((rows, 2 * columns), parts[0].dtype)] * members,
        grid_spec=pltpu.PrefetchScalarGridSpec(
            num_scalar_prefetch=1,
            grid=(2,),
            in_specs=in_specs,
            out_specs=[pl.BlockSpec((rows, columns), lambda j, order: (0, j))] * members,
        ),
        compiler_params=pltpu.CompilerParams(vmem_limit_bytes=32 * 1024 * 1024),
        cost_estimate=pl.CostEstimate(
            flops=0, bytes_accessed=8 * members * rows * columns, transcendentals=0
        ),
    )(order, *operands)


def attend_kernel(members, tokens, tok_rows, page_len, scale, page_req, page_slot, *refs):
    blocks, refs = refs[:members], refs[members:]
    if len(refs) > 4:
        query, refs = [q[...] for q in refs[:members]], refs[members:]
    else:
        query = [block[2 * tokens : 2 * tokens + tok_rows, :] for block in blocks]
    request, position, out, level = refs
    request, position = request[...], position[...]
    keys = jnp.concatenate([block[:tokens, :] for block in blocks], axis=0)
    values = jnp.concatenate([block[tokens : 2 * tokens, :] for block in blocks], axis=0)
    query = jnp.concatenate(query, axis=0)
    scores = (
        lax.dot_general(keys, query, (((1,), (1,)), ((), ())), preferred_element_type=jnp.float32)
        * scale
    )
    token = lax.broadcasted_iota(jnp.int32, (page_len, query.shape[0]), 0)
    visible = jnp.concatenate(
        [
            (request == page_req[page]) & (token + page_slot[page] * page_len <= position)
            for page in range(members * tokens // page_len)
        ],
        axis=0,
    )
    scores = jnp.where(visible, scores, -1e30)
    top = jnp.max(scores, axis=0, keepdims=True)
    weights = jnp.where(visible, jnp.exp(scores - top), 0.0)
    total = jnp.sum(weights, axis=0, keepdims=True)
    summed = lax.dot_general(
        values,
        weights.astype(jnp.bfloat16),
        (((0,), (0,)), ((), ())),
        preferred_element_type=jnp.float32,
    )
    seen = total > 0.0
    total = jnp.where(seen, total, 1.0)
    out[...] = (summed / total).astype(jnp.bfloat16)
    level[0] = jnp.where(seen, top + jnp.log(total), -1e30)


def attend(blocks, far, row_req, row_pos, page_req, page_slot, page_len, tokens, tok_rows):
    members, rows = len(blocks), row_req.shape[1]
    block_rows, columns = blocks[0].shape
    heads = columns // HEAD_DIM
    by_head = lambda n: pl.BlockSpec((n, HEAD_DIM), lambda h, *_: (0, h))
    whole = pl.BlockSpec((1, rows), lambda h, *_: (0, 0))
    return pl.pallas_call(
        functools.partial(
            attend_kernel, members, tokens, tok_rows, page_len, HEAD_DIM ** (-0.5)
        ),
        out_shape=[
            jax.ShapeDtypeStruct((columns, rows), jnp.bfloat16),
            jax.ShapeDtypeStruct((heads, 1, rows), jnp.float32),
        ],
        grid_spec=pltpu.PrefetchScalarGridSpec(
            num_scalar_prefetch=2,
            grid=(heads,),
            in_specs=[by_head(block_rows)] * members + [by_head(tok_rows)] * len(far) + [whole] * 2,
            out_specs=[
                pl.BlockSpec((HEAD_DIM, rows), lambda h, *_: (h, 0)),
                pl.BlockSpec((1, 1, rows), lambda h, *_: (h, 0, 0)),
            ],
        ),
        compiler_params=pltpu.CompilerParams(vmem_limit_bytes=48 * 1024 * 1024),
        cost_estimate=pl.CostEstimate(
            flops=4 * rows * members * tokens * columns,
            bytes_accessed=2 * members * (block_rows + tok_rows) * columns,
            transcendentals=rows * members * tokens * heads,
        ),
    )(page_req, page_slot, *blocks, *far, row_req, row_pos)


def project_kernel(order, mine, mine_level, theirs, their_level, own, *refs):
    quarters, (stay, go, proj) = refs[:-3], refs[-3:]
    rows, size = own.shape[0], quarters[0].shape[0]
    proj[:rows, :] = own[...]
    for k, quarter in enumerate(quarters):
        at = pl.multiple_of(rows + order[k] * size, size)
        proj[pl.ds(at, size), :] = quarter[...]
    parts = []
    heads = mine.shape[0] // HEAD_DIM
    for head in range(heads):
        twin = (head + heads // 2) % heads
        dims = slice(head * HEAD_DIM, (head + 1) * HEAD_DIM)
        twin_dims = slice(twin * HEAD_DIM, (twin + 1) * HEAD_DIM)
        share = 1.0 / (1.0 + jnp.exp(their_level[twin] - mine_level[head]))
        other = 1.0 / (1.0 + jnp.exp(mine_level[head] - their_level[twin]))
        both = share * mine[dims, :].astype(jnp.float32) + other * theirs[
            twin_dims, :
        ].astype(jnp.float32)
        parts.append(both.astype(jnp.bfloat16))
    attention = jnp.concatenate(parts, axis=0)
    mixed = lax.dot_general(
        attention, proj[...], (((0,), (0,)), ((), ())), preferred_element_type=jnp.float32
    )
    kept = stay.shape[0]
    stay[...] = mixed[:kept, :]
    go[...] = mixed[kept:, :].astype(jnp.bfloat16)


def project(place, order, mine, mine_level, theirs, their_level, own, quarters, tok_rows):
    dims, width = mine.shape[0], own.shape[1]
    heads = dims // HEAD_DIM
    size = mine.shape[1] // 2
    whole = lambda a: pl.BlockSpec(a.shape, lambda i, order: (0, 0))
    values = pl.BlockSpec((dims, size), lambda i, order: (0, place))
    levels = pl.BlockSpec((heads, 1, size), lambda i, order: (0, 0, place))
    return pl.pallas_call(
        project_kernel,
        out_shape=[
            jax.ShapeDtypeStruct((tok_rows, width), jnp.float32),
            jax.ShapeDtypeStruct((size - tok_rows, width), jnp.bfloat16),
        ],
        grid_spec=pltpu.PrefetchScalarGridSpec(
            num_scalar_prefetch=1,
            grid=(1,),
            in_specs=[values, levels, values, levels, whole(own)] + [whole(q) for q in quarters],
            out_specs=[
                pl.BlockSpec((tok_rows, width), lambda i, order: (0, 0)),
                pl.BlockSpec((size - tok_rows, width), lambda i, order: (0, 0)),
            ],
            scratch_shapes=[pltpu.VMEM((dims, width), jnp.bfloat16)],
        ),
        compiler_params=pltpu.CompilerParams(vmem_limit_bytes=32 * 1024 * 1024),
        cost_estimate=pl.CostEstimate(
            flops=2 * size * dims * width,
            bytes_accessed=2 * (2 * dims * size + dims * width + 3 * size * width),
            transcendentals=2 * size * heads,
        ),
    )(order, mine, mine_level, theirs, their_level, own, *quarters)


def join_kernel(*refs):
    parts, out = refs[:-1], refs[-1]
    rows = parts[0].shape[0]
    for i, part in enumerate(parts):
        out[i * rows : (i + 1) * rows, :] = part[...]


def join(parts):
    rows, width = parts[0].shape
    vmem = pl.BlockSpec(memory_space=pltpu.VMEM)
    return pl.pallas_call(
        join_kernel,
        out_shape=jax.ShapeDtypeStruct((len(parts) * rows, width), parts[0].dtype),
        in_specs=[vmem] * len(parts),
        out_specs=vmem,
        cost_estimate=pl.CostEstimate(
            flops=0, bytes_accessed=4 * len(parts) * rows * width, transcendentals=0
        ),
    )(*parts)


def silu(value):
    return value / (1.0 + jnp.exp(-value))


def shared_kernel(rows, scalar, gate_w, up_w, down_w, out, gate_v, up_v, down_v, sems):
    copies = [
        pltpu.make_async_copy(src, dst, sems.at[i])
        for i, (src, dst) in enumerate(((gate_w, gate_v), (up_w, up_v), (down_w, down_v)))
    ]
    for copy in copies:
        copy.start()
    block = rows[...]
    logit = jnp.sum(
        block.astype(jnp.float32) * scalar[...].astype(jnp.float32), axis=1, keepdims=True
    )
    scale = 1.0 / (1.0 + jnp.exp(-logit))
    copies[0].wait()
    across = (((1,), (1,)), ((), ()))
    gate = lax.dot_general(block, gate_v[...], across, preferred_element_type=jnp.float32)
    copies[1].wait()
    upper = lax.dot_general(block, up_v[...], across, preferred_element_type=jnp.float32)
    hidden = (silu(gate) * upper).astype(jnp.bfloat16)
    copies[2].wait()
    result = jnp.dot(hidden, down_v[...], preferred_element_type=jnp.float32)
    out[...] = (scale * result).astype(jnp.bfloat16)


def shared_expert(rows, scalar, gate_w, up_w, down_w):
    any_spec = pl.BlockSpec(memory_space=pl.ANY)
    vmem = pl.BlockSpec(memory_space=pltpu.VMEM)
    return pl.pallas_call(
        shared_kernel,
        out_shape=jax.ShapeDtypeStruct(rows.shape, jnp.bfloat16),
        in_specs=[vmem, vmem, any_spec, any_spec, any_spec],
        out_specs=vmem,
        scratch_shapes=[
            pltpu.VMEM(gate_w.shape, jnp.bfloat16),
            pltpu.VMEM(up_w.shape, jnp.bfloat16),
            pltpu.VMEM(down_w.shape, jnp.bfloat16),
            pltpu.SemaphoreType.DMA((3,)),
        ],
        compiler_params=pltpu.CompilerParams(vmem_limit_bytes=48 * 1024 * 1024),
        cost_estimate=pl.CostEstimate(
            flops=6 * rows.shape[0] * gate_w.size,
            bytes_accessed=6 * gate_w.size + 4 * rows.size,
            transcendentals=rows.shape[0] * gate_w.shape[0],
        ),
    )(rows, scalar.reshape(1, -1), gate_w, up_w, down_w)


def routed_kernel(parts, entries, has_extra, *refs):
    count, total = len(parts), sum(parts)
    pieces, refs = refs[:total], refs[total:]
    place, row_gate, extra, gate_w, up_w, down_w = refs[:6]
    outs, refs = refs[6 : 6 + count], refs[6 + count :]
    rows, packed, gate_v, up_v, down_v, extra_v, sems = refs
    moves, chunk_copies = [], []
    for c, n in enumerate(parts):
        at = 0
        chunk_copies.append(range(len(moves), len(moves) + n))
        for piece in pieces[sum(parts[:c]) : sum(parts[: c + 1])]:
            moves.append((piece, rows.at[c, pl.ds(at, piece.shape[0])]))
            at += piece.shape[0]
    moves += [(gate_w.at[0], gate_v), (up_w.at[0], up_v), (down_w.at[0], down_v)]
    if has_extra:
        moves.append((extra, extra_v))
    copies = [
        pltpu.make_async_copy(src, dst, sems.at[i]) for i, (src, dst) in enumerate(moves)
    ]
    for copy in copies:
        copy.start()
    size = rows.shape[1]
    wanted = lax.broadcasted_iota(jnp.int32, (entries, size), 0)
    picks, weights = [], []
    for c in range(count):
        pick = jnp.where(place[c] == wanted, 1.0, 0.0)
        picks.append(pick.astype(jnp.bfloat16))
        weights.append(jnp.sum(pick * row_gate[c], axis=1, keepdims=True))
        for i in chunk_copies[c]:
            copies[i].wait()
        packed[c * entries : (c + 1) * entries, :] = jnp.dot(
            picks[c], rows[c], preferred_element_type=jnp.float32
        ).astype(jnp.bfloat16)
    copies[total].wait()
    gate = jnp.dot(packed[...], gate_v[...], preferred_element_type=jnp.float32)
    copies[total + 1].wait()
    upper = jnp.dot(packed[...], up_v[...], preferred_element_type=jnp.float32)
    hidden = (silu(gate) * upper).astype(jnp.bfloat16)
    copies[total + 2].wait()
    answer = jnp.dot(hidden, down_v[...], preferred_element_type=jnp.float32).astype(
        jnp.bfloat16
    )
    if has_extra:
        copies[total + 3].wait()
    for c in range(count):
        scaled = answer[c * entries : (c + 1) * entries, :].astype(jnp.float32) * weights[c]
        placed = lax.dot_general(
            picks[c],
            scaled.astype(jnp.bfloat16),
            (((0,), (0,)), ((), ())),
            preferred_element_type=jnp.float32,
        )
        if c == 0 and has_extra:
            placed = placed + extra_v[...].astype(jnp.float32)
        outs[c][...] = placed.astype(jnp.bfloat16)


def routed_expert(chunks, place, row_gate, extra, gate_w, up_w, down_w, entries):
    count = len(chunks)
    parts = [len(chunk) for chunk in chunks]
    total = sum(parts)
    size = sum(piece.shape[0] for piece in chunks[0])
    width = chunks[0][0].shape[1]
    hidden = gate_w.shape[2]
    any_spec = pl.BlockSpec(memory_space=pl.ANY)
    vmem = pl.BlockSpec(memory_space=pltpu.VMEM)
    has_extra = extra is not None
    if not has_extra:
        extra = jnp.zeros((16, 128), jnp.bfloat16)
    return pl.pallas_call(
        functools.partial(routed_kernel, parts, entries, has_extra),
        out_shape=[jax.ShapeDtypeStruct((size, width), jnp.bfloat16)] * count,
        in_specs=[any_spec] * total + [vmem] * 2 + [any_spec] * 4,
        out_specs=[vmem] * count,
        scratch_shapes=[
            pltpu.VMEM((count, size, width), jnp.bfloat16),
            pltpu.VMEM((count * entries, width), jnp.bfloat16),
            pltpu.VMEM((width, hidden), jnp.bfloat16),
            pltpu.VMEM((width, hidden), jnp.bfloat16),
            pltpu.VMEM((hidden, width), jnp.bfloat16),
            pltpu.VMEM(extra.shape, jnp.bfloat16),
            pltpu.SemaphoreType.DMA((total + 4,)),
        ],
        compiler_params=pltpu.CompilerParams(vmem_limit_bytes=56 * 1024 * 1024),
        cost_estimate=pl.CostEstimate(
            flops=2 * count * entries * (3 * gate_w.size + 2 * size * width),
            bytes_accessed=6 * gate_w.size + 4 * count * size * width,
            transcendentals=count * entries * hidden,
        ),
    )(*[piece for chunk in chunks for piece in chunk], place, row_gate, extra, gate_w, up_w, down_w)


def rms_normed(stream, norm_gain):
    scale_row = lax.rsqrt(jnp.mean(stream * stream, axis=1, keepdims=True) + 1e-06)
    return (stream * scale_row * norm_gain[None, :]).astype(jnp.bfloat16)


def shards(
    resid,
    queries,
    cache_key,
    cache_value,
    page_table,
    row_request,
    row_position,
    out_proj,
    norm_gain,
    expert_gate,
    expert_up,
    expert_down,
    shared_gate,
    shared_up,
    shared_down,
    shared_scalar,
    slot_expert,
    route_expert,
    route_gate,
):
    f32, bf16, i32 = jnp.float32, jnp.bfloat16, jnp.int32
    exp_count = lax.axis_size("exp")
    req_count = lax.axis_size("req")
    slot_count = exp_count * req_count
    nc, nx, ny = CORES, exp_count // Z_CHIPS, req_count // CORES
    exp_index = lax.axis_index("exp")
    req_index = lax.axis_index("req")
    own_slot = req_index * exp_count + exp_index
    iz, ix = exp_index // nx, exp_index % nx
    ih, il = iz // 2, iz % 2
    iy, ic = req_index // nc, req_index % nc
    tok_rows, width = resid.shape
    pages_here, page_len, _ = cache_key.shape
    req_slots, max_pages = page_table.shape
    tokens = pages_here * page_len
    capacity = 3 * tok_rows * TOPK // slot_count

    zs = [(dh, dl) for dh in range(2) for dl in range(2)]

    def send(value, dh, dl, dx):
        if not (dh or dl or dx % nx):
            return value
        pairs = [
            (
                (h * 2 + l) * nx + x,
                ((h + dh) % 2 * 2 + (l + dl) % 2) * nx + (x + dx) % nx,
            )
            for h in range(2)
            for l in range(2)
            for x in range(nx)
        ]
        return lax.ppermute(value, "exp", pairs)

    def send_req(value, dy, dc):
        if not (dy % ny or dc % nc):
            return value
        pairs = [
            (y * nc + c, (y + dy) % ny * nc + (c + dc) % nc)
            for y in range(ny)
            for c in range(nc)
        ]
        return lax.ppermute(value, "req", pairs)

    def swap_y(value):
        pairs = [(y * nc + c, (y ^ 1) * nc + c) for y in range(ny) for c in range(nc)]
        return lax.ppermute(value, "req", pairs)

    tie = lax.optimization_barrier

    rel_exp = jnp.stack(
        [
            ((ih + dh) % 2 * 2 + (il + dl) % 2) * nx + (ix - dx) % nx
            for dh, dl in zs
            for dx in range(nx)
        ]
    ).astype(i32)
    rel_req = jnp.stack(
        [((iy - dy) % ny) * nc + (ic - dc) % nc for dy in range(ny) for dc in range(nc)]
    ).astype(i32)

    columns = width // exp_count
    keys = cache_key.reshape(tokens, width)
    values = cache_value.reshape(tokens, width)
    quarter_rows = out_proj.shape[0] // (2 * nc)
    quarter = lax.dynamic_slice_in_dim(
        out_proj, (iy % 2 * nc + ic) * quarter_rows, quarter_rows, 0
    )
    quarters = [send(quarter, 1, 0, 0)]
    quarter_order = jnp.stack(
        [(iy + dy) % 2 * nc + (ic + dc) % nc for dc in range(nc) for dy in range(2)]
    ).astype(i32)
    far_queries = send(queries, 1, 0, 0)
    members = [(dl, dx) for dl in range(2) for dx in range(nx)]
    order = jnp.stack(
        [
            ((ih + j) % 2 * 2 + (il + dl) % 2) * nx + (ix + dx) % nx
            for dl, dx in members
            for j in range(2)
        ]
    ).astype(i32)
    gates = jnp.pad(jnp.transpose(route_gate), ((0, 0), (0, 2 * columns - tok_rows)))
    blocks = pack([keys, values, queries], gates, order, columns)
    blocks = [send(blocks[m], 0, *members[m]) for m in range(len(members))]
    far = list(pack([far_queries], None, order, columns))
    for m in range(1, len(members)):
        if m > 2:
            far[m], far[m - 2] = tie((far[m], far[m - 2]))
        far[m] = send(far[m], 0, *members[m])
    page_ids = (
        rel_exp[: len(members), None] * pages_here + jnp.arange(pages_here, dtype=i32)[None, :]
    ).reshape(-1)
    hits = (page_table[None, :, :] == page_ids[:, None, None]).astype(i32)
    page_request = jnp.sum(hits * jnp.arange(req_slots, dtype=i32)[None, :, None], axis=(1, 2))
    page_slot = jnp.sum(hits * jnp.arange(max_pages, dtype=i32)[None, None, :], axis=(1, 2))
    rel_rows = lambda a: a.reshape(exp_count, tok_rows)[rel_exp].reshape(2, 1, -1)
    row_req, row_pos = rel_rows(row_request), rel_rows(row_position)
    gates = [block[2 * tokens + tok_rows :, :tok_rows].astype(f32) for block in blocks]
    gates = jnp.stack([g[:TOPK] + g[TOPK : 2 * TOPK] + g[2 * TOPK : 3 * TOPK] for g in gates])
    gates = gates.reshape(2, nx, TOPK, tok_rows)

    def attend_half(side, queries):
        return attend(
            blocks,
            queries,
            row_req[side],
            row_pos[side],
            page_request,
            page_slot,
            page_len,
            tokens,
            tok_rows,
        )

    gates = jnp.stack([send(gates, dh, 0, 0) for dh in range(2)])
    quarters.append(swap_y(quarters[0]))
    theirs, their_level = attend_half(1, far)
    theirs, their_level, gates, quarters = tie((theirs, their_level, gates, quarters))
    theirs, their_level = send(theirs, 1, 0, 0), send(their_level, 1, 0, 0)
    gates = jnp.stack([send_req(gates, dy, 0) for dy in range(ny)])
    quarters += [send_req(q, 0, dc) for dc in range(1, nc) for q in quarters[:2]]
    mine, level = attend_half(0, [])
    mine, level, gates, quarters = tie((mine, level, gates, quarters))

    slot_ids = jnp.arange(slot_count, dtype=i32)
    own_mark = slot_ids == own_slot
    own_expert = jnp.sum(jnp.where(own_mark, slot_expert, 0))
    twins = slot_expert == own_expert
    copies = jnp.sum(twins.astype(i32))
    own_rank = jnp.sum((twins & (slot_ids < own_slot)).astype(i32))
    gates = jnp.stack([send_req(gates, 0, dc) for dc in range(nc)], axis=1)
    gates = jnp.transpose(gates, (0, 1, 4, 2, 3, 5, 6)).reshape(slot_count, TOPK, tok_rows)
    rel_exp = jnp.transpose(rel_exp.reshape(len(zs), nx)).reshape(-1)
    rel_slots = (rel_req[:, None] * exp_count + rel_exp[None, :]).reshape(-1)
    named = (route_expert == own_expert).reshape(slot_count, tok_rows, TOPK)[rel_slots]
    named = jnp.transpose(named, (0, 2, 1))
    chunk_rows = exp_count * tok_rows
    entries = -(-exp_count * capacity // 16) * 16
    row_gate = jnp.sum(jnp.where(named, gates, 0.0), axis=1).reshape(ny, nc, chunk_rows)
    served = jnp.any(named, axis=1) & (rel_slots % copies == own_rank)[:, None]
    served = served.reshape(ny, nc, chunk_rows)
    place = jnp.where(served, jnp.cumsum(served.astype(i32), axis=2) - 1, -1)
    place = place.reshape(ny, nc, 1, chunk_rows)
    row_gate = row_gate.reshape(ny, nc, 1, chunk_rows)

    stays, comes = {}, {}
    proj = out_proj
    for dl in (1, 0):
        stays[dl], go = project(
            dl, quarter_order, mine, level, theirs, their_level, proj, quarters, tok_rows
        )
        comes[dl] = [
            send(go[(dx - 1) * tok_rows : dx * tok_rows], 0, 0, -dx) for dx in range(1, nx)
        ]
        proj, _ = tie((proj, go))
    line = sum([come.astype(f32) for come in comes[1]], stays[1]).astype(bf16)
    comes[0], _ = tie((comes[0], line))
    line = send(line, 0, 1, 0)
    stream = sum([come.astype(f32) for come in comes[0]], resid.astype(f32) + stays[0])
    stream = stream + line.astype(f32)
    normed = rms_normed(stream, norm_gain)
    normed, place, row_gate = tie((normed, place, row_gate))

    far_line = send(normed, 1, 0, 0)
    line = [normed, send(normed, 0, 1, 0), far_line, send(far_line, 0, 1, 0)]
    piece = {}
    for i in range(len(zs)):
        piece[i, 0, 0] = line[i]
        for dx in range(1, nx):
            piece[i, dx, 0] = send(line[i], 0, 0, dx)
        for dy in range(1, ny):
            piece[i, 0, dy] = send_req(line[i], dy, 0)
    piece = tie(piece)
    chunk = join([piece[i, dx, 0] for dx in range(nx) for i in range(len(zs))])
    chunks = {(0, 0): [chunk]}
    for dc in range(1, nc):
        chunks[0, dc] = [send_req(chunk, 0, dc)]
    for dy in range(1, ny):
        half = join([piece[i, 0, dy] for i in range(len(zs))])
        chunks[dy, 0] = [send(half, 0, 0, dx) for dx in range(nx)]
    extra = shared_expert(chunk, shared_scalar, shared_gate.T, shared_up.T, shared_down)
    partners = [chunks[0, dc] for dc in range(1, nc)]
    extra, partners = tie((extra, partners))
    for dc in range(1, nc):
        chunks[0, dc] = partners[dc - 1]

    places = lambda part: part.astype(f32).reshape(nx, 2, 2, tok_rows, width)
    kept, comes = {}, {}
    for dy in range(ny):
        answers = routed_expert(
            [chunks[dy, dc] for dc in range(nc)],
            place[dy],
            row_gate[dy],
            extra,
            expert_gate,
            expert_up,
            expert_down,
            entries,
        )
        extra = None
        if dy:
            answers, comes[dy - 1] = tie((answers, comes[dy - 1]))
        if dy + 1 < ny:
            answers, chunks[dy + 1, 0] = tie((answers, chunks[dy + 1, 0]))
            for dc in range(1, nc):
                chunks[dy + 1, dc] = [send_req(part, 0, dc) for part in chunks[dy + 1, 0]]
        parts = [answers[0]] + [send_req(answers[dc], 0, -dc) for dc in range(1, nc)]
        if dy + 1 < ny:
            gone = sum([places(p)[1:] for p in parts[1:]], places(parts[0])[1:]).astype(bf16)
            comes[dy] = [send(gone[dx - 1], 0, 0, -dx) for dx in range(1, nx)]
            following = [chunks[dy + 1, dc] for dc in range(nc)]
            following, _ = tie((following, gone))
            for dc in range(nc):
                chunks[dy + 1, dc] = following[dc]
        kept[dy] = parts

    def line_of(dy, dl):
        line = [places(p)[0, :, dl] for p in kept[dy]]
        if dy + 1 < ny:
            line += [come.astype(f32)[:, dl] for come in comes[dy]]
        else:
            line += [come.astype(f32) for come in last[dl]]
        return sum(line[1:], line[0])

    last = {}
    parts = kept[ny - 1]
    for dl in (1, 0):
        gone = sum([places(p)[1:, :, dl] for p in parts[1:]], places(parts[0])[1:, :, dl])
        gone = gone.astype(bf16)
        last[dl] = [send(gone[dx - 1], 0, 0, -dx) for dx in range(1, nx)]
        parts, _ = tie((parts, gone))
    over_y = {}
    for dl in (1, 0):
        goes = [line_of(dy, dl).astype(bf16) for dy in range(1, ny)]
        if dl:
            last[0], _ = tie((last[0], goes))
        else:
            goes, over_y[1] = tie((goes, over_y[1]))
        over_y[dl] = [send_req(go, -dy, 0) for dy, go in enumerate(goes, 1)]
    near = sum([come.astype(f32) for come in over_y[1]], line_of(0, 1)).astype(bf16)
    near = send(near, 0, 1, 0)
    total = sum([come.astype(f32) for come in over_y[0]], line_of(0, 0)) + near.astype(f32)
    total = stream + total[0] + send(total[1].astype(bf16), 1, 0, 0).astype(f32)
    return total.astype(bf16)


def solution(mesh):
    placed = (
        P(("req", "exp"), None),
        P(("req", "exp"), None),
        P(("req", "exp"), None, None),
        P(("req", "exp"), None, None),
        P("req", None),
        P("req"),
        P("req"),
        P("exp", None),
        P(),
        P(("req", "exp"), None, None),
        P(("req", "exp"), None, None),
        P(("req", "exp"), None, None),
        P(None, "exp"),
        P(None, "exp"),
        P("exp", None),
        P(),
        P(),
        P(),
        P(("req", "exp"), None),
    )
    return jax.shard_map(
        shards, mesh=mesh, in_specs=placed, out_specs=P(("req", "exp"), None), check_vma=False
    )
```

```python
import functools

import jax
import jax.numpy as jnp
from jax import lax
from jax.experimental import pallas as pl
from jax.experimental.pallas import tpu as pltpu
from jax.sharding import PartitionSpec as P

HEAD_DIM = 128
TOPK = 4
CORES = 2
Z_CHIPS = 4


def pack_kernel(members, *refs):
    keys, values, queries = (refs[i * members : (i + 1) * members] for i in range(3))
    gates, blocks = refs[3 * members], refs[3 * members + 1 :]
    weights = gates[...]
    high = weights.astype(jnp.bfloat16).astype(jnp.float32)
    middle = (weights - high).astype(jnp.bfloat16).astype(jnp.float32)
    low = weights - high - middle
    weights = jnp.concatenate([high, middle, low, jnp.zeros_like(low)], axis=0)
    weights = weights.astype(jnp.bfloat16)
    for m in range(members):
        tokens, rows = keys[m].shape[0], queries[m].shape[0]
        blocks[m][:tokens, :] = keys[m][...]
        blocks[m][tokens : 2 * tokens, :] = values[m][...]
        blocks[m][2 * tokens : 2 * tokens + rows, :] = queries[m][...]
        blocks[m][2 * tokens + rows :, :] = weights


def pack_far_kernel(members, *refs):
    for m in range(members):
        refs[members + m][...] = refs[m][...]


def pack(parts, gates, order, columns):
    members = order.shape[0] // 2
    rows = sum(p.shape[0] for p in parts) + (0 if gates is None else 4 * gates.shape[0])
    kernel = functools.partial(pack_far_kernel if gates is None else pack_kernel, members)

    def column(n, m):
        return pl.BlockSpec((n, columns), lambda j, order: (0, order[2 * m + j]))

    in_specs = [column(p.shape[0], m) for p in parts for m in range(members)]
    operands = [p for p in parts for m in range(members)]
    if gates is not None:
        in_specs.append(pl.BlockSpec((gates.shape[0], columns), lambda j, order: (0, j)))
        operands.append(gates)
    return pl.pallas_call(
        lambda order, *refs: kernel(*refs),
        out_shape=[jax.ShapeDtypeStruct((rows, 2 * columns), parts[0].dtype)] * members,
        grid_spec=pltpu.PrefetchScalarGridSpec(
            num_scalar_prefetch=1,
            grid=(2,),
            in_specs=in_specs,
            out_specs=[pl.BlockSpec((rows, columns), lambda j, order: (0, j))] * members,
        ),
        compiler_params=pltpu.CompilerParams(vmem_limit_bytes=32 * 1024 * 1024),
        cost_estimate=pl.CostEstimate(
            flops=0, bytes_accessed=8 * members * rows * columns, transcendentals=0
        ),
    )(order, *operands)


def attend_kernel(members, tokens, tok_rows, page_len, scale, page_req, page_slot, *refs):
    blocks, refs = refs[:members], refs[members:]
    if len(refs) > 4:
        query, refs = [q[...] for q in refs[:members]], refs[members:]
    else:
        query = [block[2 * tokens : 2 * tokens + tok_rows, :] for block in blocks]
    request, position, out, level = refs
    request, position = request[...], position[...]
    keys = jnp.concatenate([block[:tokens, :] for block in blocks], axis=0)
    values = jnp.concatenate([block[tokens : 2 * tokens, :] for block in blocks], axis=0)
    query = jnp.concatenate(query, axis=0)
    scores = (
        lax.dot_general(keys, query, (((1,), (1,)), ((), ())), preferred_element_type=jnp.float32)
        * scale
    )
    token = lax.broadcasted_iota(jnp.int32, (page_len, query.shape[0]), 0)
    visible = jnp.concatenate(
        [
            (request == page_req[page]) & (token + page_slot[page] * page_len <= position)
            for page in range(members * tokens // page_len)
        ],
        axis=0,
    )
    scores = jnp.where(visible, scores, -1e30)
    top = jnp.max(scores, axis=0, keepdims=True)
    weights = jnp.where(visible, jnp.exp(scores - top), 0.0)
    total = jnp.sum(weights, axis=0, keepdims=True)
    summed = lax.dot_general(
        values,
        weights.astype(jnp.bfloat16),
        (((0,), (0,)), ((), ())),
        preferred_element_type=jnp.float32,
    )
    seen = total > 0.0
    total = jnp.where(seen, total, 1.0)
    out[...] = (summed / total).astype(jnp.bfloat16)
    level[0] = jnp.where(seen, top + jnp.log(total), -1e30)


def attend(blocks, far, row_req, row_pos, page_req, page_slot, page_len, tokens, tok_rows):
    members, rows = len(blocks), row_req.shape[1]
    block_rows, columns = blocks[0].shape
    heads = columns // HEAD_DIM
    by_head = lambda n: pl.BlockSpec((n, HEAD_DIM), lambda h, *_: (0, h))
    whole = pl.BlockSpec((1, rows), lambda h, *_: (0, 0))
    return pl.pallas_call(
        functools.partial(
            attend_kernel, members, tokens, tok_rows, page_len, HEAD_DIM ** (-0.5)
        ),
        out_shape=[
            jax.ShapeDtypeStruct((columns, rows), jnp.bfloat16),
            jax.ShapeDtypeStruct((heads, 1, rows), jnp.float32),
        ],
        grid_spec=pltpu.PrefetchScalarGridSpec(
            num_scalar_prefetch=2,
            grid=(heads,),
            in_specs=[by_head(block_rows)] * members + [by_head(tok_rows)] * len(far) + [whole] * 2,
            out_specs=[
                pl.BlockSpec((HEAD_DIM, rows), lambda h, *_: (h, 0)),
                pl.BlockSpec((1, 1, rows), lambda h, *_: (h, 0, 0)),
            ],
        ),
        compiler_params=pltpu.CompilerParams(vmem_limit_bytes=48 * 1024 * 1024),
        cost_estimate=pl.CostEstimate(
            flops=4 * rows * members * tokens * columns,
            bytes_accessed=2 * members * (block_rows + tok_rows) * columns,
            transcendentals=rows * members * tokens * heads,
        ),
    )(page_req, page_slot, *blocks, *far, row_req, row_pos)


def project_kernel(order, mine, mine_level, theirs, their_level, own, *refs):
    quarters, (stay, go, proj) = refs[:-3], refs[-3:]
    rows, size = own.shape[0], quarters[0].shape[0]
    proj[:rows, :] = own[...]
    for k, quarter in enumerate(quarters):
        at = pl.multiple_of(rows + order[k] * size, size)
        proj[pl.ds(at, size), :] = quarter[...]
    parts = []
    heads = mine.shape[0] // HEAD_DIM
    for head in range(heads):
        twin = (head + heads // 2) % heads
        dims = slice(head * HEAD_DIM, (head + 1) * HEAD_DIM)
        twin_dims = slice(twin * HEAD_DIM, (twin + 1) * HEAD_DIM)
        share = 1.0 / (1.0 + jnp.exp(their_level[twin] - mine_level[head]))
        other = 1.0 / (1.0 + jnp.exp(mine_level[head] - their_level[twin]))
        both = share * mine[dims, :].astype(jnp.float32) + other * theirs[
            twin_dims, :
        ].astype(jnp.float32)
        parts.append(both.astype(jnp.bfloat16))
    attention = jnp.concatenate(parts, axis=0)
    mixed = lax.dot_general(
        attention, proj[...], (((0,), (0,)), ((), ())), preferred_element_type=jnp.float32
    )
    kept = stay.shape[0]
    stay[...] = mixed[:kept, :]
    go[...] = mixed[kept:, :].astype(jnp.bfloat16)


def project(place, order, mine, mine_level, theirs, their_level, own, quarters, tok_rows):
    dims, width = mine.shape[0], own.shape[1]
    heads = dims // HEAD_DIM
    size = mine.shape[1] // 2
    whole = lambda a: pl.BlockSpec(a.shape, lambda i, order: (0, 0))
    values = pl.BlockSpec((dims, size), lambda i, order: (0, place))
    levels = pl.BlockSpec((heads, 1, size), lambda i, order: (0, 0, place))
    return pl.pallas_call(
        project_kernel,
        out_shape=[
            jax.ShapeDtypeStruct((tok_rows, width), jnp.float32),
            jax.ShapeDtypeStruct((size - tok_rows, width), jnp.bfloat16),
        ],
        grid_spec=pltpu.PrefetchScalarGridSpec(
            num_scalar_prefetch=1,
            grid=(1,),
            in_specs=[values, levels, values, levels, whole(own)] + [whole(q) for q in quarters],
            out_specs=[
                pl.BlockSpec((tok_rows, width), lambda i, order: (0, 0)),
                pl.BlockSpec((size - tok_rows, width), lambda i, order: (0, 0)),
            ],
            scratch_shapes=[pltpu.VMEM((dims, width), jnp.bfloat16)],
        ),
        compiler_params=pltpu.CompilerParams(vmem_limit_bytes=32 * 1024 * 1024),
        cost_estimate=pl.CostEstimate(
            flops=2 * size * dims * width,
            bytes_accessed=2 * (2 * dims * size + dims * width + 3 * size * width),
            transcendentals=2 * size * heads,
        ),
    )(order, mine, mine_level, theirs, their_level, own, *quarters)


def join_kernel(*refs):
    parts, out = refs[:-1], refs[-1]
    rows = parts[0].shape[0]
    for i, part in enumerate(parts):
        out[i * rows : (i + 1) * rows, :] = part[...]


def join(parts):
    rows, width = parts[0].shape
    vmem = pl.BlockSpec(memory_space=pltpu.VMEM)
    return pl.pallas_call(
        join_kernel,
        out_shape=jax.ShapeDtypeStruct((len(parts) * rows, width), parts[0].dtype),
        in_specs=[vmem] * len(parts),
        out_specs=vmem,
        cost_estimate=pl.CostEstimate(
            flops=0, bytes_accessed=4 * len(parts) * rows * width, transcendentals=0
        ),
    )(*parts)


def silu(value):
    return value / (1.0 + jnp.exp(-value))


def shared_kernel(count, *refs):
    pieces, (scalar, gate_w, up_w, down_w, out, gate_v, up_v, down_v, sems) = (
        refs[:count],
        refs[count:],
    )
    copies = [
        pltpu.make_async_copy(src, dst, sems.at[i])
        for i, (src, dst) in enumerate(((gate_w, gate_v), (up_w, up_v), (down_w, down_v)))
    ]
    for copy in copies:
        copy.start()
    block = jnp.concatenate([piece[...] for piece in pieces], axis=0)
    logit = jnp.sum(
        block.astype(jnp.float32) * scalar[...].astype(jnp.float32), axis=1, keepdims=True
    )
    scale = 1.0 / (1.0 + jnp.exp(-logit))
    across = (((1,), (1,)), ((), ()))
    copies[0].wait()
    gate = lax.dot_general(block, gate_v[...], across, preferred_element_type=jnp.float32)
    copies[1].wait()
    upper = lax.dot_general(block, up_v[...], across, preferred_element_type=jnp.float32)
    hidden = (silu(gate) * upper).astype(jnp.bfloat16)
    copies[2].wait()
    result = jnp.dot(hidden, down_v[...], preferred_element_type=jnp.float32)
    out[...] = (scale * result).astype(jnp.bfloat16)


def shared_expert(pieces, scalar, gate_w, up_w, down_w):
    any_spec = pl.BlockSpec(memory_space=pl.ANY)
    vmem = pl.BlockSpec(memory_space=pltpu.VMEM)
    rows = sum(piece.shape[0] for piece in pieces)
    width = pieces[0].shape[1]
    return pl.pallas_call(
        functools.partial(shared_kernel, len(pieces)),
        out_shape=jax.ShapeDtypeStruct((rows, width), jnp.bfloat16),
        in_specs=[vmem] * (len(pieces) + 1) + [any_spec] * 3,
        out_specs=vmem,
        scratch_shapes=[
            pltpu.VMEM(gate_w.shape, jnp.bfloat16),
            pltpu.VMEM(up_w.shape, jnp.bfloat16),
            pltpu.VMEM(down_w.shape, jnp.bfloat16),
            pltpu.SemaphoreType.DMA((3,)),
        ],
        compiler_params=pltpu.CompilerParams(vmem_limit_bytes=40 * 1024 * 1024),
        cost_estimate=pl.CostEstimate(
            flops=6 * rows * gate_w.size,
            bytes_accessed=6 * gate_w.size + 4 * rows * width,
            transcendentals=rows * gate_w.shape[0],
        ),
    )(*pieces, scalar.reshape(1, -1), gate_w, up_w, down_w)


def routed_kernel(parts, extras, entries, cuts, *refs):
    count, total = len(parts), sum(parts)
    pieces, refs = refs[:total], refs[total:]
    place, row_gate = refs[:2]
    more, refs = refs[2 : 2 + extras], refs[2 + extras :]
    (gate_w, up_w, down_w), refs = refs[:3], refs[3:]
    outs, refs = refs[: count * cuts], refs[count * cuts :]
    rows, packed, gate_v, up_v, down_v, more_v, sems = refs
    moves, chunk_copies = [], []
    for c, n in enumerate(parts):
        at = 0
        chunk_copies.append(range(len(moves), len(moves) + n))
        for piece in pieces[sum(parts[:c]) : sum(parts[: c + 1])]:
            moves.append((piece, rows.at[c, pl.ds(at, piece.shape[0])]))
            at += piece.shape[0]
    moves += [(gate_w.at[0], gate_v), (up_w.at[0], up_v), (down_w.at[0], down_v)]
    at = 0
    for extra in more:
        moves.append((extra, more_v.at[pl.ds(at, extra.shape[0])]))
        at += extra.shape[0]
    copies = [
        pltpu.make_async_copy(src, dst, sems.at[i]) for i, (src, dst) in enumerate(moves)
    ]
    for copy in copies:
        copy.start()
    size = rows.shape[1]
    wanted = lax.broadcasted_iota(jnp.int32, (entries, size), 0)
    picks, weights = [], []
    for c in range(count):
        pick = jnp.where(place[c] == wanted, 1.0, 0.0)
        picks.append(pick.astype(jnp.bfloat16))
        weights.append(jnp.sum(pick * row_gate[c], axis=1, keepdims=True))
        for i in chunk_copies[c]:
            copies[i].wait()
        packed[c * entries : (c + 1) * entries, :] = jnp.dot(
            picks[c], rows[c], preferred_element_type=jnp.float32
        ).astype(jnp.bfloat16)
    copies[total].wait()
    gate = jnp.dot(packed[...], gate_v[...], preferred_element_type=jnp.float32)
    copies[total + 1].wait()
    upper = jnp.dot(packed[...], up_v[...], preferred_element_type=jnp.float32)
    hidden = (silu(gate) * upper).astype(jnp.bfloat16)
    copies[total + 2].wait()
    answer = jnp.dot(hidden, down_v[...], preferred_element_type=jnp.float32).astype(
        jnp.bfloat16
    )
    for i in range(extras):
        copies[total + 3 + i].wait()
    cut = size // cuts
    for c in range(count):
        scaled = answer[c * entries : (c + 1) * entries, :].astype(jnp.float32) * weights[c]
        placed = lax.dot_general(
            picks[c],
            scaled.astype(jnp.bfloat16),
            (((0,), (0,)), ((), ())),
            preferred_element_type=jnp.float32,
        )
        if c == 0 and extras:
            placed = placed + more_v[...].astype(jnp.float32)
        placed = placed.astype(jnp.bfloat16)
        for k in range(cuts):
            outs[c * cuts + k][...] = placed[k * cut : (k + 1) * cut, :]


def routed_expert(chunks, place, row_gate, more, gate_w, up_w, down_w, entries, cuts):
    count = len(chunks)
    parts = [len(chunk) for chunk in chunks]
    total = sum(parts)
    size = sum(piece.shape[0] for piece in chunks[0])
    width = chunks[0][0].shape[1]
    hidden = gate_w.shape[2]
    any_spec = pl.BlockSpec(memory_space=pl.ANY)
    vmem = pl.BlockSpec(memory_space=pltpu.VMEM)
    out_shape = jax.ShapeDtypeStruct((size // cuts, width), jnp.bfloat16)
    more_rows = sum(extra.shape[0] for extra in more) if more else 16
    outs = pl.pallas_call(
        functools.partial(routed_kernel, parts, len(more), entries, cuts),
        out_shape=[out_shape] * (count * cuts),
        in_specs=[any_spec] * total + [vmem] * 2 + [any_spec] * (len(more) + 3),
        out_specs=[vmem] * (count * cuts),
        scratch_shapes=[
            pltpu.VMEM((count, size, width), jnp.bfloat16),
            pltpu.VMEM((count * entries, width), jnp.bfloat16),
            pltpu.VMEM((width, hidden), jnp.bfloat16),
            pltpu.VMEM((width, hidden), jnp.bfloat16),
            pltpu.VMEM((hidden, width), jnp.bfloat16),
            pltpu.VMEM((more_rows, width), jnp.bfloat16),
            pltpu.SemaphoreType.DMA((total + 3 + len(more),)),
        ],
        compiler_params=pltpu.CompilerParams(vmem_limit_bytes=56 * 1024 * 1024),
        cost_estimate=pl.CostEstimate(
            flops=2 * count * entries * (3 * gate_w.size + 2 * size * width),
            bytes_accessed=6 * gate_w.size + 4 * count * size * width,
            transcendentals=count * entries * hidden,
        ),
    )(*[piece for chunk in chunks for piece in chunk], place, row_gate, *more, gate_w, up_w, down_w)
    return [outs[c * cuts : (c + 1) * cuts] for c in range(count)]


def rms_normed(stream, norm_gain):
    scale_row = lax.rsqrt(jnp.mean(stream * stream, axis=1, keepdims=True) + 1e-06)
    return (stream * scale_row * norm_gain[None, :]).astype(jnp.bfloat16)


def shards(
    resid,
    queries,
    cache_key,
    cache_value,
    page_table,
    row_request,
    row_position,
    out_proj,
    norm_gain,
    expert_gate,
    expert_up,
    expert_down,
    shared_gate,
    shared_up,
    shared_down,
    shared_scalar,
    slot_expert,
    route_expert,
    route_gate,
):
    f32, bf16, i32 = jnp.float32, jnp.bfloat16, jnp.int32
    exp_count = lax.axis_size("exp")
    req_count = lax.axis_size("req")
    slot_count = exp_count * req_count
    nc, nx, ny = CORES, exp_count // Z_CHIPS, req_count // CORES
    exp_index = lax.axis_index("exp")
    req_index = lax.axis_index("req")
    own_slot = req_index * exp_count + exp_index
    iz, ix = exp_index // nx, exp_index % nx
    ih, il = iz // 2, iz % 2
    iy, ic = req_index // nc, req_index % nc
    tok_rows, width = resid.shape
    pages_here, page_len, _ = cache_key.shape
    req_slots, max_pages = page_table.shape
    tokens = pages_here * page_len
    capacity = 3 * tok_rows * TOPK // slot_count

    zs = [(dh, dl) for dh in range(2) for dl in range(2)]

    def send(value, dh, dl, dx):
        if not (dh or dl or dx % nx):
            return value
        pairs = [
            (
                (h * 2 + l) * nx + x,
                ((h + dh) % 2 * 2 + (l + dl) % 2) * nx + (x + dx) % nx,
            )
            for h in range(2)
            for l in range(2)
            for x in range(nx)
        ]
        return lax.ppermute(value, "exp", pairs)

    def send_req(value, dy, dc):
        if not (dy % ny or dc % nc):
            return value
        pairs = [
            (y * nc + c, (y + dy) % ny * nc + (c + dc) % nc)
            for y in range(ny)
            for c in range(nc)
        ]
        return lax.ppermute(value, "req", pairs)

    def swap_y(value):
        pairs = [(y * nc + c, (y ^ 1) * nc + c) for y in range(ny) for c in range(nc)]
        return lax.ppermute(value, "req", pairs)

    tie = lax.optimization_barrier

    rel_exp = jnp.stack(
        [
            ((ih + dh) % 2 * 2 + (il + dl) % 2) * nx + (ix - dx) % nx
            for dh, dl in zs
            for dx in range(nx)
        ]
    ).astype(i32)
    rel_req = jnp.stack(
        [((iy - dy) % ny) * nc + (ic - dc) % nc for dy in range(ny) for dc in range(nc)]
    ).astype(i32)

    columns = width // exp_count
    keys = cache_key.reshape(tokens, width)
    values = cache_value.reshape(tokens, width)
    quarter_rows = out_proj.shape[0] // (2 * nc)
    quarter = lax.dynamic_slice_in_dim(
        out_proj, (iy % 2 * nc + ic) * quarter_rows, quarter_rows, 0
    )
    quarters = [send(quarter, 1, 0, 0)]
    quarter_order = jnp.stack(
        [(iy + dy) % 2 * nc + (ic + dc) % nc for dc in range(nc) for dy in range(2)]
    ).astype(i32)
    far_queries = send(queries, 1, 0, 0)
    members = [(dl, dx) for dl in range(2) for dx in range(nx)]
    order = jnp.stack(
        [
            ((ih + j) % 2 * 2 + (il + dl) % 2) * nx + (ix + dx) % nx
            for dl, dx in members
            for j in range(2)
        ]
    ).astype(i32)
    gates = jnp.pad(jnp.transpose(route_gate), ((0, 0), (0, 2 * columns - tok_rows)))
    blocks = pack([keys, values, queries], gates, order, columns)
    blocks = [send(blocks[m], 0, *members[m]) for m in range(len(members))]
    far = list(pack([far_queries], None, order, columns))
    for m in range(1, len(members)):
        if m > 2:
            far[m], far[m - 2] = tie((far[m], far[m - 2]))
        far[m] = send(far[m], 0, *members[m])
    page_ids = (
        rel_exp[: len(members), None] * pages_here + jnp.arange(pages_here, dtype=i32)[None, :]
    ).reshape(-1)
    hits = (page_table[None, :, :] == page_ids[:, None, None]).astype(i32)
    page_request = jnp.sum(hits * jnp.arange(req_slots, dtype=i32)[None, :, None], axis=(1, 2))
    page_slot = jnp.sum(hits * jnp.arange(max_pages, dtype=i32)[None, None, :], axis=(1, 2))
    by_place = lambda a: a.reshape(exp_count, tok_rows)[rel_exp].reshape(2, 1, -1)
    row_req, row_pos = by_place(row_request), by_place(row_position)
    gates = [block[2 * tokens + tok_rows :, :tok_rows].astype(f32) for block in blocks]
    gates = jnp.stack([g[:TOPK] + g[TOPK : 2 * TOPK] + g[2 * TOPK : 3 * TOPK] for g in gates])
    gates = gates.reshape(2, nx, TOPK, tok_rows)

    slot_ids = jnp.arange(slot_count, dtype=i32)
    own_mark = slot_ids == own_slot
    own_expert = jnp.sum(jnp.where(own_mark, slot_expert, 0))
    twins = slot_expert == own_expert
    copies = jnp.sum(twins.astype(i32))
    own_rank = jnp.sum((twins & (slot_ids < own_slot)).astype(i32))
    rel_rows = jnp.transpose(rel_exp.reshape(2, 2, nx)[:, ::-1], (2, 1, 0)).reshape(-1)
    rel_slots = (rel_req[:, None] * exp_count + rel_rows[None, :]).reshape(-1)
    named = (route_expert == own_expert).reshape(slot_count, tok_rows, TOPK)[rel_slots]
    named = jnp.transpose(named, (0, 2, 1))
    chunk_rows = exp_count * tok_rows
    entries = -(-exp_count * capacity // 16) * 16
    served = jnp.any(named, axis=1) & (rel_slots % copies == own_rank)[:, None]
    served = served.reshape(ny, nc, chunk_rows)
    place = jnp.where(served, jnp.cumsum(served.astype(i32), axis=2) - 1, -1)
    place = place.reshape(ny, nc, 1, chunk_rows)

    place, named, blocks = tie((place, named, blocks))

    def attend_half(side, queries):
        return attend(
            blocks,
            queries,
            row_req[side],
            row_pos[side],
            page_request,
            page_slot,
            page_len,
            tokens,
            tok_rows,
        )

    gates = jnp.stack([send(gates, dh, 0, 0) for dh in range(2)])
    quarters.append(swap_y(quarters[0]))
    theirs, their_level = attend_half(1, far)
    theirs, their_level, gates, quarters = tie((theirs, their_level, gates, quarters))
    theirs, their_level = send(theirs, 1, 0, 0), send(their_level, 1, 0, 0)
    gates = jnp.stack([send_req(gates, dy, 0) for dy in range(ny)])
    quarters += [send_req(q, 0, dc) for dc in range(1, nc) for q in quarters[:2]]
    mine, level = attend_half(0, [])
    mine, level, gates, quarters = tie((mine, level, gates, quarters))

    stays, comes = {}, {}
    proj = out_proj
    for dl in (1, 0):
        stays[dl], go = project(
            dl, quarter_order, mine, level, theirs, their_level, proj, quarters, tok_rows
        )
        comes[dl] = [
            send(go[(dx - 1) * tok_rows : dx * tok_rows], 0, 0, -dx) for dx in range(1, nx)
        ]
        proj, _ = tie((proj, go))
    line = sum([come.astype(f32) for come in comes[1]], stays[1]).astype(bf16)
    comes[0], _ = tie((comes[0], line))
    line = send(line, 0, 1, 0)
    stream = sum([come.astype(f32) for come in comes[0]], resid.astype(f32) + stays[0])
    stream = stream + line.astype(f32)
    normed = rms_normed(stream, norm_gain)
    gates = jnp.stack([send_req(gates, 0, dc) for dc in range(nc)], axis=1)
    gates = jnp.transpose(gates[:, :, :, ::-1], (0, 1, 4, 3, 2, 5, 6))
    gates = gates.reshape(slot_count, TOPK, tok_rows)
    row_gate = jnp.sum(jnp.where(named, gates, 0.0), axis=1).reshape(ny, nc, 1, chunk_rows)

    far_line = send(normed, 1, 0, 0)
    line = [normed, send(normed, 0, 1, 0), far_line, send(far_line, 0, 1, 0)]
    order = [1, 3, 0, 2]
    over_x = {(i, dx): send(line[i], 0, 0, dx) for i in order for dx in range(1, nx)}
    over_y = {(i, dy): send_req(line[i], dy, 0) for i in order for dy in range(1, ny)}

    halves = [[line[i] for i in order]]
    shared_weights = (shared_scalar, shared_gate.T, shared_up.T, shared_down)
    shared = [shared_expert(halves[0], *shared_weights)]
    chunks = {(0, 0): [join(halves[0])]}
    for dc in range(1, nc):
        chunks[0, dc] = [send_req(chunks[0, 0][0], 0, dc)]
    over_x, over_y, shared, row_gate = tie((over_x, over_y, shared, row_gate))
    for dx in range(1, nx):
        half = [over_x[i, dx] for i in order]
        chunks[0, 0].append(join(half))
        for dc in range(1, nc):
            chunks[0, dc].append(send_req(chunks[0, 0][dx], 0, dc))
        halves.append(half)
    for dy in range(1, ny):
        half = join([over_y[i, dy] for i in order])
        chunks[dy, 0] = [half] + [send(half, 0, 0, dx) for dx in range(1, nx)]
        for dc in range(1, nc):
            chunks[dy, dc] = [send_req(half, 0, dc)]
    for dx in range(1, nx):
        shared.append(shared_expert(halves[dx], *shared_weights))
    early = [chunks[0, dc] for dc in range(1, nc)] + [
        chunks[dy, dc] for dy in range(1, ny) for dc in range(1, nc)
    ]
    shared, early = tie((shared, early))
    names = [(0, dc) for dc in range(1, nc)] + [
        (dy, dc) for dy in range(1, ny) for dc in range(1, nc)
    ]
    for name, chunk in zip(names, early):
        chunks[name] = chunk

    def answers_of(dy, dcs, more, cuts):
        return routed_expert(
            [chunks[dy, dc] for dc in dcs],
            jnp.concatenate([place[dy, dc : dc + 1] for dc in dcs]),
            jnp.concatenate([row_gate[dy, dc : dc + 1] for dc in dcs]),
            more,
            expert_gate,
            expert_up,
            expert_down,
            entries,
            cuts,
        )

    def add_up(parts):
        return sum([part.astype(f32) for part in parts[1:]], parts[0].astype(f32))

    cores = list(range(nc))
    kept, comes = {}, {}
    for dy in range(ny - 1):
        answers = answers_of(dy, cores, shared, nx)
        shared = []
        if dy:
            answers, comes[dy - 1] = tie((answers, comes[dy - 1]))
        answers, chunks[dy + 1, 0] = tie((answers, chunks[dy + 1, 0]))
        for dc in range(1, nc):
            chunks[dy + 1, dc] += [send_req(part, 0, dc) for part in chunks[dy + 1, 0][1:]]
        others = [[send_req(part, 0, -dc) for part in answers[dc][::-1]][::-1] for dc in cores[1:]]
        kept[dy] = [answers[0][0]] + [other[0] for other in others]
        gone = [
            add_up([answers[0][dx]] + [other[dx] for other in others]).astype(bf16)
            for dx in range(1, nx)
        ]
        comes[dy] = [send(go, 0, 0, -dx) for dx, go in enumerate(gone, 1)]
        following = [chunks[dy + 1, dc] for dc in cores]
        following, _ = tie((following, gone))
        for dc in cores:
            chunks[dy + 1, dc] = following[dc]
    end = ny - 1
    others = []
    for dc in cores[1:]:
        (answer,) = answers_of(end, [dc], [], 1)
        chunks[end, 0], _ = tie((chunks[end, 0], answer))
        others.append(send_req(answer[0], 0, -dc))
    (answer,) = answers_of(end, [0], shared, 2 * nx)
    answer, others, comes = tie((answer, others, comes))
    cut = chunk_rows // (2 * nx)

    last = {}
    for k in range(2):
        gone = [
            add_up(
                [answer[2 * dx + k]]
                + [other[(2 * dx + k) * cut : (2 * dx + k + 1) * cut] for other in others]
            ).astype(bf16)
            for dx in range(1, nx)
        ]
        last[k] = [send(go, 0, 0, -dx) for dx, go in enumerate(gone, 1)]
        others, _ = tie((others, gone))

    def line_of(dy, k):
        rows = slice(k * cut, (k + 1) * cut)
        if dy < end:
            return add_up([part[rows] for part in kept[dy] + comes[dy]])
        return add_up([answer[k]] + [other[rows] for other in others] + last[k])

    home = {}
    for k in range(2):
        goes = [line_of(dy, k).astype(bf16) for dy in range(1, ny)]
        if k:
            goes, home[0] = tie((goes, home[0]))
        else:
            last[1], _ = tie((last[1], goes))
        home[k] = [send_req(go, -dy, 0) for dy, go in enumerate(goes, 1)]
    near = send(add_up([line_of(0, 0)] + home[0]).astype(bf16), 0, 1, 0)
    total = add_up([line_of(0, 1)] + home[1] + [near])
    far = send(total[tok_rows:].astype(bf16), 1, 0, 0)
    total = add_up([stream, total[:tok_rows], far])
    return total.astype(bf16)


def solution(mesh):
    placed = (
        P(("req", "exp"), None),
        P(("req", "exp"), None),
        P(("req", "exp"), None, None),
        P(("req", "exp"), None, None),
        P("req", None),
        P("req"),
        P("req"),
        P("exp", None),
        P(),
        P(("req", "exp"), None, None),
        P(("req", "exp"), None, None),
        P(("req", "exp"), None, None),
        P(None, "exp"),
        P(None, "exp"),
        P("exp", None),
        P(),
        P(),
        P(),
        P(("req", "exp"), None),
    )
    return jax.shard_map(
        shards, mesh=mesh, in_specs=placed, out_specs=P(("req", "exp"), None), check_vma=False
    )
```

```python
import functools

import jax
import jax.numpy as jnp
from jax import lax
from jax.experimental import pallas as pl
from jax.experimental.pallas import tpu as pltpu
from jax.sharding import PartitionSpec as P

HEAD_DIM = 128
TOPK = 4
CORES = 2
Z_CHIPS = 4


def pack_kernel(members, parts, columns, order, *refs):
    sources, refs = refs[:parts], refs[parts:]
    gates, blocks, sems = refs[:-1 - members], refs[-1 - members : -1], refs[-1]
    copies = []
    for m in range(members):
        at = 0
        for source in sources:
            rows = source.shape[0]
            for j in range(2):
                place = pl.multiple_of(order[2 * m + j] * columns, columns)
                copies.append(
                    pltpu.make_async_copy(
                        source.at[:, pl.ds(place, columns)],
                        blocks[m].at[pl.ds(at, rows), pl.ds(j * columns, columns)],
                        sems.at[len(copies)],
                    )
                )
            at += rows
    for copy in copies:
        copy.start()
    if gates:
        weights = gates[0][...]
        high = weights.astype(jnp.bfloat16).astype(jnp.float32)
        middle = (weights - high).astype(jnp.bfloat16).astype(jnp.float32)
        low = weights - high - middle
        weights = jnp.concatenate([high, middle, low, jnp.zeros_like(low)], axis=0)
        for m in range(members):
            blocks[m][at:, :] = weights.astype(jnp.bfloat16)
    for copy in copies:
        copy.wait()


def pack(parts, gates, order, columns):
    members = order.shape[0] // 2
    rows = sum(p.shape[0] for p in parts) + (0 if gates is None else 4 * gates.shape[0])
    vmem = pl.BlockSpec(memory_space=pltpu.VMEM)
    in_specs = [pl.BlockSpec(memory_space=pltpu.SMEM)]
    in_specs += [pl.BlockSpec(memory_space=pl.ANY)] * len(parts)
    operands = list(parts)
    if gates is not None:
        in_specs.append(vmem)
        operands.append(gates)
    return pl.pallas_call(
        functools.partial(pack_kernel, members, len(parts), columns),
        out_shape=[jax.ShapeDtypeStruct((rows, 2 * columns), parts[0].dtype)] * members,
        in_specs=in_specs,
        out_specs=[vmem] * members,
        scratch_shapes=[pltpu.SemaphoreType.DMA((2 * members * len(parts),))],
        compiler_params=pltpu.CompilerParams(vmem_limit_bytes=32 * 1024 * 1024),
        cost_estimate=pl.CostEstimate(
            flops=0, bytes_accessed=8 * members * rows * columns, transcendentals=0
        ),
    )(order, *operands)


def attend_kernel(members, tokens, tok_rows, page_len, scale, page_req, page_slot, *refs):
    blocks, refs = refs[:members], refs[members:]
    if len(refs) > 4:
        query, refs = [q[...] for q in refs[:members]], refs[members:]
    else:
        query = [block[2 * tokens : 2 * tokens + tok_rows, :] for block in blocks]
    request, position, out, level = refs
    request, position = request[...], position[...]
    keys = jnp.concatenate([block[:tokens, :] for block in blocks], axis=0)
    values = jnp.concatenate([block[tokens : 2 * tokens, :] for block in blocks], axis=0)
    query = jnp.concatenate(query, axis=0)
    scores = (
        lax.dot_general(keys, query, (((1,), (1,)), ((), ())), preferred_element_type=jnp.float32)
        * scale
    )
    token = lax.broadcasted_iota(jnp.int32, (page_len, query.shape[0]), 0)
    visible = jnp.concatenate(
        [
            (request == page_req[page]) & (token + page_slot[page] * page_len <= position)
            for page in range(members * tokens // page_len)
        ],
        axis=0,
    )
    scores = jnp.where(visible, scores, -1e30)
    top = jnp.max(scores, axis=0, keepdims=True)
    weights = jnp.where(visible, jnp.exp(scores - top), 0.0)
    total = jnp.sum(weights, axis=0, keepdims=True)
    summed = lax.dot_general(
        values,
        weights.astype(jnp.bfloat16),
        (((0,), (0,)), ((), ())),
        preferred_element_type=jnp.float32,
    )
    seen = total > 0.0
    total = jnp.where(seen, total, 1.0)
    out[...] = (summed / total).astype(jnp.bfloat16)
    level[0] = jnp.where(seen, top + jnp.log(total), -1e30)


def attend(blocks, far, row_req, row_pos, page_req, page_slot, page_len, tokens, tok_rows):
    members, rows = len(blocks), row_req.shape[1]
    block_rows, columns = blocks[0].shape
    heads = columns // HEAD_DIM
    by_head = lambda n: pl.BlockSpec((n, HEAD_DIM), lambda h, *_: (0, h))
    whole = pl.BlockSpec((1, rows), lambda h, *_: (0, 0))
    return pl.pallas_call(
        functools.partial(
            attend_kernel, members, tokens, tok_rows, page_len, HEAD_DIM ** (-0.5)
        ),
        out_shape=[
            jax.ShapeDtypeStruct((columns, rows), jnp.bfloat16),
            jax.ShapeDtypeStruct((heads, 1, rows), jnp.float32),
        ],
        grid_spec=pltpu.PrefetchScalarGridSpec(
            num_scalar_prefetch=2,
            grid=(heads,),
            in_specs=[by_head(block_rows)] * members + [by_head(tok_rows)] * len(far) + [whole] * 2,
            out_specs=[
                pl.BlockSpec((HEAD_DIM, rows), lambda h, *_: (h, 0)),
                pl.BlockSpec((1, 1, rows), lambda h, *_: (h, 0, 0)),
            ],
        ),
        compiler_params=pltpu.CompilerParams(vmem_limit_bytes=48 * 1024 * 1024),
        cost_estimate=pl.CostEstimate(
            flops=4 * rows * members * tokens * columns,
            bytes_accessed=2 * members * (block_rows + tok_rows) * columns,
            transcendentals=rows * members * tokens * heads,
        ),
    )(page_req, page_slot, *blocks, *far, row_req, row_pos)


def project_kernel(order, mine, mine_level, theirs, their_level, own, *refs):
    quarters, (stay, go, proj) = refs[:-3], refs[-3:]
    rows, size = own.shape[0], quarters[0].shape[0]
    proj[:rows, :] = own[...]
    for k, quarter in enumerate(quarters):
        at = pl.multiple_of(rows + order[k] * size, size)
        proj[pl.ds(at, size), :] = quarter[...]
    parts = []
    heads = mine.shape[0] // HEAD_DIM
    for head in range(heads):
        twin = (head + heads // 2) % heads
        dims = slice(head * HEAD_DIM, (head + 1) * HEAD_DIM)
        twin_dims = slice(twin * HEAD_DIM, (twin + 1) * HEAD_DIM)
        share = 1.0 / (1.0 + jnp.exp(their_level[twin] - mine_level[head]))
        other = 1.0 / (1.0 + jnp.exp(mine_level[head] - their_level[twin]))
        both = share * mine[dims, :].astype(jnp.float32) + other * theirs[
            twin_dims, :
        ].astype(jnp.float32)
        parts.append(both.astype(jnp.bfloat16))
    attention = jnp.concatenate(parts, axis=0)
    mixed = lax.dot_general(
        attention, proj[...], (((0,), (0,)), ((), ())), preferred_element_type=jnp.float32
    )
    kept = stay.shape[0]
    stay[...] = mixed[:kept, :]
    go[...] = mixed[kept:, :].astype(jnp.bfloat16)


def project(place, order, mine, mine_level, theirs, their_level, own, quarters, tok_rows):
    dims, width = mine.shape[0], own.shape[1]
    heads = dims // HEAD_DIM
    size = mine.shape[1] // 2
    whole = lambda a: pl.BlockSpec(a.shape, lambda i, order: (0, 0))
    values = pl.BlockSpec((dims, size), lambda i, order: (0, place))
    levels = pl.BlockSpec((heads, 1, size), lambda i, order: (0, 0, place))
    return pl.pallas_call(
        project_kernel,
        out_shape=[
            jax.ShapeDtypeStruct((tok_rows, width), jnp.float32),
            jax.ShapeDtypeStruct((size - tok_rows, width), jnp.bfloat16),
        ],
        grid_spec=pltpu.PrefetchScalarGridSpec(
            num_scalar_prefetch=1,
            grid=(1,),
            in_specs=[values, levels, values, levels, whole(own)] + [whole(q) for q in quarters],
            out_specs=[
                pl.BlockSpec((tok_rows, width), lambda i, order: (0, 0)),
                pl.BlockSpec((size - tok_rows, width), lambda i, order: (0, 0)),
            ],
            scratch_shapes=[pltpu.VMEM((dims, width), jnp.bfloat16)],
        ),
        compiler_params=pltpu.CompilerParams(vmem_limit_bytes=32 * 1024 * 1024),
        cost_estimate=pl.CostEstimate(
            flops=2 * size * dims * width,
            bytes_accessed=2 * (2 * dims * size + dims * width + 3 * size * width),
            transcendentals=2 * size * heads,
        ),
    )(order, mine, mine_level, theirs, their_level, own, *quarters)


def join_kernel(*refs):
    parts, out = refs[:-1], refs[-1]
    rows = parts[0].shape[0]
    for i, part in enumerate(parts):
        out[i * rows : (i + 1) * rows, :] = part[...]


def join(parts):
    rows, width = parts[0].shape
    vmem = pl.BlockSpec(memory_space=pltpu.VMEM)
    return pl.pallas_call(
        join_kernel,
        out_shape=jax.ShapeDtypeStruct((len(parts) * rows, width), parts[0].dtype),
        in_specs=[vmem] * len(parts),
        out_specs=vmem,
        cost_estimate=pl.CostEstimate(
            flops=0, bytes_accessed=4 * len(parts) * rows * width, transcendentals=0
        ),
    )(*parts)


def silu(value):
    return value / (1.0 + jnp.exp(-value))


def shared_kernel(count, *refs):
    pieces, (scalar, gate_w, up_w, down_w, out, rows, gate_v, up_v, down_v, sems) = (
        refs[:count],
        refs[count:],
    )
    moves = [(gate_w, gate_v), (up_w, up_v), (down_w, down_v)]
    size = pieces[0].shape[0]
    moves += [(piece, rows.at[pl.ds(i * size, size)]) for i, piece in enumerate(pieces)]
    copies = [
        pltpu.make_async_copy(src, dst, sems.at[i]) for i, (src, dst) in enumerate(moves)
    ]
    for copy in copies[3:] + copies[:3]:
        copy.start()
    for copy in copies[3:]:
        copy.wait()
    block = rows[...]
    logit = jnp.sum(
        block.astype(jnp.float32) * scalar[...].astype(jnp.float32), axis=1, keepdims=True
    )
    scale = 1.0 / (1.0 + jnp.exp(-logit))
    across = (((1,), (1,)), ((), ()))
    copies[0].wait()
    gate = lax.dot_general(block, gate_v[...], across, preferred_element_type=jnp.float32)
    copies[1].wait()
    upper = lax.dot_general(block, up_v[...], across, preferred_element_type=jnp.float32)
    hidden = (silu(gate) * upper).astype(jnp.bfloat16)
    copies[2].wait()
    result = jnp.dot(hidden, down_v[...], preferred_element_type=jnp.float32)
    out[...] = (scale * result).astype(jnp.bfloat16)


def shared_expert(pieces, scalar, gate_w, up_w, down_w):
    any_spec = pl.BlockSpec(memory_space=pl.ANY)
    vmem = pl.BlockSpec(memory_space=pltpu.VMEM)
    rows = sum(piece.shape[0] for piece in pieces)
    width = pieces[0].shape[1]
    return pl.pallas_call(
        functools.partial(shared_kernel, len(pieces)),
        out_shape=jax.ShapeDtypeStruct((rows, width), jnp.bfloat16),
        in_specs=[any_spec] * len(pieces) + [vmem] + [any_spec] * 3,
        out_specs=vmem,
        scratch_shapes=[
            pltpu.VMEM((rows, width), jnp.bfloat16),
            pltpu.VMEM(gate_w.shape, jnp.bfloat16),
            pltpu.VMEM(up_w.shape, jnp.bfloat16),
            pltpu.VMEM(down_w.shape, jnp.bfloat16),
            pltpu.SemaphoreType.DMA((3 + len(pieces),)),
        ],
        compiler_params=pltpu.CompilerParams(vmem_limit_bytes=40 * 1024 * 1024),
        cost_estimate=pl.CostEstimate(
            flops=6 * rows * gate_w.size,
            bytes_accessed=6 * gate_w.size + 4 * rows * width,
            transcendentals=rows * gate_w.shape[0],
        ),
    )(*pieces, scalar.reshape(1, -1), gate_w, up_w, down_w)


def routed_kernel(parts, extras, entries, cuts, *refs):
    count, total = len(parts), sum(parts)
    pieces, refs = refs[:total], refs[total:]
    place, row_gate = refs[:2]
    more, refs = refs[2 : 2 + extras], refs[2 + extras :]
    (gate_w, up_w, down_w), refs = refs[:3], refs[3:]
    outs, refs = refs[: count * cuts], refs[count * cuts :]
    rows, packed, gate_v, up_v, down_v, more_v, sems = refs
    moves, chunk_copies = [], []
    for c, n in enumerate(parts):
        at = 0
        chunk_copies.append(range(len(moves), len(moves) + n))
        for piece in pieces[sum(parts[:c]) : sum(parts[: c + 1])]:
            moves.append((piece, rows.at[c, pl.ds(at, piece.shape[0])]))
            at += piece.shape[0]
    moves += [(gate_w.at[0], gate_v), (up_w.at[0], up_v), (down_w.at[0], down_v)]
    at = 0
    for extra in more:
        moves.append((extra, more_v.at[pl.ds(at, extra.shape[0])]))
        at += extra.shape[0]
    copies = [
        pltpu.make_async_copy(src, dst, sems.at[i]) for i, (src, dst) in enumerate(moves)
    ]
    for copy in copies:
        copy.start()
    size = rows.shape[1]
    wanted = lax.broadcasted_iota(jnp.int32, (entries, size), 0)
    picks, weights = [], []
    for c in range(count):
        pick = jnp.where(place[c] == wanted, 1.0, 0.0)
        picks.append(pick.astype(jnp.bfloat16))
        weights.append(jnp.sum(pick * row_gate[c], axis=1, keepdims=True))
        for i in chunk_copies[c]:
            copies[i].wait()
        packed[c * entries : (c + 1) * entries, :] = jnp.dot(
            picks[c], rows[c], preferred_element_type=jnp.float32
        ).astype(jnp.bfloat16)
    copies[total].wait()
    gate = jnp.dot(packed[...], gate_v[...], preferred_element_type=jnp.float32)
    copies[total + 1].wait()
    upper = jnp.dot(packed[...], up_v[...], preferred_element_type=jnp.float32)
    hidden = (silu(gate) * upper).astype(jnp.bfloat16)
    copies[total + 2].wait()
    answer = jnp.dot(hidden, down_v[...], preferred_element_type=jnp.float32).astype(
        jnp.bfloat16
    )
    for i in range(extras):
        copies[total + 3 + i].wait()
    cut = size // cuts
    for c in range(count):
        scaled = answer[c * entries : (c + 1) * entries, :].astype(jnp.float32) * weights[c]
        placed = lax.dot_general(
            picks[c],
            scaled.astype(jnp.bfloat16),
            (((0,), (0,)), ((), ())),
            preferred_element_type=jnp.float32,
        )
        if c == 0 and extras:
            placed = placed + more_v[...].astype(jnp.float32)
        placed = placed.astype(jnp.bfloat16)
        for k in range(cuts):
            outs[c * cuts + k][...] = placed[k * cut : (k + 1) * cut, :]


def routed_expert(chunks, place, row_gate, more, gate_w, up_w, down_w, entries, cuts):
    count = len(chunks)
    parts = [len(chunk) for chunk in chunks]
    total = sum(parts)
    size = sum(piece.shape[0] for piece in chunks[0])
    width = chunks[0][0].shape[1]
    hidden = gate_w.shape[2]
    any_spec = pl.BlockSpec(memory_space=pl.ANY)
    vmem = pl.BlockSpec(memory_space=pltpu.VMEM)
    out_shape = jax.ShapeDtypeStruct((size // cuts, width), jnp.bfloat16)
    more_rows = sum(extra.shape[0] for extra in more) if more else 16
    outs = pl.pallas_call(
        functools.partial(routed_kernel, parts, len(more), entries, cuts),
        out_shape=[out_shape] * (count * cuts),
        in_specs=[any_spec] * total + [vmem] * 2 + [any_spec] * (len(more) + 3),
        out_specs=[vmem] * (count * cuts),
        scratch_shapes=[
            pltpu.VMEM((count, size, width), jnp.bfloat16),
            pltpu.VMEM((count * entries, width), jnp.bfloat16),
            pltpu.VMEM((width, hidden), jnp.bfloat16),
            pltpu.VMEM((width, hidden), jnp.bfloat16),
            pltpu.VMEM((hidden, width), jnp.bfloat16),
            pltpu.VMEM((more_rows, width), jnp.bfloat16),
            pltpu.SemaphoreType.DMA((total + 3 + len(more),)),
        ],
        compiler_params=pltpu.CompilerParams(vmem_limit_bytes=56 * 1024 * 1024),
        cost_estimate=pl.CostEstimate(
            flops=2 * count * entries * (3 * gate_w.size + 2 * size * width),
            bytes_accessed=6 * gate_w.size + 4 * count * size * width,
            transcendentals=count * entries * hidden,
        ),
    )(*[piece for chunk in chunks for piece in chunk], place, row_gate, *more, gate_w, up_w, down_w)
    return [outs[c * cuts : (c + 1) * cuts] for c in range(count)]


def rms_normed(stream, norm_gain):
    scale_row = lax.rsqrt(jnp.mean(stream * stream, axis=1, keepdims=True) + 1e-06)
    return (stream * scale_row * norm_gain[None, :]).astype(jnp.bfloat16)


def shards(
    resid,
    queries,
    cache_key,
    cache_value,
    page_table,
    row_request,
    row_position,
    out_proj,
    norm_gain,
    expert_gate,
    expert_up,
    expert_down,
    shared_gate,
    shared_up,
    shared_down,
    shared_scalar,
    slot_expert,
    route_expert,
    route_gate,
):
    f32, bf16, i32 = jnp.float32, jnp.bfloat16, jnp.int32
    exp_count = lax.axis_size("exp")
    req_count = lax.axis_size("req")
    slot_count = exp_count * req_count
    nc, nx, ny = CORES, exp_count // Z_CHIPS, req_count // CORES
    exp_index = lax.axis_index("exp")
    req_index = lax.axis_index("req")
    own_slot = req_index * exp_count + exp_index
    iz, ix = exp_index // nx, exp_index % nx
    ih, il = iz // 2, iz % 2
    iy, ic = req_index // nc, req_index % nc
    tok_rows, width = resid.shape
    pages_here, page_len, _ = cache_key.shape
    req_slots, max_pages = page_table.shape
    tokens = pages_here * page_len
    capacity = 3 * tok_rows * TOPK // slot_count

    zs = [(dh, dl) for dh in range(2) for dl in range(2)]

    def send(value, dh, dl, dx):
        if not (dh or dl or dx % nx):
            return value
        pairs = [
            (
                (h * 2 + l) * nx + x,
                ((h + dh) % 2 * 2 + (l + dl) % 2) * nx + (x + dx) % nx,
            )
            for h in range(2)
            for l in range(2)
            for x in range(nx)
        ]
        return lax.ppermute(value, "exp", pairs)

    def send_req(value, dy, dc):
        if not (dy % ny or dc % nc):
            return value
        pairs = [
            (y * nc + c, (y + dy) % ny * nc + (c + dc) % nc)
            for y in range(ny)
            for c in range(nc)
        ]
        return lax.ppermute(value, "req", pairs)

    def swap_y(value):
        pairs = [(y * nc + c, (y ^ 1) * nc + c) for y in range(ny) for c in range(nc)]
        return lax.ppermute(value, "req", pairs)

    tie = lax.optimization_barrier

    rel_exp = jnp.stack(
        [
            ((ih + dh) % 2 * 2 + (il + dl) % 2) * nx + (ix - dx) % nx
            for dh, dl in zs
            for dx in range(nx)
        ]
    ).astype(i32)
    rel_req = jnp.stack(
        [((iy - dy) % ny) * nc + (ic - dc) % nc for dy in range(ny) for dc in range(nc)]
    ).astype(i32)

    columns = width // exp_count
    keys = cache_key.reshape(tokens, width)
    values = cache_value.reshape(tokens, width)
    quarter_rows = out_proj.shape[0] // (2 * nc)
    quarter = lax.dynamic_slice_in_dim(
        out_proj, (iy % 2 * nc + ic) * quarter_rows, quarter_rows, 0
    )
    quarters = [send(quarter, 1, 0, 0)]
    quarter_order = jnp.stack(
        [(iy + dy) % 2 * nc + (ic + dc) % nc for dc in range(nc) for dy in range(2)]
    ).astype(i32)
    far_queries = send(queries, 1, 0, 0)
    members = [(dl, dx) for dl in range(2) for dx in range(nx)]
    order = jnp.stack(
        [
            ((ih + j) % 2 * 2 + (il + dl) % 2) * nx + (ix + dx) % nx
            for dl, dx in members
            for j in range(2)
        ]
    ).astype(i32)
    gates = jnp.pad(jnp.transpose(route_gate), ((0, 0), (0, 2 * columns - tok_rows)))
    blocks = pack([keys, values, queries], gates, order, columns)
    blocks = [send(blocks[m], 0, *members[m]) for m in range(len(members))]
    far = list(pack([far_queries], None, order, columns))
    for m in range(1, len(members)):
        if m > 2:
            far[m], far[m - 2] = tie((far[m], far[m - 2]))
        far[m] = send(far[m], 0, *members[m])
    page_ids = (
        rel_exp[: len(members), None] * pages_here + jnp.arange(pages_here, dtype=i32)[None, :]
    ).reshape(-1)
    hits = (page_table[None, :, :] == page_ids[:, None, None]).astype(i32)
    page_request = jnp.sum(hits * jnp.arange(req_slots, dtype=i32)[None, :, None], axis=(1, 2))
    page_slot = jnp.sum(hits * jnp.arange(max_pages, dtype=i32)[None, None, :], axis=(1, 2))
    by_place = lambda a: a.reshape(exp_count, tok_rows)[rel_exp].reshape(2, 1, -1)
    row_req, row_pos = by_place(row_request), by_place(row_position)
    gates = [block[2 * tokens + tok_rows :, :tok_rows].astype(f32) for block in blocks]
    gates = jnp.stack([g[:TOPK] + g[TOPK : 2 * TOPK] + g[2 * TOPK : 3 * TOPK] for g in gates])
    gates = gates.reshape(2, nx, TOPK, tok_rows)

    slot_ids = jnp.arange(slot_count, dtype=i32)
    own_mark = slot_ids == own_slot
    own_expert = jnp.sum(jnp.where(own_mark, slot_expert, 0))
    twins = slot_expert == own_expert
    copies = jnp.sum(twins.astype(i32))
    own_rank = jnp.sum((twins & (slot_ids < own_slot)).astype(i32))
    rel_rows = jnp.transpose(rel_exp.reshape(2, 2, nx)[:, ::-1], (2, 1, 0)).reshape(-1)
    rel_slots = (rel_req[:, None] * exp_count + rel_rows[None, :]).reshape(-1)
    named = (route_expert == own_expert).reshape(slot_count, tok_rows, TOPK)[rel_slots]
    named = jnp.transpose(named, (0, 2, 1))
    chunk_rows = exp_count * tok_rows
    entries = -(-exp_count * capacity // 16) * 16
    served = jnp.any(named, axis=1) & (rel_slots % copies == own_rank)[:, None]
    served = served.reshape(ny, nc, chunk_rows)
    place = jnp.where(served, jnp.cumsum(served.astype(i32), axis=2) - 1, -1)
    place = place.reshape(ny, nc, 1, chunk_rows)

    place, named, blocks = tie((place, named, blocks))

    def attend_half(side, queries):
        return attend(
            blocks,
            queries,
            row_req[side],
            row_pos[side],
            page_request,
            page_slot,
            page_len,
            tokens,
            tok_rows,
        )

    gates = jnp.stack([send(gates, dh, 0, 0) for dh in range(2)])
    quarters.append(swap_y(quarters[0]))
    theirs, their_level = attend_half(1, far)
    theirs, their_level, gates, quarters = tie((theirs, their_level, gates, quarters))
    theirs, their_level = send(theirs, 1, 0, 0), send(their_level, 1, 0, 0)
    gates = jnp.stack([send_req(gates, dy, 0) for dy in range(ny)])
    quarters += [send_req(q, 0, dc) for dc in range(1, nc) for q in quarters[:2]]
    mine, level = attend_half(0, [])
    mine, level, gates, quarters = tie((mine, level, gates, quarters))

    stays, comes = {}, {}
    proj = out_proj
    for dl in (1, 0):
        stays[dl], go = project(
            dl, quarter_order, mine, level, theirs, their_level, proj, quarters, tok_rows
        )
        comes[dl] = [
            send(go[(dx - 1) * tok_rows : dx * tok_rows], 0, 0, -dx) for dx in range(1, nx)
        ]
        proj, _ = tie((proj, go))
    line = sum([come.astype(f32) for come in comes[1]], stays[1]).astype(bf16)
    comes[0], _ = tie((comes[0], line))
    line = send(line, 0, 1, 0)
    stream = sum([come.astype(f32) for come in comes[0]], resid.astype(f32) + stays[0])
    stream = stream + line.astype(f32)
    normed = rms_normed(stream, norm_gain)
    gates = jnp.stack([send_req(gates, 0, dc) for dc in range(nc)], axis=1)
    gates = jnp.transpose(gates[:, :, :, ::-1], (0, 1, 4, 3, 2, 5, 6))
    gates = gates.reshape(slot_count, TOPK, tok_rows)
    row_gate = jnp.sum(jnp.where(named, gates, 0.0), axis=1).reshape(ny, nc, 1, chunk_rows)

    far_line = send(normed, 1, 0, 0)
    line = [normed, send(normed, 0, 1, 0), far_line, send(far_line, 0, 1, 0)]
    order = [1, 3, 0, 2]
    over_x = {(i, dx): send(line[i], 0, 0, dx) for i in order for dx in range(1, nx)}
    over_y = {(i, dy): send_req(line[i], dy, 0) for i in order for dy in range(1, ny)}

    halves = [[line[i] for i in order]]
    shared_weights = (shared_scalar, shared_gate.T, shared_up.T, shared_down)
    shared = [shared_expert(halves[0], *shared_weights)]
    chunks = {(0, 0): [join(halves[0])]}
    for dc in range(1, nc):
        chunks[0, dc] = [send_req(chunks[0, 0][0], 0, dc)]
    over_x, over_y, shared, row_gate = tie((over_x, over_y, shared, row_gate))
    for dx in range(1, nx):
        half = [over_x[i, dx] for i in order]
        chunks[0, 0].append(join(half))
        for dc in range(1, nc):
            chunks[0, dc].append(send_req(chunks[0, 0][dx], 0, dc))
        halves.append(half)
    for dy in range(1, ny):
        half = join([over_y[i, dy] for i in order])
        chunks[dy, 0] = [half] + [send(half, 0, 0, dx) for dx in range(1, nx)]
        for dc in range(1, nc):
            chunks[dy, dc] = [send_req(half, 0, dc)]
    def answers_of(dy, dcs, more, cuts):
        return routed_expert(
            [chunks[dy, dc] for dc in dcs],
            jnp.concatenate([place[dy, dc : dc + 1] for dc in dcs]),
            jnp.concatenate([row_gate[dy, dc : dc + 1] for dc in dcs]),
            more,
            expert_gate,
            expert_up,
            expert_down,
            entries,
            cuts,
        )

    def add_up(parts):
        return sum([part.astype(f32) for part in parts[1:]], parts[0].astype(f32))

    cores = list(range(nc))
    kept, comes = {}, {}
    for dy in range(ny - 1):
        answers = answers_of(dy, cores, [], nx)
        if dy:
            answers, comes[dy - 1] = tie((answers, comes[dy - 1]))
        answers, chunks[dy + 1, 0] = tie((answers, chunks[dy + 1, 0]))
        for dc in range(1, nc):
            chunks[dy + 1, dc] += [send_req(part, 0, dc) for part in chunks[dy + 1, 0][1:]]
        others = [[send_req(part, 0, -dc) for part in answers[dc][::-1]][::-1] for dc in cores[1:]]
        parts = [answers[0]] + others
        if not dy:
            for dx in range(1, nx):
                halves[dx], _ = tie((halves[dx], answers[0]))
                shared.append(shared_expert(halves[dx], *shared_weights))
            parts.append(shared)
        gone = [add_up([part[dx] for part in parts]).astype(bf16) for dx in range(1, nx)]
        kept[dy] = [part[0] for part in parts]
        cut = chunk_rows // (2 * nx)
        comes[dy] = [
            [send(go[k * cut : (k + 1) * cut], 0, 0, -dx) for dx, go in enumerate(gone, 1)]
            for k in range(2)
        ]
        following = [chunks[dy + 1, dc] for dc in cores]
        following, _ = tie((following, gone))
        for dc in cores:
            chunks[dy + 1, dc] = following[dc]
    end = ny - 1
    others = []
    for dc in cores[1:]:
        (answer,) = answers_of(end, [dc], [], 1)
        answer, comes[end - 1][0] = tie((answer, comes[end - 1][0]))
        chunks[end, 0], _ = tie((chunks[end, 0], answer))
        others.append(send_req(answer[0], 0, -dc))
    (answer,) = answers_of(end, [0], [], 2 * nx)
    answer, others, comes = tie((answer, others, comes))

    last = {}
    for k in range(2):
        gone = [
            add_up(
                [answer[2 * dx + k]]
                + [other[(2 * dx + k) * cut : (2 * dx + k + 1) * cut] for other in others]
            ).astype(bf16)
            for dx in range(1, nx)
        ]
        last[k] = [send(go, 0, 0, -dx) for dx, go in enumerate(gone, 1)]
        others, _ = tie((others, gone))

    def line_of(dy, k):
        rows = slice(k * cut, (k + 1) * cut)
        if dy < end:
            return add_up([part[rows] for part in kept[dy]] + comes[dy][k])
        return add_up([answer[k]] + [other[rows] for other in others] + last[k])

    home = {}
    for k in range(2):
        goes = [line_of(dy, k).astype(bf16) for dy in range(1, ny)]
        if k:
            goes, home[0] = tie((goes, home[0]))
        else:
            last[1], _ = tie((last[1], goes))
        home[k] = [send_req(go, -dy, 0) for dy, go in enumerate(goes, 1)]
    near = send(add_up([line_of(0, 0)] + home[0]).astype(bf16), 0, 1, 0)
    total = add_up([line_of(0, 1)] + home[1] + [near])
    far = send(total[tok_rows:].astype(bf16), 1, 0, 0)
    total = add_up([stream, total[:tok_rows], far])
    return total.astype(bf16)


def solution(mesh):
    placed = (
        P(("req", "exp"), None),
        P(("req", "exp"), None),
        P(("req", "exp"), None, None),
        P(("req", "exp"), None, None),
        P("req", None),
        P("req"),
        P("req"),
        P("exp", None),
        P(),
        P(("req", "exp"), None, None),
        P(("req", "exp"), None, None),
        P(("req", "exp"), None, None),
        P(None, "exp"),
        P(None, "exp"),
        P("exp", None),
        P(),
        P(),
        P(),
        P(("req", "exp"), None),
    )
    return jax.shard_map(
        shards, mesh=mesh, in_specs=placed, out_specs=P(("req", "exp"), None), check_vma=False
    )
```

```python
import functools

import jax
import jax.numpy as jnp
from jax import lax
from jax.experimental import pallas as pl
from jax.experimental.pallas import tpu as pltpu
from jax.sharding import PartitionSpec as P

HEAD_DIM = 128
TOPK = 4
CORES = 2
Z_CHIPS = 4


def pack_kernel(members, parts, columns, order, *refs):
    sources, refs = refs[:parts], refs[parts:]
    gates, blocks, sems = refs[:-1 - members], refs[-1 - members : -1], refs[-1]
    copies = []
    for m in range(members):
        at = 0
        for source in sources:
            rows = source.shape[0]
            for j in range(2):
                place = pl.multiple_of(order[2 * m + j] * columns, columns)
                copies.append(
                    pltpu.make_async_copy(
                        source.at[:, pl.ds(place, columns)],
                        blocks[m].at[pl.ds(at, rows), pl.ds(j * columns, columns)],
                        sems.at[len(copies)],
                    )
                )
            at += rows
    for copy in copies:
        copy.start()
    if gates:
        weights = gates[0][...]
        high = weights.astype(jnp.bfloat16).astype(jnp.float32)
        middle = (weights - high).astype(jnp.bfloat16).astype(jnp.float32)
        low = weights - high - middle
        weights = jnp.concatenate([high, middle, low, jnp.zeros_like(low)], axis=0)
        for m in range(members):
            blocks[m][at:, :] = weights.astype(jnp.bfloat16)
    for copy in copies:
        copy.wait()


def pack(parts, gates, order, columns):
    members = order.shape[0] // 2
    rows = sum(p.shape[0] for p in parts) + (0 if gates is None else 4 * gates.shape[0])
    vmem = pl.BlockSpec(memory_space=pltpu.VMEM)
    in_specs = [pl.BlockSpec(memory_space=pltpu.SMEM)]
    in_specs += [pl.BlockSpec(memory_space=pl.ANY)] * len(parts)
    operands = list(parts)
    if gates is not None:
        in_specs.append(vmem)
        operands.append(gates)
    return pl.pallas_call(
        functools.partial(pack_kernel, members, len(parts), columns),
        out_shape=[jax.ShapeDtypeStruct((rows, 2 * columns), parts[0].dtype)] * members,
        in_specs=in_specs,
        out_specs=[vmem] * members,
        scratch_shapes=[pltpu.SemaphoreType.DMA((2 * members * len(parts),))],
        compiler_params=pltpu.CompilerParams(vmem_limit_bytes=56 * 1024 * 1024),
        cost_estimate=pl.CostEstimate(
            flops=0, bytes_accessed=8 * members * rows * columns, transcendentals=0
        ),
    )(order, *operands)


def attend_kernel(members, tokens, tok_rows, page_len, scale, page_req, page_slot, *refs):
    blocks, refs = refs[:members], refs[members:]
    if len(refs) > 4:
        query, refs = [q[...] for q in refs[:members]], refs[members:]
    else:
        query = [block[2 * tokens : 2 * tokens + tok_rows, :] for block in blocks]
    request, position, out, level = refs
    request, position = request[...], position[...]
    keys = jnp.concatenate([block[:tokens, :] for block in blocks], axis=0)
    values = jnp.concatenate([block[tokens : 2 * tokens, :] for block in blocks], axis=0)
    query = jnp.concatenate(query, axis=0)
    scores = (
        lax.dot_general(keys, query, (((1,), (1,)), ((), ())), preferred_element_type=jnp.float32)
        * scale
    )
    token = lax.broadcasted_iota(jnp.int32, (page_len, query.shape[0]), 0)
    visible = jnp.concatenate(
        [
            (request == page_req[page]) & (token + page_slot[page] * page_len <= position)
            for page in range(members * tokens // page_len)
        ],
        axis=0,
    )
    scores = jnp.where(visible, scores, -1e30)
    top = jnp.max(scores, axis=0, keepdims=True)
    weights = jnp.where(visible, jnp.exp(scores - top), 0.0)
    total = jnp.sum(weights, axis=0, keepdims=True)
    summed = lax.dot_general(
        values,
        weights.astype(jnp.bfloat16),
        (((0,), (0,)), ((), ())),
        preferred_element_type=jnp.float32,
    )
    seen = total > 0.0
    total = jnp.where(seen, total, 1.0)
    out[...] = (summed / total).astype(jnp.bfloat16)
    level[0] = jnp.where(seen, top + jnp.log(total), -1e30)


def attend(blocks, far, row_req, row_pos, page_req, page_slot, page_len, tokens, tok_rows):
    members, rows = len(blocks), row_req.shape[1]
    block_rows, columns = blocks[0].shape
    heads = columns // HEAD_DIM
    by_head = lambda n: pl.BlockSpec((n, HEAD_DIM), lambda h, *_: (0, h))
    whole = pl.BlockSpec((1, rows), lambda h, *_: (0, 0))
    return pl.pallas_call(
        functools.partial(
            attend_kernel, members, tokens, tok_rows, page_len, HEAD_DIM ** (-0.5)
        ),
        out_shape=[
            jax.ShapeDtypeStruct((columns, rows), jnp.bfloat16),
            jax.ShapeDtypeStruct((heads, 1, rows), jnp.float32),
        ],
        grid_spec=pltpu.PrefetchScalarGridSpec(
            num_scalar_prefetch=2,
            grid=(heads,),
            in_specs=[by_head(block_rows)] * members + [by_head(tok_rows)] * len(far) + [whole] * 2,
            out_specs=[
                pl.BlockSpec((HEAD_DIM, rows), lambda h, *_: (h, 0)),
                pl.BlockSpec((1, 1, rows), lambda h, *_: (h, 0, 0)),
            ],
        ),
        compiler_params=pltpu.CompilerParams(vmem_limit_bytes=48 * 1024 * 1024),
        cost_estimate=pl.CostEstimate(
            flops=4 * rows * members * tokens * columns,
            bytes_accessed=2 * members * (block_rows + tok_rows) * columns,
            transcendentals=rows * members * tokens * heads,
        ),
    )(page_req, page_slot, *blocks, *far, row_req, row_pos)


def project_kernel(order, mine, mine_level, theirs, their_level, own, *refs):
    quarters, (stay, go, proj) = refs[:-3], refs[-3:]
    rows, size = own.shape[0], quarters[0].shape[0]
    proj[:rows, :] = own[...]
    for k, quarter in enumerate(quarters):
        at = pl.multiple_of(rows + order[k] * size, size)
        proj[pl.ds(at, size), :] = quarter[...]
    parts = []
    heads = mine.shape[0] // HEAD_DIM
    for head in range(heads):
        twin = (head + heads // 2) % heads
        dims = slice(head * HEAD_DIM, (head + 1) * HEAD_DIM)
        twin_dims = slice(twin * HEAD_DIM, (twin + 1) * HEAD_DIM)
        share = 1.0 / (1.0 + jnp.exp(their_level[twin] - mine_level[head]))
        other = 1.0 / (1.0 + jnp.exp(mine_level[head] - their_level[twin]))
        both = share * mine[dims, :].astype(jnp.float32) + other * theirs[
            twin_dims, :
        ].astype(jnp.float32)
        parts.append(both.astype(jnp.bfloat16))
    attention = jnp.concatenate(parts, axis=0)
    mixed = lax.dot_general(
        attention, proj[...], (((0,), (0,)), ((), ())), preferred_element_type=jnp.float32
    )
    kept = stay.shape[0]
    stay[...] = mixed[:kept, :]
    go[...] = mixed[kept:, :].astype(jnp.bfloat16)


def project(place, order, mine, mine_level, theirs, their_level, own, quarters, tok_rows):
    dims, width = mine.shape[0], own.shape[1]
    heads = dims // HEAD_DIM
    size = mine.shape[1] // 2
    whole = lambda a: pl.BlockSpec(a.shape, lambda i, order: (0, 0))
    values = pl.BlockSpec((dims, size), lambda i, order: (0, place))
    levels = pl.BlockSpec((heads, 1, size), lambda i, order: (0, 0, place))
    return pl.pallas_call(
        project_kernel,
        out_shape=[
            jax.ShapeDtypeStruct((tok_rows, width), jnp.float32),
            jax.ShapeDtypeStruct((size - tok_rows, width), jnp.bfloat16),
        ],
        grid_spec=pltpu.PrefetchScalarGridSpec(
            num_scalar_prefetch=1,
            grid=(1,),
            in_specs=[values, levels, values, levels, whole(own)] + [whole(q) for q in quarters],
            out_specs=[
                pl.BlockSpec((tok_rows, width), lambda i, order: (0, 0)),
                pl.BlockSpec((size - tok_rows, width), lambda i, order: (0, 0)),
            ],
            scratch_shapes=[pltpu.VMEM((dims, width), jnp.bfloat16)],
        ),
        compiler_params=pltpu.CompilerParams(vmem_limit_bytes=32 * 1024 * 1024),
        cost_estimate=pl.CostEstimate(
            flops=2 * size * dims * width,
            bytes_accessed=2 * (2 * dims * size + dims * width + 3 * size * width),
            transcendentals=2 * size * heads,
        ),
    )(order, mine, mine_level, theirs, their_level, own, *quarters)


def join_kernel(*refs):
    parts, out = refs[:-1], refs[-1]
    rows = parts[0].shape[0]
    for i, part in enumerate(parts):
        out[i * rows : (i + 1) * rows, :] = part[...]


def join(parts):
    rows, width = parts[0].shape
    vmem = pl.BlockSpec(memory_space=pltpu.VMEM)
    return pl.pallas_call(
        join_kernel,
        out_shape=jax.ShapeDtypeStruct((len(parts) * rows, width), parts[0].dtype),
        in_specs=[vmem] * len(parts),
        out_specs=vmem,
        cost_estimate=pl.CostEstimate(
            flops=0, bytes_accessed=4 * len(parts) * rows * width, transcendentals=0
        ),
    )(*parts)


def silu(value):
    return value / (1.0 + jnp.exp(-value))


def shared_kernel(count, *refs):
    pieces, (scalar, gate_w, up_w, down_w, out, rows, gate_v, up_v, down_v, sems) = (
        refs[:count],
        refs[count:],
    )
    moves = [(gate_w, gate_v), (up_w, up_v), (down_w, down_v)]
    size = pieces[0].shape[0]
    moves += [(piece, rows.at[pl.ds(i * size, size)]) for i, piece in enumerate(pieces)]
    copies = [
        pltpu.make_async_copy(src, dst, sems.at[i]) for i, (src, dst) in enumerate(moves)
    ]
    for copy in copies[3:] + copies[:3]:
        copy.start()
    for copy in copies[3:]:
        copy.wait()
    block = rows[...]
    logit = jnp.sum(
        block.astype(jnp.float32) * scalar[...].astype(jnp.float32), axis=1, keepdims=True
    )
    scale = 1.0 / (1.0 + jnp.exp(-logit))
    across = (((1,), (1,)), ((), ()))
    copies[0].wait()
    gate = lax.dot_general(block, gate_v[...], across, preferred_element_type=jnp.float32)
    copies[1].wait()
    upper = lax.dot_general(block, up_v[...], across, preferred_element_type=jnp.float32)
    hidden = (silu(gate) * upper).astype(jnp.bfloat16)
    copies[2].wait()
    result = jnp.dot(hidden, down_v[...], preferred_element_type=jnp.float32)
    out[...] = (scale * result).astype(jnp.bfloat16)


def shared_expert(pieces, scalar, gate_w, up_w, down_w):
    any_spec = pl.BlockSpec(memory_space=pl.ANY)
    vmem = pl.BlockSpec(memory_space=pltpu.VMEM)
    rows = sum(piece.shape[0] for piece in pieces)
    width = pieces[0].shape[1]
    return pl.pallas_call(
        functools.partial(shared_kernel, len(pieces)),
        out_shape=jax.ShapeDtypeStruct((rows, width), jnp.bfloat16),
        in_specs=[any_spec] * len(pieces) + [vmem] + [any_spec] * 3,
        out_specs=vmem,
        scratch_shapes=[
            pltpu.VMEM((rows, width), jnp.bfloat16),
            pltpu.VMEM(gate_w.shape, jnp.bfloat16),
            pltpu.VMEM(up_w.shape, jnp.bfloat16),
            pltpu.VMEM(down_w.shape, jnp.bfloat16),
            pltpu.SemaphoreType.DMA((3 + len(pieces),)),
        ],
        compiler_params=pltpu.CompilerParams(vmem_limit_bytes=56 * 1024 * 1024),
        cost_estimate=pl.CostEstimate(
            flops=6 * rows * gate_w.size,
            bytes_accessed=6 * gate_w.size + 4 * rows * width,
            transcendentals=rows * gate_w.shape[0],
        ),
    )(*pieces, scalar.reshape(1, -1), gate_w, up_w, down_w)


def routed_kernel(parts, extras, entries, cuts, *refs):
    count, total = len(parts), sum(parts)
    pieces, refs = refs[:total], refs[total:]
    place, row_gate = refs[:2]
    more, refs = refs[2 : 2 + extras], refs[2 + extras :]
    (gate_w, up_w, down_w), refs = refs[:3], refs[3:]
    outs, refs = refs[: count * cuts], refs[count * cuts :]
    rows, packed, gate_v, up_v, down_v, more_v, sems = refs
    moves, chunk_copies = [], []
    for c, n in enumerate(parts):
        at = 0
        chunk_copies.append(range(len(moves), len(moves) + n))
        for piece in pieces[sum(parts[:c]) : sum(parts[: c + 1])]:
            moves.append((piece, rows.at[c, pl.ds(at, piece.shape[0])]))
            at += piece.shape[0]
    moves += [(gate_w.at[0], gate_v), (up_w.at[0], up_v), (down_w.at[0], down_v)]
    at = 0
    for extra in more:
        moves.append((extra, more_v.at[pl.ds(at, extra.shape[0])]))
        at += extra.shape[0]
    copies = [
        pltpu.make_async_copy(src, dst, sems.at[i]) for i, (src, dst) in enumerate(moves)
    ]
    for copy in copies:
        copy.start()
    size = rows.shape[1]
    wanted = lax.broadcasted_iota(jnp.int32, (entries, size), 0)
    picks, weights = [], []
    for c in range(count):
        pick = jnp.where(place[c] == wanted, 1.0, 0.0)
        picks.append(pick.astype(jnp.bfloat16))
        weights.append(jnp.sum(pick * row_gate[c], axis=1, keepdims=True))
        for i in chunk_copies[c]:
            copies[i].wait()
        packed[c * entries : (c + 1) * entries, :] = jnp.dot(
            picks[c], rows[c], preferred_element_type=jnp.float32
        ).astype(jnp.bfloat16)
    copies[total].wait()
    gate = jnp.dot(packed[...], gate_v[...], preferred_element_type=jnp.float32)
    copies[total + 1].wait()
    upper = jnp.dot(packed[...], up_v[...], preferred_element_type=jnp.float32)
    hidden = (silu(gate) * upper).astype(jnp.bfloat16)
    copies[total + 2].wait()
    answer = jnp.dot(hidden, down_v[...], preferred_element_type=jnp.float32).astype(
        jnp.bfloat16
    )
    for i in range(extras):
        copies[total + 3 + i].wait()
    cut = size // cuts
    for c in range(count):
        scaled = answer[c * entries : (c + 1) * entries, :].astype(jnp.float32) * weights[c]
        placed = lax.dot_general(
            picks[c],
            scaled.astype(jnp.bfloat16),
            (((0,), (0,)), ((), ())),
            preferred_element_type=jnp.float32,
        )
        if c == 0 and extras:
            placed = placed + more_v[...].astype(jnp.float32)
        placed = placed.astype(jnp.bfloat16)
        for k in range(cuts):
            outs[c * cuts + k][...] = placed[k * cut : (k + 1) * cut, :]


def routed_expert(chunks, place, row_gate, more, gate_w, up_w, down_w, entries, cuts):
    count = len(chunks)
    parts = [len(chunk) for chunk in chunks]
    total = sum(parts)
    size = sum(piece.shape[0] for piece in chunks[0])
    width = chunks[0][0].shape[1]
    hidden = gate_w.shape[2]
    any_spec = pl.BlockSpec(memory_space=pl.ANY)
    vmem = pl.BlockSpec(memory_space=pltpu.VMEM)
    out_shape = jax.ShapeDtypeStruct((size // cuts, width), jnp.bfloat16)
    more_rows = sum(extra.shape[0] for extra in more) if more else 16
    outs = pl.pallas_call(
        functools.partial(routed_kernel, parts, len(more), entries, cuts),
        out_shape=[out_shape] * (count * cuts),
        in_specs=[any_spec] * total + [vmem] * 2 + [any_spec] * (len(more) + 3),
        out_specs=[vmem] * (count * cuts),
        scratch_shapes=[
            pltpu.VMEM((count, size, width), jnp.bfloat16),
            pltpu.VMEM((count * entries, width), jnp.bfloat16),
            pltpu.VMEM((width, hidden), jnp.bfloat16),
            pltpu.VMEM((width, hidden), jnp.bfloat16),
            pltpu.VMEM((hidden, width), jnp.bfloat16),
            pltpu.VMEM((more_rows, width), jnp.bfloat16),
            pltpu.SemaphoreType.DMA((total + 3 + len(more),)),
        ],
        compiler_params=pltpu.CompilerParams(vmem_limit_bytes=56 * 1024 * 1024),
        cost_estimate=pl.CostEstimate(
            flops=2 * count * entries * (3 * gate_w.size + 2 * size * width),
            bytes_accessed=6 * gate_w.size + 4 * count * size * width,
            transcendentals=count * entries * hidden,
        ),
    )(*[piece for chunk in chunks for piece in chunk], place, row_gate, *more, gate_w, up_w, down_w)
    return [outs[c * cuts : (c + 1) * cuts] for c in range(count)]


def rms_normed(stream, norm_gain):
    scale_row = lax.rsqrt(jnp.mean(stream * stream, axis=1, keepdims=True) + 1e-06)
    return (stream * scale_row * norm_gain[None, :]).astype(jnp.bfloat16)


def shards(
    resid,
    queries,
    cache_key,
    cache_value,
    page_table,
    row_request,
    row_position,
    out_proj,
    norm_gain,
    expert_gate,
    expert_up,
    expert_down,
    shared_gate,
    shared_up,
    shared_down,
    shared_scalar,
    slot_expert,
    route_expert,
    route_gate,
):
    f32, bf16, i32 = jnp.float32, jnp.bfloat16, jnp.int32
    exp_count = lax.axis_size("exp")
    req_count = lax.axis_size("req")
    slot_count = exp_count * req_count
    nc, nx, ny = CORES, exp_count // Z_CHIPS, req_count // CORES
    exp_index = lax.axis_index("exp")
    req_index = lax.axis_index("req")
    own_slot = req_index * exp_count + exp_index
    iz, ix = exp_index // nx, exp_index % nx
    ih, il = iz // 2, iz % 2
    iy, ic = req_index // nc, req_index % nc
    tok_rows, width = resid.shape
    pages_here, page_len, _ = cache_key.shape
    req_slots, max_pages = page_table.shape
    tokens = pages_here * page_len
    capacity = 3 * tok_rows * TOPK // slot_count

    zs = [(dh, dl) for dh in range(2) for dl in range(2)]

    def send(value, dh, dl, dx):
        if not (dh or dl or dx % nx):
            return value
        pairs = [
            (
                (h * 2 + l) * nx + x,
                ((h + dh) % 2 * 2 + (l + dl) % 2) * nx + (x + dx) % nx,
            )
            for h in range(2)
            for l in range(2)
            for x in range(nx)
        ]
        return lax.ppermute(value, "exp", pairs)

    def send_req(value, dy, dc):
        if not (dy % ny or dc % nc):
            return value
        pairs = [
            (y * nc + c, (y + dy) % ny * nc + (c + dc) % nc)
            for y in range(ny)
            for c in range(nc)
        ]
        return lax.ppermute(value, "req", pairs)

    def swap_y(value):
        pairs = [(y * nc + c, (y ^ 1) * nc + c) for y in range(ny) for c in range(nc)]
        return lax.ppermute(value, "req", pairs)

    tie = lax.optimization_barrier

    rel_exp = jnp.stack(
        [
            ((ih + dh) % 2 * 2 + (il + dl) % 2) * nx + (ix - dx) % nx
            for dh, dl in zs
            for dx in range(nx)
        ]
    ).astype(i32)
    rel_req = jnp.stack(
        [((iy - dy) % ny) * nc + (ic - dc) % nc for dy in range(ny) for dc in range(nc)]
    ).astype(i32)

    columns = width // exp_count
    keys = cache_key.reshape(tokens, width)
    values = cache_value.reshape(tokens, width)
    quarter_rows = out_proj.shape[0] // (2 * nc)
    quarter = lax.dynamic_slice_in_dim(
        out_proj, (iy % 2 * nc + ic) * quarter_rows, quarter_rows, 0
    )
    quarters = [send(quarter, 1, 0, 0)]
    quarter_order = jnp.stack(
        [(iy + dy) % 2 * nc + (ic + dc) % nc for dc in range(nc) for dy in range(2)]
    ).astype(i32)
    far_queries = send(queries, 1, 0, 0)
    members = [(dl, dx) for dl in range(2) for dx in range(nx)]
    order = jnp.stack(
        [
            ((ih + j) % 2 * 2 + (il + dl) % 2) * nx + (ix + dx) % nx
            for dl, dx in members
            for j in range(2)
        ]
    ).astype(i32)
    gates = jnp.pad(jnp.transpose(route_gate), ((0, 0), (0, 2 * columns - tok_rows)))
    blocks = pack([keys, values, queries], gates, order, columns)
    blocks = [send(blocks[m], 0, *members[m]) for m in range(len(members))]
    far = list(pack([far_queries], None, order, columns))
    for m in range(1, len(members)):
        if m > 2:
            far[m], far[m - 2] = tie((far[m], far[m - 2]))
        far[m] = send(far[m], 0, *members[m])
    page_ids = (
        rel_exp[: len(members), None] * pages_here + jnp.arange(pages_here, dtype=i32)[None, :]
    ).reshape(-1)
    hits = (page_table[None, :, :] == page_ids[:, None, None]).astype(i32)
    page_request = jnp.sum(hits * jnp.arange(req_slots, dtype=i32)[None, :, None], axis=(1, 2))
    page_slot = jnp.sum(hits * jnp.arange(max_pages, dtype=i32)[None, None, :], axis=(1, 2))
    by_place = lambda a: a.reshape(exp_count, tok_rows)[rel_exp].reshape(2, 1, -1)
    row_req, row_pos = by_place(row_request), by_place(row_position)
    gates = [block[2 * tokens + tok_rows :, :tok_rows].astype(f32) for block in blocks]
    gates = jnp.stack([g[:TOPK] + g[TOPK : 2 * TOPK] + g[2 * TOPK : 3 * TOPK] for g in gates])
    gates = gates.reshape(2, nx, TOPK, tok_rows)

    slot_ids = jnp.arange(slot_count, dtype=i32)
    own_mark = slot_ids == own_slot
    own_expert = jnp.sum(jnp.where(own_mark, slot_expert, 0))
    twins = slot_expert == own_expert
    copies = jnp.sum(twins.astype(i32))
    own_rank = jnp.sum((twins & (slot_ids < own_slot)).astype(i32))
    rel_rows = jnp.transpose(rel_exp.reshape(2, 2, nx)[:, ::-1], (2, 1, 0)).reshape(-1)
    rel_slots = (rel_req[:, None] * exp_count + rel_rows[None, :]).reshape(-1)
    named = (route_expert == own_expert).reshape(slot_count, tok_rows, TOPK)[rel_slots]
    named = jnp.transpose(named, (0, 2, 1))
    chunk_rows = exp_count * tok_rows
    entries = -(-exp_count * capacity // 16) * 16
    served = jnp.any(named, axis=1) & (rel_slots % copies == own_rank)[:, None]
    served = served.reshape(ny, nc, chunk_rows)
    place = jnp.where(served, jnp.cumsum(served.astype(i32), axis=2) - 1, -1)
    place = place.reshape(ny, nc, 1, chunk_rows)

    place, named, blocks = tie((place, named, blocks))

    def attend_half(side, queries):
        return attend(
            blocks,
            queries,
            row_req[side],
            row_pos[side],
            page_request,
            page_slot,
            page_len,
            tokens,
            tok_rows,
        )

    gates = jnp.stack([send(gates, dh, 0, 0) for dh in range(2)])
    quarters.append(swap_y(quarters[0]))
    theirs, their_level = attend_half(1, far)
    theirs, their_level, gates, quarters = tie((theirs, their_level, gates, quarters))
    theirs, their_level = send(theirs, 1, 0, 0), send(their_level, 1, 0, 0)
    gates = jnp.stack([send_req(gates, dy, 0) for dy in range(ny)])
    quarters += [send_req(q, 0, dc) for dc in range(1, nc) for q in quarters[:2]]
    mine, level = attend_half(0, [])
    mine, level, gates, quarters = tie((mine, level, gates, quarters))

    stays, comes = {}, {}
    proj = out_proj
    for dl in (1, 0):
        stays[dl], go = project(
            dl, quarter_order, mine, level, theirs, their_level, proj, quarters, tok_rows
        )
        comes[dl] = [
            send(go[(dx - 1) * tok_rows : dx * tok_rows], 0, 0, -dx) for dx in range(1, nx)
        ]
        proj, _ = tie((proj, go))
    line = sum([come.astype(f32) for come in comes[1]], stays[1]).astype(bf16)
    comes[0], _ = tie((comes[0], line))
    line = send(line, 0, 1, 0)
    stream = sum([come.astype(f32) for come in comes[0]], resid.astype(f32) + stays[0])
    stream = stream + line.astype(f32)
    normed = rms_normed(stream, norm_gain)
    gates = jnp.stack([send_req(gates, 0, dc) for dc in range(nc)], axis=1)
    gates = jnp.transpose(gates[:, :, :, ::-1], (0, 1, 4, 3, 2, 5, 6))
    gates = gates.reshape(slot_count, TOPK, tok_rows)
    row_gate = jnp.sum(jnp.where(named, gates, 0.0), axis=1).reshape(ny, nc, 1, chunk_rows)

    far_line = send(normed, 1, 0, 0)
    line = [normed, send(normed, 0, 1, 0), far_line, send(far_line, 0, 1, 0)]
    order = [1, 3, 0, 2]
    over_x = {(i, dx): send(line[i], 0, 0, dx) for i in order for dx in range(1, nx)}
    over_y = {(i, dy): send_req(line[i], dy, 0) for i in order for dy in range(1, ny)}

    halves = [[line[i] for i in order]]
    shared_weights = (shared_scalar, shared_gate.T, shared_up.T, shared_down)
    shared = [shared_expert(halves[0], *shared_weights)]
    chunks = {(0, 0): [join(halves[0])]}
    for dc in range(1, nc):
        chunks[0, dc] = [send_req(chunks[0, 0][0], 0, dc)]
    over_x, over_y, shared, row_gate = tie((over_x, over_y, shared, row_gate))
    for dy in range(1, ny):
        half = join([over_y[i, dy] for i in order])
        chunks[dy, 0] = [half] + [send(half, 0, 0, dx) for dx in range(1, nx)]
        for dc in range(1, nc):
            chunks[dy, dc] = [send_req(half, 0, dc)]
        over_x, _ = tie((over_x, half))
    for dx in range(1, nx):
        half = [over_x[i, dx] for i in order]
        chunks[0, 0].append(join(half))
        for dc in range(1, nc):
            chunks[0, dc].append(send_req(chunks[0, 0][dx], 0, dc))
        halves.append(half)

    def answers_of(dy, dcs, more, cuts):
        return routed_expert(
            [chunks[dy, dc] for dc in dcs],
            jnp.concatenate([place[dy, dc : dc + 1] for dc in dcs]),
            jnp.concatenate([row_gate[dy, dc : dc + 1] for dc in dcs]),
            more,
            expert_gate,
            expert_up,
            expert_down,
            entries,
            cuts,
        )

    def add_up(parts):
        return sum([part.astype(f32) for part in parts[1:]], parts[0].astype(f32))

    cores = list(range(nc))
    kept, comes = {}, {}
    half_rows = 2 * tok_rows
    for dy in range(ny - 1):
        answers = answers_of(dy, cores, [], nx)
        if dy:
            answers, comes[dy - 1] = tie((answers, comes[dy - 1]))
        others = [[send_req(part, 0, -dc) for part in answers[dc][::-1]][::-1] for dc in cores[1:]]
        parts = [answers[0]] + others
        if dy:
            following = answers[0][0]
        else:
            for dx in range(1, nx):
                halves[dx], _ = tie((halves[dx], answers[0]))
                shared.append(shared_expert(halves[dx], *shared_weights))
            parts.append(shared)
            following = shared[-1]
        chunks[dy + 1, 0], _ = tie((chunks[dy + 1, 0], following))
        for dc in range(1, nc):
            chunks[dy + 1, dc] += [send_req(part, 0, dc) for part in chunks[dy + 1, 0][1:]]
        gone = [add_up([part[dx] for part in parts]).astype(bf16) for dx in range(1, nx)]
        kept[dy] = [part[0] for part in parts]
        comes[dy] = [
            [
                send(go[k * half_rows : (k + 1) * half_rows], 0, 0, -dx)
                for dx, go in enumerate(gone, 1)
            ]
            for k in range(2)
        ]
        following = [chunks[dy + 1, dc] for dc in cores]
        following, _ = tie((following, gone))
        for dc in cores:
            chunks[dy + 1, dc] = following[dc]
    end = ny - 1
    others = []
    for dc in cores[1:]:
        (answer,) = answers_of(end, [dc], [], 1)
        answer, comes[end - 1][0] = tie((answer, comes[end - 1][0]))
        chunks[end, 0], _ = tie((chunks[end, 0], answer))
        others.append(send_req(answer[0], 0, -dc))
    (answer,) = answers_of(end, [0], [], 4 * nx)
    answer, others, comes = tie((answer, others, comes))

    turns = [1, 3, 0, 2]
    block = lambda a, p: a[p * tok_rows : (p + 1) * tok_rows]
    last = {}
    for p in turns:
        gone = [
            add_up([answer[4 * dx + p]] + [block(other, 4 * dx + p) for other in others])
            for dx in range(1, nx)
        ]
        gone = [go.astype(bf16) for go in gone]
        last[p] = [send(go, 0, 0, -dx) for dx, go in enumerate(gone, 1)]
        others, _ = tie((others, gone))

    def line_of(dy, p):
        if dy < end:
            arrived = [block(come, p % 2) for come in comes[dy][p // 2]]
            return add_up([block(part, p) for part in kept[dy]] + arrived)
        return add_up([answer[p]] + [block(other, p) for other in others] + last[p])

    home, near = {}, {}
    for turn, p in enumerate(turns):
        goes = [line_of(dy, p).astype(bf16) for dy in range(1, ny)]
        home[p] = [send_req(go, -dy, 0) for dy, go in enumerate(goes, 1)]
        if turn + 1 < len(turns):
            after = turns[turn + 1]
            last[after], _ = tie((last[after], goes))
    for p in (1, 0):
        go = add_up([line_of(0, p)] + home[p]).astype(bf16)
        if p:
            home[0], _ = tie((home[0], go))
        near[p] = send(go, 0, 1, 0)
    far = add_up([line_of(0, 3)] + home[3] + [near[1]]).astype(bf16)
    far = send(far, 1, 0, 0)
    total = add_up([stream, line_of(0, 2)] + home[2] + [near[0], far])
    return total.astype(bf16)


def solution(mesh):
    placed = (
        P(("req", "exp"), None),
        P(("req", "exp"), None),
        P(("req", "exp"), None, None),
        P(("req", "exp"), None, None),
        P("req", None),
        P("req"),
        P("req"),
        P("exp", None),
        P(),
        P(("req", "exp"), None, None),
        P(("req", "exp"), None, None),
        P(("req", "exp"), None, None),
        P(None, "exp"),
        P(None, "exp"),
        P("exp", None),
        P(),
        P(),
        P(),
        P(("req", "exp"), None),
    )
    return jax.shard_map(
        shards, mesh=mesh, in_specs=placed, out_specs=P(("req", "exp"), None), check_vma=False
    )
```

```python
import functools

import jax
import jax.numpy as jnp
from jax import lax
from jax.experimental import pallas as pl
from jax.experimental.pallas import tpu as pltpu
from jax.sharding import PartitionSpec as P

HEAD_DIM = 128
TOPK = 4
CORES = 2
Z_CHIPS = 4


def pack_kernel(members, parts, columns, order, *refs):
    sources, refs = refs[:parts], refs[parts:]
    gates, blocks, sems = refs[:-1 - members], refs[-1 - members : -1], refs[-1]
    copies = []
    for m in range(members):
        at = 0
        for source in sources:
            rows = source.shape[0]
            for j in range(2):
                place = pl.multiple_of(order[2 * m + j] * columns, columns)
                copies.append(
                    pltpu.make_async_copy(
                        source.at[:, pl.ds(place, columns)],
                        blocks[m].at[pl.ds(at, rows), pl.ds(j * columns, columns)],
                        sems.at[len(copies)],
                    )
                )
            at += rows
    for copy in copies:
        copy.start()
    if gates:
        weights = gates[0][...]
        high = weights.astype(jnp.bfloat16).astype(jnp.float32)
        middle = (weights - high).astype(jnp.bfloat16).astype(jnp.float32)
        low = weights - high - middle
        weights = jnp.concatenate([high, middle, low, jnp.zeros_like(low)], axis=0)
        for m in range(members):
            blocks[m][at:, :] = weights.astype(jnp.bfloat16)
    for copy in copies:
        copy.wait()


def pack(parts, gates, order, columns):
    members = order.shape[0] // 2
    rows = sum(p.shape[0] for p in parts) + (0 if gates is None else 4 * gates.shape[0])
    vmem = pl.BlockSpec(memory_space=pltpu.VMEM)
    in_specs = [pl.BlockSpec(memory_space=pltpu.SMEM)]
    in_specs += [pl.BlockSpec(memory_space=pl.ANY)] * len(parts)
    operands = list(parts)
    if gates is not None:
        in_specs.append(vmem)
        operands.append(gates)
    return pl.pallas_call(
        functools.partial(pack_kernel, members, len(parts), columns),
        out_shape=[jax.ShapeDtypeStruct((rows, 2 * columns), parts[0].dtype)] * members,
        in_specs=in_specs,
        out_specs=[vmem] * members,
        scratch_shapes=[pltpu.SemaphoreType.DMA((2 * members * len(parts),))],
        compiler_params=pltpu.CompilerParams(vmem_limit_bytes=56 * 1024 * 1024),
        cost_estimate=pl.CostEstimate(
            flops=0, bytes_accessed=8 * members * rows * columns, transcendentals=0
        ),
    )(order, *operands)


def attend_kernel(members, tokens, tok_rows, page_len, scale, page_req, page_slot, *refs):
    blocks, refs = refs[:members], refs[members:]
    if len(refs) > 4:
        query, refs = [q[...] for q in refs[:members]], refs[members:]
    else:
        query = [block[2 * tokens : 2 * tokens + tok_rows, :] for block in blocks]
    request, position, out, level = refs
    request, position = request[...], position[...]
    keys = jnp.concatenate([block[:tokens, :] for block in blocks], axis=0)
    values = jnp.concatenate([block[tokens : 2 * tokens, :] for block in blocks], axis=0)
    query = jnp.concatenate(query, axis=0)
    scores = (
        lax.dot_general(keys, query, (((1,), (1,)), ((), ())), preferred_element_type=jnp.float32)
        * scale
    )
    token = lax.broadcasted_iota(jnp.int32, (page_len, query.shape[0]), 0)
    visible = jnp.concatenate(
        [
            (request == page_req[page]) & (token + page_slot[page] * page_len <= position)
            for page in range(members * tokens // page_len)
        ],
        axis=0,
    )
    scores = jnp.where(visible, scores, -1e30)
    top = jnp.max(scores, axis=0, keepdims=True)
    weights = jnp.where(visible, jnp.exp(scores - top), 0.0)
    total = jnp.sum(weights, axis=0, keepdims=True)
    summed = lax.dot_general(
        values,
        weights.astype(jnp.bfloat16),
        (((0,), (0,)), ((), ())),
        preferred_element_type=jnp.float32,
    )
    seen = total > 0.0
    total = jnp.where(seen, total, 1.0)
    out[...] = (summed / total).astype(jnp.bfloat16)
    level[0] = jnp.where(seen, top + jnp.log(total), -1e30)


def attend(blocks, far, row_req, row_pos, page_req, page_slot, page_len, tokens, tok_rows):
    members, rows = len(blocks), row_req.shape[1]
    block_rows, columns = blocks[0].shape
    heads = columns // HEAD_DIM
    by_head = lambda n: pl.BlockSpec((n, HEAD_DIM), lambda h, *_: (0, h))
    whole = pl.BlockSpec((1, rows), lambda h, *_: (0, 0))
    return pl.pallas_call(
        functools.partial(
            attend_kernel, members, tokens, tok_rows, page_len, HEAD_DIM ** (-0.5)
        ),
        out_shape=[
            jax.ShapeDtypeStruct((columns, rows), jnp.bfloat16),
            jax.ShapeDtypeStruct((heads, 1, rows), jnp.float32),
        ],
        grid_spec=pltpu.PrefetchScalarGridSpec(
            num_scalar_prefetch=2,
            grid=(heads,),
            in_specs=[by_head(block_rows)] * members + [by_head(tok_rows)] * len(far) + [whole] * 2,
            out_specs=[
                pl.BlockSpec((HEAD_DIM, rows), lambda h, *_: (h, 0)),
                pl.BlockSpec((1, 1, rows), lambda h, *_: (h, 0, 0)),
            ],
        ),
        compiler_params=pltpu.CompilerParams(vmem_limit_bytes=48 * 1024 * 1024),
        cost_estimate=pl.CostEstimate(
            flops=4 * rows * members * tokens * columns,
            bytes_accessed=2 * members * (block_rows + tok_rows) * columns,
            transcendentals=rows * members * tokens * heads,
        ),
    )(page_req, page_slot, *blocks, *far, row_req, row_pos)


def project_kernel(order, mine, mine_level, theirs, their_level, own, *refs):
    quarters, (stay, go, proj) = refs[:-3], refs[-3:]
    rows, size = own.shape[0], quarters[0].shape[0]
    proj[:rows, :] = own[...]
    for k, quarter in enumerate(quarters):
        at = pl.multiple_of(rows + order[k] * size, size)
        proj[pl.ds(at, size), :] = quarter[...]
    parts = []
    heads = mine.shape[0] // HEAD_DIM
    for head in range(heads):
        twin = (head + heads // 2) % heads
        dims = slice(head * HEAD_DIM, (head + 1) * HEAD_DIM)
        twin_dims = slice(twin * HEAD_DIM, (twin + 1) * HEAD_DIM)
        share = 1.0 / (1.0 + jnp.exp(their_level[twin] - mine_level[head]))
        other = 1.0 / (1.0 + jnp.exp(mine_level[head] - their_level[twin]))
        both = share * mine[dims, :].astype(jnp.float32) + other * theirs[
            twin_dims, :
        ].astype(jnp.float32)
        parts.append(both.astype(jnp.bfloat16))
    attention = jnp.concatenate(parts, axis=0)
    mixed = lax.dot_general(
        attention, proj[...], (((0,), (0,)), ((), ())), preferred_element_type=jnp.float32
    )
    kept = stay.shape[0]
    stay[...] = mixed[:kept, :]
    go[...] = mixed[kept:, :].astype(jnp.bfloat16)


def project(place, order, mine, mine_level, theirs, their_level, own, quarters, tok_rows):
    dims, width = mine.shape[0], own.shape[1]
    heads = dims // HEAD_DIM
    size = mine.shape[1] // 2
    whole = lambda a: pl.BlockSpec(a.shape, lambda i, order: (0, 0))
    values = pl.BlockSpec((dims, size), lambda i, order: (0, place))
    levels = pl.BlockSpec((heads, 1, size), lambda i, order: (0, 0, place))
    return pl.pallas_call(
        project_kernel,
        out_shape=[
            jax.ShapeDtypeStruct((tok_rows, width), jnp.float32),
            jax.ShapeDtypeStruct((size - tok_rows, width), jnp.bfloat16),
        ],
        grid_spec=pltpu.PrefetchScalarGridSpec(
            num_scalar_prefetch=1,
            grid=(1,),
            in_specs=[values, levels, values, levels, whole(own)] + [whole(q) for q in quarters],
            out_specs=[
                pl.BlockSpec((tok_rows, width), lambda i, order: (0, 0)),
                pl.BlockSpec((size - tok_rows, width), lambda i, order: (0, 0)),
            ],
            scratch_shapes=[pltpu.VMEM((dims, width), jnp.bfloat16)],
        ),
        compiler_params=pltpu.CompilerParams(vmem_limit_bytes=32 * 1024 * 1024),
        cost_estimate=pl.CostEstimate(
            flops=2 * size * dims * width,
            bytes_accessed=2 * (2 * dims * size + dims * width + 3 * size * width),
            transcendentals=2 * size * heads,
        ),
    )(order, mine, mine_level, theirs, their_level, own, *quarters)


def join_kernel(*refs):
    parts, out = refs[:-1], refs[-1]
    rows = parts[0].shape[0]
    for i, part in enumerate(parts):
        out[i * rows : (i + 1) * rows, :] = part[...]


def join(parts):
    rows, width = parts[0].shape
    vmem = pl.BlockSpec(memory_space=pltpu.VMEM)
    return pl.pallas_call(
        join_kernel,
        out_shape=jax.ShapeDtypeStruct((len(parts) * rows, width), parts[0].dtype),
        in_specs=[vmem] * len(parts),
        out_specs=vmem,
        cost_estimate=pl.CostEstimate(
            flops=0, bytes_accessed=4 * len(parts) * rows * width, transcendentals=0
        ),
    )(*parts)


def silu(value):
    return value / (1.0 + jnp.exp(-value))


def shared_kernel(count, *refs):
    pieces, (scalar, gate_w, up_w, down_w, out, rows, gate_v, up_v, down_v, sems) = (
        refs[:count],
        refs[count:],
    )
    moves = [(gate_w, gate_v), (up_w, up_v), (down_w, down_v)]
    size = pieces[0].shape[0]
    moves += [(piece, rows.at[pl.ds(i * size, size)]) for i, piece in enumerate(pieces)]
    copies = [
        pltpu.make_async_copy(src, dst, sems.at[i]) for i, (src, dst) in enumerate(moves)
    ]
    for copy in copies[3:] + copies[:3]:
        copy.start()
    for copy in copies[3:]:
        copy.wait()
    block = rows[...]
    logit = jnp.sum(
        block.astype(jnp.float32) * scalar[...].astype(jnp.float32), axis=1, keepdims=True
    )
    scale = 1.0 / (1.0 + jnp.exp(-logit))
    across, along = (((1,), (1,)), ((), ())), (((0,), (0,)), ((), ()))
    copies[0].wait()
    gate = lax.dot_general(gate_v[...], block, across, preferred_element_type=jnp.float32)
    copies[1].wait()
    upper = lax.dot_general(up_v[...], block, across, preferred_element_type=jnp.float32)
    hidden = (silu(gate) * upper).astype(jnp.bfloat16)
    copies[2].wait()
    result = lax.dot_general(hidden, down_v[...], along, preferred_element_type=jnp.float32)
    out[...] = (scale * result).astype(jnp.bfloat16)


def shared_expert(pieces, scalar, gate_w, up_w, down_w):
    any_spec = pl.BlockSpec(memory_space=pl.ANY)
    vmem = pl.BlockSpec(memory_space=pltpu.VMEM)
    rows = sum(piece.shape[0] for piece in pieces)
    width = pieces[0].shape[1]
    return pl.pallas_call(
        functools.partial(shared_kernel, len(pieces)),
        out_shape=jax.ShapeDtypeStruct((rows, width), jnp.bfloat16),
        in_specs=[any_spec] * len(pieces) + [vmem] + [any_spec] * 3,
        out_specs=vmem,
        scratch_shapes=[
            pltpu.VMEM((rows, width), jnp.bfloat16),
            pltpu.VMEM(gate_w.shape, jnp.bfloat16),
            pltpu.VMEM(up_w.shape, jnp.bfloat16),
            pltpu.VMEM(down_w.shape, jnp.bfloat16),
            pltpu.SemaphoreType.DMA((3 + len(pieces),)),
        ],
        compiler_params=pltpu.CompilerParams(vmem_limit_bytes=56 * 1024 * 1024),
        cost_estimate=pl.CostEstimate(
            flops=6 * rows * gate_w.size,
            bytes_accessed=6 * gate_w.size + 4 * rows * width,
            transcendentals=rows * gate_w.shape[0],
        ),
    )(*pieces, scalar.reshape(1, -1), gate_w, up_w, down_w)


def routed_kernel(parts, extras, entries, cuts, *refs):
    count, total = len(parts), sum(parts)
    pieces, refs = refs[:total], refs[total:]
    place, row_gate = refs[:2]
    more, refs = refs[2 : 2 + extras], refs[2 + extras :]
    (gate_w, up_w, down_w), refs = refs[:3], refs[3:]
    outs, refs = refs[: sum(cuts)], refs[sum(cuts) :]
    rows, packed, gate_v, up_v, down_v, more_v, sems = refs
    moves, chunk_copies = [], []
    for c, n in enumerate(parts):
        at = 0
        chunk_copies.append(range(len(moves), len(moves) + n))
        for piece in pieces[sum(parts[:c]) : sum(parts[: c + 1])]:
            moves.append((piece, rows.at[c, pl.ds(at, piece.shape[0])]))
            at += piece.shape[0]
    moves += [(gate_w.at[0], gate_v), (up_w.at[0], up_v), (down_w.at[0], down_v)]
    at = 0
    for extra in more:
        moves.append((extra, more_v.at[pl.ds(at, extra.shape[0])]))
        at += extra.shape[0]
    copies = [
        pltpu.make_async_copy(src, dst, sems.at[i]) for i, (src, dst) in enumerate(moves)
    ]
    for copy in copies:
        copy.start()
    size = rows.shape[1]
    wanted = lax.broadcasted_iota(jnp.int32, (entries, size), 0)
    picks, weights = [], []
    for c in range(count):
        pick = jnp.where(place[c] == wanted, 1.0, 0.0)
        picks.append(pick.astype(jnp.bfloat16))
        weights.append(jnp.sum(pick * row_gate[c], axis=1, keepdims=True))
        for i in chunk_copies[c]:
            copies[i].wait()
        packed[c * entries : (c + 1) * entries, :] = jnp.dot(
            picks[c], rows[c], preferred_element_type=jnp.float32
        ).astype(jnp.bfloat16)
    copies[total].wait()
    gate = jnp.dot(packed[...], gate_v[...], preferred_element_type=jnp.float32)
    copies[total + 1].wait()
    upper = jnp.dot(packed[...], up_v[...], preferred_element_type=jnp.float32)
    hidden = (silu(gate) * upper).astype(jnp.bfloat16)
    copies[total + 2].wait()
    answer = jnp.dot(hidden, down_v[...], preferred_element_type=jnp.float32).astype(
        jnp.bfloat16
    )
    for i in range(extras):
        copies[total + 3 + i].wait()
    for c in range(count):
        scaled = answer[c * entries : (c + 1) * entries, :].astype(jnp.float32) * weights[c]
        placed = lax.dot_general(
            picks[c],
            scaled.astype(jnp.bfloat16),
            (((0,), (0,)), ((), ())),
            preferred_element_type=jnp.float32,
        )
        if c == 0 and extras:
            placed = placed + more_v[...].astype(jnp.float32)
        placed = placed.astype(jnp.bfloat16)
        cut = size // cuts[c]
        for k in range(cuts[c]):
            outs[sum(cuts[:c]) + k][...] = placed[k * cut : (k + 1) * cut, :]


def routed_expert(chunks, place, row_gate, more, gate_w, up_w, down_w, entries, cuts):
    count = len(chunks)
    parts = [len(chunk) for chunk in chunks]
    total = sum(parts)
    size = sum(piece.shape[0] for piece in chunks[0])
    width = chunks[0][0].shape[1]
    hidden = gate_w.shape[2]
    any_spec = pl.BlockSpec(memory_space=pl.ANY)
    vmem = pl.BlockSpec(memory_space=pltpu.VMEM)
    out_shape = [
        jax.ShapeDtypeStruct((size // n, width), jnp.bfloat16) for n in cuts for k in range(n)
    ]
    more_rows = sum(extra.shape[0] for extra in more) if more else 16
    outs = pl.pallas_call(
        functools.partial(routed_kernel, parts, len(more), entries, cuts),
        out_shape=out_shape,
        in_specs=[any_spec] * total + [vmem] * 2 + [any_spec] * (len(more) + 3),
        out_specs=[vmem] * sum(cuts),
        scratch_shapes=[
            pltpu.VMEM((count, size, width), jnp.bfloat16),
            pltpu.VMEM((count * entries, width), jnp.bfloat16),
            pltpu.VMEM((width, hidden), jnp.bfloat16),
            pltpu.VMEM((width, hidden), jnp.bfloat16),
            pltpu.VMEM((hidden, width), jnp.bfloat16),
            pltpu.VMEM((more_rows, width), jnp.bfloat16),
            pltpu.SemaphoreType.DMA((total + 3 + len(more),)),
        ],
        compiler_params=pltpu.CompilerParams(vmem_limit_bytes=56 * 1024 * 1024),
        cost_estimate=pl.CostEstimate(
            flops=2 * count * entries * (3 * gate_w.size + 2 * size * width),
            bytes_accessed=6 * gate_w.size + 4 * count * size * width,
            transcendentals=count * entries * hidden,
        ),
    )(*[piece for chunk in chunks for piece in chunk], place, row_gate, *more, gate_w, up_w, down_w)
    return [outs[sum(cuts[:c]) : sum(cuts[: c + 1])] for c in range(count)]


def rms_normed(stream, norm_gain):
    scale_row = lax.rsqrt(jnp.mean(stream * stream, axis=1, keepdims=True) + 1e-06)
    return (stream * scale_row * norm_gain[None, :]).astype(jnp.bfloat16)


def shards(
    resid,
    queries,
    cache_key,
    cache_value,
    page_table,
    row_request,
    row_position,
    out_proj,
    norm_gain,
    expert_gate,
    expert_up,
    expert_down,
    shared_gate,
    shared_up,
    shared_down,
    shared_scalar,
    slot_expert,
    route_expert,
    route_gate,
):
    f32, bf16, i32 = jnp.float32, jnp.bfloat16, jnp.int32
    exp_count = lax.axis_size("exp")
    req_count = lax.axis_size("req")
    slot_count = exp_count * req_count
    nc, nx, ny = CORES, exp_count // Z_CHIPS, req_count // CORES
    exp_index = lax.axis_index("exp")
    req_index = lax.axis_index("req")
    own_slot = req_index * exp_count + exp_index
    iz, ix = exp_index // nx, exp_index % nx
    ih, il = iz // 2, iz % 2
    iy, ic = req_index // nc, req_index % nc
    tok_rows, width = resid.shape
    pages_here, page_len, _ = cache_key.shape
    req_slots, max_pages = page_table.shape
    tokens = pages_here * page_len
    capacity = 3 * tok_rows * TOPK // slot_count

    zs = [(dh, dl) for dh in range(2) for dl in range(2)]

    def send(value, dh, dl, dx):
        if not (dh or dl or dx % nx):
            return value
        pairs = [
            (
                (h * 2 + l) * nx + x,
                ((h + dh) % 2 * 2 + (l + dl) % 2) * nx + (x + dx) % nx,
            )
            for h in range(2)
            for l in range(2)
            for x in range(nx)
        ]
        return lax.ppermute(value, "exp", pairs)

    def send_req(value, dy, dc):
        if not (dy % ny or dc % nc):
            return value
        pairs = [
            (y * nc + c, (y + dy) % ny * nc + (c + dc) % nc)
            for y in range(ny)
            for c in range(nc)
        ]
        return lax.ppermute(value, "req", pairs)

    def swap_y(value):
        pairs = [(y * nc + c, (y ^ 1) * nc + c) for y in range(ny) for c in range(nc)]
        return lax.ppermute(value, "req", pairs)

    tie = lax.optimization_barrier

    rel_exp = jnp.stack(
        [
            ((ih + dh) % 2 * 2 + (il + dl) % 2) * nx + (ix - dx) % nx
            for dh, dl in zs
            for dx in range(nx)
        ]
    ).astype(i32)
    rel_req = jnp.stack(
        [((iy - dy) % ny) * nc + (ic - dc) % nc for dy in range(ny) for dc in range(nc)]
    ).astype(i32)

    columns = width // exp_count
    keys = cache_key.reshape(tokens, width)
    values = cache_value.reshape(tokens, width)
    quarter_rows = out_proj.shape[0] // (2 * nc)
    quarter = lax.dynamic_slice_in_dim(
        out_proj, (iy % 2 * nc + ic) * quarter_rows, quarter_rows, 0
    )
    quarter_order = jnp.stack(
        [(iy + dy) % 2 * nc + (ic + dc) % nc for dc in range(nc) for dy in range(2)]
    ).astype(i32)
    far_queries = send(queries, 1, 0, 0)
    members = [(dl, dx) for dl in range(2) for dx in range(nx)]
    member_columns = jnp.stack(
        [
            ((ih + j) % 2 * 2 + (il + dl) % 2) * nx + (ix + dx) % nx
            for dl, dx in members
            for j in range(2)
        ]
    ).astype(i32)
    gates = jnp.pad(jnp.transpose(route_gate), ((0, 0), (0, 2 * columns - tok_rows)))
    blocks = pack([keys, values, queries], gates, member_columns, columns)
    blocks = [send(blocks[m], 0, *members[m]) for m in range(len(members))]
    far = list(pack([far_queries], None, member_columns, columns))
    for m in range(1, len(members)):
        if m > 2:
            far[m], far[m - 2] = tie((far[m], far[m - 2]))
        far[m] = send(far[m], 0, *members[m])
    quarter, far[1] = tie((quarter, far[1]))
    quarters = [send(quarter, 1, 0, 0)]
    page_ids = (
        rel_exp[: len(members), None] * pages_here + jnp.arange(pages_here, dtype=i32)[None, :]
    ).reshape(-1)
    hits = (page_table[None, :, :] == page_ids[:, None, None]).astype(i32)
    page_request = jnp.sum(hits * jnp.arange(req_slots, dtype=i32)[None, :, None], axis=(1, 2))
    page_slot = jnp.sum(hits * jnp.arange(max_pages, dtype=i32)[None, None, :], axis=(1, 2))
    by_place = lambda a: a.reshape(exp_count, tok_rows)[rel_exp].reshape(2, 1, -1)
    row_req, row_pos = by_place(row_request), by_place(row_position)
    gates = [block[2 * tokens + tok_rows :, :tok_rows].astype(f32) for block in blocks]
    gates = jnp.stack([g[:TOPK] + g[TOPK : 2 * TOPK] + g[2 * TOPK : 3 * TOPK] for g in gates])
    gates = gates.reshape(2, nx, TOPK, tok_rows)

    slot_ids = jnp.arange(slot_count, dtype=i32)
    own_mark = slot_ids == own_slot
    own_expert = jnp.sum(jnp.where(own_mark, slot_expert, 0))
    twins = slot_expert == own_expert
    copies = jnp.sum(twins.astype(i32))
    own_rank = jnp.sum((twins & (slot_ids < own_slot)).astype(i32))
    order = [1, 3, 2, 0]
    rel_rows = jnp.stack([rel_exp.reshape(4, nx)[i] for i in order], axis=1).reshape(-1)
    rel_slots = (rel_req[:, None] * exp_count + rel_rows[None, :]).reshape(-1)
    named = (route_expert == own_expert).reshape(slot_count, tok_rows, TOPK)[rel_slots]
    named = jnp.transpose(named, (0, 2, 1))
    chunk_rows = exp_count * tok_rows
    entries = -(-exp_count * capacity // 16) * 16
    served = jnp.any(named, axis=1) & (rel_slots % copies == own_rank)[:, None]
    served = served.reshape(ny, nc, chunk_rows)
    place = jnp.where(served, jnp.cumsum(served.astype(i32), axis=2) - 1, -1)
    place = place.reshape(ny, nc, 1, chunk_rows)

    place, named, blocks = tie((place, named, blocks))

    def attend_half(side, queries):
        return attend(
            blocks,
            queries,
            row_req[side],
            row_pos[side],
            page_request,
            page_slot,
            page_len,
            tokens,
            tok_rows,
        )

    theirs, their_level = attend_half(1, far)
    theirs, their_level, quarters = tie((theirs, their_level, quarters))
    theirs, their_level = send(theirs, 1, 0, 0), send(their_level, 1, 0, 0)
    quarters.append(swap_y(quarters[0]))
    gates = jnp.stack([send(gates, dh, 0, 0) for dh in range(2)])
    mine, level = attend_half(0, [])
    mine, level, gates, quarters = tie((mine, level, gates, quarters))
    quarters += [send_req(q, 0, dc) for dc in range(1, nc) for q in quarters[:2]]
    gates = jnp.stack([send_req(gates, dy, 0) for dy in range(ny)])
    theirs, their_level, gates, quarters = tie((theirs, their_level, gates, quarters))

    stays, comes = {}, {}
    proj = out_proj
    for dl in (1, 0):
        stays[dl], go = project(
            dl, quarter_order, mine, level, theirs, their_level, proj, quarters, tok_rows
        )
        comes[dl] = [
            send(go[(dx - 1) * tok_rows : dx * tok_rows], 0, 0, -dx) for dx in range(1, nx)
        ]
        proj, _ = tie((proj, go))
    line = sum([come.astype(f32) for come in comes[1]], stays[1]).astype(bf16)
    comes[0], _ = tie((comes[0], line))
    line = send(line, 0, 1, 0)
    stream = sum([come.astype(f32) for come in comes[0]], resid.astype(f32) + stays[0])
    stream = stream + line.astype(f32)
    normed = rms_normed(stream, norm_gain)
    gates = jnp.stack([send_req(gates, 0, dc) for dc in range(nc)], axis=1)
    gates = gates.reshape(ny, nc, 4, nx, TOPK, tok_rows)
    gates = jnp.stack([gates[:, :, i] for i in order], axis=3)
    gates = gates.reshape(slot_count, TOPK, tok_rows)
    row_gate = jnp.sum(jnp.where(named, gates, 0.0), axis=1).reshape(ny, nc, 1, chunk_rows)

    far_line = send(normed, 1, 0, 0)
    line = [normed, send(normed, 0, 1, 0), far_line, send(far_line, 0, 1, 0)]
    over_x = {(i, dx): send(line[i], 0, 0, dx) for i in order for dx in range(1, nx)}
    over_y = {(i, dy): send_req(line[i], dy, 0) for i in order for dy in range(1, ny)}

    halves = [[line[i] for i in order]]
    shared_weights = (shared_scalar, shared_gate.T, shared_up.T, shared_down)
    shared = [shared_expert(halves[0], *shared_weights)]
    chunks = {(0, 0): [join(halves[0])]}
    for dc in range(1, nc):
        chunks[0, dc] = [send_req(chunks[0, 0][0], 0, dc)]
    over_x, over_y, shared, row_gate = tie((over_x, over_y, shared, row_gate))
    for dy in range(1, ny):
        half = join([over_y[i, dy] for i in order])
        chunks[dy, 0] = [half] + [send(half, 0, 0, dx) for dx in range(1, nx)]
        for dc in range(1, nc):
            chunks[dy, dc] = [send_req(half, 0, dc)]
        over_x, _ = tie((over_x, half))
    for dx in range(1, nx):
        half = [over_x[i, dx] for i in order]
        chunks[0, 0].append(join(half))
        for dc in range(1, nc):
            chunks[0, dc].append(send_req(chunks[0, 0][dx], 0, dc))
        halves.append(half)

    def answers_of(dy, dcs, more, cuts):
        return routed_expert(
            [chunks[dy, dc] for dc in dcs],
            jnp.concatenate([place[dy, dc : dc + 1] for dc in dcs]),
            jnp.concatenate([row_gate[dy, dc : dc + 1] for dc in dcs]),
            more,
            expert_gate,
            expert_up,
            expert_down,
            entries,
            cuts,
        )

    def add_up(parts):
        return sum([part.astype(f32) for part in parts[1:]], parts[0].astype(f32))

    cores = list(range(nc))
    kept, comes = {}, {}
    cuts = [slice(0, 3 * tok_rows), slice(3 * tok_rows, 4 * tok_rows)]
    for dy in range(ny - 1):
        answers = answers_of(dy, cores, [], [nx] * nc)
        if dy:
            answers, comes[dy - 1] = tie((answers, comes[dy - 1]))
        others = [[send_req(part, 0, -dc) for part in answers[dc][::-1]][::-1] for dc in cores[1:]]
        parts = [answers[0]] + others
        if dy:
            following = answers[0][0]
        else:
            for dx in range(1, nx):
                halves[dx], _ = tie((halves[dx], answers[0]))
                shared.append(shared_expert(halves[dx], *shared_weights))
            parts.append(shared)
            following = shared[-1]
        chunks[dy + 1, 0], _ = tie((chunks[dy + 1, 0], following))
        for dc in range(1, nc):
            chunks[dy + 1, dc] += [send_req(part, 0, dc) for part in chunks[dy + 1, 0][1:]]
        gone = [add_up([part[dx] for part in parts]).astype(bf16) for dx in range(1, nx)]
        kept[dy] = [part[0] for part in parts]
        comes[dy] = [
            [send(go[rows], 0, 0, -dx) for dx, go in enumerate(gone, 1)] for rows in cuts
        ]
        following = [chunks[dy + 1, dc] for dc in cores]
        following, _ = tie((following, gone))
        for dc in cores:
            chunks[dy + 1, dc] = following[dc]
    end = ny - 1
    answers = answers_of(end, cores, [], [4 * nx] + [nx] * (nc - 1))
    answers, comes[end - 1][0] = tie((answers, comes[end - 1][0]))
    answer = answers[0]
    others = [[send_req(part, 0, -dc) for part in answers[dc][::-1]][::-1] for dc in cores[1:]]

    turns = [1, 2, 0, 3]
    block = lambda a, p: a[p * tok_rows : (p + 1) * tok_rows]
    last = {}
    for p in turns:
        gone = [
            add_up([answer[4 * dx + p]] + [block(other[dx], p) for other in others])
            for dx in range(1, nx)
        ]
        gone = [go.astype(bf16) for go in gone]
        last[p] = [send(go, 0, 0, -dx) for dx, go in enumerate(gone, 1)]
        others, _ = tie((others, gone))

    def line_of(dy, p):
        if dy < end:
            arrived = [come if p == 3 else block(come, p) for come in comes[dy][p // 3]]
            return add_up([block(part, p) for part in kept[dy]] + arrived)
        return add_up([answer[p]] + [block(other[0], p) for other in others] + last[p])

    home, near = {}, {}
    for turn, p in enumerate(turns):
        goes = [line_of(dy, p).astype(bf16) for dy in range(1, ny)]
        home[p] = [send_req(go, -dy, 0) for dy, go in enumerate(goes, 1)]
        if turn == 1:
            go = add_up([line_of(0, 1)] + home[1]).astype(bf16)
            near[1] = send(go, 0, 1, 0)
            goes.append(go)
        if turn + 1 < len(turns):
            after = turns[turn + 1]
            last[after], _ = tie((last[after], goes))
    far = add_up([line_of(0, 2)] + home[2] + [near[1]]).astype(bf16)
    home[0], _ = tie((home[0], far))
    far = send(far, 1, 0, 0)
    near[0] = send(add_up([line_of(0, 0)] + home[0]).astype(bf16), 0, 1, 0)
    total = add_up([stream, line_of(0, 3)] + home[3] + [near[0], far])
    return total.astype(bf16)


def solution(mesh):
    placed = (
        P(("req", "exp"), None),
        P(("req", "exp"), None),
        P(("req", "exp"), None, None),
        P(("req", "exp"), None, None),
        P("req", None),
        P("req"),
        P("req"),
        P("exp", None),
        P(),
        P(("req", "exp"), None, None),
        P(("req", "exp"), None, None),
        P(("req", "exp"), None, None),
        P(None, "exp"),
        P(None, "exp"),
        P("exp", None),
        P(),
        P(),
        P(),
        P(("req", "exp"), None),
    )
    return jax.shard_map(
        shards, mesh=mesh, in_specs=placed, out_specs=P(("req", "exp"), None), check_vma=False
    )
```

```python
import functools

import jax
import jax.numpy as jnp
from jax import lax
from jax.experimental import pallas as pl
from jax.experimental.pallas import tpu as pltpu
from jax.sharding import PartitionSpec as P

HEAD_DIM = 128
TOPK = 4
CORES = 2
Z_CHIPS = 4


def pack_kernel(members, parts, columns, order, *refs):
    sources, refs = refs[:parts], refs[parts:]
    gates, blocks, sems = refs[:-1 - members], refs[-1 - members : -1], refs[-1]
    copies = []
    for m in range(members):
        at = 0
        for source in sources:
            rows = source.shape[0]
            for j in range(2):
                place = pl.multiple_of(order[2 * m + j] * columns, columns)
                copies.append(
                    pltpu.make_async_copy(
                        source.at[:, pl.ds(place, columns)],
                        blocks[m].at[pl.ds(at, rows), pl.ds(j * columns, columns)],
                        sems.at[len(copies)],
                    )
                )
            at += rows
    for copy in copies:
        copy.start()
    if gates:
        weights = gates[0][...]
        high = weights.astype(jnp.bfloat16).astype(jnp.float32)
        middle = (weights - high).astype(jnp.bfloat16).astype(jnp.float32)
        low = weights - high - middle
        weights = jnp.concatenate([high, middle, low, jnp.zeros_like(low)], axis=0)
        for m in range(members):
            blocks[m][at:, :] = weights.astype(jnp.bfloat16)
    for copy in copies:
        copy.wait()


def pack(parts, gates, order, columns):
    members = order.shape[0] // 2
    rows = sum(p.shape[0] for p in parts) + (0 if gates is None else 4 * gates.shape[0])
    vmem = pl.BlockSpec(memory_space=pltpu.VMEM)
    in_specs = [pl.BlockSpec(memory_space=pltpu.SMEM)]
    in_specs += [pl.BlockSpec(memory_space=pl.ANY)] * len(parts)
    operands = list(parts)
    if gates is not None:
        in_specs.append(vmem)
        operands.append(gates)
    return pl.pallas_call(
        functools.partial(pack_kernel, members, len(parts), columns),
        out_shape=[jax.ShapeDtypeStruct((rows, 2 * columns), parts[0].dtype)] * members,
        in_specs=in_specs,
        out_specs=[vmem] * members,
        scratch_shapes=[pltpu.SemaphoreType.DMA((2 * members * len(parts),))],
        compiler_params=pltpu.CompilerParams(vmem_limit_bytes=56 * 1024 * 1024),
        cost_estimate=pl.CostEstimate(
            flops=0, bytes_accessed=8 * members * rows * columns, transcendentals=0
        ),
    )(order, *operands)


def attend_kernel(members, tokens, tok_rows, page_len, scale, page_req, page_slot, *refs):
    blocks, refs = refs[:members], refs[members:]
    if len(refs) > 4:
        query, refs = [q[...] for q in refs[:members]], refs[members:]
    else:
        query = [block[2 * tokens : 2 * tokens + tok_rows, :] for block in blocks]
    request, position, out, level = refs
    request, position = request[...], position[...]
    keys = jnp.concatenate([block[:tokens, :] for block in blocks], axis=0)
    values = jnp.concatenate([block[tokens : 2 * tokens, :] for block in blocks], axis=0)
    query = jnp.concatenate(query, axis=0)
    scores = (
        lax.dot_general(keys, query, (((1,), (1,)), ((), ())), preferred_element_type=jnp.float32)
        * scale
    )
    token = lax.broadcasted_iota(jnp.int32, (page_len, query.shape[0]), 0)
    visible = jnp.concatenate(
        [
            (request == page_req[page]) & (token + page_slot[page] * page_len <= position)
            for page in range(members * tokens // page_len)
        ],
        axis=0,
    )
    scores = jnp.where(visible, scores, -1e30)
    top = jnp.max(scores, axis=0, keepdims=True)
    weights = jnp.where(visible, jnp.exp(scores - top), 0.0)
    total = jnp.sum(weights, axis=0, keepdims=True)
    summed = lax.dot_general(
        values,
        weights.astype(jnp.bfloat16),
        (((0,), (0,)), ((), ())),
        preferred_element_type=jnp.float32,
    )
    seen = total > 0.0
    total = jnp.where(seen, total, 1.0)
    out[...] = (summed / total).astype(jnp.bfloat16)
    level[0] = jnp.where(seen, top + jnp.log(total), -1e30)


def attend(blocks, far, row_req, row_pos, page_req, page_slot, page_len, tokens, tok_rows):
    members, rows = len(blocks), row_req.shape[1]
    block_rows, columns = blocks[0].shape
    heads = columns // HEAD_DIM
    by_head = lambda n: pl.BlockSpec((n, HEAD_DIM), lambda h, *_: (0, h))
    whole = pl.BlockSpec((1, rows), lambda h, *_: (0, 0))
    return pl.pallas_call(
        functools.partial(
            attend_kernel, members, tokens, tok_rows, page_len, HEAD_DIM ** (-0.5)
        ),
        out_shape=[
            jax.ShapeDtypeStruct((columns, rows), jnp.bfloat16),
            jax.ShapeDtypeStruct((heads, 1, rows), jnp.float32),
        ],
        grid_spec=pltpu.PrefetchScalarGridSpec(
            num_scalar_prefetch=2,
            grid=(heads,),
            in_specs=[by_head(block_rows)] * members + [by_head(tok_rows)] * len(far) + [whole] * 2,
            out_specs=[
                pl.BlockSpec((HEAD_DIM, rows), lambda h, *_: (h, 0)),
                pl.BlockSpec((1, 1, rows), lambda h, *_: (h, 0, 0)),
            ],
        ),
        compiler_params=pltpu.CompilerParams(vmem_limit_bytes=48 * 1024 * 1024),
        cost_estimate=pl.CostEstimate(
            flops=4 * rows * members * tokens * columns,
            bytes_accessed=2 * members * (block_rows + tok_rows) * columns,
            transcendentals=rows * members * tokens * heads,
        ),
    )(page_req, page_slot, *blocks, *far, row_req, row_pos)


def project_kernel(order, mine, mine_level, theirs, their_level, own, *refs):
    quarters, (stay, go, proj) = refs[:-3], refs[-3:]
    rows, size = own.shape[0], quarters[0].shape[0]
    proj[:rows, :] = own[...]
    for k, quarter in enumerate(quarters):
        at = pl.multiple_of(rows + order[k] * size, size)
        proj[pl.ds(at, size), :] = quarter[...]
    parts = []
    heads = mine.shape[0] // HEAD_DIM
    for head in range(heads):
        twin = (head + heads // 2) % heads
        dims = slice(head * HEAD_DIM, (head + 1) * HEAD_DIM)
        twin_dims = slice(twin * HEAD_DIM, (twin + 1) * HEAD_DIM)
        share = 1.0 / (1.0 + jnp.exp(their_level[twin] - mine_level[head]))
        other = 1.0 / (1.0 + jnp.exp(mine_level[head] - their_level[twin]))
        both = share * mine[dims, :].astype(jnp.float32) + other * theirs[
            twin_dims, :
        ].astype(jnp.float32)
        parts.append(both.astype(jnp.bfloat16))
    attention = jnp.concatenate(parts, axis=0)
    mixed = lax.dot_general(
        attention, proj[...], (((0,), (0,)), ((), ())), preferred_element_type=jnp.float32
    )
    kept = stay.shape[0]
    stay[...] = mixed[:kept, :]
    go[...] = mixed[kept:, :].astype(jnp.bfloat16)


def project(place, order, mine, mine_level, theirs, their_level, own, quarters, tok_rows):
    dims, width = mine.shape[0], own.shape[1]
    heads = dims // HEAD_DIM
    size = mine.shape[1] // 2
    whole = lambda a: pl.BlockSpec(a.shape, lambda i, order: (0, 0))
    values = pl.BlockSpec((dims, size), lambda i, order: (0, place))
    levels = pl.BlockSpec((heads, 1, size), lambda i, order: (0, 0, place))
    return pl.pallas_call(
        project_kernel,
        out_shape=[
            jax.ShapeDtypeStruct((tok_rows, width), jnp.float32),
            jax.ShapeDtypeStruct((size - tok_rows, width), jnp.bfloat16),
        ],
        grid_spec=pltpu.PrefetchScalarGridSpec(
            num_scalar_prefetch=1,
            grid=(1,),
            in_specs=[values, levels, values, levels, whole(own)] + [whole(q) for q in quarters],
            out_specs=[
                pl.BlockSpec((tok_rows, width), lambda i, order: (0, 0)),
                pl.BlockSpec((size - tok_rows, width), lambda i, order: (0, 0)),
            ],
            scratch_shapes=[pltpu.VMEM((dims, width), jnp.bfloat16)],
        ),
        compiler_params=pltpu.CompilerParams(vmem_limit_bytes=32 * 1024 * 1024),
        cost_estimate=pl.CostEstimate(
            flops=2 * size * dims * width,
            bytes_accessed=2 * (2 * dims * size + dims * width + 3 * size * width),
            transcendentals=2 * size * heads,
        ),
    )(order, mine, mine_level, theirs, their_level, own, *quarters)


def join_kernel(*refs):
    parts, out = refs[:-1], refs[-1]
    rows = parts[0].shape[0]
    for i, part in enumerate(parts):
        out[i * rows : (i + 1) * rows, :] = part[...]


def join(parts):
    rows, width = parts[0].shape
    vmem = pl.BlockSpec(memory_space=pltpu.VMEM)
    return pl.pallas_call(
        join_kernel,
        out_shape=jax.ShapeDtypeStruct((len(parts) * rows, width), parts[0].dtype),
        in_specs=[vmem] * len(parts),
        out_specs=vmem,
        cost_estimate=pl.CostEstimate(
            flops=0, bytes_accessed=4 * len(parts) * rows * width, transcendentals=0
        ),
    )(*parts)


def silu(value):
    return value / (1.0 + jnp.exp(-value))


def shared_kernel(count, *refs):
    pieces, (scalar, gate_w, up_w, down_w, out, rows, gate_v, up_v, down_v, sems) = (
        refs[:count],
        refs[count:],
    )
    moves = [(gate_w, gate_v), (up_w, up_v), (down_w, down_v)]
    size = pieces[0].shape[0]
    moves += [(piece, rows.at[pl.ds(i * size, size)]) for i, piece in enumerate(pieces)]
    copies = [
        pltpu.make_async_copy(src, dst, sems.at[i]) for i, (src, dst) in enumerate(moves)
    ]
    for copy in copies[3:] + copies[:3]:
        copy.start()
    for copy in copies[3:]:
        copy.wait()
    block = rows[...]
    logit = jnp.sum(
        block.astype(jnp.float32) * scalar[...].astype(jnp.float32), axis=1, keepdims=True
    )
    scale = 1.0 / (1.0 + jnp.exp(-logit))
    across = (((1,), (1,)), ((), ()))
    copies[0].wait()
    gate = lax.dot_general(block, gate_v[...], across, preferred_element_type=jnp.float32)
    copies[1].wait()
    upper = lax.dot_general(block, up_v[...], across, preferred_element_type=jnp.float32)
    hidden = (silu(gate) * upper).astype(jnp.bfloat16)
    copies[2].wait()
    result = jnp.dot(hidden, down_v[...], preferred_element_type=jnp.float32)
    out[...] = (scale * result).astype(jnp.bfloat16)


def shared_expert(pieces, scalar, gate_w, up_w, down_w):
    any_spec = pl.BlockSpec(memory_space=pl.ANY)
    vmem = pl.BlockSpec(memory_space=pltpu.VMEM)
    rows = sum(piece.shape[0] for piece in pieces)
    width = pieces[0].shape[1]
    return pl.pallas_call(
        functools.partial(shared_kernel, len(pieces)),
        out_shape=jax.ShapeDtypeStruct((rows, width), jnp.bfloat16),
        in_specs=[any_spec] * len(pieces) + [vmem] + [any_spec] * 3,
        out_specs=vmem,
        scratch_shapes=[
            pltpu.VMEM((rows, width), jnp.bfloat16),
            pltpu.VMEM(gate_w.shape, jnp.bfloat16),
            pltpu.VMEM(up_w.shape, jnp.bfloat16),
            pltpu.VMEM(down_w.shape, jnp.bfloat16),
            pltpu.SemaphoreType.DMA((3 + len(pieces),)),
        ],
        compiler_params=pltpu.CompilerParams(vmem_limit_bytes=56 * 1024 * 1024),
        cost_estimate=pl.CostEstimate(
            flops=6 * rows * gate_w.size,
            bytes_accessed=6 * gate_w.size + 4 * rows * width,
            transcendentals=rows * gate_w.shape[0],
        ),
    )(*pieces, scalar.reshape(1, -1), gate_w, up_w, down_w)


def routed_kernel(parts, extras, entries, cuts, *refs):
    count, total = len(parts), sum(parts)
    pieces, refs = refs[:total], refs[total:]
    place, row_gate = refs[:2]
    more, refs = refs[2 : 2 + extras], refs[2 + extras :]
    (gate_w, up_w, down_w), refs = refs[:3], refs[3:]
    outs, refs = refs[: sum(cuts)], refs[sum(cuts) :]
    rows, packed, gate_v, up_v, down_v, more_v, sems = refs
    moves, chunk_copies = [], []
    for c, n in enumerate(parts):
        at = 0
        chunk_copies.append(range(len(moves), len(moves) + n))
        for piece in pieces[sum(parts[:c]) : sum(parts[: c + 1])]:
            moves.append((piece, rows.at[c, pl.ds(at, piece.shape[0])]))
            at += piece.shape[0]
    moves += [(gate_w.at[0], gate_v), (up_w.at[0], up_v), (down_w.at[0], down_v)]
    at = 0
    for extra in more:
        moves.append((extra, more_v.at[pl.ds(at, extra.shape[0])]))
        at += extra.shape[0]
    copies = [
        pltpu.make_async_copy(src, dst, sems.at[i]) for i, (src, dst) in enumerate(moves)
    ]
    for copy in copies:
        copy.start()
    size = rows.shape[1]
    wanted = lax.broadcasted_iota(jnp.int32, (entries, size), 0)
    picks, weights = [], []
    for c in range(count):
        pick = jnp.where(place[c] == wanted, 1.0, 0.0)
        picks.append(pick.astype(jnp.bfloat16))
        weights.append(jnp.sum(pick * row_gate[c], axis=1, keepdims=True))
        for i in chunk_copies[c]:
            copies[i].wait()
        packed[c * entries : (c + 1) * entries, :] = jnp.dot(
            picks[c], rows[c], preferred_element_type=jnp.float32
        ).astype(jnp.bfloat16)
    copies[total].wait()
    gate = jnp.dot(packed[...], gate_v[...], preferred_element_type=jnp.float32)
    copies[total + 1].wait()
    upper = jnp.dot(packed[...], up_v[...], preferred_element_type=jnp.float32)
    hidden = (silu(gate) * upper).astype(jnp.bfloat16)
    copies[total + 2].wait()
    answer = jnp.dot(hidden, down_v[...], preferred_element_type=jnp.float32).astype(
        jnp.bfloat16
    )
    for i in range(extras):
        copies[total + 3 + i].wait()
    for c in range(count):
        scaled = answer[c * entries : (c + 1) * entries, :].astype(jnp.float32) * weights[c]
        placed = lax.dot_general(
            picks[c],
            scaled.astype(jnp.bfloat16),
            (((0,), (0,)), ((), ())),
            preferred_element_type=jnp.float32,
        )
        if c == 0 and extras:
            placed = placed + more_v[...].astype(jnp.float32)
        placed = placed.astype(jnp.bfloat16)
        cut = size // cuts[c]
        for k in range(cuts[c]):
            outs[sum(cuts[:c]) + k][...] = placed[k * cut : (k + 1) * cut, :]


def routed_expert(chunks, place, row_gate, more, gate_w, up_w, down_w, entries, cuts):
    count = len(chunks)
    parts = [len(chunk) for chunk in chunks]
    total = sum(parts)
    size = sum(piece.shape[0] for piece in chunks[0])
    width = chunks[0][0].shape[1]
    hidden = gate_w.shape[2]
    any_spec = pl.BlockSpec(memory_space=pl.ANY)
    vmem = pl.BlockSpec(memory_space=pltpu.VMEM)
    out_shape = [
        jax.ShapeDtypeStruct((size // n, width), jnp.bfloat16) for n in cuts for k in range(n)
    ]
    more_rows = sum(extra.shape[0] for extra in more) if more else 16
    outs = pl.pallas_call(
        functools.partial(routed_kernel, parts, len(more), entries, cuts),
        out_shape=out_shape,
        in_specs=[any_spec] * total + [vmem] * 2 + [any_spec] * (len(more) + 3),
        out_specs=[vmem] * sum(cuts),
        scratch_shapes=[
            pltpu.VMEM((count, size, width), jnp.bfloat16),
            pltpu.VMEM((count * entries, width), jnp.bfloat16),
            pltpu.VMEM((width, hidden), jnp.bfloat16),
            pltpu.VMEM((width, hidden), jnp.bfloat16),
            pltpu.VMEM((hidden, width), jnp.bfloat16),
            pltpu.VMEM((more_rows, width), jnp.bfloat16),
            pltpu.SemaphoreType.DMA((total + 3 + len(more),)),
        ],
        compiler_params=pltpu.CompilerParams(vmem_limit_bytes=56 * 1024 * 1024),
        cost_estimate=pl.CostEstimate(
            flops=2 * count * entries * (3 * gate_w.size + 2 * size * width),
            bytes_accessed=6 * gate_w.size + 4 * count * size * width,
            transcendentals=count * entries * hidden,
        ),
    )(*[piece for chunk in chunks for piece in chunk], place, row_gate, *more, gate_w, up_w, down_w)
    return [outs[sum(cuts[:c]) : sum(cuts[: c + 1])] for c in range(count)]


def rms_normed(stream, norm_gain):
    scale_row = lax.rsqrt(jnp.mean(stream * stream, axis=1, keepdims=True) + 1e-06)
    return (stream * scale_row * norm_gain[None, :]).astype(jnp.bfloat16)


def shards(
    resid,
    queries,
    cache_key,
    cache_value,
    page_table,
    row_request,
    row_position,
    out_proj,
    norm_gain,
    expert_gate,
    expert_up,
    expert_down,
    shared_gate,
    shared_up,
    shared_down,
    shared_scalar,
    slot_expert,
    route_expert,
    route_gate,
):
    f32, bf16, i32 = jnp.float32, jnp.bfloat16, jnp.int32
    exp_count = lax.axis_size("exp")
    req_count = lax.axis_size("req")
    slot_count = exp_count * req_count
    nc, nx, ny = CORES, exp_count // Z_CHIPS, req_count // CORES
    exp_index = lax.axis_index("exp")
    req_index = lax.axis_index("req")
    own_slot = req_index * exp_count + exp_index
    iz, ix = exp_index // nx, exp_index % nx
    ih, il = iz // 2, iz % 2
    iy, ic = req_index // nc, req_index % nc
    tok_rows, width = resid.shape
    pages_here, page_len, _ = cache_key.shape
    req_slots, max_pages = page_table.shape
    tokens = pages_here * page_len
    capacity = 3 * tok_rows * TOPK // slot_count

    zs = [(dh, dl) for dh in range(2) for dl in range(2)]

    def send(value, dh, dl, dx):
        if not (dh or dl or dx % nx):
            return value
        pairs = [
            (
                (h * 2 + l) * nx + x,
                ((h + dh) % 2 * 2 + (l + dl) % 2) * nx + (x + dx) % nx,
            )
            for h in range(2)
            for l in range(2)
            for x in range(nx)
        ]
        return lax.ppermute(value, "exp", pairs)

    def send_req(value, dy, dc):
        if not (dy % ny or dc % nc):
            return value
        pairs = [
            (y * nc + c, (y + dy) % ny * nc + (c + dc) % nc)
            for y in range(ny)
            for c in range(nc)
        ]
        return lax.ppermute(value, "req", pairs)

    def swap_y(value):
        pairs = [(y * nc + c, (y ^ 1) * nc + c) for y in range(ny) for c in range(nc)]
        return lax.ppermute(value, "req", pairs)

    tie = lax.optimization_barrier

    rel_exp = jnp.stack(
        [
            ((ih + dh) % 2 * 2 + (il + dl) % 2) * nx + (ix - dx) % nx
            for dh, dl in zs
            for dx in range(nx)
        ]
    ).astype(i32)
    rel_req = jnp.stack(
        [((iy - dy) % ny) * nc + (ic - dc) % nc for dy in range(ny) for dc in range(nc)]
    ).astype(i32)

    columns = width // exp_count
    keys = cache_key.reshape(tokens, width)
    values = cache_value.reshape(tokens, width)
    quarter_rows = out_proj.shape[0] // (2 * nc)
    quarter = lax.dynamic_slice_in_dim(
        out_proj, (iy % 2 * nc + ic) * quarter_rows, quarter_rows, 0
    )
    quarter_order = jnp.stack(
        [(iy + dy) % 2 * nc + (ic + dc) % nc for dc in range(nc) for dy in range(2)]
    ).astype(i32)
    far_queries = send(queries, 1, 0, 0)
    members = [(dl, dx) for dl in range(2) for dx in range(nx)]
    member_columns = jnp.stack(
        [
            ((ih + j) % 2 * 2 + (il + dl) % 2) * nx + (ix + dx) % nx
            for dl, dx in members
            for j in range(2)
        ]
    ).astype(i32)
    gates = jnp.pad(jnp.transpose(route_gate), ((0, 0), (0, 2 * columns - tok_rows)))
    blocks = pack([keys, values, queries], gates, member_columns, columns)
    blocks = [send(blocks[m], 0, *members[m]) for m in range(len(members))]
    far = list(pack([far_queries], None, member_columns, columns))
    for m in range(1, len(members)):
        if m > 2:
            far[m], far[m - 2] = tie((far[m], far[m - 2]))
        far[m] = send(far[m], 0, *members[m])
    quarters = [send(quarter, 1, 0, 0)]
    page_ids = (
        rel_exp[: len(members), None] * pages_here + jnp.arange(pages_here, dtype=i32)[None, :]
    ).reshape(-1)
    hits = (page_table[None, :, :] == page_ids[:, None, None]).astype(i32)
    page_request = jnp.sum(hits * jnp.arange(req_slots, dtype=i32)[None, :, None], axis=(1, 2))
    page_slot = jnp.sum(hits * jnp.arange(max_pages, dtype=i32)[None, None, :], axis=(1, 2))
    by_place = lambda a: a.reshape(exp_count, tok_rows)[rel_exp].reshape(2, 1, -1)
    row_req, row_pos = by_place(row_request), by_place(row_position)
    gates = [block[2 * tokens + tok_rows :, :tok_rows].astype(f32) for block in blocks]
    gates = jnp.stack([g[:TOPK] + g[TOPK : 2 * TOPK] + g[2 * TOPK : 3 * TOPK] for g in gates])
    gates = gates.reshape(2, nx, TOPK, tok_rows)

    slot_ids = jnp.arange(slot_count, dtype=i32)
    own_mark = slot_ids == own_slot
    own_expert = jnp.sum(jnp.where(own_mark, slot_expert, 0))
    twins = slot_expert == own_expert
    copies = jnp.sum(twins.astype(i32))
    own_rank = jnp.sum((twins & (slot_ids < own_slot)).astype(i32))
    order = [1, 3, 2, 0]
    rel_rows = jnp.stack([rel_exp.reshape(4, nx)[i] for i in order], axis=1).reshape(-1)
    rel_slots = (rel_req[:, None] * exp_count + rel_rows[None, :]).reshape(-1)
    named = (route_expert == own_expert).reshape(slot_count, tok_rows, TOPK)[rel_slots]
    named = jnp.transpose(named, (0, 2, 1))
    chunk_rows = exp_count * tok_rows
    entries = -(-exp_count * capacity // 16) * 16
    served = jnp.any(named, axis=1) & (rel_slots % copies == own_rank)[:, None]
    served = served.reshape(ny, nc, chunk_rows)
    place = jnp.where(served, jnp.cumsum(served.astype(i32), axis=2) - 1, -1)
    place = place.reshape(ny, nc, 1, chunk_rows)

    place, named, blocks = tie((place, named, blocks))

    def attend_half(side, queries):
        return attend(
            blocks,
            queries,
            row_req[side],
            row_pos[side],
            page_request,
            page_slot,
            page_len,
            tokens,
            tok_rows,
        )

    quarters.append(swap_y(quarters[0]))
    theirs, their_level = attend_half(1, far)
    theirs, their_level, quarters = tie((theirs, their_level, quarters))
    theirs, their_level = send(theirs, 1, 0, 0), send(their_level, 1, 0, 0)
    quarters += [send_req(q, 0, dc) for dc in range(1, nc) for q in quarters[:2]]
    mine, level = attend_half(0, [])
    mine, level, gates, quarters = tie((mine, level, gates, quarters))
    gates = jnp.stack([send(gates, dh, 0, 0) for dh in range(2)])
    theirs, their_level, gates = tie((theirs, their_level, gates))

    stays, comes = {}, {}
    proj = out_proj
    for dl in (1, 0):
        stays[dl], go = project(
            dl, quarter_order, mine, level, theirs, their_level, proj, quarters, tok_rows
        )
        comes[dl] = [
            send(go[(dx - 1) * tok_rows : dx * tok_rows], 0, 0, -dx) for dx in range(1, nx)
        ]
        proj, _ = tie((proj, go))
    line = sum([come.astype(f32) for come in comes[1]], stays[1]).astype(bf16)
    comes[0], _ = tie((comes[0], line))
    line = send(line, 0, 1, 0)
    stream = sum([come.astype(f32) for come in comes[0]], resid.astype(f32) + stays[0])
    stream = stream + line.astype(f32)
    gates = jnp.stack([send_req(gates, dy, 0) for dy in range(ny)])
    stream, gates = tie((stream, gates))
    normed = rms_normed(stream, norm_gain)
    gates = jnp.stack([send_req(gates, 0, dc) for dc in range(nc)], axis=1)
    gates = gates.reshape(ny, nc, 4, nx, TOPK, tok_rows)
    gates = jnp.stack([gates[:, :, i] for i in order], axis=3)
    gates = gates.reshape(slot_count, TOPK, tok_rows)
    row_gate = jnp.sum(jnp.where(named, gates, 0.0), axis=1).reshape(ny, nc, 1, chunk_rows)

    far_line = send(normed, 1, 0, 0)
    line = [normed, send(normed, 0, 1, 0), far_line, send(far_line, 0, 1, 0)]
    over_x = {(i, dx): send(line[i], 0, 0, dx) for i in order for dx in range(1, nx)}
    over_y = {(i, dy): send_req(line[i], dy, 0) for i in order for dy in range(1, ny)}

    halves = [[line[i] for i in order]]
    shared_weights = (shared_scalar, shared_gate.T, shared_up.T, shared_down)
    shared = [shared_expert(halves[0], *shared_weights)]
    chunks = {(0, 0): [join(halves[0])]}
    for dc in range(1, nc):
        chunks[0, dc] = [send_req(chunks[0, 0][0], 0, dc)]
    over_x, over_y, shared, row_gate = tie((over_x, over_y, shared, row_gate))
    for dy in range(1, ny):
        half = join([over_y[i, dy] for i in order])
        chunks[dy, 0] = [half] + [send(half, 0, 0, dx) for dx in range(1, nx)]
        for dc in range(1, nc):
            chunks[dy, dc] = [send_req(half, 0, dc)]
        over_x, _ = tie((over_x, half))
    for dx in range(1, nx):
        half = [over_x[i, dx] for i in order]
        chunks[0, 0].append(join(half))
        for dc in range(1, nc):
            chunks[0, dc].append(send_req(chunks[0, 0][dx], 0, dc))
        halves.append(half)

    def answers_of(dy, dcs, more, cuts):
        return routed_expert(
            [chunks[dy, dc] for dc in dcs],
            jnp.concatenate([place[dy, dc : dc + 1] for dc in dcs]),
            jnp.concatenate([row_gate[dy, dc : dc + 1] for dc in dcs]),
            more,
            expert_gate,
            expert_up,
            expert_down,
            entries,
            cuts,
        )

    def add_up(parts):
        return sum([part.astype(f32) for part in parts[1:]], parts[0].astype(f32))

    cores = list(range(nc))
    kept, comes = {}, {}
    cuts = [slice(0, 3 * tok_rows), slice(3 * tok_rows, 4 * tok_rows)]
    for dy in range(ny - 1):
        answers = answers_of(dy, cores, [], [nx] * nc)
        if dy:
            answers, comes[dy - 1] = tie((answers, comes[dy - 1]))
        others = [[send_req(part, 0, -dc) for part in answers[dc][::-1]][::-1] for dc in cores[1:]]
        parts = [answers[0]] + others
        if dy:
            following = answers[0][0]
        else:
            for dx in range(1, nx):
                halves[dx], _ = tie((halves[dx], answers[0]))
                shared.append(shared_expert(halves[dx], *shared_weights))
            parts.append(shared)
            following = shared[-1]
        chunks[dy + 1, 0], _ = tie((chunks[dy + 1, 0], following))
        for dc in range(1, nc):
            chunks[dy + 1, dc] += [send_req(part, 0, dc) for part in chunks[dy + 1, 0][1:]]
        gone = [add_up([part[dx] for part in parts]).astype(bf16) for dx in range(1, nx)]
        kept[dy] = [part[0] for part in parts]
        waiting = [go[cuts[1]] for go in gone]
        comes[dy] = [
            [send(go[rows], 0, 0, -dx) for dx, go in enumerate(gone, 1)]
            for rows in (cuts if dy + 2 < ny else cuts[:1])
        ]
        following = [chunks[dy + 1, dc] for dc in cores]
        following, _ = tie((following, gone))
        for dc in cores:
            chunks[dy + 1, dc] = following[dc]
    end = ny - 1
    answers = answers_of(end, cores, [], [4 * nx] + [nx] * (nc - 1))
    answers, comes, kept = tie((answers, comes, kept))
    answer = answers[0]
    others = [[send_req(part, 0, -dc) for part in answers[dc][::-1]][::-1] for dc in cores[1:]]

    turns = [1, 2, 0, 3]
    block = lambda a, p: a[p * tok_rows : (p + 1) * tok_rows]
    last = {}
    for p in turns:
        gone = [
            add_up([answer[4 * dx + p]] + [block(other[dx], p) for other in others])
            for dx in range(1, nx)
        ]
        gone = [go.astype(bf16) for go in gone]
        last[p] = [send(go, 0, 0, -dx) for dx, go in enumerate(gone, 1)]
        others, _ = tie((others, gone))
    waiting, _ = tie((waiting, gone))
    comes[end - 1].append([send(go, 0, 0, -dx) for dx, go in enumerate(waiting, 1)])

    def line_of(dy, p):
        if dy < end:
            arrived = [come if p == 3 else block(come, p) for come in comes[dy][p // 3]]
            return add_up([block(part, p) for part in kept[dy]] + arrived)
        return add_up([answer[p]] + [block(other[0], p) for other in others] + last[p])

    home, near = {}, {}
    for turn, p in enumerate(turns):
        goes = [line_of(dy, p).astype(bf16) for dy in range(1, ny)]
        home[p] = [send_req(go, -dy, 0) for dy, go in enumerate(goes, 1)]
        if turn == 1:
            go = add_up([line_of(0, 1)] + home[1]).astype(bf16)
            near[1] = send(go, 0, 1, 0)
            goes.append(go)
        if turn + 1 < len(turns):
            after = turns[turn + 1]
            last[after], _ = tie((last[after], goes))
    far = add_up([line_of(0, 2)] + home[2] + [near[1]]).astype(bf16)
    home[0], _ = tie((home[0], far))
    far = send(far, 1, 0, 0)
    near[0] = send(add_up([line_of(0, 0)] + home[0]).astype(bf16), 0, 1, 0)
    total = add_up([stream, line_of(0, 3)] + home[3] + [near[0], far])
    return total.astype(bf16)


def solution(mesh):
    placed = (
        P(("req", "exp"), None),
        P(("req", "exp"), None),
        P(("req", "exp"), None, None),
        P(("req", "exp"), None, None),
        P("req", None),
        P("req"),
        P("req"),
        P("exp", None),
        P(),
        P(("req", "exp"), None, None),
        P(("req", "exp"), None, None),
        P(("req", "exp"), None, None),
        P(None, "exp"),
        P(None, "exp"),
        P("exp", None),
        P(),
        P(),
        P(),
        P(("req", "exp"), None),
    )
    return jax.shard_map(
        shards, mesh=mesh, in_specs=placed, out_specs=P(("req", "exp"), None), check_vma=False
    )
```

```python
import functools

import jax
import jax.numpy as jnp
from jax import lax
from jax.experimental import pallas as pl
from jax.experimental.pallas import tpu as pltpu
from jax.sharding import PartitionSpec as P

HEAD_DIM = 128
TOPK = 4
CORES = 2
Z_CHIPS = 4


def pack_kernel(members, parts, columns, order, *refs):
    sources, refs = refs[:parts], refs[parts:]
    gates, blocks, sems = refs[:-1 - members], refs[-1 - members : -1], refs[-1]
    copies = []
    for m in range(members):
        at = 0
        for source in sources:
            rows = source.shape[0]
            for j in range(2):
                place = pl.multiple_of(order[2 * m + j] * columns, columns)
                copies.append(
                    pltpu.make_async_copy(
                        source.at[:, pl.ds(place, columns)],
                        blocks[m].at[pl.ds(at, rows), pl.ds(j * columns, columns)],
                        sems.at[len(copies)],
                    )
                )
            at += rows
    for copy in copies:
        copy.start()
    if gates:
        weights = gates[0][...]
        high = weights.astype(jnp.bfloat16).astype(jnp.float32)
        middle = (weights - high).astype(jnp.bfloat16).astype(jnp.float32)
        low = weights - high - middle
        weights = jnp.concatenate([high, middle, low, jnp.zeros_like(low)], axis=0)
        for m in range(members):
            blocks[m][at:, :] = weights.astype(jnp.bfloat16)
    for copy in copies:
        copy.wait()


def pack(parts, gates, order, columns):
    members = order.shape[0] // 2
    rows = sum(p.shape[0] for p in parts) + (0 if gates is None else 4 * gates.shape[0])
    vmem = pl.BlockSpec(memory_space=pltpu.VMEM)
    in_specs = [pl.BlockSpec(memory_space=pltpu.SMEM)]
    in_specs += [pl.BlockSpec(memory_space=pl.ANY)] * len(parts)
    operands = list(parts)
    if gates is not None:
        in_specs.append(vmem)
        operands.append(gates)
    return pl.pallas_call(
        functools.partial(pack_kernel, members, len(parts), columns),
        out_shape=[jax.ShapeDtypeStruct((rows, 2 * columns), parts[0].dtype)] * members,
        in_specs=in_specs,
        out_specs=[vmem] * members,
        scratch_shapes=[pltpu.SemaphoreType.DMA((2 * members * len(parts),))],
        compiler_params=pltpu.CompilerParams(vmem_limit_bytes=56 * 1024 * 1024),
        cost_estimate=pl.CostEstimate(
            flops=0, bytes_accessed=8 * members * rows * columns, transcendentals=0
        ),
    )(order, *operands)


def attend_kernel(members, tokens, tok_rows, page_len, scale, page_req, page_slot, *refs):
    blocks, refs = refs[:members], refs[members:]
    if len(refs) > 4:
        query, refs = [q[...] for q in refs[:members]], refs[members:]
    else:
        query = [block[2 * tokens : 2 * tokens + tok_rows, :] for block in blocks]
    request, position, out, level = refs
    request, position = request[...], position[...]
    keys = jnp.concatenate([block[:tokens, :] for block in blocks], axis=0)
    values = jnp.concatenate([block[tokens : 2 * tokens, :] for block in blocks], axis=0)
    query = jnp.concatenate(query, axis=0)
    scores = (
        lax.dot_general(keys, query, (((1,), (1,)), ((), ())), preferred_element_type=jnp.float32)
        * scale
    )
    token = lax.broadcasted_iota(jnp.int32, (page_len, query.shape[0]), 0)
    visible = jnp.concatenate(
        [
            (request == page_req[page]) & (token + page_slot[page] * page_len <= position)
            for page in range(members * tokens // page_len)
        ],
        axis=0,
    )
    scores = jnp.where(visible, scores, -1e30)
    top = jnp.max(scores, axis=0, keepdims=True)
    weights = jnp.where(visible, jnp.exp(scores - top), 0.0)
    total = jnp.sum(weights, axis=0, keepdims=True)
    summed = lax.dot_general(
        values,
        weights.astype(jnp.bfloat16),
        (((0,), (0,)), ((), ())),
        preferred_element_type=jnp.float32,
    )
    seen = total > 0.0
    total = jnp.where(seen, total, 1.0)
    out[...] = (summed / total).astype(jnp.bfloat16)
    level[0] = jnp.where(seen, top + jnp.log(total), -1e30)


def attend(blocks, far, row_req, row_pos, page_req, page_slot, page_len, tokens, tok_rows):
    members, rows = len(blocks), row_req.shape[1]
    block_rows, columns = blocks[0].shape
    heads = columns // HEAD_DIM
    by_head = lambda n: pl.BlockSpec((n, HEAD_DIM), lambda h, *_: (0, h))
    whole = pl.BlockSpec((1, rows), lambda h, *_: (0, 0))
    return pl.pallas_call(
        functools.partial(
            attend_kernel, members, tokens, tok_rows, page_len, HEAD_DIM ** (-0.5)
        ),
        out_shape=[
            jax.ShapeDtypeStruct((columns, rows), jnp.bfloat16),
            jax.ShapeDtypeStruct((heads, 1, rows), jnp.float32),
        ],
        grid_spec=pltpu.PrefetchScalarGridSpec(
            num_scalar_prefetch=2,
            grid=(heads,),
            in_specs=[by_head(block_rows)] * members + [by_head(tok_rows)] * len(far) + [whole] * 2,
            out_specs=[
                pl.BlockSpec((HEAD_DIM, rows), lambda h, *_: (h, 0)),
                pl.BlockSpec((1, 1, rows), lambda h, *_: (h, 0, 0)),
            ],
        ),
        compiler_params=pltpu.CompilerParams(vmem_limit_bytes=48 * 1024 * 1024),
        cost_estimate=pl.CostEstimate(
            flops=4 * rows * members * tokens * columns,
            bytes_accessed=2 * members * (block_rows + tok_rows) * columns,
            transcendentals=rows * members * tokens * heads,
        ),
    )(page_req, page_slot, *blocks, *far, row_req, row_pos)


def project_kernel(order, mine, mine_level, theirs, their_level, own, *refs):
    quarters, (stay, go, proj) = refs[:-3], refs[-3:]
    rows, size = own.shape[0], quarters[0].shape[0]
    proj[:rows, :] = own[...]
    for k, quarter in enumerate(quarters):
        at = pl.multiple_of(rows + order[k] * size, size)
        proj[pl.ds(at, size), :] = quarter[...]
    parts = []
    heads = mine.shape[0] // HEAD_DIM
    for head in range(heads):
        twin = (head + heads // 2) % heads
        dims = slice(head * HEAD_DIM, (head + 1) * HEAD_DIM)
        twin_dims = slice(twin * HEAD_DIM, (twin + 1) * HEAD_DIM)
        share = 1.0 / (1.0 + jnp.exp(their_level[twin] - mine_level[head]))
        other = 1.0 / (1.0 + jnp.exp(mine_level[head] - their_level[twin]))
        both = share * mine[dims, :].astype(jnp.float32) + other * theirs[
            twin_dims, :
        ].astype(jnp.float32)
        parts.append(both.astype(jnp.bfloat16))
    attention = jnp.concatenate(parts, axis=0)
    mixed = lax.dot_general(
        attention, proj[...], (((0,), (0,)), ((), ())), preferred_element_type=jnp.float32
    )
    kept = stay.shape[0]
    stay[...] = mixed[:kept, :]
    go[...] = mixed[kept:, :].astype(jnp.bfloat16)


def project(place, order, mine, mine_level, theirs, their_level, own, quarters, tok_rows):
    dims, width = mine.shape[0], own.shape[1]
    heads = dims // HEAD_DIM
    size = mine.shape[1] // 2
    whole = lambda a: pl.BlockSpec(a.shape, lambda i, order: (0, 0))
    values = pl.BlockSpec((dims, size), lambda i, order: (0, place))
    levels = pl.BlockSpec((heads, 1, size), lambda i, order: (0, 0, place))
    return pl.pallas_call(
        project_kernel,
        out_shape=[
            jax.ShapeDtypeStruct((tok_rows, width), jnp.float32),
            jax.ShapeDtypeStruct((size - tok_rows, width), jnp.bfloat16),
        ],
        grid_spec=pltpu.PrefetchScalarGridSpec(
            num_scalar_prefetch=1,
            grid=(1,),
            in_specs=[values, levels, values, levels, whole(own)] + [whole(q) for q in quarters],
            out_specs=[
                pl.BlockSpec((tok_rows, width), lambda i, order: (0, 0)),
                pl.BlockSpec((size - tok_rows, width), lambda i, order: (0, 0)),
            ],
            scratch_shapes=[pltpu.VMEM((dims, width), jnp.bfloat16)],
        ),
        compiler_params=pltpu.CompilerParams(vmem_limit_bytes=32 * 1024 * 1024),
        cost_estimate=pl.CostEstimate(
            flops=2 * size * dims * width,
            bytes_accessed=2 * (2 * dims * size + dims * width + 3 * size * width),
            transcendentals=2 * size * heads,
        ),
    )(order, mine, mine_level, theirs, their_level, own, *quarters)


def join_kernel(*refs):
    parts, out = refs[:-1], refs[-1]
    rows = parts[0].shape[0]
    for i, part in enumerate(parts):
        out[i * rows : (i + 1) * rows, :] = part[...]


def join(parts):
    rows, width = parts[0].shape
    vmem = pl.BlockSpec(memory_space=pltpu.VMEM)
    return pl.pallas_call(
        join_kernel,
        out_shape=jax.ShapeDtypeStruct((len(parts) * rows, width), parts[0].dtype),
        in_specs=[vmem] * len(parts),
        out_specs=vmem,
        cost_estimate=pl.CostEstimate(
            flops=0, bytes_accessed=4 * len(parts) * rows * width, transcendentals=0
        ),
    )(*parts)


def silu(value):
    return value / (1.0 + jnp.exp(-value))


def shared_kernel(count, *refs):
    pieces, (scalar, gate_w, up_w, down_w, out, rows, gate_v, up_v, down_v, sems) = (
        refs[:count],
        refs[count:],
    )
    moves = [(gate_w, gate_v), (up_w, up_v), (down_w, down_v)]
    size = pieces[0].shape[0]
    moves += [(piece, rows.at[pl.ds(i * size, size)]) for i, piece in enumerate(pieces)]
    copies = [
        pltpu.make_async_copy(src, dst, sems.at[i]) for i, (src, dst) in enumerate(moves)
    ]
    for copy in copies[3:] + copies[:3]:
        copy.start()
    for copy in copies[3:]:
        copy.wait()
    block = rows[...]
    logit = jnp.sum(
        block.astype(jnp.float32) * scalar[...].astype(jnp.float32), axis=1, keepdims=True
    )
    scale = 1.0 / (1.0 + jnp.exp(-logit))
    across = (((1,), (1,)), ((), ()))
    copies[0].wait()
    gate = lax.dot_general(block, gate_v[...], across, preferred_element_type=jnp.float32)
    copies[1].wait()
    upper = lax.dot_general(block, up_v[...], across, preferred_element_type=jnp.float32)
    hidden = (silu(gate) * upper).astype(jnp.bfloat16)
    copies[2].wait()
    result = jnp.dot(hidden, down_v[...], preferred_element_type=jnp.float32)
    out[...] = (scale * result).astype(jnp.bfloat16)


def shared_expert(pieces, scalar, gate_w, up_w, down_w):
    any_spec = pl.BlockSpec(memory_space=pl.ANY)
    vmem = pl.BlockSpec(memory_space=pltpu.VMEM)
    rows = sum(piece.shape[0] for piece in pieces)
    width = pieces[0].shape[1]
    return pl.pallas_call(
        functools.partial(shared_kernel, len(pieces)),
        out_shape=jax.ShapeDtypeStruct((rows, width), jnp.bfloat16),
        in_specs=[any_spec] * len(pieces) + [vmem] + [any_spec] * 3,
        out_specs=vmem,
        scratch_shapes=[
            pltpu.VMEM((rows, width), jnp.bfloat16),
            pltpu.VMEM(gate_w.shape, jnp.bfloat16),
            pltpu.VMEM(up_w.shape, jnp.bfloat16),
            pltpu.VMEM(down_w.shape, jnp.bfloat16),
            pltpu.SemaphoreType.DMA((3 + len(pieces),)),
        ],
        compiler_params=pltpu.CompilerParams(vmem_limit_bytes=56 * 1024 * 1024),
        cost_estimate=pl.CostEstimate(
            flops=6 * rows * gate_w.size,
            bytes_accessed=6 * gate_w.size + 4 * rows * width,
            transcendentals=rows * gate_w.shape[0],
        ),
    )(*pieces, scalar.reshape(1, -1), gate_w, up_w, down_w)


def routed_kernel(parts, extras, entries, cuts, *refs):
    count, total = len(parts), sum(parts)
    pieces, refs = refs[:total], refs[total:]
    place, row_gate = refs[:2]
    more, refs = refs[2 : 2 + extras], refs[2 + extras :]
    (gate_w, up_w, down_w), refs = refs[:3], refs[3:]
    outs, refs = refs[: sum(cuts)], refs[sum(cuts) :]
    rows, packed, hidden, gate_v, up_v, down_v, more_v, sems = refs
    moves, chunk_copies = [], []
    for c, n in enumerate(parts):
        at = 0
        chunk_copies.append(range(len(moves), len(moves) + n))
        for piece in pieces[sum(parts[:c]) : sum(parts[: c + 1])]:
            moves.append((piece, rows.at[c, pl.ds(at, piece.shape[0])]))
            at += piece.shape[0]
    hidden_units = gate_v.shape[1]
    slices = [slice(n, min(n + 512, hidden_units)) for n in range(0, hidden_units, 512)]
    for part in slices:
        units = pl.ds(part.start, part.stop - part.start)
        moves += [(w.at[0, :, units], v.at[:, units]) for w, v in ((gate_w, gate_v), (up_w, up_v))]
    moves.append((down_w.at[0], down_v))
    at = 0
    for extra in more:
        moves.append((extra, more_v.at[pl.ds(at, extra.shape[0])]))
        at += extra.shape[0]
    copies = [
        pltpu.make_async_copy(src, dst, sems.at[i]) for i, (src, dst) in enumerate(moves)
    ]
    for copy in copies:
        copy.start()
    size = rows.shape[1]
    wanted = lax.broadcasted_iota(jnp.int32, (entries, size), 0)
    picks, weights = [], []
    for c in range(count):
        pick = jnp.where(place[c] == wanted, 1.0, 0.0)
        picks.append(pick.astype(jnp.bfloat16))
        weights.append(jnp.sum(pick * row_gate[c], axis=1, keepdims=True))
        for i in chunk_copies[c]:
            copies[i].wait()
        packed[c * entries : (c + 1) * entries, :] = jnp.dot(
            picks[c], rows[c], preferred_element_type=jnp.float32
        ).astype(jnp.bfloat16)
    for k, part in enumerate(slices):
        copies[total + 2 * k].wait()
        gate = jnp.dot(packed[...], gate_v[:, part], preferred_element_type=jnp.float32)
        copies[total + 2 * k + 1].wait()
        upper = jnp.dot(packed[...], up_v[:, part], preferred_element_type=jnp.float32)
        hidden[:, part] = (silu(gate) * upper).astype(jnp.bfloat16)
    behind = total + 2 * len(slices)
    copies[behind].wait()
    answer = jnp.dot(hidden[...], down_v[...], preferred_element_type=jnp.float32).astype(
        jnp.bfloat16
    )
    for i in range(extras):
        copies[behind + 1 + i].wait()
    for c in range(count):
        scaled = answer[c * entries : (c + 1) * entries, :].astype(jnp.float32) * weights[c]
        placed = lax.dot_general(
            picks[c],
            scaled.astype(jnp.bfloat16),
            (((0,), (0,)), ((), ())),
            preferred_element_type=jnp.float32,
        )
        if c == 0 and extras:
            placed = placed + more_v[...].astype(jnp.float32)
        placed = placed.astype(jnp.bfloat16)
        cut = size // cuts[c]
        for k in range(cuts[c]):
            outs[sum(cuts[:c]) + k][...] = placed[k * cut : (k + 1) * cut, :]


def routed_expert(chunks, place, row_gate, more, gate_w, up_w, down_w, entries, cuts):
    count = len(chunks)
    parts = [len(chunk) for chunk in chunks]
    total = sum(parts)
    size = sum(piece.shape[0] for piece in chunks[0])
    width = chunks[0][0].shape[1]
    hidden = gate_w.shape[2]
    any_spec = pl.BlockSpec(memory_space=pl.ANY)
    vmem = pl.BlockSpec(memory_space=pltpu.VMEM)
    out_shape = [
        jax.ShapeDtypeStruct((size // n, width), jnp.bfloat16) for n in cuts for k in range(n)
    ]
    more_rows = sum(extra.shape[0] for extra in more) if more else 16
    outs = pl.pallas_call(
        functools.partial(routed_kernel, parts, len(more), entries, cuts),
        out_shape=out_shape,
        in_specs=[any_spec] * total + [vmem] * 2 + [any_spec] * (len(more) + 3),
        out_specs=[vmem] * sum(cuts),
        scratch_shapes=[
            pltpu.VMEM((count, size, width), jnp.bfloat16),
            pltpu.VMEM((count * entries, width), jnp.bfloat16),
            pltpu.VMEM((count * entries, hidden), jnp.bfloat16),
            pltpu.VMEM((width, hidden), jnp.bfloat16),
            pltpu.VMEM((width, hidden), jnp.bfloat16),
            pltpu.VMEM((hidden, width), jnp.bfloat16),
            pltpu.VMEM((more_rows, width), jnp.bfloat16),
            pltpu.SemaphoreType.DMA((total + 1 + 2 * -(-hidden // 512) + len(more),)),
        ],
        compiler_params=pltpu.CompilerParams(vmem_limit_bytes=56 * 1024 * 1024),
        cost_estimate=pl.CostEstimate(
            flops=2 * count * entries * (3 * gate_w.size + 2 * size * width),
            bytes_accessed=6 * gate_w.size + 4 * count * size * width,
            transcendentals=count * entries * hidden,
        ),
    )(*[piece for chunk in chunks for piece in chunk], place, row_gate, *more, gate_w, up_w, down_w)
    return [outs[sum(cuts[:c]) : sum(cuts[: c + 1])] for c in range(count)]


def rms_normed(stream, norm_gain):
    scale_row = lax.rsqrt(jnp.mean(stream * stream, axis=1, keepdims=True) + 1e-06)
    return (stream * scale_row * norm_gain[None, :]).astype(jnp.bfloat16)


def shards(
    resid,
    queries,
    cache_key,
    cache_value,
    page_table,
    row_request,
    row_position,
    out_proj,
    norm_gain,
    expert_gate,
    expert_up,
    expert_down,
    shared_gate,
    shared_up,
    shared_down,
    shared_scalar,
    slot_expert,
    route_expert,
    route_gate,
):
    f32, bf16, i32 = jnp.float32, jnp.bfloat16, jnp.int32
    exp_count = lax.axis_size("exp")
    req_count = lax.axis_size("req")
    slot_count = exp_count * req_count
    nc, nx, ny = CORES, exp_count // Z_CHIPS, req_count // CORES
    exp_index = lax.axis_index("exp")
    req_index = lax.axis_index("req")
    own_slot = req_index * exp_count + exp_index
    iz, ix = exp_index // nx, exp_index % nx
    ih, il = iz // 2, iz % 2
    iy, ic = req_index // nc, req_index % nc
    tok_rows, width = resid.shape
    pages_here, page_len, _ = cache_key.shape
    req_slots, max_pages = page_table.shape
    tokens = pages_here * page_len
    capacity = 3 * tok_rows * TOPK // slot_count

    zs = [(dh, dl) for dh in range(2) for dl in range(2)]

    def send(value, dh, dl, dx):
        if not (dh or dl or dx % nx):
            return value
        pairs = [
            (
                (h * 2 + l) * nx + x,
                ((h + dh) % 2 * 2 + (l + dl) % 2) * nx + (x + dx) % nx,
            )
            for h in range(2)
            for l in range(2)
            for x in range(nx)
        ]
        return lax.ppermute(value, "exp", pairs)

    def send_req(value, dy, dc):
        if not (dy % ny or dc % nc):
            return value
        pairs = [
            (y * nc + c, (y + dy) % ny * nc + (c + dc) % nc)
            for y in range(ny)
            for c in range(nc)
        ]
        return lax.ppermute(value, "req", pairs)

    def swap_y(value):
        pairs = [(y * nc + c, (y ^ 1) * nc + c) for y in range(ny) for c in range(nc)]
        return lax.ppermute(value, "req", pairs)

    tie = lax.optimization_barrier

    rel_exp = jnp.stack(
        [
            ((ih + dh) % 2 * 2 + (il + dl) % 2) * nx + (ix - dx) % nx
            for dh, dl in zs
            for dx in range(nx)
        ]
    ).astype(i32)
    rel_req = jnp.stack(
        [((iy - dy) % ny) * nc + (ic - dc) % nc for dy in range(ny) for dc in range(nc)]
    ).astype(i32)

    columns = width // exp_count
    keys = cache_key.reshape(tokens, width)
    values = cache_value.reshape(tokens, width)
    quarter_rows = out_proj.shape[0] // (2 * nc)
    quarter = lax.dynamic_slice_in_dim(
        out_proj, (iy % 2 * nc + ic) * quarter_rows, quarter_rows, 0
    )
    quarter_order = jnp.stack(
        [(iy + dy) % 2 * nc + (ic + dc) % nc for dc in range(nc) for dy in range(2)]
    ).astype(i32)
    far_queries = send(queries, 1, 0, 0)
    members = [(dl, dx) for dl in range(2) for dx in range(nx)]
    member_columns = jnp.stack(
        [
            ((ih + j) % 2 * 2 + (il + dl) % 2) * nx + (ix + dx) % nx
            for dl, dx in members
            for j in range(2)
        ]
    ).astype(i32)
    gates = jnp.pad(jnp.transpose(route_gate), ((0, 0), (0, 2 * columns - tok_rows)))
    blocks = pack([keys, values, queries], gates, member_columns, columns)
    blocks = [send(blocks[m], 0, *members[m]) for m in range(len(members))]
    far = list(pack([far_queries], None, member_columns, columns))
    for m in range(1, len(members)):
        if m > 2:
            far[m], far[m - 2] = tie((far[m], far[m - 2]))
        far[m] = send(far[m], 0, *members[m])
    quarter, far[1] = tie((quarter, far[1]))
    quarters = [send(quarter, 1, 0, 0)]
    page_ids = (
        rel_exp[: len(members), None] * pages_here + jnp.arange(pages_here, dtype=i32)[None, :]
    ).reshape(-1)
    hits = (page_table[None, :, :] == page_ids[:, None, None]).astype(i32)
    page_request = jnp.sum(hits * jnp.arange(req_slots, dtype=i32)[None, :, None], axis=(1, 2))
    page_slot = jnp.sum(hits * jnp.arange(max_pages, dtype=i32)[None, None, :], axis=(1, 2))
    by_place = lambda a: a.reshape(exp_count, tok_rows)[rel_exp].reshape(2, 1, -1)
    row_req, row_pos = by_place(row_request), by_place(row_position)
    gates = [block[2 * tokens + tok_rows :, :tok_rows].astype(f32) for block in blocks]
    gates = jnp.stack([g[:TOPK] + g[TOPK : 2 * TOPK] + g[2 * TOPK : 3 * TOPK] for g in gates])
    gates = gates.reshape(2, nx, TOPK, tok_rows)

    slot_ids = jnp.arange(slot_count, dtype=i32)
    own_mark = slot_ids == own_slot
    own_expert = jnp.sum(jnp.where(own_mark, slot_expert, 0))
    twins = slot_expert == own_expert
    copies = jnp.sum(twins.astype(i32))
    own_rank = jnp.sum((twins & (slot_ids < own_slot)).astype(i32))
    order = [3, 2, 1, 0]
    rel_rows = jnp.stack([rel_exp.reshape(4, nx)[i] for i in order], axis=1).reshape(-1)
    rel_slots = (rel_req[:, None] * exp_count + rel_rows[None, :]).reshape(-1)
    named = (route_expert == own_expert).reshape(slot_count, tok_rows, TOPK)[rel_slots]
    named = jnp.transpose(named, (0, 2, 1))
    chunk_rows = exp_count * tok_rows
    entries = -(-exp_count * capacity // 16) * 16
    served = jnp.any(named, axis=1) & (rel_slots % copies == own_rank)[:, None]
    served = served.reshape(ny, nc, chunk_rows)
    place = jnp.where(served, jnp.cumsum(served.astype(i32), axis=2) - 1, -1)
    place = place.reshape(ny, nc, 1, chunk_rows)

    place, named, blocks = tie((place, named, blocks))

    def attend_half(side, queries):
        return attend(
            blocks,
            queries,
            row_req[side],
            row_pos[side],
            page_request,
            page_slot,
            page_len,
            tokens,
            tok_rows,
        )

    theirs, their_level = attend_half(1, far)
    theirs, their_level = tie((theirs, their_level))
    near_blocks, _ = tie((blocks, theirs))
    theirs, their_level = send(theirs, 1, 0, 0), send(their_level, 1, 0, 0)
    blocks = near_blocks
    mine, level = attend_half(0, [])
    mine, level, gates, quarters = tie((mine, level, gates, quarters))
    quarters.append(swap_y(quarters[0]))
    gates = jnp.stack([send(gates, dh, 0, 0) for dh in range(2)])
    quarters += [send_req(q, 0, dc) for dc in range(1, nc) for q in quarters[:2]]
    theirs, their_level, gates = tie((theirs, their_level, gates))

    stays, comes = {}, {}
    proj = out_proj
    for dl in (1, 0):
        stays[dl], go = project(
            dl, quarter_order, mine, level, theirs, their_level, proj, quarters, tok_rows
        )
        comes[dl] = [
            send(go[(dx - 1) * tok_rows : dx * tok_rows], 0, 0, -dx) for dx in range(1, nx)
        ]
        proj, _ = tie((proj, go))
    line = sum([come.astype(f32) for come in comes[1]], stays[1]).astype(bf16)
    comes[0], _ = tie((comes[0], line))
    line = send(line, 0, 1, 0)
    stream = sum([come.astype(f32) for come in comes[0]], resid.astype(f32) + stays[0])
    stream = stream + line.astype(f32)
    gates = jnp.stack([send_req(gates, dy, 0) for dy in range(ny)])
    stream, gates = tie((stream, gates))
    normed = rms_normed(stream, norm_gain)
    gates = jnp.stack([send_req(gates, 0, dc) for dc in range(nc)], axis=1)
    gates = gates.reshape(ny, nc, 4, nx, TOPK, tok_rows)
    gates = jnp.stack([gates[:, :, i] for i in order], axis=3)
    gates = gates.reshape(slot_count, TOPK, tok_rows)
    row_gate = jnp.sum(jnp.where(named, gates, 0.0), axis=1).reshape(ny, nc, 1, chunk_rows)

    far_line = send(normed, 1, 0, 0)
    line = [normed, send(normed, 0, 1, 0), far_line, send(far_line, 0, 1, 0)]
    over_x = {(i, dx): send(line[i], 0, 0, dx) for i in order for dx in range(1, nx)}
    over_y = {(i, dy): send_req(line[i], dy, 0) for i in order for dy in range(1, ny)}

    halves = [[line[i] for i in order]]
    shared_weights = (shared_scalar, shared_gate.T, shared_up.T, shared_down)
    shared = [shared_expert(halves[0], *shared_weights)]
    chunks = {(0, 0): [join(halves[0])]}
    for dc in range(1, nc):
        chunks[0, dc] = [send_req(chunks[0, 0][0], 0, dc)]
    over_x, shared, row_gate = tie((over_x, shared, row_gate))
    for dx in range(1, nx):
        half = [over_x[i, dx] for i in order]
        chunks[0, 0].append(join(half))
        for dc in range(1, nc):
            chunks[0, dc].append(send_req(chunks[0, 0][dx], 0, dc))
        halves.append(half)
    over_y, _ = tie((over_y, chunks[0, 0]))
    for dy in range(1, ny):
        half = join([over_y[i, dy] for i in order])
        chunks[dy, 0] = [half] + [send(half, 0, 0, dx) for dx in range(1, nx)]
        for dc in range(1, nc):
            chunks[dy, dc] = [send_req(half, 0, dc)]

    def answers_of(dy, dcs, more, cuts):
        return routed_expert(
            [chunks[dy, dc] for dc in dcs],
            jnp.concatenate([place[dy, dc : dc + 1] for dc in dcs]),
            jnp.concatenate([row_gate[dy, dc : dc + 1] for dc in dcs]),
            more,
            expert_gate,
            expert_up,
            expert_down,
            entries,
            cuts,
        )

    def add_up(parts):
        return sum([part.astype(f32) for part in parts[1:]], parts[0].astype(f32))

    cores = list(range(nc))
    kept, comes = {}, {}
    cuts = [slice(0, 2 * tok_rows)] + [slice(p * tok_rows, (p + 1) * tok_rows) for p in (2, 3)]
    for dy in range(ny - 1):
        answers = answers_of(dy, cores, [], [nx] * nc)
        if dy:
            answers, comes[dy - 1] = tie((answers, comes[dy - 1]))
        others = [[send_req(part, 0, -dc) for part in answers[dc][::-1]][::-1] for dc in cores[1:]]
        parts = [answers[0]] + others
        if dy:
            following = answers[0][0]
        else:
            for dx in range(1, nx):
                halves[dx], _ = tie((halves[dx], answers[0]))
                shared.append(shared_expert(halves[dx], *shared_weights))
            parts.append(shared)
            following = shared[-1]
        chunks[dy + 1, 0], _ = tie((chunks[dy + 1, 0], following))
        for dc in range(1, nc):
            chunks[dy + 1, dc] += [send_req(part, 0, dc) for part in chunks[dy + 1, 0][1:]]
        gone = [add_up([part[dx] for part in parts]).astype(bf16) for dx in range(1, nx)]
        kept[dy] = [part[0] for part in parts]
        waiting = [[go[rows] for go in gone] for rows in cuts[1:]]
        comes[dy] = [
            [send(go[rows], 0, 0, -dx) for dx, go in enumerate(gone, 1)]
            for rows in (cuts if dy + 2 < ny else cuts[:1])
        ]
        following = [chunks[dy + 1, dc] for dc in cores]
        following, _ = tie((following, gone))
        for dc in cores:
            chunks[dy + 1, dc] = following[dc]
    end = ny - 1
    answers = answers_of(end, cores, [], [4 * nx] + [nx] * (nc - 1))
    answers, comes, kept = tie((answers, comes, kept))
    answer = answers[0]
    others = [[send_req(part, 0, -dc) for part in answers[dc][::-1]][::-1] for dc in cores[1:]]

    turns = [0, 1, 2, 3]
    block = lambda a, p: a[p * tok_rows : (p + 1) * tok_rows]
    last = {}
    for p in turns:
        gone = [
            add_up([answer[4 * dx + p]] + [block(other[dx], p) for other in others])
            for dx in range(1, nx)
        ]
        gone = [go.astype(bf16) for go in gone]
        last[p] = [send(go, 0, 0, -dx) for dx, go in enumerate(gone, 1)]
        others, _ = tie((others, gone))
    waiting, _ = tie((waiting, gone))
    comes[end - 1] += [
        [send(go, 0, 0, -dx) for dx, go in enumerate(piece, 1)] for piece in waiting
    ]

    def line_of(dy, p):
        if dy < end:
            if p < 2:
                arrived = [block(come, p) for come in comes[dy][0]]
            else:
                arrived = comes[dy][p - 1]
            return add_up([block(part, p) for part in kept[dy]] + arrived)
        return add_up([answer[p]] + [block(other[0], p) for other in others] + last[p])

    home, near = {}, {}
    for p in turns:
        goes = [line_of(dy, p).astype(bf16) for dy in range(1, ny)]
        home[p] = [send_req(go, -dy, 0) for dy, go in enumerate(goes, 1)]
        if p == 1:
            go = add_up([line_of(0, 0)] + home[0]).astype(bf16)
            near[0] = send(go, 0, 1, 0)
            goes.append(go)
        if p == 2:
            go = add_up([line_of(0, 1)] + home[1] + [near[0]]).astype(bf16)
            far = send(go, 1, 0, 0)
            goes.append(go)
        if p < 3:
            last[p + 1], _ = tie((last[p + 1], goes))
    near[2] = send(add_up([line_of(0, 2)] + home[2]).astype(bf16), 0, 1, 0)
    total = add_up([stream, line_of(0, 3)] + home[3] + [near[2], far])
    return total.astype(bf16)


def solution(mesh):
    placed = (
        P(("req", "exp"), None),
        P(("req", "exp"), None),
        P(("req", "exp"), None, None),
        P(("req", "exp"), None, None),
        P("req", None),
        P("req"),
        P("req"),
        P("exp", None),
        P(),
        P(("req", "exp"), None, None),
        P(("req", "exp"), None, None),
        P(("req", "exp"), None, None),
        P(None, "exp"),
        P(None, "exp"),
        P("exp", None),
        P(),
        P(),
        P(),
        P(("req", "exp"), None),
    )
    return jax.shard_map(
        shards, mesh=mesh, in_specs=placed, out_specs=P(("req", "exp"), None), check_vma=False
    )
```

```python
import functools

import jax
import jax.numpy as jnp
from jax import lax
from jax.experimental import pallas as pl
from jax.experimental.pallas import tpu as pltpu
from jax.sharding import PartitionSpec as P

HEAD_DIM = 128
TOPK = 4
CORES = 2
Z_CHIPS = 4


def pack_kernel(members, parts, columns, order, *refs):
    sources, refs = refs[:parts], refs[parts:]
    gates, blocks, sems = refs[:-1 - members], refs[-1 - members : -1], refs[-1]
    copies = []
    for m in range(members):
        at = 0
        for source in sources:
            rows = source.shape[0]
            for j in range(2):
                place = pl.multiple_of(order[2 * m + j] * columns, columns)
                copies.append(
                    pltpu.make_async_copy(
                        source.at[:, pl.ds(place, columns)],
                        blocks[m].at[pl.ds(at, rows), pl.ds(j * columns, columns)],
                        sems.at[len(copies)],
                    )
                )
            at += rows
    for copy in copies:
        copy.start()
    if gates:
        weights = gates[0][...]
        high = weights.astype(jnp.bfloat16).astype(jnp.float32)
        middle = (weights - high).astype(jnp.bfloat16).astype(jnp.float32)
        low = weights - high - middle
        weights = jnp.concatenate([high, middle, low, jnp.zeros_like(low)], axis=0)
        for m in range(members):
            blocks[m][at:, : weights.shape[1]] = weights.astype(jnp.bfloat16)
    for copy in copies:
        copy.wait()


def pack(parts, gates, order, columns):
    members = order.shape[0] // 2
    rows = sum(p.shape[0] for p in parts) + (0 if gates is None else 4 * gates.shape[0])
    vmem = pl.BlockSpec(memory_space=pltpu.VMEM)
    in_specs = [pl.BlockSpec(memory_space=pltpu.SMEM)]
    in_specs += [pl.BlockSpec(memory_space=pl.ANY)] * len(parts)
    operands = list(parts)
    if gates is not None:
        in_specs.append(vmem)
        operands.append(gates)
    return pl.pallas_call(
        functools.partial(pack_kernel, members, len(parts), columns),
        out_shape=[jax.ShapeDtypeStruct((rows, 2 * columns), parts[0].dtype)] * members,
        in_specs=in_specs,
        out_specs=[vmem] * members,
        scratch_shapes=[pltpu.SemaphoreType.DMA((2 * members * len(parts),))],
        compiler_params=pltpu.CompilerParams(vmem_limit_bytes=56 * 1024 * 1024),
        cost_estimate=pl.CostEstimate(
            flops=0, bytes_accessed=8 * members * rows * columns, transcendentals=0
        ),
    )(order, *operands)


def attend_kernel(members, tokens, tok_rows, page_len, scale, page_req, page_slot, *refs):
    blocks, refs = refs[:members], refs[members:]
    if len(refs) > 4:
        query, refs = [q[...] for q in refs[:members]], refs[members:]
    else:
        query = [block[2 * tokens : 2 * tokens + tok_rows, :] for block in blocks]
    request, position, out, level = refs
    request, position = request[...], position[...]
    keys = jnp.concatenate([block[:tokens, :] for block in blocks], axis=0)
    values = jnp.concatenate([block[tokens : 2 * tokens, :] for block in blocks], axis=0)
    query = jnp.concatenate(query, axis=0)
    scores = (
        lax.dot_general(keys, query, (((1,), (1,)), ((), ())), preferred_element_type=jnp.float32)
        * scale
    )
    token = lax.broadcasted_iota(jnp.int32, (page_len, query.shape[0]), 0)
    visible = jnp.concatenate(
        [
            (request == page_req[page]) & (token + page_slot[page] * page_len <= position)
            for page in range(members * tokens // page_len)
        ],
        axis=0,
    )
    scores = jnp.where(visible, scores, -1e30)
    top = jnp.max(scores, axis=0, keepdims=True)
    weights = jnp.where(visible, jnp.exp(scores - top), 0.0)
    total = jnp.sum(weights, axis=0, keepdims=True)
    summed = lax.dot_general(
        values,
        weights.astype(jnp.bfloat16),
        (((0,), (0,)), ((), ())),
        preferred_element_type=jnp.float32,
    )
    seen = total > 0.0
    total = jnp.where(seen, total, 1.0)
    out[...] = (summed / total).astype(jnp.bfloat16)
    level[0] = jnp.where(seen, top + jnp.log(total), -1e30)


def attend(blocks, far, row_req, row_pos, page_req, page_slot, page_len, tokens, tok_rows):
    members, rows = len(blocks), row_req.shape[1]
    block_rows, columns = blocks[0].shape
    heads = columns // HEAD_DIM
    by_head = lambda n: pl.BlockSpec((n, HEAD_DIM), lambda h, *_: (0, h))
    whole = pl.BlockSpec((1, rows), lambda h, *_: (0, 0))
    return pl.pallas_call(
        functools.partial(
            attend_kernel, members, tokens, tok_rows, page_len, HEAD_DIM ** (-0.5)
        ),
        out_shape=[
            jax.ShapeDtypeStruct((columns, rows), jnp.bfloat16),
            jax.ShapeDtypeStruct((heads, 1, rows), jnp.float32),
        ],
        grid_spec=pltpu.PrefetchScalarGridSpec(
            num_scalar_prefetch=2,
            grid=(heads,),
            in_specs=[by_head(block_rows)] * members + [by_head(tok_rows)] * len(far) + [whole] * 2,
            out_specs=[
                pl.BlockSpec((HEAD_DIM, rows), lambda h, *_: (h, 0)),
                pl.BlockSpec((1, 1, rows), lambda h, *_: (h, 0, 0)),
            ],
        ),
        compiler_params=pltpu.CompilerParams(vmem_limit_bytes=48 * 1024 * 1024),
        cost_estimate=pl.CostEstimate(
            flops=4 * rows * members * tokens * columns,
            bytes_accessed=2 * members * (block_rows + tok_rows) * columns,
            transcendentals=rows * members * tokens * heads,
        ),
    )(page_req, page_slot, *blocks, *far, row_req, row_pos)


def project_kernel(order, mine, mine_level, theirs, their_level, own, *refs):
    quarters, (stay, go, proj) = refs[:-3], refs[-3:]
    rows, size = own.shape[0], quarters[0].shape[0]
    proj[:rows, :] = own[...]
    for k, quarter in enumerate(quarters):
        at = pl.multiple_of(rows + order[k] * size, size)
        proj[pl.ds(at, size), :] = quarter[...]
    parts = []
    heads = mine.shape[0] // HEAD_DIM
    for head in range(heads):
        twin = (head + heads // 2) % heads
        dims = slice(head * HEAD_DIM, (head + 1) * HEAD_DIM)
        twin_dims = slice(twin * HEAD_DIM, (twin + 1) * HEAD_DIM)
        share = 1.0 / (1.0 + jnp.exp(their_level[twin] - mine_level[head]))
        other = 1.0 / (1.0 + jnp.exp(mine_level[head] - their_level[twin]))
        both = share * mine[dims, :].astype(jnp.float32) + other * theirs[
            twin_dims, :
        ].astype(jnp.float32)
        parts.append(both.astype(jnp.bfloat16))
    attention = jnp.concatenate(parts, axis=0)
    mixed = lax.dot_general(
        attention, proj[...], (((0,), (0,)), ((), ())), preferred_element_type=jnp.float32
    )
    kept = stay.shape[0]
    stay[...] = mixed[:kept, :]
    go[...] = mixed[kept:, :].astype(jnp.bfloat16)


def project(place, order, mine, mine_level, theirs, their_level, own, quarters, tok_rows):
    dims, width = mine.shape[0], own.shape[1]
    heads = dims // HEAD_DIM
    size = mine.shape[1] // 2
    whole = lambda a: pl.BlockSpec(a.shape, lambda i, order: (0, 0))
    values = pl.BlockSpec((dims, size), lambda i, order: (0, place))
    levels = pl.BlockSpec((heads, 1, size), lambda i, order: (0, 0, place))
    return pl.pallas_call(
        project_kernel,
        out_shape=[
            jax.ShapeDtypeStruct((tok_rows, width), jnp.float32),
            jax.ShapeDtypeStruct((size - tok_rows, width), jnp.bfloat16),
        ],
        grid_spec=pltpu.PrefetchScalarGridSpec(
            num_scalar_prefetch=1,
            grid=(1,),
            in_specs=[values, levels, values, levels, whole(own)] + [whole(q) for q in quarters],
            out_specs=[
                pl.BlockSpec((tok_rows, width), lambda i, order: (0, 0)),
                pl.BlockSpec((size - tok_rows, width), lambda i, order: (0, 0)),
            ],
            scratch_shapes=[pltpu.VMEM((dims, width), jnp.bfloat16)],
        ),
        compiler_params=pltpu.CompilerParams(vmem_limit_bytes=32 * 1024 * 1024),
        cost_estimate=pl.CostEstimate(
            flops=2 * size * dims * width,
            bytes_accessed=2 * (2 * dims * size + dims * width + 3 * size * width),
            transcendentals=2 * size * heads,
        ),
    )(order, mine, mine_level, theirs, their_level, own, *quarters)


def join_kernel(sizes, *refs):
    parts, outs = refs[: sum(sizes)], refs[sum(sizes) :]
    for n, out in enumerate(outs):
        rows = out.shape[0] // sizes[n]
        for i in range(sizes[n]):
            out[i * rows : (i + 1) * rows, :] = parts[sum(sizes[:n]) + i][...]


def join(*groups):
    rows, width = groups[0][0].shape
    sizes = [len(group) for group in groups]
    vmem = pl.BlockSpec(memory_space=pltpu.VMEM)
    return pl.pallas_call(
        functools.partial(join_kernel, sizes),
        out_shape=[jax.ShapeDtypeStruct((n * rows, width), groups[0][0].dtype) for n in sizes],
        in_specs=[vmem] * sum(sizes),
        out_specs=[vmem] * len(sizes),
        cost_estimate=pl.CostEstimate(
            flops=0, bytes_accessed=4 * sum(sizes) * rows * width, transcendentals=0
        ),
    )(*[part for group in groups for part in group])


def silu(value):
    return value / (1.0 + jnp.exp(-value))


def shared_kernel(count, *refs):
    pieces, (scalar, gate_w, up_w, down_w, out, rows, gate_v, up_v, down_v, sems) = (
        refs[:count],
        refs[count:],
    )
    moves = [(gate_w, gate_v), (up_w, up_v), (down_w, down_v)]
    size = pieces[0].shape[0]
    moves += [(piece, rows.at[pl.ds(i * size, size)]) for i, piece in enumerate(pieces)]
    copies = [
        pltpu.make_async_copy(src, dst, sems.at[i]) for i, (src, dst) in enumerate(moves)
    ]
    for copy in copies[3:] + copies[:3]:
        copy.start()
    for copy in copies[3:]:
        copy.wait()
    block = rows[...]
    logit = jnp.sum(
        block.astype(jnp.float32) * scalar[...].astype(jnp.float32), axis=1, keepdims=True
    )
    scale = 1.0 / (1.0 + jnp.exp(-logit))
    across = (((1,), (1,)), ((), ()))
    copies[0].wait()
    gate = lax.dot_general(block, gate_v[...], across, preferred_element_type=jnp.float32)
    copies[1].wait()
    upper = lax.dot_general(block, up_v[...], across, preferred_element_type=jnp.float32)
    hidden = (silu(gate) * upper).astype(jnp.bfloat16)
    copies[2].wait()
    result = jnp.dot(hidden, down_v[...], preferred_element_type=jnp.float32)
    out[...] = (scale * result).astype(jnp.bfloat16)


def shared_expert(pieces, scalar, gate_w, up_w, down_w):
    any_spec = pl.BlockSpec(memory_space=pl.ANY)
    vmem = pl.BlockSpec(memory_space=pltpu.VMEM)
    rows = sum(piece.shape[0] for piece in pieces)
    width = pieces[0].shape[1]
    return pl.pallas_call(
        functools.partial(shared_kernel, len(pieces)),
        out_shape=jax.ShapeDtypeStruct((rows, width), jnp.bfloat16),
        in_specs=[any_spec] * len(pieces) + [vmem] + [any_spec] * 3,
        out_specs=vmem,
        scratch_shapes=[
            pltpu.VMEM((rows, width), jnp.bfloat16),
            pltpu.VMEM(gate_w.shape, jnp.bfloat16),
            pltpu.VMEM(up_w.shape, jnp.bfloat16),
            pltpu.VMEM(down_w.shape, jnp.bfloat16),
            pltpu.SemaphoreType.DMA((3 + len(pieces),)),
        ],
        compiler_params=pltpu.CompilerParams(vmem_limit_bytes=56 * 1024 * 1024),
        cost_estimate=pl.CostEstimate(
            flops=6 * rows * gate_w.size,
            bytes_accessed=6 * gate_w.size + 4 * rows * width,
            transcendentals=rows * gate_w.shape[0],
        ),
    )(*pieces, scalar.reshape(1, -1), gate_w, up_w, down_w)


def routed_kernel(parts, extras, entries, cuts, *refs):
    count, total = len(parts), sum(parts)
    pieces, refs = refs[:total], refs[total:]
    place, row_gate = refs[:2]
    more, refs = refs[2 : 2 + extras], refs[2 + extras :]
    (gate_w, up_w, down_w), refs = refs[:3], refs[3:]
    outs, refs = refs[: sum(cuts)], refs[sum(cuts) :]
    rows, packed, gate_v, up_v, down_v, more_v, sems = refs
    moves, chunk_copies = [], []
    for c, n in enumerate(parts):
        at = 0
        chunk_copies.append(range(len(moves), len(moves) + n))
        for piece in pieces[sum(parts[:c]) : sum(parts[: c + 1])]:
            moves.append((piece, rows.at[c, pl.ds(at, piece.shape[0])]))
            at += piece.shape[0]
    moves += [(gate_w.at[0], gate_v), (up_w.at[0], up_v), (down_w.at[0], down_v)]
    at = 0
    for extra in more:
        moves.append((extra, more_v.at[pl.ds(at, extra.shape[0])]))
        at += extra.shape[0]
    copies = [
        pltpu.make_async_copy(src, dst, sems.at[i]) for i, (src, dst) in enumerate(moves)
    ]
    for copy in copies:
        copy.start()
    size = rows.shape[1]
    wanted = lax.broadcasted_iota(jnp.int32, (entries, size), 0)
    picks, weights = [], []
    for c in range(count):
        pick = jnp.where(place[c] == wanted, 1.0, 0.0)
        picks.append(pick.astype(jnp.bfloat16))
        weights.append(jnp.sum(pick * row_gate[c], axis=1, keepdims=True))
        for i in chunk_copies[c]:
            copies[i].wait()
        packed[c * entries : (c + 1) * entries, :] = jnp.dot(
            picks[c], rows[c], preferred_element_type=jnp.float32
        ).astype(jnp.bfloat16)
    copies[total].wait()
    gate = jnp.dot(packed[...], gate_v[...], preferred_element_type=jnp.float32)
    copies[total + 1].wait()
    upper = jnp.dot(packed[...], up_v[...], preferred_element_type=jnp.float32)
    hidden = (silu(gate) * upper).astype(jnp.bfloat16)
    copies[total + 2].wait()
    answer = jnp.dot(hidden, down_v[...], preferred_element_type=jnp.float32).astype(
        jnp.bfloat16
    )
    for i in range(extras):
        copies[total + 3 + i].wait()
    for c in range(count):
        scaled = answer[c * entries : (c + 1) * entries, :].astype(jnp.float32) * weights[c]
        placed = lax.dot_general(
            picks[c],
            scaled.astype(jnp.bfloat16),
            (((0,), (0,)), ((), ())),
            preferred_element_type=jnp.float32,
        )
        if c == 0 and extras:
            placed = placed + more_v[...].astype(jnp.float32)
        placed = placed.astype(jnp.bfloat16)
        cut = size // cuts[c]
        for k in range(cuts[c]):
            outs[sum(cuts[:c]) + k][...] = placed[k * cut : (k + 1) * cut, :]


def routed_expert(chunks, place, row_gate, more, gate_w, up_w, down_w, entries, cuts):
    count = len(chunks)
    parts = [len(chunk) for chunk in chunks]
    total = sum(parts)
    size = sum(piece.shape[0] for piece in chunks[0])
    width = chunks[0][0].shape[1]
    hidden = gate_w.shape[2]
    any_spec = pl.BlockSpec(memory_space=pl.ANY)
    vmem = pl.BlockSpec(memory_space=pltpu.VMEM)
    out_shape = [
        jax.ShapeDtypeStruct((size // n, width), jnp.bfloat16) for n in cuts for k in range(n)
    ]
    more_rows = sum(extra.shape[0] for extra in more) if more else 16
    outs = pl.pallas_call(
        functools.partial(routed_kernel, parts, len(more), entries, cuts),
        out_shape=out_shape,
        in_specs=[any_spec] * total + [vmem] * 2 + [any_spec] * (len(more) + 3),
        out_specs=[vmem] * sum(cuts),
        scratch_shapes=[
            pltpu.VMEM((count, size, width), jnp.bfloat16),
            pltpu.VMEM((count * entries, width), jnp.bfloat16),
            pltpu.VMEM((width, hidden), jnp.bfloat16),
            pltpu.VMEM((width, hidden), jnp.bfloat16),
            pltpu.VMEM((hidden, width), jnp.bfloat16),
            pltpu.VMEM((more_rows, width), jnp.bfloat16),
            pltpu.SemaphoreType.DMA((total + 3 + len(more),)),
        ],
        compiler_params=pltpu.CompilerParams(vmem_limit_bytes=56 * 1024 * 1024),
        cost_estimate=pl.CostEstimate(
            flops=2 * count * entries * (3 * gate_w.size + 2 * size * width),
            bytes_accessed=6 * gate_w.size + 4 * count * size * width,
            transcendentals=count * entries * hidden,
        ),
    )(*[piece for chunk in chunks for piece in chunk], place, row_gate, *more, gate_w, up_w, down_w)
    return [outs[sum(cuts[:c]) : sum(cuts[: c + 1])] for c in range(count)]


def rms_normed(stream, norm_gain):
    scale_row = lax.rsqrt(jnp.mean(stream * stream, axis=1, keepdims=True) + 1e-06)
    return (stream * scale_row * norm_gain[None, :]).astype(jnp.bfloat16)


def shards(
    resid,
    queries,
    cache_key,
    cache_value,
    page_table,
    row_request,
    row_position,
    out_proj,
    norm_gain,
    expert_gate,
    expert_up,
    expert_down,
    shared_gate,
    shared_up,
    shared_down,
    shared_scalar,
    slot_expert,
    route_expert,
    route_gate,
):
    f32, bf16, i32 = jnp.float32, jnp.bfloat16, jnp.int32
    exp_count = lax.axis_size("exp")
    req_count = lax.axis_size("req")
    slot_count = exp_count * req_count
    nc, nx, ny = CORES, exp_count // Z_CHIPS, req_count // CORES
    exp_index = lax.axis_index("exp")
    req_index = lax.axis_index("req")
    own_slot = req_index * exp_count + exp_index
    iz, ix = exp_index // nx, exp_index % nx
    ih, il = iz // 2, iz % 2
    iy, ic = req_index // nc, req_index % nc
    tok_rows, width = resid.shape
    pages_here, page_len, _ = cache_key.shape
    req_slots, max_pages = page_table.shape
    tokens = pages_here * page_len
    capacity = 3 * tok_rows * TOPK // slot_count

    zs = [(dh, dl) for dh in range(2) for dl in range(2)]

    def send(value, dh, dl, dx):
        if not (dh or dl or dx % nx):
            return value
        pairs = [
            (
                (h * 2 + l) * nx + x,
                ((h + dh) % 2 * 2 + (l + dl) % 2) * nx + (x + dx) % nx,
            )
            for h in range(2)
            for l in range(2)
            for x in range(nx)
        ]
        return lax.ppermute(value, "exp", pairs)

    def send_req(value, dy, dc):
        if not (dy % ny or dc % nc):
            return value
        pairs = [
            (y * nc + c, (y + dy) % ny * nc + (c + dc) % nc)
            for y in range(ny)
            for c in range(nc)
        ]
        return lax.ppermute(value, "req", pairs)

    def swap_y(value):
        pairs = [(y * nc + c, (y ^ 1) * nc + c) for y in range(ny) for c in range(nc)]
        return lax.ppermute(value, "req", pairs)

    tie = lax.optimization_barrier

    rel_exp = jnp.stack(
        [
            ((ih + dh) % 2 * 2 + (il + dl) % 2) * nx + (ix - dx) % nx
            for dh, dl in zs
            for dx in range(nx)
        ]
    ).astype(i32)
    rel_req = jnp.stack(
        [((iy - dy) % ny) * nc + (ic - dc) % nc for dy in range(ny) for dc in range(nc)]
    ).astype(i32)

    columns = width // exp_count
    keys = cache_key.reshape(tokens, width)
    values = cache_value.reshape(tokens, width)
    quarter_rows = out_proj.shape[0] // (2 * nc)
    quarter = lax.dynamic_slice_in_dim(
        out_proj, (iy % 2 * nc + ic) * quarter_rows, quarter_rows, 0
    )
    quarter_order = jnp.stack(
        [(iy + dy) % 2 * nc + (ic + dc) % nc for dc in range(nc) for dy in range(2)]
    ).astype(i32)
    far_queries = send(queries, 1, 0, 0)
    members = [(dl, dx) for dl in range(2) for dx in range(nx)]
    member_columns = jnp.stack(
        [
            ((ih + j) % 2 * 2 + (il + dl) % 2) * nx + (ix + dx) % nx
            for dl, dx in members
            for j in range(2)
        ]
    ).astype(i32)
    gates = jnp.transpose(route_gate)
    blocks = pack([keys, values, queries], gates, member_columns, columns)
    blocks = [send(blocks[m], 0, *members[m]) for m in range(len(members))]
    far = list(pack([far_queries], None, member_columns, columns))
    for m in range(1, len(members)):
        if m > 2:
            far[m], far[m - 2] = tie((far[m], far[m - 2]))
        far[m] = send(far[m], 0, *members[m])
    quarters = [send(quarter, 1, 0, 0)]
    page_ids = (
        rel_exp[: len(members), None] * pages_here + jnp.arange(pages_here, dtype=i32)[None, :]
    ).reshape(-1)
    hits = (page_table[None, :, :] == page_ids[:, None, None]).astype(i32)
    page_request = jnp.sum(hits * jnp.arange(req_slots, dtype=i32)[None, :, None], axis=(1, 2))
    page_slot = jnp.sum(hits * jnp.arange(max_pages, dtype=i32)[None, None, :], axis=(1, 2))
    by_place = lambda a: a.reshape(exp_count, tok_rows)[rel_exp].reshape(2, 1, -1)
    row_req, row_pos = by_place(row_request), by_place(row_position)
    gates = [block[2 * tokens + tok_rows :, :tok_rows].astype(f32) for block in blocks]
    gates = jnp.stack([g[:TOPK] + g[TOPK : 2 * TOPK] + g[2 * TOPK : 3 * TOPK] for g in gates])
    gates = gates.reshape(2, nx, TOPK, tok_rows)

    slot_ids = jnp.arange(slot_count, dtype=i32)
    own_mark = slot_ids == own_slot
    own_expert = jnp.sum(jnp.where(own_mark, slot_expert, 0))
    twins = slot_expert == own_expert
    copies = jnp.sum(twins.astype(i32))
    own_rank = jnp.sum((twins & (slot_ids < own_slot)).astype(i32))
    order = [1, 3, 2, 0]
    rel_rows = jnp.stack([rel_exp.reshape(4, nx)[i] for i in order], axis=1).reshape(-1)
    rel_slots = (rel_req[:, None] * exp_count + rel_rows[None, :]).reshape(-1)
    named = (route_expert == own_expert).reshape(slot_count, tok_rows, TOPK)[rel_slots]
    named = jnp.transpose(named, (0, 2, 1))
    chunk_rows = exp_count * tok_rows
    entries = -(-exp_count * capacity // 16) * 16
    served = jnp.any(named, axis=1) & (rel_slots % copies == own_rank)[:, None]
    served = served.reshape(ny, nc, chunk_rows)
    place = jnp.where(served, jnp.cumsum(served.astype(i32), axis=2) - 1, -1)
    place = place.reshape(ny, nc, 1, chunk_rows)

    place, named, blocks = tie((place, named, blocks))

    def attend_half(side, queries):
        return attend(
            blocks,
            queries,
            row_req[side],
            row_pos[side],
            page_request,
            page_slot,
            page_len,
            tokens,
            tok_rows,
        )

    quarters.append(swap_y(quarters[0]))
    theirs, their_level = attend_half(1, far)
    theirs, their_level, quarters = tie((theirs, their_level, quarters))
    theirs, their_level = send(theirs, 1, 0, 0), send(their_level, 1, 0, 0)
    quarters += [send_req(q, 0, dc) for dc in range(1, nc) for q in quarters[:2]]
    mine, level = attend_half(0, [])
    mine, level, gates, quarters = tie((mine, level, gates, quarters))
    gates = jnp.stack([send(gates, dh, 0, 0) for dh in range(2)])
    theirs, their_level, gates = tie((theirs, their_level, gates))

    stays, comes = {}, {}
    proj = out_proj
    for dl in (1, 0):
        stays[dl], go = project(
            dl, quarter_order, mine, level, theirs, their_level, proj, quarters, tok_rows
        )
        comes[dl] = [
            send(go[(dx - 1) * tok_rows : dx * tok_rows], 0, 0, -dx) for dx in range(1, nx)
        ]
        proj, _ = tie((proj, go))
    line = sum([come.astype(f32) for come in comes[1]], stays[1]).astype(bf16)
    comes[0], _ = tie((comes[0], line))
    line = send(line, 0, 1, 0)
    stream = sum([come.astype(f32) for come in comes[0]], resid.astype(f32) + stays[0])
    stream = stream + line.astype(f32)
    gates = jnp.stack([send_req(gates, dy, 0) for dy in range(ny)])
    stream, gates = tie((stream, gates))
    normed = rms_normed(stream, norm_gain)
    gates = jnp.stack([send_req(gates, 0, dc) for dc in range(nc)], axis=1)
    gates = gates.reshape(ny, nc, 4, nx, TOPK, tok_rows)
    gates = jnp.stack([gates[:, :, i] for i in order], axis=3)
    gates = gates.reshape(slot_count, TOPK, tok_rows)
    row_gate = jnp.sum(jnp.where(named, gates, 0.0), axis=1).reshape(ny, nc, 1, chunk_rows)

    far_line = send(normed, 1, 0, 0)
    line = [normed, send(normed, 0, 1, 0), far_line, send(far_line, 0, 1, 0)]
    over_x = {(i, dx): send(line[i], 0, 0, dx) for i in order for dx in range(1, nx)}
    over_y = {(i, dy): send_req(line[i], dy, 0) for i in order for dy in range(1, ny)}

    halves = [[line[i] for i in order]]
    shared_weights = (shared_scalar, shared_gate.T, shared_up.T, shared_down)
    shared = [shared_expert(halves[0], *shared_weights)]
    chunks = {(0, 0): join(halves[0])}
    for dc in range(1, nc):
        chunks[0, dc] = [send_req(chunks[0, 0][0], 0, dc)]
    over_x, over_y, shared, row_gate = tie((over_x, over_y, shared, row_gate))
    halves += [[over_x[i, dx] for i in order] for dx in range(1, nx)]
    joined = join(*halves[1:], *[[over_y[i, dy] for i in order] for dy in range(1, ny)])
    chunks[0, 0] += joined[: nx - 1]
    for dc in range(1, nc):
        chunks[0, dc] += [send_req(half, 0, dc) for half in joined[: nx - 1]]
    for dy, half in enumerate(joined[nx - 1 :], 1):
        chunks[dy, 0] = [half] + [send(half, 0, 0, dx) for dx in range(1, nx)]
        for dc in range(1, nc):
            chunks[dy, dc] = [send_req(half, 0, dc)]

    def answers_of(dy, dcs, more, cuts):
        return routed_expert(
            [chunks[dy, dc] for dc in dcs],
            jnp.concatenate([place[dy, dc : dc + 1] for dc in dcs]),
            jnp.concatenate([row_gate[dy, dc : dc + 1] for dc in dcs]),
            more,
            expert_gate,
            expert_up,
            expert_down,
            entries,
            cuts,
        )

    def add_up(parts):
        return sum([part.astype(f32) for part in parts[1:]], parts[0].astype(f32))

    cores = list(range(nc))
    kept, comes = {}, {}
    cuts = [slice(0, 3 * tok_rows), slice(3 * tok_rows, 4 * tok_rows)]
    for dy in range(ny - 1):
        answers = answers_of(dy, cores, [], [nx] * nc)
        if dy:
            answers, comes[dy - 1] = tie((answers, comes[dy - 1]))
        others = [[send_req(part, 0, -dc) for part in answers[dc][::-1]][::-1] for dc in cores[1:]]
        parts = [answers[0]] + others
        if dy:
            following = answers[0][0]
        else:
            for dx in range(1, nx):
                halves[dx], _ = tie((halves[dx], answers[0]))
                shared.append(shared_expert(halves[dx], *shared_weights))
            parts.append(shared)
            following = shared[-1]
        chunks[dy + 1, 0], _ = tie((chunks[dy + 1, 0], following))
        for dc in range(1, nc):
            chunks[dy + 1, dc] += [send_req(part, 0, dc) for part in chunks[dy + 1, 0][1:]]
        gone = [add_up([part[dx] for part in parts]).astype(bf16) for dx in range(1, nx)]
        kept[dy] = [part[0] for part in parts]
        waiting = [go[cuts[1]] for go in gone]
        comes[dy] = [
            [send(go[rows], 0, 0, -dx) for dx, go in enumerate(gone, 1)]
            for rows in (cuts if dy + 2 < ny else cuts[:1])
        ]
        following = [chunks[dy + 1, dc] for dc in cores]
        following, _ = tie((following, gone))
        for dc in cores:
            chunks[dy + 1, dc] = following[dc]
    end = ny - 1
    answers = answers_of(end, cores, [], [4 * nx] + [nx] * (nc - 1))
    answers, comes, kept = tie((answers, comes, kept))
    answer = answers[0]
    others = [[send_req(part, 0, -dc) for part in answers[dc][::-1]][::-1] for dc in cores[1:]]

    turns = [1, 2, 0, 3]
    block = lambda a, p: a[p * tok_rows : (p + 1) * tok_rows]
    last = {}
    for p in turns:
        gone = [
            add_up([answer[4 * dx + p]] + [block(other[dx], p) for other in others])
            for dx in range(1, nx)
        ]
        gone = [go.astype(bf16) for go in gone]
        last[p] = [send(go, 0, 0, -dx) for dx, go in enumerate(gone, 1)]
        others, _ = tie((others, gone))
    waiting, _ = tie((waiting, gone))
    comes[end - 1].append([send(go, 0, 0, -dx) for dx, go in enumerate(waiting, 1)])

    def line_of(dy, p):
        if dy < end:
            arrived = [come if p == 3 else block(come, p) for come in comes[dy][p // 3]]
            return add_up([block(part, p) for part in kept[dy]] + arrived)
        return add_up([answer[p]] + [block(other[0], p) for other in others] + last[p])

    home, near = {}, {}
    for turn, p in enumerate(turns):
        goes = [line_of(dy, p).astype(bf16) for dy in range(1, ny)]
        home[p] = [send_req(go, -dy, 0) for dy, go in enumerate(goes, 1)]
        if turn == 1:
            go = add_up([line_of(0, 1)] + home[1]).astype(bf16)
            near[1] = send(go, 0, 1, 0)
            goes.append(go)
        if turn == 2:
            go = add_up([line_of(0, 2)] + home[2] + [near[1]]).astype(bf16)
            far = send(go, 1, 0, 0)
            goes.append(go)
        if turn + 1 < len(turns):
            after = turns[turn + 1]
            last[after], _ = tie((last[after], goes))
    near[0] = send(add_up([line_of(0, 0)] + home[0]).astype(bf16), 0, 1, 0)
    total = add_up([stream, line_of(0, 3)] + home[3] + [near[0], far])
    return total.astype(bf16)


def solution(mesh):
    placed = (
        P(("req", "exp"), None),
        P(("req", "exp"), None),
        P(("req", "exp"), None, None),
        P(("req", "exp"), None, None),
        P("req", None),
        P("req"),
        P("req"),
        P("exp", None),
        P(),
        P(("req", "exp"), None, None),
        P(("req", "exp"), None, None),
        P(("req", "exp"), None, None),
        P(None, "exp"),
        P(None, "exp"),
        P("exp", None),
        P(),
        P(),
        P(),
        P(("req", "exp"), None),
    )
    return jax.shard_map(
        shards, mesh=mesh, in_specs=placed, out_specs=P(("req", "exp"), None), check_vma=False
    )
```

```python
import functools

import jax
import jax.numpy as jnp
from jax import lax
from jax.experimental import pallas as pl
from jax.experimental.pallas import tpu as pltpu
from jax.sharding import PartitionSpec as P

HEAD_DIM = 128
TOPK = 4
CORES = 2
Z_CHIPS = 4


def pack_kernel(members, parts, columns, order, *refs):
    sources, refs = refs[:parts], refs[parts:]
    gates, blocks, sems = refs[:-1 - members], refs[-1 - members : -1], refs[-1]
    copies = []
    for m in range(members):
        at = 0
        for source in sources:
            rows = source.shape[0]
            for j in range(2):
                place = pl.multiple_of(order[2 * m + j] * columns, columns)
                copies.append(
                    pltpu.make_async_copy(
                        source.at[:, pl.ds(place, columns)],
                        blocks[m].at[pl.ds(at, rows), pl.ds(j * columns, columns)],
                        sems.at[len(copies)],
                    )
                )
            at += rows
    for copy in copies:
        copy.start()
    if gates:
        weights = gates[0][...]
        high = weights.astype(jnp.bfloat16).astype(jnp.float32)
        middle = (weights - high).astype(jnp.bfloat16).astype(jnp.float32)
        low = weights - high - middle
        weights = jnp.concatenate([high, middle, low, jnp.zeros_like(low)], axis=0)
        for m in range(members):
            blocks[m][at:, : weights.shape[1]] = weights.astype(jnp.bfloat16)
    for copy in copies:
        copy.wait()


def pack(parts, gates, order, columns):
    members = order.shape[0] // 2
    rows = sum(p.shape[0] for p in parts) + (0 if gates is None else 4 * gates.shape[0])
    vmem = pl.BlockSpec(memory_space=pltpu.VMEM)
    in_specs = [pl.BlockSpec(memory_space=pltpu.SMEM)]
    in_specs += [pl.BlockSpec(memory_space=pl.ANY)] * len(parts)
    operands = list(parts)
    if gates is not None:
        in_specs.append(vmem)
        operands.append(gates)
    return pl.pallas_call(
        functools.partial(pack_kernel, members, len(parts), columns),
        out_shape=[jax.ShapeDtypeStruct((rows, 2 * columns), parts[0].dtype)] * members,
        in_specs=in_specs,
        out_specs=[vmem] * members,
        scratch_shapes=[pltpu.SemaphoreType.DMA((2 * members * len(parts),))],
        compiler_params=pltpu.CompilerParams(vmem_limit_bytes=56 * 1024 * 1024),
        cost_estimate=pl.CostEstimate(
            flops=0, bytes_accessed=8 * members * rows * columns, transcendentals=0
        ),
    )(order, *operands)


def attend_kernel(members, tokens, tok_rows, page_len, scale, page_req, page_slot, *refs):
    blocks, refs = refs[:members], refs[members:]
    if len(refs) > 4:
        query, refs = [q[...] for q in refs[:members]], refs[members:]
    else:
        query = [block[2 * tokens : 2 * tokens + tok_rows, :] for block in blocks]
    request, position, out, level = refs
    request, position = request[...], position[...]
    keys = jnp.concatenate([block[:tokens, :] for block in blocks], axis=0)
    values = jnp.concatenate([block[tokens : 2 * tokens, :] for block in blocks], axis=0)
    query = jnp.concatenate(query, axis=0)
    scores = (
        lax.dot_general(keys, query, (((1,), (1,)), ((), ())), preferred_element_type=jnp.float32)
        * scale
    )
    token = lax.broadcasted_iota(jnp.int32, (page_len, query.shape[0]), 0)
    visible = jnp.concatenate(
        [
            (request == page_req[page]) & (token + page_slot[page] * page_len <= position)
            for page in range(members * tokens // page_len)
        ],
        axis=0,
    )
    scores = jnp.where(visible, scores, -1e30)
    top = jnp.max(scores, axis=0, keepdims=True)
    weights = jnp.where(visible, jnp.exp(scores - top), 0.0)
    total = jnp.sum(weights, axis=0, keepdims=True)
    summed = lax.dot_general(
        values,
        weights.astype(jnp.bfloat16),
        (((0,), (0,)), ((), ())),
        preferred_element_type=jnp.float32,
    )
    seen = total > 0.0
    total = jnp.where(seen, total, 1.0)
    out[...] = (summed / total).astype(jnp.bfloat16)
    level[0] = jnp.where(seen, top + jnp.log(total), -1e30)


def attend(blocks, far, row_req, row_pos, page_req, page_slot, page_len, tokens, tok_rows):
    members, rows = len(blocks), row_req.shape[1]
    block_rows, columns = blocks[0].shape
    heads = columns // HEAD_DIM
    by_head = lambda n: pl.BlockSpec((n, HEAD_DIM), lambda h, *_: (0, h))
    whole = pl.BlockSpec((1, rows), lambda h, *_: (0, 0))
    return pl.pallas_call(
        functools.partial(
            attend_kernel, members, tokens, tok_rows, page_len, HEAD_DIM ** (-0.5)
        ),
        out_shape=[
            jax.ShapeDtypeStruct((columns, rows), jnp.bfloat16),
            jax.ShapeDtypeStruct((heads, 1, rows), jnp.float32),
        ],
        grid_spec=pltpu.PrefetchScalarGridSpec(
            num_scalar_prefetch=2,
            grid=(heads,),
            in_specs=[by_head(block_rows)] * members + [by_head(tok_rows)] * len(far) + [whole] * 2,
            out_specs=[
                pl.BlockSpec((HEAD_DIM, rows), lambda h, *_: (h, 0)),
                pl.BlockSpec((1, 1, rows), lambda h, *_: (h, 0, 0)),
            ],
        ),
        compiler_params=pltpu.CompilerParams(vmem_limit_bytes=56 * 1024 * 1024),
        cost_estimate=pl.CostEstimate(
            flops=4 * rows * members * tokens * columns,
            bytes_accessed=2 * members * (block_rows + tok_rows) * columns,
            transcendentals=rows * members * tokens * heads,
        ),
    )(page_req, page_slot, *blocks, *far, row_req, row_pos)


def project_kernel(order, mine, mine_level, theirs, their_level, own, *refs):
    quarters, (stay, go, proj) = refs[:-3], refs[-3:]
    rows, size = own.shape[0], quarters[0].shape[0]
    proj[:rows, :] = own[...]
    for k, quarter in enumerate(quarters):
        at = pl.multiple_of(rows + order[k] * size, size)
        proj[pl.ds(at, size), :] = quarter[...]
    parts = []
    heads = mine.shape[0] // HEAD_DIM
    for head in range(heads):
        twin = (head + heads // 2) % heads
        dims = slice(head * HEAD_DIM, (head + 1) * HEAD_DIM)
        twin_dims = slice(twin * HEAD_DIM, (twin + 1) * HEAD_DIM)
        share = 1.0 / (1.0 + jnp.exp(their_level[twin] - mine_level[head]))
        other = 1.0 / (1.0 + jnp.exp(mine_level[head] - their_level[twin]))
        both = share * mine[dims, :].astype(jnp.float32) + other * theirs[
            twin_dims, :
        ].astype(jnp.float32)
        parts.append(both.astype(jnp.bfloat16))
    attention = jnp.concatenate(parts, axis=0)
    mixed = lax.dot_general(
        attention, proj[...], (((0,), (0,)), ((), ())), preferred_element_type=jnp.float32
    )
    kept = stay.shape[0]
    stay[...] = mixed[:kept, :]
    go[...] = mixed[kept:, :].astype(jnp.bfloat16)


def project(place, order, mine, mine_level, theirs, their_level, own, quarters, tok_rows):
    dims, width = mine.shape[0], own.shape[1]
    heads = dims // HEAD_DIM
    size = mine.shape[1] // 2
    whole = lambda a: pl.BlockSpec(a.shape, lambda i, order: (0, 0))
    values = pl.BlockSpec((dims, size), lambda i, order: (0, place))
    levels = pl.BlockSpec((heads, 1, size), lambda i, order: (0, 0, place))
    return pl.pallas_call(
        project_kernel,
        out_shape=[
            jax.ShapeDtypeStruct((tok_rows, width), jnp.float32),
            jax.ShapeDtypeStruct((size - tok_rows, width), jnp.bfloat16),
        ],
        grid_spec=pltpu.PrefetchScalarGridSpec(
            num_scalar_prefetch=1,
            grid=(1,),
            in_specs=[values, levels, values, levels, whole(own)] + [whole(q) for q in quarters],
            out_specs=[
                pl.BlockSpec((tok_rows, width), lambda i, order: (0, 0)),
                pl.BlockSpec((size - tok_rows, width), lambda i, order: (0, 0)),
            ],
            scratch_shapes=[pltpu.VMEM((dims, width), jnp.bfloat16)],
        ),
        compiler_params=pltpu.CompilerParams(vmem_limit_bytes=32 * 1024 * 1024),
        cost_estimate=pl.CostEstimate(
            flops=2 * size * dims * width,
            bytes_accessed=2 * (2 * dims * size + dims * width + 3 * size * width),
            transcendentals=2 * size * heads,
        ),
    )(order, mine, mine_level, theirs, their_level, own, *quarters)


def join_kernel(sizes, *refs):
    parts, outs = refs[: sum(sizes)], refs[sum(sizes) :]
    for n, out in enumerate(outs):
        rows = out.shape[0] // sizes[n]
        for i in range(sizes[n]):
            out[i * rows : (i + 1) * rows, :] = parts[sum(sizes[:n]) + i][...]


def join(*groups):
    rows, width = groups[0][0].shape
    sizes = [len(group) for group in groups]
    vmem = pl.BlockSpec(memory_space=pltpu.VMEM)
    return pl.pallas_call(
        functools.partial(join_kernel, sizes),
        out_shape=[jax.ShapeDtypeStruct((n * rows, width), groups[0][0].dtype) for n in sizes],
        in_specs=[vmem] * sum(sizes),
        out_specs=[vmem] * len(sizes),
        cost_estimate=pl.CostEstimate(
            flops=0, bytes_accessed=4 * sum(sizes) * rows * width, transcendentals=0
        ),
    )(*[part for group in groups for part in group])


def silu(value):
    return value / (1.0 + jnp.exp(-value))


def shared_kernel(count, *refs):
    pieces, (scalar, gate_w, up_w, down_w, out, rows, gate_v, up_v, down_v, sems) = (
        refs[:count],
        refs[count:],
    )
    moves = [(gate_w, gate_v), (up_w, up_v), (down_w, down_v)]
    size = pieces[0].shape[0]
    moves += [(piece, rows.at[pl.ds(i * size, size)]) for i, piece in enumerate(pieces)]
    copies = [
        pltpu.make_async_copy(src, dst, sems.at[i]) for i, (src, dst) in enumerate(moves)
    ]
    for copy in copies[3:] + copies[:3]:
        copy.start()
    for copy in copies[3:]:
        copy.wait()
    block = rows[...]
    logit = jnp.sum(
        block.astype(jnp.float32) * scalar[...].astype(jnp.float32), axis=1, keepdims=True
    )
    scale = 1.0 / (1.0 + jnp.exp(-logit))
    across = (((1,), (1,)), ((), ()))
    copies[0].wait()
    gate = lax.dot_general(block, gate_v[...], across, preferred_element_type=jnp.float32)
    copies[1].wait()
    upper = lax.dot_general(block, up_v[...], across, preferred_element_type=jnp.float32)
    hidden = (silu(gate) * upper).astype(jnp.bfloat16)
    copies[2].wait()
    result = jnp.dot(hidden, down_v[...], preferred_element_type=jnp.float32)
    out[...] = (scale * result).astype(jnp.bfloat16)


def shared_expert(pieces, scalar, gate_w, up_w, down_w):
    any_spec = pl.BlockSpec(memory_space=pl.ANY)
    vmem = pl.BlockSpec(memory_space=pltpu.VMEM)
    rows = sum(piece.shape[0] for piece in pieces)
    width = pieces[0].shape[1]
    return pl.pallas_call(
        functools.partial(shared_kernel, len(pieces)),
        out_shape=jax.ShapeDtypeStruct((rows, width), jnp.bfloat16),
        in_specs=[any_spec] * len(pieces) + [vmem] + [any_spec] * 3,
        out_specs=vmem,
        scratch_shapes=[
            pltpu.VMEM((rows, width), jnp.bfloat16),
            pltpu.VMEM(gate_w.shape, jnp.bfloat16),
            pltpu.VMEM(up_w.shape, jnp.bfloat16),
            pltpu.VMEM(down_w.shape, jnp.bfloat16),
            pltpu.SemaphoreType.DMA((3 + len(pieces),)),
        ],
        compiler_params=pltpu.CompilerParams(vmem_limit_bytes=56 * 1024 * 1024),
        cost_estimate=pl.CostEstimate(
            flops=6 * rows * gate_w.size,
            bytes_accessed=6 * gate_w.size + 4 * rows * width,
            transcendentals=rows * gate_w.shape[0],
        ),
    )(*pieces, scalar.reshape(1, -1), gate_w, up_w, down_w)


def routed_kernel(parts, extras, entries, cuts, *refs):
    count, total = len(parts), sum(parts)
    pieces, refs = refs[:total], refs[total:]
    place, row_gate = refs[:2]
    more, refs = refs[2 : 2 + extras], refs[2 + extras :]
    (gate_w, up_w, down_w), refs = refs[:3], refs[3:]
    outs, refs = refs[: sum(cuts)], refs[sum(cuts) :]
    rows, packed, gate_v, up_v, down_v, more_v, sems = refs
    moves, chunk_copies = [], []
    for c, n in enumerate(parts):
        at = 0
        chunk_copies.append(range(len(moves), len(moves) + n))
        for piece in pieces[sum(parts[:c]) : sum(parts[: c + 1])]:
            moves.append((piece, rows.at[c, pl.ds(at, piece.shape[0])]))
            at += piece.shape[0]
    moves += [(gate_w.at[0], gate_v), (up_w.at[0], up_v), (down_w.at[0], down_v)]
    at = 0
    for extra in more:
        moves.append((extra, more_v.at[pl.ds(at, extra.shape[0])]))
        at += extra.shape[0]
    copies = [
        pltpu.make_async_copy(src, dst, sems.at[i]) for i, (src, dst) in enumerate(moves)
    ]
    for copy in copies:
        copy.start()
    size = rows.shape[1]
    wanted = lax.broadcasted_iota(jnp.int32, (entries, size), 0)
    picks, weights = [], []
    for c in range(count):
        pick = jnp.where(place[c] == wanted, 1.0, 0.0)
        picks.append(pick.astype(jnp.bfloat16))
        weights.append(jnp.sum(pick * row_gate[c], axis=1, keepdims=True))
        for i in chunk_copies[c]:
            copies[i].wait()
        packed[c * entries : (c + 1) * entries, :] = jnp.dot(
            picks[c], rows[c], preferred_element_type=jnp.float32
        ).astype(jnp.bfloat16)
    copies[total].wait()
    gate = jnp.dot(packed[...], gate_v[...], preferred_element_type=jnp.float32)
    copies[total + 1].wait()
    upper = jnp.dot(packed[...], up_v[...], preferred_element_type=jnp.float32)
    hidden = (silu(gate) * upper).astype(jnp.bfloat16)
    copies[total + 2].wait()
    answer = jnp.dot(hidden, down_v[...], preferred_element_type=jnp.float32).astype(
        jnp.bfloat16
    )
    for i in range(extras):
        copies[total + 3 + i].wait()
    for c in range(count):
        scaled = answer[c * entries : (c + 1) * entries, :].astype(jnp.float32) * weights[c]
        placed = lax.dot_general(
            picks[c],
            scaled.astype(jnp.bfloat16),
            (((0,), (0,)), ((), ())),
            preferred_element_type=jnp.float32,
        )
        if c == 0 and extras:
            placed = placed + more_v[...].astype(jnp.float32)
        placed = placed.astype(jnp.bfloat16)
        cut = size // cuts[c]
        for k in range(cuts[c]):
            outs[sum(cuts[:c]) + k][...] = placed[k * cut : (k + 1) * cut, :]


def routed_expert(chunks, place, row_gate, more, gate_w, up_w, down_w, entries, cuts):
    count = len(chunks)
    parts = [len(chunk) for chunk in chunks]
    total = sum(parts)
    size = sum(piece.shape[0] for piece in chunks[0])
    width = chunks[0][0].shape[1]
    hidden = gate_w.shape[2]
    any_spec = pl.BlockSpec(memory_space=pl.ANY)
    vmem = pl.BlockSpec(memory_space=pltpu.VMEM)
    out_shape = [
        jax.ShapeDtypeStruct((size // n, width), jnp.bfloat16) for n in cuts for k in range(n)
    ]
    more_rows = sum(extra.shape[0] for extra in more) if more else 16
    outs = pl.pallas_call(
        functools.partial(routed_kernel, parts, len(more), entries, cuts),
        out_shape=out_shape,
        in_specs=[any_spec] * total + [vmem] * 2 + [any_spec] * (len(more) + 3),
        out_specs=[vmem] * sum(cuts),
        scratch_shapes=[
            pltpu.VMEM((count, size, width), jnp.bfloat16),
            pltpu.VMEM((count * entries, width), jnp.bfloat16),
            pltpu.VMEM((width, hidden), jnp.bfloat16),
            pltpu.VMEM((width, hidden), jnp.bfloat16),
            pltpu.VMEM((hidden, width), jnp.bfloat16),
            pltpu.VMEM((more_rows, width), jnp.bfloat16),
            pltpu.SemaphoreType.DMA((total + 3 + len(more),)),
        ],
        compiler_params=pltpu.CompilerParams(vmem_limit_bytes=56 * 1024 * 1024),
        cost_estimate=pl.CostEstimate(
            flops=2 * count * entries * (3 * gate_w.size + 2 * size * width),
            bytes_accessed=6 * gate_w.size + 4 * count * size * width,
            transcendentals=count * entries * hidden,
        ),
    )(*[piece for chunk in chunks for piece in chunk], place, row_gate, *more, gate_w, up_w, down_w)
    return [outs[sum(cuts[:c]) : sum(cuts[: c + 1])] for c in range(count)]


def rms_normed(stream, norm_gain):
    scale_row = lax.rsqrt(jnp.mean(stream * stream, axis=1, keepdims=True) + 1e-06)
    return (stream * scale_row * norm_gain[None, :]).astype(jnp.bfloat16)


def shards(
    resid,
    queries,
    cache_key,
    cache_value,
    page_table,
    row_request,
    row_position,
    out_proj,
    norm_gain,
    expert_gate,
    expert_up,
    expert_down,
    shared_gate,
    shared_up,
    shared_down,
    shared_scalar,
    slot_expert,
    route_expert,
    route_gate,
):
    f32, bf16, i32 = jnp.float32, jnp.bfloat16, jnp.int32
    exp_count = lax.axis_size("exp")
    req_count = lax.axis_size("req")
    slot_count = exp_count * req_count
    nc, nx, ny = CORES, exp_count // Z_CHIPS, req_count // CORES
    exp_index = lax.axis_index("exp")
    req_index = lax.axis_index("req")
    own_slot = req_index * exp_count + exp_index
    iz, ix = exp_index // nx, exp_index % nx
    ih, il = iz // 2, iz % 2
    iy, ic = req_index // nc, req_index % nc
    tok_rows, width = resid.shape
    pages_here, page_len, _ = cache_key.shape
    req_slots, max_pages = page_table.shape
    tokens = pages_here * page_len
    capacity = 3 * tok_rows * TOPK // slot_count

    zs = [(dh, dl) for dh in range(2) for dl in range(2)]

    def send(value, dh, dl, dx):
        if not (dh or dl or dx % nx):
            return value
        pairs = [
            (
                (h * 2 + l) * nx + x,
                ((h + dh) % 2 * 2 + (l + dl) % 2) * nx + (x + dx) % nx,
            )
            for h in range(2)
            for l in range(2)
            for x in range(nx)
        ]
        return lax.ppermute(value, "exp", pairs)

    def send_req(value, dy, dc):
        if not (dy % ny or dc % nc):
            return value
        pairs = [
            (y * nc + c, (y + dy) % ny * nc + (c + dc) % nc)
            for y in range(ny)
            for c in range(nc)
        ]
        return lax.ppermute(value, "req", pairs)

    def swap_y(value):
        pairs = [(y * nc + c, (y ^ 1) * nc + c) for y in range(ny) for c in range(nc)]
        return lax.ppermute(value, "req", pairs)

    tie = lax.optimization_barrier

    rel_exp = jnp.stack(
        [
            ((ih + dh) % 2 * 2 + (il + dl) % 2) * nx + (ix - dx) % nx
            for dh, dl in zs
            for dx in range(nx)
        ]
    ).astype(i32)
    rel_req = jnp.stack(
        [((iy - dy) % ny) * nc + (ic - dc) % nc for dy in range(ny) for dc in range(nc)]
    ).astype(i32)

    columns = width // exp_count
    keys = cache_key.reshape(tokens, width)
    values = cache_value.reshape(tokens, width)
    quarter_rows = out_proj.shape[0] // (2 * nc)
    quarter = lax.dynamic_slice_in_dim(
        out_proj, (iy % 2 * nc + ic) * quarter_rows, quarter_rows, 0
    )
    quarter_order = jnp.stack(
        [(iy + dy) % 2 * nc + (ic + dc) % nc for dc in range(nc) for dy in range(2)]
    ).astype(i32)
    far_queries = send(queries, 1, 0, 0)
    members = [(dl, dx) for dl in range(2) for dx in range(nx)]
    member_columns = jnp.stack(
        [
            ((ih + j) % 2 * 2 + (il + dl) % 2) * nx + (ix + dx) % nx
            for dl, dx in members
            for j in range(2)
        ]
    ).astype(i32)
    gates = jnp.transpose(route_gate)
    blocks = pack([keys, values, queries], gates, member_columns, columns)
    blocks = [send(blocks[m], 0, *members[m]) for m in range(len(members))]
    far = list(pack([far_queries], None, member_columns, columns))
    for m in range(1, len(members)):
        if m > 2:
            far[m], far[m - 2] = tie((far[m], far[m - 2]))
        far[m] = send(far[m], 0, *members[m])
    quarters = [send(quarter, 1, 0, 0)]
    page_ids = (
        rel_exp[: len(members), None] * pages_here + jnp.arange(pages_here, dtype=i32)[None, :]
    ).reshape(-1)
    hits = (page_table[None, :, :] == page_ids[:, None, None]).astype(i32)
    page_request = jnp.sum(hits * jnp.arange(req_slots, dtype=i32)[None, :, None], axis=(1, 2))
    page_slot = jnp.sum(hits * jnp.arange(max_pages, dtype=i32)[None, None, :], axis=(1, 2))
    by_place = lambda a: a.reshape(exp_count, tok_rows)[rel_exp].reshape(2, 1, -1)
    row_req, row_pos = by_place(row_request), by_place(row_position)
    gates = [block[2 * tokens + tok_rows :, :tok_rows].astype(f32) for block in blocks]
    gates = jnp.stack([g[:TOPK] + g[TOPK : 2 * TOPK] + g[2 * TOPK : 3 * TOPK] for g in gates])
    gates = gates.reshape(2, nx, TOPK, tok_rows)

    slot_ids = jnp.arange(slot_count, dtype=i32)
    own_mark = slot_ids == own_slot
    own_expert = jnp.sum(jnp.where(own_mark, slot_expert, 0))
    twins = slot_expert == own_expert
    copies = jnp.sum(twins.astype(i32))
    own_rank = jnp.sum((twins & (slot_ids < own_slot)).astype(i32))
    order = [1, 3, 2, 0]
    rel_rows = jnp.stack([rel_exp.reshape(4, nx)[i] for i in order], axis=1).reshape(-1)
    rel_slots = (rel_req[:, None] * exp_count + rel_rows[None, :]).reshape(-1)
    named = (route_expert == own_expert).reshape(slot_count, tok_rows, TOPK)[rel_slots]
    named = jnp.transpose(named, (0, 2, 1))
    chunk_rows = exp_count * tok_rows
    entries = -(-exp_count * capacity // 16) * 16
    served = jnp.any(named, axis=1) & (rel_slots % copies == own_rank)[:, None]
    served = served.reshape(ny, nc, chunk_rows)
    place = jnp.where(served, jnp.cumsum(served.astype(i32), axis=2) - 1, -1)
    place = place.reshape(ny, nc, 1, chunk_rows)

    place, named, blocks = tie((place, named, blocks))

    def attend_half(side, queries):
        return attend(
            blocks,
            queries,
            row_req[side],
            row_pos[side],
            page_request,
            page_slot,
            page_len,
            tokens,
            tok_rows,
        )

    quarters.append(swap_y(quarters[0]))
    theirs, their_level = attend_half(1, far)
    theirs, their_level, quarters = tie((theirs, their_level, quarters))
    theirs, their_level = send(theirs, 1, 0, 0), send(their_level, 1, 0, 0)
    quarters += [send_req(q, 0, dc) for dc in range(1, nc) for q in quarters[:2]]
    mine, level = attend_half(0, [])
    mine, level, gates, quarters = tie((mine, level, gates, quarters))
    gates = jnp.stack([send(gates, dh, 0, 0) for dh in range(2)])
    theirs, their_level, gates = tie((theirs, their_level, gates))

    stays, comes = {}, {}
    proj = out_proj
    for dl in (1, 0):
        stays[dl], go = project(
            dl, quarter_order, mine, level, theirs, their_level, proj, quarters, tok_rows
        )
        comes[dl] = [
            send(go[(dx - 1) * tok_rows : dx * tok_rows], 0, 0, -dx) for dx in range(1, nx)
        ]
        proj, _ = tie((proj, go))
    line = sum([come.astype(f32) for come in comes[1]], stays[1]).astype(bf16)
    comes[0], _ = tie((comes[0], line))
    line = send(line, 0, 1, 0)
    stream = sum([come.astype(f32) for come in comes[0]], resid.astype(f32) + stays[0])
    stream = stream + line.astype(f32)
    gates = jnp.stack([send_req(gates, dy, 0) for dy in range(ny)])
    stream, gates = tie((stream, gates))
    normed = rms_normed(stream, norm_gain)
    gates = jnp.stack([send_req(gates, 0, dc) for dc in range(nc)], axis=1)
    gates = gates.reshape(ny, nc, 4, nx, TOPK, tok_rows)
    gates = jnp.stack([gates[:, :, i] for i in order], axis=3)
    gates = gates.reshape(slot_count, TOPK, tok_rows)
    row_gate = jnp.sum(jnp.where(named, gates, 0.0), axis=1).reshape(ny, nc, 1, chunk_rows)

    far_line = send(normed, 1, 0, 0)
    line = [normed, send(normed, 0, 1, 0), far_line, send(far_line, 0, 1, 0)]
    over_x = {(i, dx): send(line[i], 0, 0, dx) for i in order for dx in range(1, nx)}
    over_y = {(i, dy): send_req(line[i], dy, 0) for i in order for dy in range(1, ny)}

    halves = [[line[i] for i in order]]
    shared_weights = (shared_scalar, shared_gate.T, shared_up.T, shared_down)
    shared = [shared_expert(halves[0], *shared_weights)]
    chunks = {(0, 0): join(halves[0])}
    for dc in range(1, nc):
        chunks[0, dc] = [send_req(chunks[0, 0][0], 0, dc)]
    over_x, over_y, shared, row_gate = tie((over_x, over_y, shared, row_gate))
    halves += [[over_x[i, dx] for i in order] for dx in range(1, nx)]
    joined = join(*halves[1:], *[[over_y[i, dy] for i in order] for dy in range(1, ny)])
    chunks[0, 0] += joined[: nx - 1]
    for dc in range(1, nc):
        chunks[0, dc] += [send_req(half, 0, dc) for half in joined[: nx - 1]]
    for dy, half in enumerate(joined[nx - 1 :], 1):
        chunks[dy, 0] = [half] + [send(half, 0, 0, dx) for dx in range(1, nx)]
        for dc in range(1, nc):
            chunks[dy, dc] = [send_req(half, 0, dc)]

    def answers_of(dy, dcs, more, cuts):
        return routed_expert(
            [chunks[dy, dc] for dc in dcs],
            jnp.concatenate([place[dy, dc : dc + 1] for dc in dcs]),
            jnp.concatenate([row_gate[dy, dc : dc + 1] for dc in dcs]),
            more,
            expert_gate,
            expert_up,
            expert_down,
            entries,
            cuts,
        )

    def add_up(parts):
        return sum([part.astype(f32) for part in parts[1:]], parts[0].astype(f32))

    cores = list(range(nc))
    kept, comes = {}, {}
    cuts = [slice(0, 3 * tok_rows), slice(3 * tok_rows, 4 * tok_rows)]
    for dy in range(ny - 1):
        answers = answers_of(dy, cores, [], [nx] * nc)
        if dy:
            answers, comes[dy - 1] = tie((answers, comes[dy - 1]))
        others = [[send_req(part, 0, -dc) for part in answers[dc][::-1]][::-1] for dc in cores[1:]]
        parts = [answers[0]] + others
        if dy:
            following = answers[0][0]
        else:
            for dx in range(1, nx):
                halves[dx], _ = tie((halves[dx], answers[0]))
                shared.append(shared_expert(halves[dx], *shared_weights))
            parts.append(shared)
            following = shared[-1]
        chunks[dy + 1, 0], _ = tie((chunks[dy + 1, 0], following))
        for dc in range(1, nc):
            chunks[dy + 1, dc] += [send_req(part, 0, dc) for part in chunks[dy + 1, 0][1:]]
        gone = [add_up([part[dx] for part in parts]).astype(bf16) for dx in range(1, nx)]
        kept[dy] = [part[0] for part in parts]
        waiting = [go[cuts[1]] for go in gone]
        comes[dy] = [
            [send(go[rows], 0, 0, -dx) for dx, go in enumerate(gone, 1)]
            for rows in (cuts if dy + 2 < ny else cuts[:1])
        ]
        following = [chunks[dy + 1, dc] for dc in cores]
        following, _ = tie((following, gone))
        for dc in cores:
            chunks[dy + 1, dc] = following[dc]
    end = ny - 1
    answers = answers_of(end, cores, [], [4 * nx] + [nx] * (nc - 1))
    answers, comes, kept = tie((answers, comes, kept))
    answer = answers[0]
    others = [[send_req(part, 0, -dc) for part in answers[dc][::-1]][::-1] for dc in cores[1:]]

    turns = [1, 2, 0, 3]
    block = lambda a, p: a[p * tok_rows : (p + 1) * tok_rows]
    last = {}
    for p in turns:
        gone = [
            add_up([answer[4 * dx + p]] + [block(other[dx], p) for other in others])
            for dx in range(1, nx)
        ]
        gone = [go.astype(bf16) for go in gone]
        last[p] = [send(go, 0, 0, -dx) for dx, go in enumerate(gone, 1)]
        others, _ = tie((others, gone))
    waiting, _ = tie((waiting, gone))
    comes[end - 1].append([send(go, 0, 0, -dx) for dx, go in enumerate(waiting, 1)])

    def line_of(dy, p):
        if dy < end:
            arrived = [come if p == 3 else block(come, p) for come in comes[dy][p // 3]]
            return add_up([block(part, p) for part in kept[dy]] + arrived)
        return add_up([answer[p]] + [block(other[0], p) for other in others] + last[p])

    home, near = {}, {}
    for turn, p in enumerate(turns):
        goes = [line_of(dy, p).astype(bf16) for dy in range(1, ny)]
        home[p] = [send_req(go, -dy, 0) for dy, go in enumerate(goes, 1)]
        if turn == 1:
            go = add_up([line_of(0, 1)] + home[1]).astype(bf16)
            near[1] = send(go, 0, 1, 0)
            goes.append(go)
        if turn + 1 < len(turns):
            after = turns[turn + 1]
            last[after], _ = tie((last[after], goes))
    far = add_up([line_of(0, 2)] + home[2] + [near[1]]).astype(bf16)
    home[0], _ = tie((home[0], far))
    far = send(far, 1, 0, 0)
    near[0] = send(add_up([line_of(0, 0)] + home[0]).astype(bf16), 0, 1, 0)
    total = add_up([stream, line_of(0, 3)] + home[3] + [near[0], far])
    return total.astype(bf16)


def solution(mesh):
    placed = (
        P(("req", "exp"), None),
        P(("req", "exp"), None),
        P(("req", "exp"), None, None),
        P(("req", "exp"), None, None),
        P("req", None),
        P("req"),
        P("req"),
        P("exp", None),
        P(),
        P(("req", "exp"), None, None),
        P(("req", "exp"), None, None),
        P(("req", "exp"), None, None),
        P(None, "exp"),
        P(None, "exp"),
        P("exp", None),
        P(),
        P(),
        P(),
        P(("req", "exp"), None),
    )
    return jax.shard_map(
        shards, mesh=mesh, in_specs=placed, out_specs=P(("req", "exp"), None), check_vma=False
    )
```

```python
import functools

import jax
import jax.numpy as jnp
from jax import lax
from jax.experimental import pallas as pl
from jax.experimental.pallas import tpu as pltpu
from jax.sharding import PartitionSpec as P

HEAD_DIM = 128
TOPK = 4
CORES = 2
Z_CHIPS = 4


def pack_kernel(members, parts, columns, order, *refs):
    sources, refs = refs[:parts], refs[parts:]
    gates, blocks, sems = refs[:-1 - members], refs[-1 - members : -1], refs[-1]
    copies = []
    for m in range(members):
        at = 0
        for source in sources:
            rows = source.shape[0]
            for j in range(2):
                place = pl.multiple_of(order[2 * m + j] * columns, columns)
                copies.append(
                    pltpu.make_async_copy(
                        source.at[:, pl.ds(place, columns)],
                        blocks[m].at[pl.ds(at, rows), pl.ds(j * columns, columns)],
                        sems.at[len(copies)],
                    )
                )
            at += rows
    for copy in copies:
        copy.start()
    if gates:
        weights = gates[0][...]
        high = weights.astype(jnp.bfloat16).astype(jnp.float32)
        middle = (weights - high).astype(jnp.bfloat16).astype(jnp.float32)
        low = weights - high - middle
        weights = jnp.concatenate([high, middle, low, jnp.zeros_like(low)], axis=0)
        for m in range(members):
            blocks[m][at:, : weights.shape[1]] = weights.astype(jnp.bfloat16)
    for copy in copies:
        copy.wait()


def pack(parts, gates, order, columns):
    members = order.shape[0] // 2
    rows = sum(p.shape[0] for p in parts) + (0 if gates is None else 4 * gates.shape[0])
    vmem = pl.BlockSpec(memory_space=pltpu.VMEM)
    in_specs = [pl.BlockSpec(memory_space=pltpu.SMEM)]
    in_specs += [pl.BlockSpec(memory_space=pl.ANY)] * len(parts)
    operands = list(parts)
    if gates is not None:
        in_specs.append(vmem)
        operands.append(gates)
    return pl.pallas_call(
        functools.partial(pack_kernel, members, len(parts), columns),
        out_shape=[jax.ShapeDtypeStruct((rows, 2 * columns), parts[0].dtype)] * members,
        in_specs=in_specs,
        out_specs=[vmem] * members,
        scratch_shapes=[pltpu.SemaphoreType.DMA((2 * members * len(parts),))],
        compiler_params=pltpu.CompilerParams(vmem_limit_bytes=56 * 1024 * 1024),
        cost_estimate=pl.CostEstimate(
            flops=0, bytes_accessed=8 * members * rows * columns, transcendentals=0
        ),
    )(order, *operands)


def attend_kernel(members, tokens, tok_rows, page_len, scale, page_req, page_slot, *refs):
    blocks, refs = refs[:members], refs[members:]
    if len(refs) > 4:
        query, refs = [q[...] for q in refs[:members]], refs[members:]
    else:
        query = [block[2 * tokens : 2 * tokens + tok_rows, :] for block in blocks]
    request, position, out, level = refs
    request, position = request[...], position[...]
    keys = jnp.concatenate([block[:tokens, :] for block in blocks], axis=0)
    values = jnp.concatenate([block[tokens : 2 * tokens, :] for block in blocks], axis=0)
    query = jnp.concatenate(query, axis=0)
    scores = (
        lax.dot_general(keys, query, (((1,), (1,)), ((), ())), preferred_element_type=jnp.float32)
        * scale
    )
    token = lax.broadcasted_iota(jnp.int32, (page_len, query.shape[0]), 0)
    visible = jnp.concatenate(
        [
            (request == page_req[page]) & (token + page_slot[page] * page_len <= position)
            for page in range(members * tokens // page_len)
        ],
        axis=0,
    )
    scores = jnp.where(visible, scores, -1e30)
    top = jnp.max(scores, axis=0, keepdims=True)
    weights = jnp.where(visible, jnp.exp(scores - top), 0.0)
    total = jnp.sum(weights, axis=0, keepdims=True)
    summed = lax.dot_general(
        values,
        weights.astype(jnp.bfloat16),
        (((0,), (0,)), ((), ())),
        preferred_element_type=jnp.float32,
    )
    seen = total > 0.0
    total = jnp.where(seen, total, 1.0)
    out[...] = (summed / total).astype(jnp.bfloat16)
    level[0] = jnp.where(seen, top + jnp.log(total), -1e30)


def attend(blocks, far, row_req, row_pos, page_req, page_slot, page_len, tokens, tok_rows):
    members, rows = len(blocks), row_req.shape[1]
    block_rows, columns = blocks[0].shape
    heads = columns // HEAD_DIM
    by_head = lambda n: pl.BlockSpec((n, HEAD_DIM), lambda h, *_: (0, h))
    whole = pl.BlockSpec((1, rows), lambda h, *_: (0, 0))
    return pl.pallas_call(
        functools.partial(
            attend_kernel, members, tokens, tok_rows, page_len, HEAD_DIM ** (-0.5)
        ),
        out_shape=[
            jax.ShapeDtypeStruct((columns, rows), jnp.bfloat16),
            jax.ShapeDtypeStruct((heads, 1, rows), jnp.float32),
        ],
        grid_spec=pltpu.PrefetchScalarGridSpec(
            num_scalar_prefetch=2,
            grid=(heads,),
            in_specs=[by_head(block_rows)] * members + [by_head(tok_rows)] * len(far) + [whole] * 2,
            out_specs=[
                pl.BlockSpec((HEAD_DIM, rows), lambda h, *_: (h, 0)),
                pl.BlockSpec((1, 1, rows), lambda h, *_: (h, 0, 0)),
            ],
        ),
        compiler_params=pltpu.CompilerParams(vmem_limit_bytes=48 * 1024 * 1024),
        cost_estimate=pl.CostEstimate(
            flops=4 * rows * members * tokens * columns,
            bytes_accessed=2 * members * (block_rows + tok_rows) * columns,
            transcendentals=rows * members * tokens * heads,
        ),
    )(page_req, page_slot, *blocks, *far, row_req, row_pos)


def project_kernel(order, mine, mine_level, theirs, their_level, own, *refs):
    quarters, (stay, go, proj) = refs[:-3], refs[-3:]
    rows, size = own.shape[0], quarters[0].shape[0]
    proj[:rows, :] = own[...]
    for k, quarter in enumerate(quarters):
        at = pl.multiple_of(rows + order[k] * size, size)
        proj[pl.ds(at, size), :] = quarter[...]
    parts = []
    heads = mine.shape[0] // HEAD_DIM
    for head in range(heads):
        twin = (head + heads // 2) % heads
        dims = slice(head * HEAD_DIM, (head + 1) * HEAD_DIM)
        twin_dims = slice(twin * HEAD_DIM, (twin + 1) * HEAD_DIM)
        share = 1.0 / (1.0 + jnp.exp(their_level[twin] - mine_level[head]))
        other = 1.0 / (1.0 + jnp.exp(mine_level[head] - their_level[twin]))
        both = share * mine[dims, :].astype(jnp.float32) + other * theirs[
            twin_dims, :
        ].astype(jnp.float32)
        parts.append(both.astype(jnp.bfloat16))
    attention = jnp.concatenate(parts, axis=0)
    mixed = lax.dot_general(
        attention, proj[...], (((0,), (0,)), ((), ())), preferred_element_type=jnp.float32
    )
    kept = stay.shape[0]
    stay[...] = mixed[:kept, :]
    go[...] = mixed[kept:, :].astype(jnp.bfloat16)


def project(place, order, mine, mine_level, theirs, their_level, own, quarters, tok_rows):
    dims, width = mine.shape[0], own.shape[1]
    heads = dims // HEAD_DIM
    size = mine.shape[1] // 2
    whole = lambda a: pl.BlockSpec(a.shape, lambda i, order: (0, 0))
    values = pl.BlockSpec((dims, size), lambda i, order: (0, place))
    levels = pl.BlockSpec((heads, 1, size), lambda i, order: (0, 0, place))
    return pl.pallas_call(
        project_kernel,
        out_shape=[
            jax.ShapeDtypeStruct((tok_rows, width), jnp.float32),
            jax.ShapeDtypeStruct((size - tok_rows, width), jnp.bfloat16),
        ],
        grid_spec=pltpu.PrefetchScalarGridSpec(
            num_scalar_prefetch=1,
            grid=(1,),
            in_specs=[values, levels, values, levels, whole(own)] + [whole(q) for q in quarters],
            out_specs=[
                pl.BlockSpec((tok_rows, width), lambda i, order: (0, 0)),
                pl.BlockSpec((size - tok_rows, width), lambda i, order: (0, 0)),
            ],
            scratch_shapes=[pltpu.VMEM((dims, width), jnp.bfloat16)],
        ),
        compiler_params=pltpu.CompilerParams(vmem_limit_bytes=32 * 1024 * 1024),
        cost_estimate=pl.CostEstimate(
            flops=2 * size * dims * width,
            bytes_accessed=2 * (2 * dims * size + dims * width + 3 * size * width),
            transcendentals=2 * size * heads,
        ),
    )(order, mine, mine_level, theirs, their_level, own, *quarters)


def join_kernel(sizes, *refs):
    parts, outs = refs[: sum(sizes)], refs[sum(sizes) :]
    for n, out in enumerate(outs):
        rows = out.shape[0] // sizes[n]
        for i in range(sizes[n]):
            out[i * rows : (i + 1) * rows, :] = parts[sum(sizes[:n]) + i][...]


def join(*groups):
    rows, width = groups[0][0].shape
    sizes = [len(group) for group in groups]
    vmem = pl.BlockSpec(memory_space=pltpu.VMEM)
    return pl.pallas_call(
        functools.partial(join_kernel, sizes),
        out_shape=[jax.ShapeDtypeStruct((n * rows, width), groups[0][0].dtype) for n in sizes],
        in_specs=[vmem] * sum(sizes),
        out_specs=[vmem] * len(sizes),
        cost_estimate=pl.CostEstimate(
            flops=0, bytes_accessed=4 * sum(sizes) * rows * width, transcendentals=0
        ),
    )(*[part for group in groups for part in group])


def silu(value):
    return value / (1.0 + jnp.exp(-value))


def shared_kernel(count, *refs):
    pieces, (scalar, gate_w, up_w, down_w, out, rows, gate_v, up_v, down_v, sems) = (
        refs[:count],
        refs[count:],
    )
    moves = [(gate_w, gate_v), (up_w, up_v), (down_w, down_v)]
    size = pieces[0].shape[0]
    moves += [(piece, rows.at[pl.ds(i * size, size)]) for i, piece in enumerate(pieces)]
    copies = [
        pltpu.make_async_copy(src, dst, sems.at[i]) for i, (src, dst) in enumerate(moves)
    ]
    for copy in copies[3:] + copies[:3]:
        copy.start()
    for copy in copies[3:]:
        copy.wait()
    block = rows[...]
    logit = jnp.sum(
        block.astype(jnp.float32) * scalar[...].astype(jnp.float32), axis=1, keepdims=True
    )
    scale = 1.0 / (1.0 + jnp.exp(-logit))
    across = (((1,), (1,)), ((), ()))
    copies[0].wait()
    gate = lax.dot_general(block, gate_v[...], across, preferred_element_type=jnp.float32)
    copies[1].wait()
    upper = lax.dot_general(block, up_v[...], across, preferred_element_type=jnp.float32)
    hidden = (silu(gate) * upper).astype(jnp.bfloat16)
    copies[2].wait()
    result = jnp.dot(hidden, down_v[...], preferred_element_type=jnp.float32)
    out[...] = (scale * result).astype(jnp.bfloat16)


def shared_expert(pieces, scalar, gate_w, up_w, down_w):
    any_spec = pl.BlockSpec(memory_space=pl.ANY)
    vmem = pl.BlockSpec(memory_space=pltpu.VMEM)
    rows = sum(piece.shape[0] for piece in pieces)
    width = pieces[0].shape[1]
    return pl.pallas_call(
        functools.partial(shared_kernel, len(pieces)),
        out_shape=jax.ShapeDtypeStruct((rows, width), jnp.bfloat16),
        in_specs=[any_spec] * len(pieces) + [vmem] + [any_spec] * 3,
        out_specs=vmem,
        scratch_shapes=[
            pltpu.VMEM((rows, width), jnp.bfloat16),
            pltpu.VMEM(gate_w.shape, jnp.bfloat16),
            pltpu.VMEM(up_w.shape, jnp.bfloat16),
            pltpu.VMEM(down_w.shape, jnp.bfloat16),
            pltpu.SemaphoreType.DMA((3 + len(pieces),)),
        ],
        compiler_params=pltpu.CompilerParams(vmem_limit_bytes=56 * 1024 * 1024),
        cost_estimate=pl.CostEstimate(
            flops=6 * rows * gate_w.size,
            bytes_accessed=6 * gate_w.size + 4 * rows * width,
            transcendentals=rows * gate_w.shape[0],
        ),
    )(*pieces, scalar.reshape(1, -1), gate_w, up_w, down_w)


def routed_kernel(parts, extras, entries, cuts, *refs):
    count, total = len(parts), sum(parts)
    pieces, refs = refs[:total], refs[total:]
    place, row_gate = refs[:2]
    more, refs = refs[2 : 2 + extras], refs[2 + extras :]
    (gate_w, up_w, down_w), refs = refs[:3], refs[3:]
    outs, refs = refs[: sum(cuts)], refs[sum(cuts) :]
    rows, packed, gate_v, up_v, down_v, more_v, sems = refs
    moves, chunk_copies = [], []
    for c, n in enumerate(parts):
        at = 0
        chunk_copies.append(range(len(moves), len(moves) + n))
        for piece in pieces[sum(parts[:c]) : sum(parts[: c + 1])]:
            moves.append((piece, rows.at[c, pl.ds(at, piece.shape[0])]))
            at += piece.shape[0]
    moves += [(gate_w.at[0], gate_v), (up_w.at[0], up_v), (down_w.at[0], down_v)]
    at = 0
    for extra in more:
        moves.append((extra, more_v.at[pl.ds(at, extra.shape[0])]))
        at += extra.shape[0]
    copies = [
        pltpu.make_async_copy(src, dst, sems.at[i]) for i, (src, dst) in enumerate(moves)
    ]
    for copy in copies:
        copy.start()
    size = rows.shape[1]
    wanted = lax.broadcasted_iota(jnp.int32, (entries, size), 0)
    picks, weights = [], []
    for c in range(count):
        pick = jnp.where(place[c] == wanted, 1.0, 0.0)
        picks.append(pick.astype(jnp.bfloat16))
        weights.append(jnp.sum(pick * row_gate[c], axis=1, keepdims=True))
        for i in chunk_copies[c]:
            copies[i].wait()
        packed[c * entries : (c + 1) * entries, :] = jnp.dot(
            picks[c], rows[c], preferred_element_type=jnp.float32
        ).astype(jnp.bfloat16)
    copies[total].wait()
    gate = jnp.dot(packed[...], gate_v[...], preferred_element_type=jnp.float32)
    copies[total + 1].wait()
    upper = jnp.dot(packed[...], up_v[...], preferred_element_type=jnp.float32)
    hidden = (silu(gate) * upper).astype(jnp.bfloat16)
    copies[total + 2].wait()
    answer = jnp.dot(hidden, down_v[...], preferred_element_type=jnp.float32).astype(
        jnp.bfloat16
    )
    for i in range(extras):
        copies[total + 3 + i].wait()
    for c in range(count):
        scaled = answer[c * entries : (c + 1) * entries, :].astype(jnp.float32) * weights[c]
        placed = lax.dot_general(
            picks[c],
            scaled.astype(jnp.bfloat16),
            (((0,), (0,)), ((), ())),
            preferred_element_type=jnp.float32,
        )
        if c == 0 and extras:
            placed = placed + more_v[...].astype(jnp.float32)
        placed = placed.astype(jnp.bfloat16)
        cut = size // cuts[c]
        for k in range(cuts[c]):
            outs[sum(cuts[:c]) + k][...] = placed[k * cut : (k + 1) * cut, :]


def routed_expert(chunks, place, row_gate, more, gate_w, up_w, down_w, entries, cuts):
    count = len(chunks)
    parts = [len(chunk) for chunk in chunks]
    total = sum(parts)
    size = sum(piece.shape[0] for piece in chunks[0])
    width = chunks[0][0].shape[1]
    hidden = gate_w.shape[2]
    any_spec = pl.BlockSpec(memory_space=pl.ANY)
    vmem = pl.BlockSpec(memory_space=pltpu.VMEM)
    out_shape = [
        jax.ShapeDtypeStruct((size // n, width), jnp.bfloat16) for n in cuts for k in range(n)
    ]
    more_rows = sum(extra.shape[0] for extra in more) if more else 16
    outs = pl.pallas_call(
        functools.partial(routed_kernel, parts, len(more), entries, cuts),
        out_shape=out_shape,
        in_specs=[any_spec] * total + [vmem] * 2 + [any_spec] * (len(more) + 3),
        out_specs=[vmem] * sum(cuts),
        scratch_shapes=[
            pltpu.VMEM((count, size, width), jnp.bfloat16),
            pltpu.VMEM((count * entries, width), jnp.bfloat16),
            pltpu.VMEM((width, hidden), jnp.bfloat16),
            pltpu.VMEM((width, hidden), jnp.bfloat16),
            pltpu.VMEM((hidden, width), jnp.bfloat16),
            pltpu.VMEM((more_rows, width), jnp.bfloat16),
            pltpu.SemaphoreType.DMA((total + 3 + len(more),)),
        ],
        compiler_params=pltpu.CompilerParams(vmem_limit_bytes=56 * 1024 * 1024),
        cost_estimate=pl.CostEstimate(
            flops=2 * count * entries * (3 * gate_w.size + 2 * size * width),
            bytes_accessed=6 * gate_w.size + 4 * count * size * width,
            transcendentals=count * entries * hidden,
        ),
    )(*[piece for chunk in chunks for piece in chunk], place, row_gate, *more, gate_w, up_w, down_w)
    return [outs[sum(cuts[:c]) : sum(cuts[: c + 1])] for c in range(count)]


def rms_normed(stream, norm_gain):
    scale_row = lax.rsqrt(jnp.mean(stream * stream, axis=1, keepdims=True) + 1e-06)
    return (stream * scale_row * norm_gain[None, :]).astype(jnp.bfloat16)


def shards(
    resid,
    queries,
    cache_key,
    cache_value,
    page_table,
    row_request,
    row_position,
    out_proj,
    norm_gain,
    expert_gate,
    expert_up,
    expert_down,
    shared_gate,
    shared_up,
    shared_down,
    shared_scalar,
    slot_expert,
    route_expert,
    route_gate,
):
    f32, bf16, i32 = jnp.float32, jnp.bfloat16, jnp.int32
    exp_count = lax.axis_size("exp")
    req_count = lax.axis_size("req")
    slot_count = exp_count * req_count
    nc, nx, ny = CORES, exp_count // Z_CHIPS, req_count // CORES
    exp_index = lax.axis_index("exp")
    req_index = lax.axis_index("req")
    own_slot = req_index * exp_count + exp_index
    iz, ix = exp_index // nx, exp_index % nx
    ih, il = iz // 2, iz % 2
    iy, ic = req_index // nc, req_index % nc
    tok_rows, width = resid.shape
    pages_here, page_len, _ = cache_key.shape
    req_slots, max_pages = page_table.shape
    tokens = pages_here * page_len
    capacity = 3 * tok_rows * TOPK // slot_count

    zs = [(dh, dl) for dh in range(2) for dl in range(2)]

    def send(value, dh, dl, dx):
        if not (dh or dl or dx % nx):
            return value
        pairs = [
            (
                (h * 2 + l) * nx + x,
                ((h + dh) % 2 * 2 + (l + dl) % 2) * nx + (x + dx) % nx,
            )
            for h in range(2)
            for l in range(2)
            for x in range(nx)
        ]
        return lax.ppermute(value, "exp", pairs)

    def send_req(value, dy, dc):
        if not (dy % ny or dc % nc):
            return value
        pairs = [
            (y * nc + c, (y + dy) % ny * nc + (c + dc) % nc)
            for y in range(ny)
            for c in range(nc)
        ]
        return lax.ppermute(value, "req", pairs)

    def swap_y(value):
        pairs = [(y * nc + c, (y ^ 1) * nc + c) for y in range(ny) for c in range(nc)]
        return lax.ppermute(value, "req", pairs)

    tie = lax.optimization_barrier

    rel_exp = jnp.stack(
        [
            ((ih + dh) % 2 * 2 + (il + dl) % 2) * nx + (ix - dx) % nx
            for dh, dl in zs
            for dx in range(nx)
        ]
    ).astype(i32)
    rel_req = jnp.stack(
        [((iy - dy) % ny) * nc + (ic - dc) % nc for dy in range(ny) for dc in range(nc)]
    ).astype(i32)

    columns = width // exp_count
    keys = cache_key.reshape(tokens, width)
    values = cache_value.reshape(tokens, width)
    quarter_rows = out_proj.shape[0] // (2 * nc)
    quarter = lax.dynamic_slice_in_dim(
        out_proj, (iy % 2 * nc + ic) * quarter_rows, quarter_rows, 0
    )
    quarter_order = jnp.stack(
        [(iy + dy) % 2 * nc + (ic + dc) % nc for dc in range(nc) for dy in range(2)]
    ).astype(i32)
    far_queries = send(queries, 1, 0, 0)
    members = [(dl, dx) for dl in range(2) for dx in range(nx)]
    member_columns = jnp.stack(
        [
            ((ih + j) % 2 * 2 + (il + dl) % 2) * nx + (ix + dx) % nx
            for dl, dx in members
            for j in range(2)
        ]
    ).astype(i32)
    gates = jnp.transpose(route_gate)
    blocks = pack([keys, values, queries], gates, member_columns, columns)
    blocks = [send(blocks[m], 0, *members[m]) for m in range(len(members))]
    far = list(pack([far_queries], None, member_columns, columns))
    for m in range(1, len(members)):
        if m > 2:
            far[m], far[m - 2] = tie((far[m], far[m - 2]))
        far[m] = send(far[m], 0, *members[m])
    quarters = [send(quarter, 1, 0, 0)]
    page_ids = (
        rel_exp[: len(members), None] * pages_here + jnp.arange(pages_here, dtype=i32)[None, :]
    ).reshape(-1)
    hits = (page_table[None, :, :] == page_ids[:, None, None]).astype(i32)
    page_request = jnp.sum(hits * jnp.arange(req_slots, dtype=i32)[None, :, None], axis=(1, 2))
    page_slot = jnp.sum(hits * jnp.arange(max_pages, dtype=i32)[None, None, :], axis=(1, 2))
    by_place = lambda a: a.reshape(exp_count, tok_rows)[rel_exp].reshape(2, 1, -1)
    row_req, row_pos = by_place(row_request), by_place(row_position)
    gates = [block[2 * tokens + tok_rows :, :tok_rows].astype(f32) for block in blocks]
    gates = jnp.stack([g[:TOPK] + g[TOPK : 2 * TOPK] + g[2 * TOPK : 3 * TOPK] for g in gates])
    gates = gates.reshape(2, nx, TOPK, tok_rows)

    slot_ids = jnp.arange(slot_count, dtype=i32)
    own_mark = slot_ids == own_slot
    own_expert = jnp.sum(jnp.where(own_mark, slot_expert, 0))
    twins = slot_expert == own_expert
    copies = jnp.sum(twins.astype(i32))
    own_rank = jnp.sum((twins & (slot_ids < own_slot)).astype(i32))
    order = [1, 3, 2, 0]
    rel_rows = jnp.stack([rel_exp.reshape(4, nx)[i] for i in order], axis=1).reshape(-1)
    rel_slots = (rel_req[:, None] * exp_count + rel_rows[None, :]).reshape(-1)
    named = (route_expert == own_expert).reshape(slot_count, tok_rows, TOPK)[rel_slots]
    named = jnp.transpose(named, (0, 2, 1))
    chunk_rows = exp_count * tok_rows
    entries = -(-exp_count * capacity // 16) * 16
    served = jnp.any(named, axis=1) & (rel_slots % copies == own_rank)[:, None]
    served = served.reshape(ny, nc, chunk_rows)
    place = jnp.where(served, jnp.cumsum(served.astype(i32), axis=2) - 1, -1)
    place = place.reshape(ny, nc, 1, chunk_rows)

    place, named, blocks = tie((place, named, blocks))

    def attend_half(side, queries):
        return attend(
            blocks,
            queries,
            row_req[side],
            row_pos[side],
            page_request,
            page_slot,
            page_len,
            tokens,
            tok_rows,
        )

    quarters.append(swap_y(quarters[0]))
    theirs, their_level = attend_half(1, far)
    theirs, their_level, quarters = tie((theirs, their_level, quarters))
    theirs, their_level = send(theirs, 1, 0, 0), send(their_level, 1, 0, 0)
    quarters += [send_req(q, 0, dc) for dc in range(1, nc) for q in quarters[:2]]
    mine, level = attend_half(0, [])
    mine, level, gates, quarters = tie((mine, level, gates, quarters))
    gates = jnp.stack([send(gates, dh, 0, 0) for dh in range(2)])
    theirs, their_level, gates = tie((theirs, their_level, gates))

    stays, comes = {}, {}
    proj = out_proj
    for dl in (1, 0):
        stays[dl], go = project(
            dl, quarter_order, mine, level, theirs, their_level, proj, quarters, tok_rows
        )
        comes[dl] = [
            send(go[(dx - 1) * tok_rows : dx * tok_rows], 0, 0, -dx) for dx in range(1, nx)
        ]
        proj, _ = tie((proj, go))
    line = sum([come.astype(f32) for come in comes[1]], stays[1]).astype(bf16)
    comes[0], _ = tie((comes[0], line))
    line = send(line, 0, 1, 0)
    stream = sum([come.astype(f32) for come in comes[0]], resid.astype(f32) + stays[0])
    stream = stream + line.astype(f32)
    gates = jnp.stack([send_req(gates, dy, 0) for dy in range(ny)])
    stream, gates = tie((stream, gates))
    normed = rms_normed(stream, norm_gain)
    gates = jnp.stack([send_req(gates, 0, dc) for dc in range(nc)], axis=1)
    gates = gates.reshape(ny, nc, 4, nx, TOPK, tok_rows)
    gates = jnp.stack([gates[:, :, i] for i in order], axis=3)
    gates = gates.reshape(slot_count, TOPK, tok_rows)
    row_gate = jnp.sum(jnp.where(named, gates, 0.0), axis=1).reshape(ny, nc, 1, chunk_rows)

    far_line = send(normed, 1, 0, 0)
    line = [normed, send(normed, 0, 1, 0), far_line, send(far_line, 0, 1, 0)]
    over_x = {(i, dx): send(line[i], 0, 0, dx) for i in order for dx in range(1, nx)}
    over_y = {(i, dy): send_req(line[i], dy, 0) for i in order for dy in range(1, ny)}

    halves = [[line[i] for i in order]]
    shared_weights = (shared_scalar, shared_gate.T, shared_up.T, shared_down)
    shared = [shared_expert(halves[0], *shared_weights)]
    chunks = {(0, 0): join(halves[0])}
    for dc in range(1, nc):
        chunks[0, dc] = [send_req(chunks[0, 0][0], 0, dc)]
    over_x, over_y, shared, row_gate = tie((over_x, over_y, shared, row_gate))
    halves += [[over_x[i, dx] for i in order] for dx in range(1, nx)]
    joined = join(*halves[1:], *[[over_y[i, dy] for i in order] for dy in range(1, ny)])
    chunks[0, 0] += joined[: nx - 1]
    for dc in range(1, nc):
        chunks[0, dc] += [send_req(half, 0, dc) for half in joined[: nx - 1]]
    for dy, half in enumerate(joined[nx - 1 :], 1):
        chunks[dy, 0] = [half] + [send(half, 0, 0, dx) for dx in range(1, nx)]
        for dc in range(1, nc):
            chunks[dy, dc] = [send_req(half, 0, dc)]

    def answers_of(dy, dcs, more, cuts):
        return routed_expert(
            [chunks[dy, dc] for dc in dcs],
            jnp.concatenate([place[dy, dc : dc + 1] for dc in dcs]),
            jnp.concatenate([row_gate[dy, dc : dc + 1] for dc in dcs]),
            more,
            expert_gate,
            expert_up,
            expert_down,
            entries,
            cuts,
        )

    def add_up(parts):
        return sum([part.astype(f32) for part in parts[1:]], parts[0].astype(f32))

    cores = list(range(nc))
    kept, comes = {}, {}
    cuts = [slice(0, 3 * tok_rows), slice(3 * tok_rows, 4 * tok_rows)]
    for dy in range(ny - 1):
        answers = answers_of(dy, cores, [], [nx] * nc)
        if dy:
            answers, comes[dy - 1] = tie((answers, comes[dy - 1]))
        others = [[send_req(part, 0, -dc) for part in answers[dc][::-1]][::-1] for dc in cores[1:]]
        parts = [answers[0]] + others
        if dy:
            following = answers[0][0]
        else:
            for dx in range(1, nx):
                halves[dx], _ = tie((halves[dx], answers[0]))
                shared.append(shared_expert(halves[dx], *shared_weights))
            parts.append(shared)
            following = shared[-1]
        chunks[dy + 1, 0], _ = tie((chunks[dy + 1, 0], following))
        for dc in range(1, nc):
            chunks[dy + 1, dc] += [send_req(part, 0, dc) for part in chunks[dy + 1, 0][1:]]
        gone = [add_up([part[dx] for part in parts]).astype(bf16) for dx in range(1, nx)]
        kept[dy] = [part[0] for part in parts]
        waiting = [go[cuts[1]] for go in gone]
        comes[dy] = [
            [send(go[rows], 0, 0, -dx) for dx, go in enumerate(gone, 1)]
            for rows in (cuts if dy + 2 < ny else cuts[:1])
        ]
        following = [chunks[dy + 1, dc] for dc in cores]
        following, _ = tie((following, gone))
        for dc in cores:
            chunks[dy + 1, dc] = following[dc]
    end = ny - 1
    answers = answers_of(end, cores, [], [4 * nx] + [nx] * (nc - 1))
    answers, comes, kept = tie((answers, comes, kept))
    answer = answers[0]
    others = [[send_req(part, 0, -dc) for part in answers[dc][::-1]][::-1] for dc in cores[1:]]

    turns = [1, 2, 0, 3]
    block = lambda a, p: a[p * tok_rows : (p + 1) * tok_rows]
    last = {}
    for p in turns:
        gone = [
            add_up([answer[4 * dx + p]] + [block(other[dx], p) for other in others])
            for dx in range(1, nx)
        ]
        gone = [go.astype(bf16) for go in gone]
        last[p] = [send(go, 0, 0, -dx) for dx, go in enumerate(gone, 1)]
        others, _ = tie((others, gone))
    waiting, _ = tie((waiting, gone))
    comes[end - 1].append([send(go, 0, 0, -dx) for dx, go in enumerate(waiting, 1)])

    def line_of(dy, p):
        if dy < end:
            arrived = [come if p == 3 else block(come, p) for come in comes[dy][p // 3]]
            return add_up([block(part, p) for part in kept[dy]] + arrived)
        return add_up([answer[p]] + [block(other[0], p) for other in others] + last[p])

    home, near = {}, {}
    for turn, p in enumerate(turns):
        goes = [line_of(dy, p).astype(bf16) for dy in range(1, ny)]
        home[p] = [send_req(go, -dy, 0) for dy, go in enumerate(goes, 1)]
        if turn == 1:
            go = add_up([line_of(0, 1)] + home[1]).astype(bf16)
            near[1] = send(go, 0, 1, 0)
            goes.append(go)
        if turn + 1 < len(turns):
            after = turns[turn + 1]
            last[after], _ = tie((last[after], goes))
    far = add_up([line_of(0, 2)] + home[2] + [near[1]]).astype(bf16)
    home[0], _ = tie((home[0], far))
    far = send(far, 1, 0, 0)
    near[0] = send(add_up([line_of(0, 0)] + home[0]).astype(bf16), 0, 1, 0)
    total = add_up([stream, line_of(0, 3)] + home[3] + [near[0], far])
    return total.astype(bf16)


def solution(mesh):
    placed = (
        P(("req", "exp"), None),
        P(("req", "exp"), None),
        P(("req", "exp"), None, None),
        P(("req", "exp"), None, None),
        P("req", None),
        P("req"),
        P("req"),
        P("exp", None),
        P(),
        P(("req", "exp"), None, None),
        P(("req", "exp"), None, None),
        P(("req", "exp"), None, None),
        P(None, "exp"),
        P(None, "exp"),
        P("exp", None),
        P(),
        P(),
        P(),
        P(("req", "exp"), None),
    )
    return jax.shard_map(
        shards, mesh=mesh, in_specs=placed, out_specs=P(("req", "exp"), None), check_vma=False
    )
```

```python
import functools

import jax
import jax.numpy as jnp
from jax import lax
from jax.experimental import pallas as pl
from jax.experimental.pallas import tpu as pltpu
from jax.sharding import PartitionSpec as P

HEAD_DIM = 128
TOPK = 4
CORES = 2
Z_CHIPS = 4


def pack_kernel(members, parts, columns, order, *refs):
    sources, refs = refs[:parts], refs[parts:]
    gates, blocks, sems = refs[:-1 - members], refs[-1 - members : -1], refs[-1]
    copies = []
    for m in range(members):
        at = 0
        for source in sources:
            rows = source.shape[0]
            for j in range(2):
                place = pl.multiple_of(order[2 * m + j] * columns, columns)
                copies.append(
                    pltpu.make_async_copy(
                        source.at[:, pl.ds(place, columns)],
                        blocks[m].at[pl.ds(at, rows), pl.ds(j * columns, columns)],
                        sems.at[len(copies)],
                    )
                )
            at += rows
    for copy in copies:
        copy.start()
    if gates:
        weights = gates[0][...]
        high = weights.astype(jnp.bfloat16).astype(jnp.float32)
        middle = (weights - high).astype(jnp.bfloat16).astype(jnp.float32)
        low = weights - high - middle
        weights = jnp.concatenate([high, middle, low, jnp.zeros_like(low)], axis=0)
        for m in range(members):
            blocks[m][at:, : weights.shape[1]] = weights.astype(jnp.bfloat16)
    for copy in copies:
        copy.wait()


def pack(parts, gates, order, columns):
    members = order.shape[0] // 2
    rows = sum(p.shape[0] for p in parts) + (0 if gates is None else 4 * gates.shape[0])
    vmem = pl.BlockSpec(memory_space=pltpu.VMEM)
    in_specs = [pl.BlockSpec(memory_space=pltpu.SMEM)]
    in_specs += [pl.BlockSpec(memory_space=pl.ANY)] * len(parts)
    operands = list(parts)
    if gates is not None:
        in_specs.append(vmem)
        operands.append(gates)
    return pl.pallas_call(
        functools.partial(pack_kernel, members, len(parts), columns),
        out_shape=[jax.ShapeDtypeStruct((rows, 2 * columns), parts[0].dtype)] * members,
        in_specs=in_specs,
        out_specs=[vmem] * members,
        scratch_shapes=[pltpu.SemaphoreType.DMA((2 * members * len(parts),))],
        compiler_params=pltpu.CompilerParams(vmem_limit_bytes=56 * 1024 * 1024),
        cost_estimate=pl.CostEstimate(
            flops=0, bytes_accessed=8 * members * rows * columns, transcendentals=0
        ),
    )(order, *operands)


def attend_kernel(members, tokens, tok_rows, page_len, scale, page_req, page_slot, *refs):
    blocks, refs = refs[:members], refs[members:]
    if len(refs) > 4:
        query, refs = [q[...] for q in refs[:members]], refs[members:]
    else:
        query = [block[2 * tokens : 2 * tokens + tok_rows, :] for block in blocks]
    request, position, out, level = refs
    request, position = request[...], position[...]
    keys = jnp.concatenate([block[:tokens, :] for block in blocks], axis=0)
    values = jnp.concatenate([block[tokens : 2 * tokens, :] for block in blocks], axis=0)
    query = jnp.concatenate(query, axis=0)
    scores = (
        lax.dot_general(keys, query, (((1,), (1,)), ((), ())), preferred_element_type=jnp.float32)
        * scale
    )
    token = lax.broadcasted_iota(jnp.int32, (page_len, query.shape[0]), 0)
    visible = jnp.concatenate(
        [
            (request == page_req[page]) & (token + page_slot[page] * page_len <= position)
            for page in range(members * tokens // page_len)
        ],
        axis=0,
    )
    scores = jnp.where(visible, scores, -1e30)
    top = jnp.max(scores, axis=0, keepdims=True)
    weights = jnp.where(visible, jnp.exp(scores - top), 0.0)
    total = jnp.sum(weights, axis=0, keepdims=True)
    summed = lax.dot_general(
        values,
        weights.astype(jnp.bfloat16),
        (((0,), (0,)), ((), ())),
        preferred_element_type=jnp.float32,
    )
    seen = total > 0.0
    total = jnp.where(seen, total, 1.0)
    out[...] = (summed / total).astype(jnp.bfloat16)
    level[0] = jnp.where(seen, top + jnp.log(total), -1e30)


def attend(blocks, far, row_req, row_pos, page_req, page_slot, page_len, tokens, tok_rows):
    members, rows = len(blocks), row_req.shape[1]
    block_rows, columns = blocks[0].shape
    heads = columns // HEAD_DIM
    by_head = lambda n: pl.BlockSpec((n, HEAD_DIM), lambda h, *_: (0, h))
    whole = pl.BlockSpec((1, rows), lambda h, *_: (0, 0))
    return pl.pallas_call(
        functools.partial(
            attend_kernel, members, tokens, tok_rows, page_len, HEAD_DIM ** (-0.5)
        ),
        out_shape=[
            jax.ShapeDtypeStruct((columns, rows), jnp.bfloat16),
            jax.ShapeDtypeStruct((heads, 1, rows), jnp.float32),
        ],
        grid_spec=pltpu.PrefetchScalarGridSpec(
            num_scalar_prefetch=2,
            grid=(heads,),
            in_specs=[by_head(block_rows)] * members + [by_head(tok_rows)] * len(far) + [whole] * 2,
            out_specs=[
                pl.BlockSpec((HEAD_DIM, rows), lambda h, *_: (h, 0)),
                pl.BlockSpec((1, 1, rows), lambda h, *_: (h, 0, 0)),
            ],
        ),
        compiler_params=pltpu.CompilerParams(vmem_limit_bytes=48 * 1024 * 1024),
        cost_estimate=pl.CostEstimate(
            flops=4 * rows * members * tokens * columns,
            bytes_accessed=2 * members * (block_rows + tok_rows) * columns,
            transcendentals=rows * members * tokens * heads,
        ),
    )(page_req, page_slot, *blocks, *far, row_req, row_pos)


def project_kernel(order, mine, mine_level, theirs, their_level, own, *refs):
    quarters, (stay, go, proj) = refs[:-3], refs[-3:]
    rows, size = own.shape[0], quarters[0].shape[0]
    proj[:rows, :] = own[...]
    for k, quarter in enumerate(quarters):
        at = pl.multiple_of(rows + order[k] * size, size)
        proj[pl.ds(at, size), :] = quarter[...]
    parts = []
    heads = mine.shape[0] // HEAD_DIM
    for head in range(heads):
        twin = (head + heads // 2) % heads
        dims = slice(head * HEAD_DIM, (head + 1) * HEAD_DIM)
        twin_dims = slice(twin * HEAD_DIM, (twin + 1) * HEAD_DIM)
        share = 1.0 / (1.0 + jnp.exp(their_level[twin] - mine_level[head]))
        other = 1.0 / (1.0 + jnp.exp(mine_level[head] - their_level[twin]))
        both = share * mine[dims, :].astype(jnp.float32) + other * theirs[
            twin_dims, :
        ].astype(jnp.float32)
        parts.append(both.astype(jnp.bfloat16))
    attention = jnp.concatenate(parts, axis=0)
    mixed = lax.dot_general(
        attention, proj[...], (((0,), (0,)), ((), ())), preferred_element_type=jnp.float32
    )
    kept = stay.shape[0]
    stay[...] = mixed[:kept, :]
    go[...] = mixed[kept:, :].astype(jnp.bfloat16)


def project(place, order, mine, mine_level, theirs, their_level, own, quarters, tok_rows):
    dims, width = mine.shape[0], own.shape[1]
    heads = dims // HEAD_DIM
    size = mine.shape[1] // 2
    whole = lambda a: pl.BlockSpec(a.shape, lambda i, order: (0, 0))
    values = pl.BlockSpec((dims, size), lambda i, order: (0, place))
    levels = pl.BlockSpec((heads, 1, size), lambda i, order: (0, 0, place))
    return pl.pallas_call(
        project_kernel,
        out_shape=[
            jax.ShapeDtypeStruct((tok_rows, width), jnp.float32),
            jax.ShapeDtypeStruct((size - tok_rows, width), jnp.bfloat16),
        ],
        grid_spec=pltpu.PrefetchScalarGridSpec(
            num_scalar_prefetch=1,
            grid=(1,),
            in_specs=[values, levels, values, levels, whole(own)] + [whole(q) for q in quarters],
            out_specs=[
                pl.BlockSpec((tok_rows, width), lambda i, order: (0, 0)),
                pl.BlockSpec((size - tok_rows, width), lambda i, order: (0, 0)),
            ],
            scratch_shapes=[pltpu.VMEM((dims, width), jnp.bfloat16)],
        ),
        compiler_params=pltpu.CompilerParams(vmem_limit_bytes=32 * 1024 * 1024),
        cost_estimate=pl.CostEstimate(
            flops=2 * size * dims * width,
            bytes_accessed=2 * (2 * dims * size + dims * width + 3 * size * width),
            transcendentals=2 * size * heads,
        ),
    )(order, mine, mine_level, theirs, their_level, own, *quarters)


def join_kernel(sizes, *refs):
    parts, outs = refs[: sum(sizes)], refs[sum(sizes) :]
    for n, out in enumerate(outs):
        rows = out.shape[0] // sizes[n]
        for i in range(sizes[n]):
            out[i * rows : (i + 1) * rows, :] = parts[sum(sizes[:n]) + i][...]


def join(*groups):
    rows, width = groups[0][0].shape
    sizes = [len(group) for group in groups]
    vmem = pl.BlockSpec(memory_space=pltpu.VMEM)
    return pl.pallas_call(
        functools.partial(join_kernel, sizes),
        out_shape=[jax.ShapeDtypeStruct((n * rows, width), groups[0][0].dtype) for n in sizes],
        in_specs=[vmem] * sum(sizes),
        out_specs=[vmem] * len(sizes),
        cost_estimate=pl.CostEstimate(
            flops=0, bytes_accessed=4 * sum(sizes) * rows * width, transcendentals=0
        ),
    )(*[part for group in groups for part in group])


def silu(value):
    return value / (1.0 + jnp.exp(-value))


def shared_kernel(count, *refs):
    pieces, (scalar, gate_w, up_w, down_w, out, rows, gate_v, up_v, down_v, sems) = (
        refs[:count],
        refs[count:],
    )
    moves = [(gate_w, gate_v), (up_w, up_v), (down_w, down_v)]
    size = pieces[0].shape[0]
    moves += [(piece, rows.at[pl.ds(i * size, size)]) for i, piece in enumerate(pieces)]
    copies = [
        pltpu.make_async_copy(src, dst, sems.at[i]) for i, (src, dst) in enumerate(moves)
    ]
    for copy in copies[3:] + copies[:3]:
        copy.start()
    for copy in copies[3:]:
        copy.wait()
    block = rows[...]
    logit = jnp.sum(
        block.astype(jnp.float32) * scalar[...].astype(jnp.float32), axis=1, keepdims=True
    )
    scale = 1.0 / (1.0 + jnp.exp(-logit))
    across = (((1,), (1,)), ((), ()))
    copies[0].wait()
    gate = lax.dot_general(block, gate_v[...], across, preferred_element_type=jnp.float32)
    copies[1].wait()
    upper = lax.dot_general(block, up_v[...], across, preferred_element_type=jnp.float32)
    hidden = (silu(gate) * upper).astype(jnp.bfloat16)
    copies[2].wait()
    result = jnp.dot(hidden, down_v[...], preferred_element_type=jnp.float32)
    out[...] = (scale * result).astype(jnp.bfloat16)


def shared_expert(pieces, scalar, gate_w, up_w, down_w):
    any_spec = pl.BlockSpec(memory_space=pl.ANY)
    vmem = pl.BlockSpec(memory_space=pltpu.VMEM)
    rows = sum(piece.shape[0] for piece in pieces)
    width = pieces[0].shape[1]
    return pl.pallas_call(
        functools.partial(shared_kernel, len(pieces)),
        out_shape=jax.ShapeDtypeStruct((rows, width), jnp.bfloat16),
        in_specs=[any_spec] * len(pieces) + [vmem] + [any_spec] * 3,
        out_specs=vmem,
        scratch_shapes=[
            pltpu.VMEM((rows, width), jnp.bfloat16),
            pltpu.VMEM(gate_w.shape, jnp.bfloat16),
            pltpu.VMEM(up_w.shape, jnp.bfloat16),
            pltpu.VMEM(down_w.shape, jnp.bfloat16),
            pltpu.SemaphoreType.DMA((3 + len(pieces),)),
        ],
        compiler_params=pltpu.CompilerParams(vmem_limit_bytes=56 * 1024 * 1024),
        cost_estimate=pl.CostEstimate(
            flops=6 * rows * gate_w.size,
            bytes_accessed=6 * gate_w.size + 4 * rows * width,
            transcendentals=rows * gate_w.shape[0],
        ),
    )(*pieces, scalar.reshape(1, -1), gate_w, up_w, down_w)


def routed_kernel(parts, extras, entries, cuts, *refs):
    count, total = len(parts), sum(parts)
    pieces, refs = refs[:total], refs[total:]
    place, row_gate = refs[:2]
    more, refs = refs[2 : 2 + extras], refs[2 + extras :]
    (gate_w, up_w, down_w), refs = refs[:3], refs[3:]
    outs, refs = refs[: sum(cuts)], refs[sum(cuts) :]
    rows, packed, gate_v, up_v, down_v, more_v, sems = refs
    moves, chunk_copies = [], []
    for c, n in enumerate(parts):
        at = 0
        chunk_copies.append(range(len(moves), len(moves) + n))
        for piece in pieces[sum(parts[:c]) : sum(parts[: c + 1])]:
            moves.append((piece, rows.at[c, pl.ds(at, piece.shape[0])]))
            at += piece.shape[0]
    moves += [(gate_w.at[0], gate_v), (up_w.at[0], up_v), (down_w.at[0], down_v)]
    at = 0
    for extra in more:
        moves.append((extra, more_v.at[pl.ds(at, extra.shape[0])]))
        at += extra.shape[0]
    copies = [
        pltpu.make_async_copy(src, dst, sems.at[i]) for i, (src, dst) in enumerate(moves)
    ]
    for copy in copies:
        copy.start()
    size = rows.shape[1]
    wanted = lax.broadcasted_iota(jnp.int32, (entries, size), 0)
    picks, weights = [], []
    for c in range(count):
        pick = jnp.where(place[c] == wanted, 1.0, 0.0)
        picks.append(pick.astype(jnp.bfloat16))
        weights.append(jnp.sum(pick * row_gate[c], axis=1, keepdims=True))
        for i in chunk_copies[c]:
            copies[i].wait()
        packed[c * entries : (c + 1) * entries, :] = jnp.dot(
            picks[c], rows[c], preferred_element_type=jnp.float32
        ).astype(jnp.bfloat16)
    copies[total].wait()
    gate = jnp.dot(packed[...], gate_v[...], preferred_element_type=jnp.float32)
    copies[total + 1].wait()
    upper = jnp.dot(packed[...], up_v[...], preferred_element_type=jnp.float32)
    hidden = (silu(gate) * upper).astype(jnp.bfloat16)
    copies[total + 2].wait()
    answer = jnp.dot(hidden, down_v[...], preferred_element_type=jnp.float32).astype(
        jnp.bfloat16
    )
    for i in range(extras):
        copies[total + 3 + i].wait()
    for c in range(count):
        scaled = answer[c * entries : (c + 1) * entries, :].astype(jnp.float32) * weights[c]
        placed = lax.dot_general(
            picks[c],
            scaled.astype(jnp.bfloat16),
            (((0,), (0,)), ((), ())),
            preferred_element_type=jnp.float32,
        )
        if c == 0 and extras:
            placed = placed + more_v[...].astype(jnp.float32)
        placed = placed.astype(jnp.bfloat16)
        cut = size // cuts[c]
        for k in range(cuts[c]):
            outs[sum(cuts[:c]) + k][...] = placed[k * cut : (k + 1) * cut, :]


def routed_expert(chunks, place, row_gate, more, gate_w, up_w, down_w, entries, cuts):
    count = len(chunks)
    parts = [len(chunk) for chunk in chunks]
    total = sum(parts)
    size = sum(piece.shape[0] for piece in chunks[0])
    width = chunks[0][0].shape[1]
    hidden = gate_w.shape[2]
    any_spec = pl.BlockSpec(memory_space=pl.ANY)
    vmem = pl.BlockSpec(memory_space=pltpu.VMEM)
    out_shape = [
        jax.ShapeDtypeStruct((size // n, width), jnp.bfloat16) for n in cuts for k in range(n)
    ]
    more_rows = sum(extra.shape[0] for extra in more) if more else 16
    outs = pl.pallas_call(
        functools.partial(routed_kernel, parts, len(more), entries, cuts),
        out_shape=out_shape,
        in_specs=[any_spec] * total + [vmem] * 2 + [any_spec] * (len(more) + 3),
        out_specs=[vmem] * sum(cuts),
        scratch_shapes=[
            pltpu.VMEM((count, size, width), jnp.bfloat16),
            pltpu.VMEM((count * entries, width), jnp.bfloat16),
            pltpu.VMEM((width, hidden), jnp.bfloat16),
            pltpu.VMEM((width, hidden), jnp.bfloat16),
            pltpu.VMEM((hidden, width), jnp.bfloat16),
            pltpu.VMEM((more_rows, width), jnp.bfloat16),
            pltpu.SemaphoreType.DMA((total + 3 + len(more),)),
        ],
        compiler_params=pltpu.CompilerParams(vmem_limit_bytes=56 * 1024 * 1024),
        cost_estimate=pl.CostEstimate(
            flops=2 * count * entries * (3 * gate_w.size + 2 * size * width),
            bytes_accessed=6 * gate_w.size + 4 * count * size * width,
            transcendentals=count * entries * hidden,
        ),
    )(*[piece for chunk in chunks for piece in chunk], place, row_gate, *more, gate_w, up_w, down_w)
    return [outs[sum(cuts[:c]) : sum(cuts[: c + 1])] for c in range(count)]


def rms_normed(stream, norm_gain):
    scale_row = lax.rsqrt(jnp.mean(stream * stream, axis=1, keepdims=True) + 1e-06)
    return (stream * scale_row * norm_gain[None, :]).astype(jnp.bfloat16)


def shards(
    resid,
    queries,
    cache_key,
    cache_value,
    page_table,
    row_request,
    row_position,
    out_proj,
    norm_gain,
    expert_gate,
    expert_up,
    expert_down,
    shared_gate,
    shared_up,
    shared_down,
    shared_scalar,
    slot_expert,
    route_expert,
    route_gate,
):
    f32, bf16, i32 = jnp.float32, jnp.bfloat16, jnp.int32
    exp_count = lax.axis_size("exp")
    req_count = lax.axis_size("req")
    slot_count = exp_count * req_count
    nc, nx, ny = CORES, exp_count // Z_CHIPS, req_count // CORES
    exp_index = lax.axis_index("exp")
    req_index = lax.axis_index("req")
    own_slot = req_index * exp_count + exp_index
    iz, ix = exp_index // nx, exp_index % nx
    ih, il = iz // 2, iz % 2
    iy, ic = req_index // nc, req_index % nc
    tok_rows, width = resid.shape
    pages_here, page_len, _ = cache_key.shape
    req_slots, max_pages = page_table.shape
    tokens = pages_here * page_len
    capacity = 3 * tok_rows * TOPK // slot_count

    zs = [(dh, dl) for dh in range(2) for dl in range(2)]

    def send(value, dh, dl, dx):
        if not (dh or dl or dx % nx):
            return value
        pairs = [
            (
                (h * 2 + l) * nx + x,
                ((h + dh) % 2 * 2 + (l + dl) % 2) * nx + (x + dx) % nx,
            )
            for h in range(2)
            for l in range(2)
            for x in range(nx)
        ]
        return lax.ppermute(value, "exp", pairs)

    def send_req(value, dy, dc):
        if not (dy % ny or dc % nc):
            return value
        pairs = [
            (y * nc + c, (y + dy) % ny * nc + (c + dc) % nc)
            for y in range(ny)
            for c in range(nc)
        ]
        return lax.ppermute(value, "req", pairs)

    def swap_y(value):
        pairs = [(y * nc + c, (y ^ 1) * nc + c) for y in range(ny) for c in range(nc)]
        return lax.ppermute(value, "req", pairs)

    tie = lax.optimization_barrier

    rel_exp = jnp.stack(
        [
            ((ih + dh) % 2 * 2 + (il + dl) % 2) * nx + (ix - dx) % nx
            for dh, dl in zs
            for dx in range(nx)
        ]
    ).astype(i32)
    rel_req = jnp.stack(
        [((iy - dy) % ny) * nc + (ic - dc) % nc for dy in range(ny) for dc in range(nc)]
    ).astype(i32)

    columns = width // exp_count
    keys = cache_key.reshape(tokens, width)
    values = cache_value.reshape(tokens, width)
    quarter_rows = out_proj.shape[0] // (2 * nc)
    quarter = lax.dynamic_slice_in_dim(
        out_proj, (iy % 2 * nc + ic) * quarter_rows, quarter_rows, 0
    )
    quarter_order = jnp.stack(
        [(iy + dy) % 2 * nc + (ic + dc) % nc for dc in range(nc) for dy in range(2)]
    ).astype(i32)
    far_queries = send(queries, 1, 0, 0)
    members = [(dl, dx) for dl in range(2) for dx in range(nx)]
    member_columns = jnp.stack(
        [
            ((ih + j) % 2 * 2 + (il + dl) % 2) * nx + (ix + dx) % nx
            for dl, dx in members
            for j in range(2)
        ]
    ).astype(i32)
    gates = jnp.transpose(route_gate)
    blocks = pack([keys, values, queries], gates, member_columns, columns)
    blocks = [send(blocks[m], 0, *members[m]) for m in range(len(members))]
    far = list(pack([far_queries], None, member_columns, columns))
    for m in range(1, len(members)):
        if m > 2:
            far[m], far[m - 2] = tie((far[m], far[m - 2]))
        far[m] = send(far[m], 0, *members[m])
    quarters = [send(quarter, 1, 0, 0)]
    page_ids = (
        rel_exp[: len(members), None] * pages_here + jnp.arange(pages_here, dtype=i32)[None, :]
    ).reshape(-1)
    hits = (page_table[None, :, :] == page_ids[:, None, None]).astype(i32)
    page_request = jnp.sum(hits * jnp.arange(req_slots, dtype=i32)[None, :, None], axis=(1, 2))
    page_slot = jnp.sum(hits * jnp.arange(max_pages, dtype=i32)[None, None, :], axis=(1, 2))
    by_place = lambda a: a.reshape(exp_count, tok_rows)[rel_exp].reshape(2, 1, -1)
    row_req, row_pos = by_place(row_request), by_place(row_position)
    gates = [block[2 * tokens + tok_rows :, :tok_rows].astype(f32) for block in blocks]
    gates = jnp.stack([g[:TOPK] + g[TOPK : 2 * TOPK] + g[2 * TOPK : 3 * TOPK] for g in gates])
    gates = gates.reshape(2, nx, TOPK, tok_rows)

    slot_ids = jnp.arange(slot_count, dtype=i32)
    own_mark = slot_ids == own_slot
    own_expert = jnp.sum(jnp.where(own_mark, slot_expert, 0))
    twins = slot_expert == own_expert
    copies = jnp.sum(twins.astype(i32))
    own_rank = jnp.sum((twins & (slot_ids < own_slot)).astype(i32))
    order = [1, 3, 2, 0]
    rel_rows = jnp.stack([rel_exp.reshape(4, nx)[i] for i in order], axis=1).reshape(-1)
    rel_slots = (rel_req[:, None] * exp_count + rel_rows[None, :]).reshape(-1)
    named = (route_expert == own_expert).reshape(slot_count, tok_rows, TOPK)[rel_slots]
    named = jnp.transpose(named, (0, 2, 1))
    chunk_rows = exp_count * tok_rows
    entries = -(-exp_count * capacity // 16) * 16
    served = jnp.any(named, axis=1) & (rel_slots % copies == own_rank)[:, None]
    served = served.reshape(ny, nc, chunk_rows)
    place = jnp.where(served, jnp.cumsum(served.astype(i32), axis=2) - 1, -1)
    place = place.reshape(ny, nc, 1, chunk_rows)

    place, named, blocks = tie((place, named, blocks))

    def attend_half(side, queries):
        return attend(
            blocks,
            queries,
            row_req[side],
            row_pos[side],
            page_request,
            page_slot,
            page_len,
            tokens,
            tok_rows,
        )

    quarters.append(swap_y(quarters[0]))
    theirs, their_level = attend_half(1, far)
    theirs, their_level, quarters = tie((theirs, their_level, quarters))
    theirs, their_level = send(theirs, 1, 0, 0), send(their_level, 1, 0, 0)
    quarters += [send_req(q, 0, dc) for dc in range(1, nc) for q in quarters[:2]]
    mine, level = attend_half(0, [])
    mine, level, gates, quarters = tie((mine, level, gates, quarters))
    gates = jnp.stack([send(gates, dh, 0, 0) for dh in range(2)])
    theirs, their_level, gates = tie((theirs, their_level, gates))

    stays, comes = {}, {}
    proj = out_proj
    for dl in (1, 0):
        stays[dl], go = project(
            dl, quarter_order, mine, level, theirs, their_level, proj, quarters, tok_rows
        )
        comes[dl] = [
            send(go[(dx - 1) * tok_rows : dx * tok_rows], 0, 0, -dx) for dx in range(1, nx)
        ]
        proj, _ = tie((proj, go))
    line = sum([come.astype(f32) for come in comes[1]], stays[1]).astype(bf16)
    comes[0], _ = tie((comes[0], line))
    line = send(line, 0, 1, 0)
    stream = sum([come.astype(f32) for come in comes[0]], resid.astype(f32) + stays[0])
    stream = stream + line.astype(f32)
    gates = jnp.stack([send_req(gates, dy, 0) for dy in range(ny)])
    stream, gates = tie((stream, gates))
    normed = rms_normed(stream, norm_gain)
    gates = jnp.stack([send_req(gates, 0, dc) for dc in range(nc)], axis=1)
    gates = gates.reshape(ny, nc, 4, nx, TOPK, tok_rows)
    gates = jnp.stack([gates[:, :, i] for i in order], axis=3)
    gates = gates.reshape(slot_count, TOPK, tok_rows)
    row_gate = jnp.sum(jnp.where(named, gates, 0.0), axis=1).reshape(ny, nc, 1, chunk_rows)

    far_line = send(normed, 1, 0, 0)
    line = [normed, send(normed, 0, 1, 0), far_line, send(far_line, 0, 1, 0)]
    over_y = {(i, dy): send_req(line[i], dy, 0) for i in order for dy in range(1, ny)}
    over_x = {(i, dx): send(line[i], 0, 0, dx) for i in order for dx in range(1, nx)}

    halves = [[line[i] for i in order]]
    shared_weights = (shared_scalar, shared_gate.T, shared_up.T, shared_down)
    shared = [shared_expert(halves[0], *shared_weights)]
    chunks = {(0, 0): join(halves[0])}
    for dc in range(1, nc):
        chunks[0, dc] = [send_req(chunks[0, 0][0], 0, dc)]
    over_y, over_x, shared, row_gate = tie((over_y, over_x, shared, row_gate))
    halves += [[over_x[i, dx] for i in order] for dx in range(1, nx)]
    joined = join(*halves[1:], *[[over_y[i, dy] for i in order] for dy in range(1, ny)])
    chunks[0, 0] += joined[: nx - 1]
    for dc in range(1, nc):
        chunks[0, dc] += [send_req(half, 0, dc) for half in joined[: nx - 1]]
    for dy, half in enumerate(joined[nx - 1 :], 1):
        chunks[dy, 0] = [half] + [send(half, 0, 0, dx) for dx in range(1, nx)]
        for dc in range(1, nc):
            chunks[dy, dc] = [send_req(half, 0, dc)]

    def answers_of(dy, dcs, more, cuts):
        return routed_expert(
            [chunks[dy, dc] for dc in dcs],
            jnp.concatenate([place[dy, dc : dc + 1] for dc in dcs]),
            jnp.concatenate([row_gate[dy, dc : dc + 1] for dc in dcs]),
            more,
            expert_gate,
            expert_up,
            expert_down,
            entries,
            cuts,
        )

    def add_up(parts):
        return sum([part.astype(f32) for part in parts[1:]], parts[0].astype(f32))

    cores = list(range(nc))
    kept, comes = {}, {}
    cuts = [slice(0, 3 * tok_rows), slice(3 * tok_rows, 4 * tok_rows)]
    for dy in range(ny - 1):
        answers = answers_of(dy, cores, [], [nx] * nc)
        if dy:
            answers, comes[dy - 1] = tie((answers, comes[dy - 1]))
        others = [[send_req(part, 0, -dc) for part in answers[dc][::-1]][::-1] for dc in cores[1:]]
        parts = [answers[0]] + others
        if dy:
            following = answers[0][0]
        else:
            for dx in range(1, nx):
                halves[dx], _ = tie((halves[dx], answers[0]))
                shared.append(shared_expert(halves[dx], *shared_weights))
            parts.append(shared)
            following = shared[-1]
        chunks[dy + 1, 0], _ = tie((chunks[dy + 1, 0], following))
        for dc in range(1, nc):
            chunks[dy + 1, dc] += [send_req(part, 0, dc) for part in chunks[dy + 1, 0][1:]]
        gone = [add_up([part[dx] for part in parts]).astype(bf16) for dx in range(1, nx)]
        kept[dy] = [part[0] for part in parts]
        waiting = [go[cuts[1]] for go in gone]
        comes[dy] = [
            [send(go[rows], 0, 0, -dx) for dx, go in enumerate(gone, 1)]
            for rows in (cuts if dy + 2 < ny else cuts[:1])
        ]
        following = [chunks[dy + 1, dc] for dc in cores]
        following, _ = tie((following, gone))
        for dc in cores:
            chunks[dy + 1, dc] = following[dc]
    end = ny - 1
    answers = answers_of(end, cores, [], [4 * nx] + [nx] * (nc - 1))
    answers, comes, kept = tie((answers, comes, kept))
    answer = answers[0]
    others = [[send_req(part, 0, -dc) for part in answers[dc][::-1]][::-1] for dc in cores[1:]]

    turns = [1, 2, 0, 3]
    block = lambda a, p: a[p * tok_rows : (p + 1) * tok_rows]
    last = {}
    for p in turns:
        gone = [
            add_up([answer[4 * dx + p]] + [block(other[dx], p) for other in others])
            for dx in range(1, nx)
        ]
        gone = [go.astype(bf16) for go in gone]
        last[p] = [send(go, 0, 0, -dx) for dx, go in enumerate(gone, 1)]
        others, _ = tie((others, gone))
    waiting, _ = tie((waiting, gone))
    comes[end - 1].append([send(go, 0, 0, -dx) for dx, go in enumerate(waiting, 1)])

    def line_of(dy, p):
        if dy < end:
            arrived = [come if p == 3 else block(come, p) for come in comes[dy][p // 3]]
            return add_up([block(part, p) for part in kept[dy]] + arrived)
        return add_up([answer[p]] + [block(other[0], p) for other in others] + last[p])

    home, near = {}, {}
    for turn, p in enumerate(turns):
        goes = [line_of(dy, p).astype(bf16) for dy in range(1, ny)]
        home[p] = [send_req(go, -dy, 0) for dy, go in enumerate(goes, 1)]
        if turn == 1:
            go = add_up([line_of(0, 1)] + home[1]).astype(bf16)
            near[1] = send(go, 0, 1, 0)
            goes.append(go)
        if turn + 1 < len(turns):
            after = turns[turn + 1]
            last[after], _ = tie((last[after], goes))
    far = add_up([line_of(0, 2)] + home[2] + [near[1]]).astype(bf16)
    home[0], _ = tie((home[0], far))
    far = send(far, 1, 0, 0)
    near[0] = send(add_up([line_of(0, 0)] + home[0]).astype(bf16), 0, 1, 0)
    total = add_up([stream, line_of(0, 3)] + home[3] + [near[0], far])
    return total.astype(bf16)


def solution(mesh):
    placed = (
        P(("req", "exp"), None),
        P(("req", "exp"), None),
        P(("req", "exp"), None, None),
        P(("req", "exp"), None, None),
        P("req", None),
        P("req"),
        P("req"),
        P("exp", None),
        P(),
        P(("req", "exp"), None, None),
        P(("req", "exp"), None, None),
        P(("req", "exp"), None, None),
        P(None, "exp"),
        P(None, "exp"),
        P("exp", None),
        P(),
        P(),
        P(),
        P(("req", "exp"), None),
    )
    return jax.shard_map(
        shards, mesh=mesh, in_specs=placed, out_specs=P(("req", "exp"), None), check_vma=False
    )
```
